32 devices in a mesh: dp: 16 (over z, y, x), head: 2 (over core).
Axes of the slice: x: 2, y: 2, z: 4, core: 2. Of those that a mesh axis runs over, the one named last changes fastest.
Arguments:
- tokens: bfloat16 [98304, 384], P(('dp', 'head')), may hold values from -6 to 6
- grad_out: bfloat16 [98304, 384], P(('dp', 'head')), may hold values from -6 to 6
- segments: int32 [96, 1024], P('dp'), may hold values from 0 to 7, as said below
- counts: int32 [96], P('dp'), may hold values from 1 to 6
- attn_w: float32 [4, 384, 384], P(None, 'dp', 'head')
- attn_m: float32 [4, 384, 384], P(None, 'dp', 'head')
- attn_v: float32 [4, 384, 384], P(None, 'dp', 'head')
- mlp_w: float32 [2, 384, 1536], P(None, 'dp', 'head')
- mlp_m: float32 [2, 384, 1536], P(None, 'dp', 'head')
- mlp_v: float32 [2, 384, 1536], P(None, 'dp', 'head')
- conv_w: float32 [9, 1536], P(None, 'head')
- conv_m: float32 [9, 1536], P(None, 'head')
- conv_v: float32 [9, 1536], P(None, 'head')
- norm_w: float32 [4, 384], replicated
- norm_m: float32 [4, 384], replicated
- norm_v: float32 [4, 384], replicated
Outputs:
- output: bfloat16 [98304, 384], P(('dp', 'head'))
- grad_tokens: float32 [98304, 384], P(('dp', 'head'))
- new_attn_w: float32 [4, 384, 384], P(None, 'dp', 'head')
- new_attn_m: float32 [4, 384, 384], P(None, 'dp', 'head')
- new_attn_v: float32 [4, 384, 384], P(None, 'dp', 'head')
- new_mlp_w: float32 [2, 384, 1536], P(None, 'dp', 'head')
- new_mlp_m: float32 [2, 384, 1536], P(None, 'dp', 'head')
- new_mlp_v: float32 [2, 384, 1536], P(None, 'dp', 'head')
- new_conv_w: float32 [9, 1536], P(None, 'head')
- new_conv_m: float32 [9, 1536], P(None, 'head')
- new_conv_v: float32 [9, 1536], P(None, 'head')
- new_norm_w: float32 [4, 384], replicated
- new_norm_m: float32 [4, 384], replicated
- new_norm_v: float32 [4, 384], replicated
The draws below stay inside these ranges and needn't reach their ends.
Inputs may be any that keep to these rules, and one draw needn't show every extreme that they name: `segments`: within each packed row of 1024 tokens the ids start at 0 and grow by one at the first token of each image; an image is a run of whole grid rows of 16 tokens, and every row holds exactly 8 images.
All inputs are finite; a program needn't handle non-finite values.
Results may differ from the reference program's by a relative error of at most 0.012.
Values may be sent and summed in bfloat16 or wider, within the bound.
No kernel may reach another device: no remote copies, remote signals or barrier semaphores. Data moves between devices by JAX's collectives and lax.ppermute only.
A program may use at most 640 MiB of HBM per device.

```python
import jax
import jax.numpy as jnp
from jax import lax

D = 384
HEADS = 6
HEAD_DIM = 64
FF = 1536
GRID_W = 16
ROW_LEN = 1024
ROWS_DEV = 6
STEP = 10
IMAGES = 8
TOK_DEV = 6144
ROWS = 96
TOKENS = 98304
N_DP = 16


def rising(extent, low_end, high_end):
    return low_end + (high_end - low_end) * jnp.arange(extent, dtype=jnp.float32) / extent


def first_moment(key, shape, scale):
    return jnp.clip(jax.random.normal(key, shape, jnp.float32), -4.0, 4.0) * (scale / 9.0)


def second_moment(key, shape, scale):
    spread = jax.random.uniform(key, shape, jnp.float32, minval=0.6, maxval=1.4)
    return spread * (scale * scale / 999.0)


def draw_segments(key, part):
    key = jax.random.fold_in(key, 1)
    grid_rows = ROW_LEN // GRID_W
    row_keys = jax.random.split(key, ROWS)
    orders = jax.vmap(lambda row_key: jax.random.permutation(row_key, grid_rows - 1))(row_keys)
    later_starts = orders < IMAGES - 1
    starts = jnp.concatenate([jnp.ones((ROWS, 1), jnp.int32), later_starts.astype(jnp.int32)], axis=1)
    image_ids = jnp.cumsum(starts, axis=1) - 1
    return jnp.repeat(image_ids, GRID_W, axis=1).astype(jnp.int32)


def draw_attn_w(key, part):
    key = jax.random.fold_in(key, 2)
    base = jnp.clip(jax.random.normal(key, (4, D, D), jnp.float32), -4.0, 4.0)
    scales = jnp.array([1.0, 1.0, 1.0, 4.0], jnp.float32)[:, None, None] * D ** (-0.5)
    return base * scales * rising(D, 0.75, 1.3)[None, :, None]


def draw_attn_m(key, part):
    key = jax.random.fold_in(key, 3)
    return first_moment(key, (4, D, D), 0.3 * TOKENS ** 0.5)


def draw_attn_v(key, part):
    key = jax.random.fold_in(key, 4)
    return second_moment(key, (4, D, D), 0.3 * TOKENS ** 0.5) * rising(D, 4.0, 1.0)[None, :, None]


def draw_mlp_w(key, part):
    key = jax.random.fold_in(key, 5)
    base = jnp.clip(jax.random.normal(key, (2, D, FF), jnp.float32), -4.0, 4.0)
    scales = jnp.array([D ** (-0.5), FF ** (-0.5)], jnp.float32)[:, None, None]
    return base * scales * rising(D, 0.75, 1.3)[None, :, None]


def draw_mlp_m(key, part):
    key = jax.random.fold_in(key, 6)
    scales = jnp.array([0.4, 0.8], jnp.float32)[:, None, None]
    return first_moment(key, (2, D, FF), TOKENS ** 0.5) * scales


def draw_mlp_v(key, part):
    key = jax.random.fold_in(key, 7)
    scales = jnp.array([0.16, 0.64], jnp.float32)[:, None, None]
    return second_moment(key, (2, D, FF), TOKENS ** 0.5) * scales * rising(D, 4.0, 1.0)[None, :, None]


def draw_conv_w(key, part):
    key = jax.random.fold_in(key, 8)
    base = jnp.clip(jax.random.normal(key, (9, FF), jnp.float32), -4.0, 4.0)
    return base * 0.25


def draw_conv_m(key, part):
    key = jax.random.fold_in(key, 9)
    return first_moment(key, (9, FF), 0.4 * TOKENS ** 0.5)


def draw_conv_v(key, part):
    key = jax.random.fold_in(key, 10)
    return second_moment(key, (9, FF), 0.4 * TOKENS ** 0.5) * 2.0


def draw_norm_w(key, part):
    key = jax.random.fold_in(key, 11)
    base = jnp.clip(jax.random.normal(key, (4, D), jnp.float32), -4.0, 4.0)
    gains = rising(D, 0.7, 1.3)[None, :] * (1.0 + 0.12 * base)
    biases = 0.5 * base
    is_gain = jnp.array([1.0, 0.0, 1.0, 0.0], jnp.float32)[:, None]
    return is_gain * gains + (1.0 - is_gain) * biases


def draw_norm_m(key, part):
    key = jax.random.fold_in(key, 12)
    return first_moment(key, (4, D), 0.5 * TOKENS ** 0.5)


def draw_norm_v(key, part):
    key = jax.random.fold_in(key, 13)
    return second_moment(key, (4, D), 0.5 * TOKENS ** 0.5) * 2.0


def with_ends(values, own_key, smallest, high):
    index_at = [jax.random.randint(jax.random.fold_in(own_key, axis), (), 0, length) for axis, length in enumerate(values.shape)]
    widest = values.shape.index(max(values.shape))
    beside = index_at[:widest] + [(index_at[widest] + 1) % values.shape[widest]] + index_at[widest + 1:]
    return values.at[tuple(index_at)].set(smallest).at[tuple(beside)].set(high)


def levels(key, shape, cuts, least, top_value):
    def one(position, shards_of):
        heights = jax.random.uniform(jax.random.fold_in(jax.random.fold_in(key, 6), position), (shards_of,), jnp.float32, least / len(cuts), top_value / len(cuts))
        return jnp.repeat(jnp.exp(heights), shape[position] // shards_of).reshape((-1,) + (1,) * (len(shape) - position - 1))

    factor_of = one(*cuts[0])
    for cut in cuts[1:]:
        factor_of = factor_of * one(*cut)
    return factor_of


def gaussian(key, dims, scale, limit, shards=(), held_as=jnp.bfloat16):
    loudness = levels(key, dims, shards, -0.22, 0.18) if shards else 1.0
    values = jax.random.normal(key, dims, jnp.float32) * scale * loudness
    return jnp.minimum(jnp.maximum(values, -limit), limit).astype(held_as)


def setup_inputs(seed: int = 0) -> dict:
    keys = jax.random.split(jax.random.key(seed), 17)
    return {
        "tokens": gaussian(keys[0], (TOKENS, D), 1.0, 6.0, ((0, 32),)),
        "grad_out": gaussian(keys[1], (TOKENS, D), 1.0, 6.0, ((0, 32),)),
        "segments": draw_segments(jax.random.fold_in(keys[16], 71), 0),
        "counts": with_ends(jax.random.randint(keys[3], (ROWS,), 1, HEADS + 1), jax.random.fold_in(keys[3], 1), 1, HEADS).astype(jnp.int32),
        "attn_w": draw_attn_w(jax.random.fold_in(keys[16], 71), 0),
        "attn_m": draw_attn_m(jax.random.fold_in(keys[16], 71), 0),
        "attn_v": draw_attn_v(jax.random.fold_in(keys[16], 71), 0),
        "mlp_w": draw_mlp_w(jax.random.fold_in(keys[16], 71), 0),
        "mlp_m": draw_mlp_m(jax.random.fold_in(keys[16], 71), 0),
        "mlp_v": draw_mlp_v(jax.random.fold_in(keys[16], 71), 0),
        "conv_w": draw_conv_w(jax.random.fold_in(keys[16], 71), 0),
        "conv_m": draw_conv_m(jax.random.fold_in(keys[16], 71), 0),
        "conv_v": draw_conv_v(jax.random.fold_in(keys[16], 71), 0),
        "norm_w": draw_norm_w(jax.random.fold_in(keys[16], 71), 0),
        "norm_m": draw_norm_m(jax.random.fold_in(keys[16], 71), 0),
        "norm_v": draw_norm_v(jax.random.fold_in(keys[16], 71), 0),
    }


HIGHEST = lax.Precision.HIGHEST
NORM_EPS = 1e-06
NEG_LARGE = -1e+30
BETA_ONE = 0.9
BETA_TWO = 0.999
ADAM_EPS = 1e-06
DECAY = 0.01
RATE = 0.5

@jax.custom_vjp
def low(v):
    return lax.optimization_barrier(v.astype(jnp.bfloat16)).astype(jnp.float32)

@jax.custom_vjp
def low_back(v):
    return v

def low_keep(v):
    return (low(v), None)

def low_pass(kept, grad):
    return (grad,)

def back_keep(v):
    return (v, None)

def back_low(kept, grad):
    return (low(grad),)
low.defvjp(low_keep, low_pass)
low_back.defvjp(back_keep, back_low)

def norm_rows(values, gain_row, bias_row):
    average = lax.optimization_barrier(jnp.mean(values, axis=-1, keepdims=True))
    centered = values - average
    variance = lax.optimization_barrier(jnp.mean(centered * centered, axis=-1, keepdims=True))
    return centered * lax.rsqrt(variance + NORM_EPS) * gain_row + bias_row

def shifted(values, offset):
    if offset == 0:
        return values
    padding = jnp.zeros_like(values[:, :abs(offset)])
    if offset > 0:
        return jnp.concatenate([values[:, offset:], padding], axis=1)
    return jnp.concatenate([padding, values[:, :offset]], axis=1)

def build_masks(segments):
    length = segments.shape[1]
    column = jnp.arange(length, dtype=jnp.int32) % GRID_W
    tagged = segments + 1
    tap_mask = []
    for row_step in (-1, 0, 1):
        for col_step in (-1, 0, 1):
            offset = row_step * GRID_W + col_step
            inside = (column + col_step >= 0) & (column + col_step < GRID_W)
            same_image = shifted(tagged, offset) == tagged
            tap_mask.append((same_image & inside[None, :]).astype(jnp.float32))
    return jnp.stack(tap_mask)

def depthwise(hidden, tap_weights, tap_mask):
    summed = hidden
    tap_index = 0
    for row_step in (-1, 0, 1):
        for col_step in (-1, 0, 1):
            offset = row_step * GRID_W + col_step
            summed = summed + tap_weights[tap_index] * tap_mask[tap_index][:, :, None] * shifted(hidden, offset)
            tap_index += 1
    return summed

def attend_row(row_item):
    projected_row, segment_row, count_row = row_item
    score_scale = HEAD_DIM ** (-0.5)
    scores = jnp.einsum('qhe,khe->hqk', projected_row[:, 0], projected_row[:, 1], precision=HIGHEST) * score_scale
    scores = low_back(scores)
    same_image = segment_row[:, None] == segment_row[None, :]
    scores = jnp.where(same_image[None], scores, NEG_LARGE)
    probability = low(jax.nn.softmax(scores, axis=-1))
    context = jnp.einsum('hqk,khe->qhe', probability, projected_row[:, 2], precision=HIGHEST)
    active = (jnp.arange(HEADS, dtype=jnp.int32) < count_row).astype(jnp.float32)
    return context * active[None, :, None]

def layer(tokens, attn_use, mlp_use, conv_use, norm_use, segments, counts):
    row_count = segments.shape[0]
    normed_one = low(norm_rows(tokens, norm_use[0], norm_use[1]))
    projected = jnp.einsum('td,kde->tke', normed_one, attn_use[:3], precision=HIGHEST)
    projected = low_back(low(projected)).reshape(row_count, ROW_LEN, 3, HEADS, HEAD_DIM)
    context = lax.map(jax.checkpoint(attend_row), (projected, segments, counts))
    context = low_back(low(context.reshape(row_count * ROW_LEN, D)))
    attn_out = low_back(jnp.einsum('tj,dj->td', context, attn_use[3], precision=HIGHEST))
    middle = tokens + attn_out
    normed_two = low(norm_rows(middle, norm_use[2], norm_use[3]))
    hidden = low_back(jnp.dot(normed_two, mlp_use[0], precision=HIGHEST))
    mixed_rows = depthwise(hidden.reshape(row_count, ROW_LEN, FF), conv_use, build_masks(segments))
    activated = low(jax.nn.gelu(mixed_rows).reshape(row_count * ROW_LEN, FF))
    mlp_out = low_back(jnp.einsum('tf,df->td', activated, mlp_use[1], precision=HIGHEST))
    return middle + mlp_out

def adam_terms(grad_sum, first_old, second):
    first_new = BETA_ONE * first_old + (1.0 - BETA_ONE) * grad_sum
    second_new = BETA_TWO * second + (1.0 - BETA_TWO) * grad_sum * grad_sum
    direction = first_new / (1.0 - BETA_ONE ** STEP) / (jnp.sqrt(second_new / (1.0 - BETA_TWO ** STEP)) + ADAM_EPS)
    return (first_new, second_new, direction)

def lamb_matrix(weight, grad_sum, first_old, second, axes):
    first_new, second_new, direction = adam_terms(grad_sum, first_old, second)
    update = direction + DECAY * weight
    ratio = jnp.sqrt(lax.optimization_barrier(jnp.sum(weight * weight, axis=axes, keepdims=True))) / jnp.sqrt(lax.optimization_barrier(jnp.sum(update * update, axis=axes, keepdims=True)))
    return (weight - RATE * ratio * update, first_new, second_new)

def reference(tokens, grad_out, segments, counts, attn_w, attn_m, attn_v, mlp_w, mlp_m, mlp_v, conv_w, conv_m, conv_v, norm_w, norm_m, norm_v):
    attn_use = attn_w.astype(jnp.bfloat16).astype(jnp.float32)
    mlp_use = mlp_w.astype(jnp.bfloat16).astype(jnp.float32)
    conv_use = conv_w.astype(jnp.bfloat16).astype(jnp.float32)
    token_groups = tokens.astype(jnp.float32).reshape(N_DP, TOK_DEV, D)
    grad_groups = grad_out.astype(jnp.float32).reshape(N_DP, TOK_DEV, D)
    seg_groups = segments.reshape(N_DP, ROWS_DEV, ROW_LEN)
    count_groups = counts.reshape(N_DP, ROWS_DEV)

    def one_group(running, group_data):
        part_tokens, part_grad, part_seg, part_count = group_data

        def forward(token_rows, attn_rows, mlp_rows, conv_rows, norm_rows_in):
            return layer(token_rows, attn_rows, mlp_rows, conv_rows, norm_rows_in, part_seg, part_count)
        result, pullback = jax.vjp(forward, part_tokens, attn_use, mlp_use, conv_use, norm_w)
        gradients = pullback(part_grad)
        running = tuple((total_old + fresh for total_old, fresh in zip(running, gradients[1:])))
        return (running, (result.astype(jnp.bfloat16), gradients[0]))
    initial = (jnp.zeros(attn_w.shape, jnp.float32), jnp.zeros(mlp_w.shape, jnp.float32), jnp.zeros(conv_w.shape, jnp.float32), jnp.zeros(norm_w.shape, jnp.float32))
    summed, (outputs, grad_tokens) = lax.scan(one_group, initial, (token_groups, grad_groups, seg_groups, count_groups))
    grad_attn, grad_mlp, grad_conv, grad_norms = summed
    new_attn_w, new_attn_m, new_attn_v = lamb_matrix(attn_w, grad_attn, attn_m, attn_v, (1, 2))
    new_mlp_w, new_mlp_m, new_mlp_v = lamb_matrix(mlp_w, grad_mlp, mlp_m, mlp_v, (1, 2))
    new_conv_w, new_conv_m, new_conv_v = lamb_matrix(conv_w, grad_conv, conv_m, conv_v, (0, 1))
    new_norm_m, new_norm_v, norm_direction = adam_terms(grad_norms, norm_m, norm_v)
    new_norm_w = norm_w - RATE * norm_direction
    return (outputs.reshape(TOKENS, D), grad_tokens.reshape(TOKENS, D), new_attn_w, new_attn_m, new_attn_v, new_mlp_w, new_mlp_m, new_mlp_v, new_conv_w, new_conv_m, new_conv_v, new_norm_w, new_norm_m, new_norm_v)
```

```python
import functools
import jax
import jax.numpy as jnp
from jax import lax
from jax.experimental import pallas as pl
from jax.experimental.pallas import tpu as pltpu
from jax.sharding import PartitionSpec as P

HEAD_DIM = 64
GRID_W = 16
STEP = 10
IMAGES = 8

NORM_EPS = 1e-06
BETA_ONE = 0.9
BETA_TWO = 0.999
ADAM_EPS = 1e-06
DECAY = 0.01
RATE = 0.5
LOG2E = 1.4426950408889634
LN2 = 0.6931471805599453
BIG = 2.0**100
GELU_ONE = 0.7978845608028654
GELU_TWO = 0.044715
TILE = 128
LANES = 128
VMEM_BYTES = 60 * 1024 * 1024

f32 = jnp.float32
bf16 = jnp.bfloat16
NN = (((1,), (0,)), ((), ()))
NT = (((1,), (1,)), ((), ()))
TN = (((0,), (0,)), ((), ()))


def dot(left, right, dims=NN):
    return lax.dot_general(left, right, dims, preferred_element_type=f32)


def widths_for(length):
    return [w for w in (256, 384, 512, 768) if w < length] + [length]


def lane_iota(rows):
    return lax.broadcasted_iota(jnp.int32, (rows, LANES), 1)


def norm_parts(values):
    average = jnp.mean(values, axis=-1, keepdims=True)
    centered = values - average
    inverse = lax.rsqrt(jnp.mean(centered * centered, axis=-1, keepdims=True) + NORM_EPS)
    return centered * inverse, inverse


def norm_back(upstream, gain_row, unit_rows, inverse):
    grad_unit = upstream * gain_row
    first_term = jnp.mean(grad_unit, axis=-1, keepdims=True)
    second_term = jnp.mean(grad_unit * unit_rows, axis=-1, keepdims=True)
    return inverse * (grad_unit - first_term - unit_rows * second_term)


def fold_rows(values):
    rows, columns = values.shape
    return jnp.sum(values.reshape(rows // 8, 8, columns), axis=0)


def half_masks():
    lane = lax.broadcasted_iota(jnp.int32, (1, LANES), 1)
    first = (lane < HEAD_DIM).astype(f32).astype(bf16)
    second = (lane >= HEAD_DIM).astype(f32).astype(bf16)
    return first, second


def split_lanes(column, lane, at):
    high = column.astype(bf16).astype(f32)
    rest = column - high
    middle = rest.astype(bf16).astype(f32)
    low = rest - middle
    return jnp.where(lane == at, high, jnp.where(lane == at + 1, middle, jnp.where(lane == at + 2, low, 0.0)))


def attn_forward_kernel(
    start_ref, class_ref, count_ref, tokens_ref, w_ref, norm_ref, image_ref,
    middle_ref, qkv_ref, context_ref, ext_ref, tag_ref,
):
    row = pl.program_id(0)
    length, width = tokens_ref.shape
    pairs = width // LANES
    big = 256
    gain, bias = norm_ref[0:1, :], norm_ref[1:2, :]
    first_row, last_row = image_ref[0, 0:1, :], image_ref[0, 1:2, :]

    def project(step, carry):
        rows = pl.ds(pl.multiple_of(step * big, big), big)
        unit, _ = norm_parts(tokens_ref[rows, :].astype(f32))
        normed = (unit * gain + bias).astype(bf16)
        for k in range(3):
            product = dot(normed, w_ref[k])
            if k == 0:
                product = product * (HEAD_DIM**-0.5 * LOG2E)
            qkv_ref[rows, k * width : (k + 1) * width] = product.astype(bf16)
        place = step * big + lax.broadcasted_iota(jnp.int32, (big, LANES), 0)
        inside = (place >= first_row) & (place < last_row)
        tag_ref[rows, :] = jnp.where(inside, 1.0, 0.0).astype(bf16)
        return carry

    lax.fori_loop(0, length // big, project, 0)
    first_half, second_half = half_masks()

    def tile(step, carry):
        q0 = pl.multiple_of(step * TILE, TILE)
        here = pl.ds(q0, TILE)

        def attend(window):
            there = pl.ds(pl.multiple_of(start_ref[row, step], GRID_W), window)
            lane = lane_iota(TILE)
            tags = tag_ref[there, :]
            base = jnp.where(lane < IMAGES, (tag_ref[here, :].astype(f32) - 1.0) * BIG, 0.0)
            base_low = base.astype(bf16)
            for p in range(pairs):
                at = slice(p * LANES, (p + 1) * LANES)
                queries = qkv_ref[here, at]
                keys = qkv_ref[there, width + p * LANES : width + (p + 1) * LANES]
                values = qkv_ref[there, 2 * width + p * LANES : 2 * width + (p + 1) * LANES]
                left = jnp.concatenate(
                    [
                        jnp.concatenate([queries * first_half, base_low], axis=1),
                        jnp.concatenate([queries * second_half, base_low], axis=1),
                    ],
                    axis=0,
                )
                scores = dot(left, jnp.concatenate([keys, tags], axis=1), NT)
                row_max = jnp.max(scores, axis=1, keepdims=True)
                exponent = jnp.exp2(scores - row_max).astype(bf16)
                mixed = dot(exponent, jnp.concatenate([values, tags], axis=1))
                total = mixed[:, LANES + IMAGES : LANES + IMAGES + 1]
                minus_lse = -(row_max + jnp.log(total) * LOG2E)
                scale = 1.0 / total
                active_one = jnp.where(2 * p < count_ref[row], 1.0, 0.0)
                active_two = jnp.where(2 * p + 1 < count_ref[row], 1.0, 0.0)
                context = jnp.where(
                    lane < HEAD_DIM,
                    mixed[:TILE, :LANES] * (scale[:TILE] * active_one),
                    mixed[TILE:, :LANES] * (scale[TILE:] * active_two),
                )
                context_ref[here, at] = context.astype(bf16)
                base = base + split_lanes(minus_lse[:TILE], lane, IMAGES + 6 * p)
                base = base + split_lanes(minus_lse[TILE:], lane, IMAGES + 6 * p + 3)
            ext_ref[here, :] = base.astype(bf16)

        for index, window in enumerate(widths_for(length)):
            pl.when(class_ref[row, step] == index)(functools.partial(attend, window))
        return carry

    lax.fori_loop(0, length // TILE, tile, 0)

    def finish(step, carry):
        rows = pl.ds(pl.multiple_of(step * big, big), big)
        middle_ref[rows, :] = tokens_ref[rows, :].astype(f32) + dot(context_ref[rows, :], w_ref[3], NT)
        return carry

    lax.fori_loop(0, length // big, finish, 0)


def attn_forward(starts, classes, counts, tokens, attn_use, norm_w, images):
    rows_all, width = tokens.shape
    row_count = counts.shape[0]
    length = rows_all // row_count
    by_row = lambda columns: pl.BlockSpec((length, columns), lambda r, *_: (r, 0))
    return pl.pallas_call(
        attn_forward_kernel,
        grid_spec=pltpu.PrefetchScalarGridSpec(
            num_scalar_prefetch=3,
            grid=(row_count,),
            in_specs=[
                by_row(width),
                pl.BlockSpec(attn_use.shape, lambda r, *_: (0, 0, 0)),
                pl.BlockSpec(norm_w.shape, lambda r, *_: (0, 0)),
                pl.BlockSpec((1, 8, LANES), lambda r, *_: (r, 0, 0)),
            ],
            out_specs=[by_row(width), by_row(3 * width), by_row(width), by_row(LANES)],
            scratch_shapes=[pltpu.VMEM((length, LANES), bf16)],
        ),
        out_shape=[
            jax.ShapeDtypeStruct((rows_all, width), f32),
            jax.ShapeDtypeStruct((rows_all, 3 * width), bf16),
            jax.ShapeDtypeStruct((rows_all, width), bf16),
            jax.ShapeDtypeStruct((rows_all, LANES), bf16),
        ],
        compiler_params=pltpu.CompilerParams(vmem_limit_bytes=VMEM_BYTES),
    )(starts, classes, counts, tokens, attn_use, norm_w, images)


def attn_backward_kernel(
    start_ref, class_ref, count_ref, tokens_ref, middle_grad_ref, qkv_ref, context_ref, ext_ref, w_ref, norm_ref, image_ref,
    tokens_grad_ref, w_grad_ref, norm_grad_ref,
    tag_ref, up_ref, delta_ref, normed_ref, dq_ref, dk_ref, dv_ref, low_ref, proj_ref,
):
    row = pl.program_id(0)
    length, width = tokens_ref.shape
    pairs = width // LANES
    heads = 2 * pairs
    big = 256
    gain, bias = norm_ref[0:1, :], norm_ref[1:2, :]
    first_row, last_row = image_ref[0, 0:1, :], image_ref[0, 1:2, :]

    @pl.when(row == 0)
    def _():
        w_grad_ref[...] = jnp.zeros_like(w_grad_ref)
        norm_grad_ref[...] = jnp.zeros_like(norm_grad_ref)

    source = lax.broadcasted_iota(jnp.int32, (width, LANES), 0)
    target = lax.broadcasted_iota(jnp.int32, (width, LANES), 1) - IMAGES
    low_edge = source // HEAD_DIM * 3
    collect = jnp.where((target >= low_edge) & (target < low_edge + 3), 1.0, 0.0).astype(bf16)
    active = jnp.where(
        lax.broadcasted_iota(jnp.int32, (1, width), 1) // HEAD_DIM < count_ref[row], 1.0, 0.0
    )

    def prepare(step, carry):
        rows = pl.ds(pl.multiple_of(step * big, big), big)
        unit, _ = norm_parts(tokens_ref[rows, :].astype(f32))
        normed_ref[rows, :] = (unit * gain + bias).astype(bf16)
        place = step * big + lax.broadcasted_iota(jnp.int32, (big, LANES), 0)
        inside = (place >= first_row) & (place < last_row)
        tag_ref[rows, :] = jnp.where(inside, 1.0, 0.0).astype(bf16)
        low = middle_grad_ref[rows, :].astype(bf16)
        low_ref[rows, :] = low
        up = (dot(low, w_ref[3]) * active).astype(bf16)
        up_ref[rows, :] = up
        product = up.astype(f32) * context_ref[rows, :].astype(f32)
        high = product.astype(bf16)
        rest = (product - high.astype(f32)).astype(bf16)
        delta = -(dot(high, collect) + dot(rest, collect))
        lane = lane_iota(big)
        part = lax.rem(lane + 3 * LANES - IMAGES, 3)
        d_high = delta.astype(bf16).astype(f32)
        d_rest = delta - d_high
        d_mid = d_rest.astype(bf16).astype(f32)
        delta_ref[rows, :] = jnp.where(
            part == 0, d_high, jnp.where(part == 1, d_mid, d_rest - d_mid)
        ).astype(bf16)
        dk_ref[rows, :] = jnp.zeros((big, width), f32)
        dv_ref[rows, :] = jnp.zeros((big, width), f32)
        return carry

    lax.fori_loop(0, length // big, prepare, 0)
    first_half, second_half = half_masks()

    def tile(step, carry):
        q0 = pl.multiple_of(step * TILE, TILE)
        here = pl.ds(q0, TILE)

        def attend(window):
            there = pl.ds(pl.multiple_of(start_ref[row, step], GRID_W), window)
            lane = lax.broadcasted_iota(jnp.int32, (1, LANES), 1)
            tags = tag_ref[there, :]
            ext = ext_ref[here, :]
            delta = delta_ref[here, :]
            for p in range(pairs):
                at = slice(p * LANES, (p + 1) * LANES)
                queries = qkv_ref[here, at]
                keys = qkv_ref[there, width + p * LANES : width + (p + 1) * LANES]
                values = qkv_ref[there, 2 * width + p * LANES : 2 * width + (p + 1) * LANES]
                ups = up_ref[here, at]
                edge = IMAGES + 6 * p
                keep_one = jnp.where((lane < IMAGES) | ((lane >= edge) & (lane < edge + 3)), 1.0, 0.0).astype(bf16)
                keep_two = jnp.where((lane < IMAGES) | ((lane >= edge + 3) & (lane < edge + 6)), 1.0, 0.0).astype(bf16)
                only_one = jnp.where((lane >= edge) & (lane < edge + 3), 1.0, 0.0).astype(bf16)
                only_two = jnp.where((lane >= edge + 3) & (lane < edge + 6), 1.0, 0.0).astype(bf16)
                q_pair = jnp.concatenate([queries * first_half, queries * second_half], axis=0)
                up_pair = jnp.concatenate([ups * first_half, ups * second_half], axis=0)
                q_side = jnp.concatenate(
                    [q_pair, jnp.concatenate([ext * keep_one, ext * keep_two], axis=0)], axis=1
                )
                up_side = jnp.concatenate(
                    [up_pair, jnp.concatenate([delta * only_one, delta * only_two], axis=0)], axis=1
                )
                probs = jnp.exp2(dot(jnp.concatenate([keys, tags], axis=1), q_side, NT))
                grad_probs = dot(jnp.concatenate([values, tags], axis=1), up_side, NT)
                grad_scores = (probs * grad_probs).astype(bf16)
                dv_ref[there, at] += dot(probs.astype(bf16), up_pair)
                dk_ref[there, at] += dot(grad_scores, q_pair)
                dq = dot(keys, grad_scores, TN)
                half = lax.broadcasted_iota(jnp.int32, (LANES, TILE), 0)
                dq = jnp.where(half < HEAD_DIM, dq[:, :TILE], dq[:, TILE:])
                dq_ref[here, at] = jnp.transpose(dq * HEAD_DIM**-0.5).astype(bf16)

        for index, window in enumerate(widths_for(length)):
            pl.when(class_ref[row, step] == index)(functools.partial(attend, window))
        return carry

    lax.fori_loop(0, length // TILE, tile, 0)

    def finish(step, carry):
        rows = pl.ds(pl.multiple_of(step * big, big), big)
        queries_grad = dq_ref[rows, :]
        keys_grad = (dk_ref[rows, :] * LN2).astype(bf16)
        values_grad = dv_ref[rows, :].astype(bf16)
        proj_ref[rows, :] = jnp.concatenate([queries_grad, keys_grad, values_grad], axis=1)
        upstream = dot(queries_grad, w_ref[0], NT) + dot(keys_grad, w_ref[1], NT) + dot(values_grad, w_ref[2], NT)
        unit, inverse = norm_parts(tokens_ref[rows, :].astype(f32))
        tokens_grad_ref[rows, :] = middle_grad_ref[rows, :] + norm_back(upstream, gain, unit, inverse)
        norm_grad_ref[0:8, :] += fold_rows(upstream * unit)
        norm_grad_ref[8:16, :] += fold_rows(upstream)
        return carry

    lax.fori_loop(0, length // big, finish, 0)
    normed_t = jnp.transpose(normed_ref[...])
    for k in range(3):
        w_grad_ref[k] += dot(normed_t, proj_ref[:, k * width : (k + 1) * width])
    w_grad_ref[3] += dot(jnp.transpose(low_ref[...]), context_ref[...])


def attn_backward(starts, classes, counts, tokens, middle_grad, qkv, context, ext, attn_use, norm_w, images):
    rows_all, width = tokens.shape
    row_count = counts.shape[0]
    length = rows_all // row_count
    by_row = lambda columns: pl.BlockSpec((length, columns), lambda r, *_: (r, 0))
    return pl.pallas_call(
        attn_backward_kernel,
        grid_spec=pltpu.PrefetchScalarGridSpec(
            num_scalar_prefetch=3,
            grid=(row_count,),
            in_specs=[
                by_row(width),
                by_row(width),
                by_row(3 * width),
                by_row(width),
                by_row(LANES),
                pl.BlockSpec(attn_use.shape, lambda r, *_: (0, 0, 0)),
                pl.BlockSpec(norm_w.shape, lambda r, *_: (0, 0)),
                pl.BlockSpec((1, 8, LANES), lambda r, *_: (r, 0, 0)),
            ],
            out_specs=[
                by_row(width),
                pl.BlockSpec(attn_use.shape, lambda r, *_: (0, 0, 0)),
                pl.BlockSpec((16, width), lambda r, *_: (0, 0)),
            ],
            scratch_shapes=[
                pltpu.VMEM((length, LANES), bf16),
                pltpu.VMEM((length, width), bf16),
                pltpu.VMEM((length, LANES), bf16),
                pltpu.VMEM((length, width), bf16),
                pltpu.VMEM((length, width), bf16),
                pltpu.VMEM((length, width), f32),
                pltpu.VMEM((length, width), f32),
                pltpu.VMEM((length, width), bf16),
                pltpu.VMEM((length, 3 * width), bf16),
            ],
        ),
        out_shape=[
            jax.ShapeDtypeStruct((rows_all, width), f32),
            jax.ShapeDtypeStruct(attn_use.shape, f32),
            jax.ShapeDtypeStruct((16, width), f32),
        ],
        compiler_params=pltpu.CompilerParams(vmem_limit_bytes=VMEM_BYTES),
    )(starts, classes, counts, tokens, middle_grad, qkv, context, ext, attn_use, norm_w, images)


def mlp_kernel(
    middle_ref, out_grad_ref, w_ref, taps_ref, norm_ref, near_ref,
    output_ref, middle_grad_ref, w_grad_ref, taps_grad_ref, norm_grad_ref,
    normed_ref, hm_ref, h0_ref, hp_ref, act_ref, g_ref, gh_ref, tap_sum_ref,
):
    row = pl.program_id(0)
    length, width = middle_ref.shape
    hidden = w_ref.shape[2]
    chunk = 256
    block = 128
    sub = 32
    halo = GRID_W
    gain, bias = norm_ref[2:3, :], norm_ref[3:4, :]

    @pl.when(row == 0)
    def _():
        w_grad_ref[...] = jnp.zeros_like(w_grad_ref)
        norm_grad_ref[...] = jnp.zeros_like(norm_grad_ref)
        tap_sum_ref[...] = jnp.zeros_like(tap_sum_ref)
        for ref in (hm_ref, h0_ref, hp_ref, g_ref):
            ref[0:halo, :] = jnp.zeros((halo, hidden), bf16)
            ref[halo + length :, :] = jnp.zeros((halo, hidden), bf16)

    def normalize(step, carry):
        rows = pl.ds(pl.multiple_of(step * chunk, chunk), chunk)
        unit, _ = norm_parts(middle_ref[rows, :])
        normed_ref[rows, :] = (unit * gain + bias).astype(bf16)
        return carry

    lax.fori_loop(0, length // chunk, normalize, 0)
    column = lax.rem(lax.broadcasted_iota(jnp.int32, (block, LANES), 0), GRID_W)
    not_first = column != 0
    not_last = column != GRID_W - 1

    def expand(step, carry):
        c = step // (length // block)
        t = step - c * (length // block)
        rows = pl.ds(pl.multiple_of(t * block, block), block)
        place = pl.ds(pl.multiple_of(t * block + halo, GRID_W), block)
        values = dot(normed_ref[rows, :], w_ref[0, :, pl.ds(pl.multiple_of(c * chunk, chunk), chunk)])
        for part in range(chunk // LANES):
            lanes = pl.ds(pl.multiple_of(c * chunk + part * LANES, LANES), LANES)
            one = values[:, part * LANES : (part + 1) * LANES]
            h0_ref[place, lanes] = one.astype(bf16)
            hm_ref[place, lanes] = jnp.where(not_first, pltpu.roll(one, 1, 0), 0.0).astype(bf16)
            hp_ref[place, lanes] = jnp.where(not_last, pltpu.roll(one, block - 1, 0), 0.0).astype(bf16)
        return carry

    lax.fori_loop(0, (hidden // chunk) * (length // block), expand, 0)

    def tile_rows(values, rows):
        return jnp.concatenate([values] * (rows // GRID_W), axis=0)

    def activate(step, carry):
        c = step // (length // block)
        t = step - c * (length // block)
        rows = pl.ds(pl.multiple_of(t * block, block), block)
        act_grad = dot(out_grad_ref[rows, :], w_ref[1, :, pl.ds(pl.multiple_of(c * chunk, chunk), chunk)])
        for part in range(chunk // LANES):
            lanes = pl.ds(pl.multiple_of(c * chunk + part * LANES, LANES), LANES)
            taps = [tile_rows(taps_ref[k * GRID_W : (k + 1) * GRID_W, lanes], sub) for k in range(9)]
            for s in range(block // sub):
                base = t * block + s * sub
                near = pl.ds(pl.multiple_of(base, GRID_W), sub)
                mixed = None
                for a in (-1, 0, 1):
                    at = pl.ds(pl.multiple_of(base + halo + a * GRID_W, GRID_W), sub)
                    total = None
                    for b, ref in ((-1, hm_ref), (0, h0_ref), (1, hp_ref)):
                        term = ref[at, lanes] * taps[3 * (a + 1) + b + 1]
                        total = term if total is None else total + term
                    if a == 0:
                        total = total + h0_ref[at, lanes]
                    elif a == -1:
                        total = total * near_ref[0, near, :]
                    else:
                        total = total * near_ref[1, near, :]
                    mixed = total if mixed is None else mixed + total
                x = mixed.astype(f32)
                square = x * x
                t_value = jnp.tanh(x * (GELU_ONE + (GELU_ONE * GELU_TWO) * square))
                half = 0.5 * x
                act_ref[near, lanes] = (half + half * t_value).astype(bf16)
                slope = (0.5 + 0.5 * t_value) + half * (1.0 - t_value * t_value) * (
                    GELU_ONE + (3.0 * GELU_ONE * GELU_TWO) * square
                )
                grad = act_grad[s * sub : (s + 1) * sub, part * LANES : (part + 1) * LANES] * slope
                g_ref[pl.ds(pl.multiple_of(base + halo, GRID_W), sub), lanes] = grad.astype(bf16)
        return carry

    lax.fori_loop(0, (hidden // chunk) * (length // block), activate, 0)

    def conv_back(step, carry):
        c = step // (length // block)
        t = step - c * (length // block)
        lanes = pl.ds(pl.multiple_of(c * LANES, LANES), LANES)
        taps = [tile_rows(taps_ref[k * GRID_W : (k + 1) * GRID_W, lanes], sub) for k in range(9)]
        sums = [None] * 9
        col = lax.rem(lax.broadcasted_iota(jnp.int32, (sub, LANES), 0), GRID_W)
        for s in range(block // sub):
            base = t * block + s * sub
            near = pl.ds(pl.multiple_of(base, GRID_W), sub)
            at = pl.ds(pl.multiple_of(base + halo, GRID_W), sub)
            before = pl.ds(pl.multiple_of(base, GRID_W), sub)
            after = pl.ds(pl.multiple_of(base + 2 * halo, GRID_W), sub)
            here = g_ref[at, lanes]
            sources = (
                g_ref[after, lanes] * near_ref[1, near, :],
                here,
                g_ref[before, lanes] * near_ref[0, near, :],
            )
            side = {}
            for b, ref in ((-1, hm_ref), (0, h0_ref), (1, hp_ref)):
                moved = ref[at, lanes]
                total = None
                for a in (-1, 0, 1):
                    k = 3 * (a + 1) + b + 1
                    term = sources[a + 1] * taps[k]
                    total = term if total is None else total + term
                    product = moved * sources[a + 1]
                    folded = product[:GRID_W]
                    for piece in range(1, sub // GRID_W):
                        folded = folded + product[piece * GRID_W : (piece + 1) * GRID_W]
                    sums[k] = folded if sums[k] is None else sums[k] + folded
                side[b] = total
            result = (side[0] + here).astype(f32)
            result = result + jnp.where(col != 0, pltpu.roll(side[1].astype(f32), 1, 0), 0.0)
            result = result + jnp.where(col != GRID_W - 1, pltpu.roll(side[-1].astype(f32), sub - 1, 0), 0.0)
            gh_ref[near, lanes] = result.astype(bf16)
        for k in range(9):
            tap_sum_ref[k * GRID_W : (k + 1) * GRID_W, lanes] += sums[k].astype(f32)
        return carry

    lax.fori_loop(0, (hidden // LANES) * (length // block), conv_back, 0)

    def finish(step, carry):
        rows = pl.ds(pl.multiple_of(step * chunk, chunk), chunk)
        middle = middle_ref[rows, :]
        output_ref[rows, :] = (middle + dot(act_ref[rows, :], w_ref[1], NT)).astype(bf16)
        upstream = dot(gh_ref[rows, :], w_ref[0], NT)
        unit, inverse = norm_parts(middle)
        middle_grad_ref[rows, :] = out_grad_ref[rows, :].astype(f32) + norm_back(upstream, gain, unit, inverse)
        norm_grad_ref[0:8, :] += fold_rows(upstream * unit)
        norm_grad_ref[8:16, :] += fold_rows(upstream)
        return carry

    lax.fori_loop(0, length // chunk, finish, 0)
    normed_t = jnp.transpose(normed_ref[...])
    out_grad_t = jnp.transpose(out_grad_ref[...])

    def weights(c, carry):
        lanes = pl.ds(pl.multiple_of(c * chunk, chunk), chunk)
        w_grad_ref[0, :, lanes] += dot(normed_t, gh_ref[:, lanes])
        w_grad_ref[1, :, lanes] += dot(out_grad_t, act_ref[:, lanes])
        return carry

    lax.fori_loop(0, hidden // chunk, weights, 0)

    @pl.when(row == pl.num_programs(0) - 1)
    def _():
        taps_grad_ref[...] = jnp.zeros_like(taps_grad_ref)
        for k in range(9):
            taps_grad_ref[k : k + 1, :] = jnp.sum(tap_sum_ref[k * GRID_W : (k + 1) * GRID_W, :], axis=0, keepdims=True)


def mlp_layer(middle, out_grad, mlp_use, taps, norm_w, near, row_count):
    rows_all, width = middle.shape
    length = rows_all // row_count
    hidden = mlp_use.shape[2]
    by_row = lambda columns: pl.BlockSpec((length, columns), lambda r: (r, 0))
    return pl.pallas_call(
        mlp_kernel,
        grid=(row_count,),
        in_specs=[
            by_row(width),
            by_row(width),
            pl.BlockSpec(mlp_use.shape, lambda r: (0, 0, 0)),
            pl.BlockSpec(taps.shape, lambda r: (0, 0)),
            pl.BlockSpec(norm_w.shape, lambda r: (0, 0)),
            pl.BlockSpec((2, length, LANES), lambda r: (0, r, 0)),
        ],
        out_specs=[
            by_row(width),
            by_row(width),
            pl.BlockSpec(mlp_use.shape, lambda r: (0, 0, 0)),
            pl.BlockSpec((16, hidden), lambda r: (0, 0)),
            pl.BlockSpec((16, width), lambda r: (0, 0)),
        ],
        out_shape=[
            jax.ShapeDtypeStruct((rows_all, width), bf16),
            jax.ShapeDtypeStruct((rows_all, width), f32),
            jax.ShapeDtypeStruct(mlp_use.shape, f32),
            jax.ShapeDtypeStruct((16, hidden), f32),
            jax.ShapeDtypeStruct((16, width), f32),
        ],
        scratch_shapes=[
            pltpu.VMEM((length, width), bf16),
            pltpu.VMEM((length + 2 * GRID_W, hidden), bf16),
            pltpu.VMEM((length + 2 * GRID_W, hidden), bf16),
            pltpu.VMEM((length + 2 * GRID_W, hidden), bf16),
            pltpu.VMEM((length, hidden), bf16),
            pltpu.VMEM((length + 2 * GRID_W, hidden), bf16),
            pltpu.VMEM((length, hidden), bf16),
            pltpu.VMEM((9 * GRID_W, hidden), f32),
        ],
        compiler_params=pltpu.CompilerParams(vmem_limit_bytes=VMEM_BYTES),
    )(middle, out_grad, mlp_use, taps, norm_w, near)


def attention_plan(segments):
    row_count, length = segments.shape
    tiles = segments.reshape(row_count, length // TILE, TILE)
    first, last = tiles[:, :, 0], tiles[:, :, -1]
    low_end = jnp.sum((segments[:, None, :] < first[:, :, None]).astype(jnp.int32), axis=-1)
    high_end = jnp.sum((segments[:, None, :] <= last[:, :, None]).astype(jnp.int32), axis=-1)
    widths = widths_for(length)
    classes = sum(((high_end - low_end) > w).astype(jnp.int32) for w in widths[:-1])
    chosen = jnp.full_like(classes, widths[-1])
    for index, w in enumerate(widths):
        chosen = jnp.where(classes == index, w, chosen)
    starts = jnp.minimum(low_end, length - chosen)
    lane = jnp.arange(LANES, dtype=jnp.int32)
    begins = jnp.sum((segments[:, :, None] < lane).astype(jnp.int32), axis=1)
    ends = jnp.sum((segments[:, :, None] <= lane).astype(jnp.int32), axis=1)
    used = lane < IMAGES
    open_lane = (lane >= IMAGES) & (lane < IMAGES + 3 * 6)
    begins = jnp.where(used, begins, 0)
    ends = jnp.where(used, ends, jnp.where(open_lane, length, 0))
    images = jnp.zeros((row_count, 8, LANES), jnp.int32).at[:, 0].set(begins).at[:, 1].set(ends)
    return starts, classes, images


def neighbour_masks(segments):
    same = (segments[:, GRID_W:] == segments[:, :-GRID_W]).astype(bf16)
    zeros = jnp.zeros((segments.shape[0], GRID_W), bf16)
    above = jnp.concatenate([zeros, same], axis=1).reshape(-1)
    below = jnp.concatenate([same, zeros], axis=1).reshape(-1)
    return jnp.broadcast_to(jnp.stack([above, below])[:, :, None], (2, above.shape[0], LANES))


def bits_of(size):
    bits = []
    b = 1
    while b < size:
        bits.append(b)
        b *= 2
    return bits


def swap(values, axis, size, bit):
    return lax.ppermute(values, axis, [(i, i ^ bit) for i in range(size)])


def gather_lines(shard, size):
    place = lax.axis_index("dp")
    held = shard[None]
    for bit in reversed(bits_of(size)):
        other = swap(held, "dp", size, bit)
        mine_first = (place & bit) == 0
        pair = jnp.stack([jnp.where(mine_first, held, other), jnp.where(mine_first, other, held)], axis=1)
        held = pair.reshape((-1,) + shard.shape)
    return held


def join_columns(mine, other, rank):
    first = jnp.where(rank == 0, mine, other)
    second = jnp.where(rank == 0, other, mine)
    return jnp.concatenate([first, second], axis=-1)


def gather_weights(shard, size, rank):
    count, part, columns = shard.shape
    held = gather_lines(shard, size)
    full = join_columns(held, swap(held, "head", 2, 1), rank)
    return jnp.moveaxis(full, 0, 1).reshape(count, size * part, 2 * columns)


def own_columns(values, rank):
    half = values.shape[-1] // 2
    mine = lax.dynamic_slice_in_dim(values, rank * half, half, axis=values.ndim - 1)
    other = lax.dynamic_slice_in_dim(values, (1 - rank) * half, half, axis=values.ndim - 1)
    return mine + swap(other.astype(bf16), "head", 2, 1).astype(f32)


def scatter_lines(values, size):
    count, rows, columns = values.shape
    place = lax.axis_index("dp")
    held = jnp.moveaxis(values.reshape(count, size, rows // size, columns), 1, 0)
    for bit in bits_of(size):
        held = held.reshape((-1, 2) + held.shape[1:])
        side = (place & bit) // bit
        mine = lax.dynamic_index_in_dim(held, side, 1, keepdims=False)
        other = lax.dynamic_index_in_dim(held, 1 - side, 1, keepdims=False)
        held = mine + swap(other.astype(bf16), "dp", size, bit).astype(f32)
    return held[0]


def sum_everywhere(values, size):
    values = values + swap(values, "head", 2, 1)
    for bit in bits_of(size):
        values = values + swap(values, "dp", size, bit)
    return values


def adam_terms(grad_sum, first_old, second):
    first_new = BETA_ONE * first_old + (1.0 - BETA_ONE) * grad_sum
    second_new = BETA_TWO * second + (1.0 - BETA_TWO) * grad_sum * grad_sum
    direction = (
        first_new
        / (1.0 - BETA_ONE**STEP)
        / (jnp.sqrt(second_new / (1.0 - BETA_TWO**STEP)) + ADAM_EPS)
    )
    return (first_new, second_new, direction)


def body(
    size,
    tokens, grad_out, segments, counts,
    attn_w, attn_m, attn_v, mlp_w, mlp_m, mlp_v, conv_w, conv_m, conv_v, norm_w, norm_m, norm_v,
):
    rank = lax.axis_index("head")
    own_rows = segments.shape[0] // 2
    segments = lax.dynamic_slice_in_dim(segments, rank * own_rows, own_rows, axis=0)
    counts = lax.dynamic_slice_in_dim(counts, rank * own_rows, own_rows, axis=0)
    attn_use = gather_weights(attn_w.astype(bf16), size, rank)
    mlp_lines = lax.all_gather(mlp_w.astype(bf16), "dp", axis=1, tiled=True)
    mlp_use = join_columns(mlp_lines, swap(mlp_lines, "head", 2, 1), rank)
    conv_low = conv_w.astype(bf16)
    conv_use = join_columns(conv_low, swap(conv_low, "head", 2, 1), rank)
    starts, classes, images = attention_plan(segments)
    middle, qkv, context, ext = attn_forward(starts, classes, counts, tokens, attn_use, norm_w, images)
    output, grad_middle, grad_mlp, grad_conv, grad_norm_two = mlp_layer(
        middle, grad_out, mlp_use, jnp.repeat(conv_use, GRID_W, axis=0), norm_w, neighbour_masks(segments), own_rows
    )
    grad_tokens, grad_attn, grad_norm_one = attn_backward(
        starts, classes, counts, tokens, grad_middle, qkv, context, ext, attn_use, norm_w, images
    )
    grad_mlp = scatter_lines(own_columns(grad_mlp, rank), size)
    grad_conv = own_columns(grad_conv[:9], rank)
    for bit in bits_of(size):
        grad_conv = grad_conv + swap(grad_conv, "dp", size, bit)
    grad_attn = scatter_lines(own_columns(grad_attn, rank), size)
    new_attn_m, new_attn_v, attn_direction = adam_terms(grad_attn, attn_m, attn_v)
    new_mlp_m, new_mlp_v, mlp_direction = adam_terms(grad_mlp, mlp_m, mlp_v)
    new_conv_m, new_conv_v, conv_direction = adam_terms(grad_conv, conv_m, conv_v)
    attn_update = attn_direction + DECAY * attn_w
    mlp_update = mlp_direction + DECAY * mlp_w
    conv_update = conv_direction + DECAY * conv_w
    first_line = (lax.axis_index("dp") == 0).astype(f32)
    weight_squares = jnp.concatenate(
        [
            jnp.sum(attn_w * attn_w, axis=(1, 2)),
            jnp.sum(mlp_w * mlp_w, axis=(1, 2)),
            (first_line * jnp.sum(conv_w * conv_w))[None],
        ]
    )
    update_squares = jnp.concatenate(
        [
            jnp.sum(attn_update * attn_update, axis=(1, 2)),
            jnp.sum(mlp_update * mlp_update, axis=(1, 2)),
            (first_line * jnp.sum(conv_update * conv_update))[None],
        ]
    )
    width = norm_w.shape[1]
    norm_part = jnp.concatenate(
        [
            jnp.sum(grad_norm_one.reshape(2, 8, width), axis=1),
            jnp.sum(grad_norm_two.reshape(2, 8, width), axis=1),
        ]
    )
    squares = jnp.pad(jnp.stack([weight_squares, update_squares]), ((0, 0), (0, width - 7)))
    summed = sum_everywhere(jnp.concatenate([squares, norm_part, jnp.zeros((2, width), f32)]), size)
    squares, norm_grads = summed[:2, :7], summed[2:6]
    ratio = jnp.sqrt(squares[0]) / jnp.sqrt(squares[1])
    new_attn_w = attn_w - RATE * ratio[:4, None, None] * attn_update
    new_mlp_w = mlp_w - RATE * ratio[4:6, None, None] * mlp_update
    new_conv_w = conv_w - RATE * ratio[6] * conv_update
    new_norm_m, new_norm_v, norm_direction = adam_terms(norm_grads, norm_m, norm_v)
    new_norm_w = norm_w - RATE * norm_direction
    return (
        output, grad_tokens, new_attn_w, new_attn_m, new_attn_v, new_mlp_w, new_mlp_m, new_mlp_v,
        new_conv_w, new_conv_m, new_conv_v, new_norm_w, new_norm_m, new_norm_v,
    )


def solution(mesh):
    rows, lines = P(("dp", "head"), None), P("dp", None)
    shards, columns = P(None, "dp", "head"), P(None, "head")
    in_specs = (rows, rows, lines, P("dp")) + (shards,) * 6 + (columns,) * 3 + (P(),) * 3
    out_specs = (rows, rows) + (shards,) * 6 + (columns,) * 3 + (P(),) * 3
    return jax.shard_map(
        functools.partial(body, mesh.shape["dp"]), mesh=mesh, in_specs=in_specs, out_specs=out_specs, check_vma=False
    )
```

```python
import functools
import jax
import jax.numpy as jnp
from jax import lax
from jax.experimental import pallas as pl
from jax.experimental.pallas import tpu as pltpu
from jax.sharding import PartitionSpec as P

HEAD_DIM = 64
GRID_W = 16
STEP = 10
IMAGES = 8

NORM_EPS = 1e-06
BETA_ONE = 0.9
BETA_TWO = 0.999
ADAM_EPS = 1e-06
DECAY = 0.01
RATE = 0.5
LOG2E = 1.4426950408889634
LN2 = 0.6931471805599453
BIG = 2.0**100
GELU_ONE = 0.7978845608028654
GELU_TWO = 0.044715
GELU_S = (GELU_ONE * GELU_TWO) ** (1.0 / 3.0)
GELU_A = GELU_ONE / GELU_S
ACT_SCALE = 0.5 / GELU_S
MXU_ROWS = 64
MXU_LAG = 6
TILE = 128
LANES = 128
STRIDE = GRID_W + 8
VMEM_BYTES = 60 * 1024 * 1024

f32 = jnp.float32
bf16 = jnp.bfloat16
NN = (((1,), (0,)), ((), ()))
NT = (((1,), (1,)), ((), ()))
TN = (((0,), (0,)), ((), ()))


def dot(left, right, dims=NN):
    return lax.dot_general(left, right, dims, preferred_element_type=f32)


def widths_for(length):
    return [w for w in (256, 384, 512, 768) if w < length] + [length]


def lane_iota(rows):
    return lax.broadcasted_iota(jnp.int32, (rows, LANES), 1)


def norm_parts(values):
    average = jnp.mean(values, axis=-1, keepdims=True)
    centered = values - average
    inverse = lax.rsqrt(jnp.mean(centered * centered, axis=-1, keepdims=True) + NORM_EPS)
    return centered * inverse, inverse


def norm_back(upstream, gain_row, unit_rows, inverse):
    grad_unit = upstream * gain_row
    first_term = jnp.mean(grad_unit, axis=-1, keepdims=True)
    second_term = jnp.mean(grad_unit * unit_rows, axis=-1, keepdims=True)
    return inverse * (grad_unit - first_term - unit_rows * second_term)


def fold_rows(values):
    rows, columns = values.shape
    return jnp.sum(values.reshape(rows // 8, 8, columns), axis=0)


def half_masks():
    lane = lax.broadcasted_iota(jnp.int32, (1, LANES), 1)
    first = (lane < HEAD_DIM).astype(f32).astype(bf16)
    second = (lane >= HEAD_DIM).astype(f32).astype(bf16)
    return first, second


def split_lanes(column, lane, at):
    high = column.astype(bf16).astype(f32)
    rest = column - high
    middle = rest.astype(bf16).astype(f32)
    low = rest - middle
    return jnp.where(lane == at, high, jnp.where(lane == at + 1, middle, jnp.where(lane == at + 2, low, 0.0)))


def attn_forward_kernel(
    start_ref, class_ref, count_ref, tokens_ref, w_ref, norm_ref, image_ref,
    middle_ref, qkv_ref, context_ref, ext_ref, tag_ref,
):
    row = pl.program_id(0)
    length, width = tokens_ref.shape
    pairs = width // LANES
    big = 256
    gain, bias = norm_ref[0:1, :], norm_ref[1:2, :]
    first_row, last_row = image_ref[0, 0:1, :], image_ref[0, 1:2, :]

    def project(step, carry):
        rows = pl.ds(pl.multiple_of(step * big, big), big)
        unit, _ = norm_parts(tokens_ref[rows, :].astype(f32))
        normed = (unit * gain + bias).astype(bf16)
        for k in range(3):
            product = dot(normed, w_ref[k])
            if k == 0:
                product = product * (HEAD_DIM**-0.5 * LOG2E)
            qkv_ref[rows, k * width : (k + 1) * width] = product.astype(bf16)
        place = step * big + lax.broadcasted_iota(jnp.int32, (big, LANES), 0)
        inside = (place >= first_row) & (place < last_row)
        tag_ref[rows, :] = jnp.where(inside, 1.0, 0.0).astype(bf16)
        return carry

    lax.fori_loop(0, length // big, project, 0)
    first_half, second_half = half_masks()

    def tile(step, carry):
        q0 = pl.multiple_of(step * TILE, TILE)
        here = pl.ds(q0, TILE)

        def attend(window):
            there = pl.ds(pl.multiple_of(start_ref[row, step], GRID_W), window)
            lane = lane_iota(TILE)
            tags = tag_ref[there, :]
            base = jnp.where(lane < IMAGES, (tag_ref[here, :].astype(f32) - 1.0) * BIG, 0.0)
            base_low = base.astype(bf16)
            for p in range(pairs):
                at = slice(p * LANES, (p + 1) * LANES)
                queries = qkv_ref[here, at]
                keys = qkv_ref[there, width + p * LANES : width + (p + 1) * LANES]
                values = qkv_ref[there, 2 * width + p * LANES : 2 * width + (p + 1) * LANES]
                left = jnp.concatenate(
                    [
                        jnp.concatenate([queries * first_half, base_low], axis=1),
                        jnp.concatenate([queries * second_half, base_low], axis=1),
                    ],
                    axis=0,
                )
                scores = dot(left, jnp.concatenate([keys, tags], axis=1), NT)
                row_max = jnp.max(scores, axis=1, keepdims=True)
                exponent = jnp.exp2(scores - row_max).astype(bf16)
                mixed = dot(exponent, jnp.concatenate([values, tags], axis=1))
                total = mixed[:, LANES + IMAGES : LANES + IMAGES + 1]
                minus_lse = -(row_max + jnp.log(total) * LOG2E)
                scale = 1.0 / total
                active_one = jnp.where(2 * p < count_ref[row], 1.0, 0.0)
                active_two = jnp.where(2 * p + 1 < count_ref[row], 1.0, 0.0)
                context = jnp.where(
                    lane < HEAD_DIM,
                    mixed[:TILE, :LANES] * (scale[:TILE] * active_one),
                    mixed[TILE:, :LANES] * (scale[TILE:] * active_two),
                )
                context_ref[here, at] = context.astype(bf16)
                base = base + split_lanes(minus_lse[:TILE], lane, IMAGES + 6 * p)
                base = base + split_lanes(minus_lse[TILE:], lane, IMAGES + 6 * p + 3)
            ext_ref[here, :] = base.astype(bf16)

        for index, window in enumerate(widths_for(length)):
            pl.when(class_ref[row, step] == index)(functools.partial(attend, window))
        return carry

    lax.fori_loop(0, length // TILE, tile, 0)

    def finish(step, carry):
        rows = pl.ds(pl.multiple_of(step * big, big), big)
        middle_ref[rows, :] = tokens_ref[rows, :].astype(f32) + dot(context_ref[rows, :], w_ref[3], NT)
        return carry

    lax.fori_loop(0, length // big, finish, 0)


def attn_forward(starts, classes, counts, tokens, attn_use, norm_w, images):
    rows_all, width = tokens.shape
    row_count = counts.shape[0]
    length = rows_all // row_count
    by_row = lambda columns: pl.BlockSpec((length, columns), lambda r, *_: (r, 0))
    return pl.pallas_call(
        attn_forward_kernel,
        grid_spec=pltpu.PrefetchScalarGridSpec(
            num_scalar_prefetch=3,
            grid=(row_count,),
            in_specs=[
                by_row(width),
                pl.BlockSpec(attn_use.shape, lambda r, *_: (0, 0, 0)),
                pl.BlockSpec(norm_w.shape, lambda r, *_: (0, 0)),
                pl.BlockSpec((1, 8, LANES), lambda r, *_: (r, 0, 0)),
            ],
            out_specs=[by_row(width), by_row(3 * width), by_row(width), by_row(LANES)],
            scratch_shapes=[pltpu.VMEM((length, LANES), bf16)],
        ),
        out_shape=[
            jax.ShapeDtypeStruct((rows_all, width), f32),
            jax.ShapeDtypeStruct((rows_all, 3 * width), bf16),
            jax.ShapeDtypeStruct((rows_all, width), bf16),
            jax.ShapeDtypeStruct((rows_all, LANES), bf16),
        ],
        compiler_params=pltpu.CompilerParams(vmem_limit_bytes=VMEM_BYTES),
    )(starts, classes, counts, tokens, attn_use, norm_w, images)


def attn_backward_kernel(
    first, start_ref, class_ref, count_ref, tokens_ref, middle_grad_ref, qkv_ref, context_ref, ext_ref, w_ref, norm_ref, image_ref,
    *refs,
):
    if first:
        attn_backward_row(
            first, refs[1:3], start_ref, class_ref, count_ref, tokens_ref, middle_grad_ref, qkv_ref, context_ref, ext_ref, w_ref,
            norm_ref, image_ref, *refs[3:],
        )
    else:
        attn_backward_row(
            first, None, start_ref, class_ref, count_ref, tokens_ref, middle_grad_ref, qkv_ref, context_ref, ext_ref, w_ref,
            norm_ref, image_ref, *refs,
        )


def attn_backward_row(
    first, sums, start_ref, class_ref, count_ref, tokens_ref, middle_grad_ref, qkv_ref, context_ref, ext_ref, w_ref, norm_ref, image_ref,
    tokens_grad_ref, w_grad_ref, norm_grad_ref,
    tag_ref, up_ref, delta_ref, normed_ref, dq_ref, dk_ref, dv_ref, low_ref, proj_ref,
):
    step_at = pl.program_id(0)
    row = first + step_at
    length, width = tokens_ref.shape
    pairs = width // LANES
    heads = 2 * pairs
    big = 256
    gain, bias = norm_ref[0:1, :], norm_ref[1:2, :]
    first_row, last_row = image_ref[0, 0:1, :], image_ref[0, 1:2, :]

    @pl.when(step_at == 0)
    def _():
        for n, ref in enumerate((w_grad_ref, norm_grad_ref)):
            ref[...] = sums[n][...] if sums else jnp.zeros_like(ref)

    source = lax.broadcasted_iota(jnp.int32, (width, LANES), 0)
    target = lax.broadcasted_iota(jnp.int32, (width, LANES), 1) - IMAGES
    low_edge = source // HEAD_DIM * 3
    collect = jnp.where((target >= low_edge) & (target < low_edge + 3), 1.0, 0.0).astype(bf16)
    active = jnp.where(
        lax.broadcasted_iota(jnp.int32, (1, width), 1) // HEAD_DIM < count_ref[row], 1.0, 0.0
    )

    def prepare(step, carry):
        rows = pl.ds(pl.multiple_of(step * big, big), big)
        unit, _ = norm_parts(tokens_ref[rows, :].astype(f32))
        normed_ref[rows, :] = (unit * gain + bias).astype(bf16)
        place = step * big + lax.broadcasted_iota(jnp.int32, (big, LANES), 0)
        inside = (place >= first_row) & (place < last_row)
        tag_ref[rows, :] = jnp.where(inside, 1.0, 0.0).astype(bf16)
        low = middle_grad_ref[rows, :].astype(bf16)
        low_ref[rows, :] = low
        up = (dot(low, w_ref[3]) * active).astype(bf16)
        up_ref[rows, :] = up
        product = up.astype(f32) * context_ref[rows, :].astype(f32)
        high = product.astype(bf16)
        rest = (product - high.astype(f32)).astype(bf16)
        delta = -(dot(high, collect) + dot(rest, collect))
        lane = lane_iota(big)
        part = lax.rem(lane + 3 * LANES - IMAGES, 3)
        d_high = delta.astype(bf16).astype(f32)
        d_rest = delta - d_high
        d_mid = d_rest.astype(bf16).astype(f32)
        delta_ref[rows, :] = jnp.where(
            part == 0, d_high, jnp.where(part == 1, d_mid, d_rest - d_mid)
        ).astype(bf16)
        dk_ref[rows, :] = jnp.zeros((big, width), f32)
        dv_ref[rows, :] = jnp.zeros((big, width), f32)
        return carry

    lax.fori_loop(0, length // big, prepare, 0)
    first_half, second_half = half_masks()

    def tile(step, carry):
        q0 = pl.multiple_of(step * TILE, TILE)
        here = pl.ds(q0, TILE)

        def attend(window):
            there = pl.ds(pl.multiple_of(start_ref[row, step], GRID_W), window)
            lane = lax.broadcasted_iota(jnp.int32, (1, LANES), 1)
            tags = tag_ref[there, :]
            ext = ext_ref[here, :]
            delta = delta_ref[here, :]
            for p in range(pairs):
                at = slice(p * LANES, (p + 1) * LANES)
                queries = qkv_ref[here, at]
                keys = qkv_ref[there, width + p * LANES : width + (p + 1) * LANES]
                values = qkv_ref[there, 2 * width + p * LANES : 2 * width + (p + 1) * LANES]
                ups = up_ref[here, at]
                edge = IMAGES + 6 * p
                keep_one = jnp.where((lane < IMAGES) | ((lane >= edge) & (lane < edge + 3)), 1.0, 0.0).astype(bf16)
                keep_two = jnp.where((lane < IMAGES) | ((lane >= edge + 3) & (lane < edge + 6)), 1.0, 0.0).astype(bf16)
                only_one = jnp.where((lane >= edge) & (lane < edge + 3), 1.0, 0.0).astype(bf16)
                only_two = jnp.where((lane >= edge + 3) & (lane < edge + 6), 1.0, 0.0).astype(bf16)
                q_pair = jnp.concatenate([queries * first_half, queries * second_half], axis=0)
                up_pair = jnp.concatenate([ups * first_half, ups * second_half], axis=0)
                q_side = jnp.concatenate(
                    [q_pair, jnp.concatenate([ext * keep_one, ext * keep_two], axis=0)], axis=1
                )
                up_side = jnp.concatenate(
                    [up_pair, jnp.concatenate([delta * only_one, delta * only_two], axis=0)], axis=1
                )
                probs = jnp.exp2(dot(jnp.concatenate([keys, tags], axis=1), q_side, NT))
                grad_probs = dot(jnp.concatenate([values, tags], axis=1), up_side, NT)
                grad_scores = (probs * grad_probs).astype(bf16)
                dv_ref[there, at] += dot(probs.astype(bf16), up_pair)
                dk_ref[there, at] += dot(grad_scores, q_pair)
                dq = dot(keys, grad_scores, TN)
                half = lax.broadcasted_iota(jnp.int32, (LANES, TILE), 0)
                dq = jnp.where(half < HEAD_DIM, dq[:, :TILE], dq[:, TILE:])
                dq_ref[here, at] = jnp.transpose(dq * HEAD_DIM**-0.5).astype(bf16)

        for index, window in enumerate(widths_for(length)):
            pl.when(class_ref[row, step] == index)(functools.partial(attend, window))
        return carry

    lax.fori_loop(0, length // TILE, tile, 0)

    def finish(step, carry):
        rows = pl.ds(pl.multiple_of(step * big, big), big)
        queries_grad = dq_ref[rows, :]
        keys_grad = (dk_ref[rows, :] * LN2).astype(bf16)
        values_grad = dv_ref[rows, :].astype(bf16)
        proj_ref[rows, :] = jnp.concatenate([queries_grad, keys_grad, values_grad], axis=1)
        upstream = dot(queries_grad, w_ref[0], NT) + dot(keys_grad, w_ref[1], NT) + dot(values_grad, w_ref[2], NT)
        unit, inverse = norm_parts(tokens_ref[rows, :].astype(f32))
        tokens_grad_ref[rows, :] = middle_grad_ref[rows, :] + norm_back(upstream, gain, unit, inverse)
        norm_grad_ref[0:8, :] += fold_rows(upstream * unit)
        norm_grad_ref[8:16, :] += fold_rows(upstream)
        return carry

    lax.fori_loop(0, length // big, finish, 0)
    normed_t = jnp.transpose(normed_ref[...])
    for k in range(3):
        w_grad_ref[k] += dot(normed_t, proj_ref[:, k * width : (k + 1) * width])
    w_grad_ref[3] += dot(jnp.transpose(low_ref[...]), context_ref[...])


def attn_backward(first, count, so_far, starts, classes, counts, tokens, middle_grad, qkv, context, ext, attn_use, norm_w, images):
    rows_all, width = tokens.shape
    length = rows_all // counts.shape[0]
    by_row = lambda columns: pl.BlockSpec((length, columns), lambda r, *_: (first + r, 0))
    whole = pl.BlockSpec(attn_use.shape, lambda r, *_: (0, 0, 0))
    sums = pl.BlockSpec((16, width), lambda r, *_: (0, 0))
    return pl.pallas_call(
        functools.partial(attn_backward_kernel, first),
        grid_spec=pltpu.PrefetchScalarGridSpec(
            num_scalar_prefetch=3,
            grid=(count,),
            in_specs=[
                by_row(width),
                by_row(width),
                by_row(3 * width),
                by_row(width),
                by_row(LANES),
                whole,
                pl.BlockSpec(norm_w.shape, lambda r, *_: (0, 0)),
                pl.BlockSpec((1, 8, LANES), lambda r, *_: (first + r, 0, 0)),
            ]
            + ([pl.BlockSpec(memory_space=pl.ANY), whole, sums] if first else []),
            out_specs=[by_row(width), whole, sums],
            scratch_shapes=[
                pltpu.VMEM((length, LANES), bf16),
                pltpu.VMEM((length, width), bf16),
                pltpu.VMEM((length, LANES), bf16),
                pltpu.VMEM((length, width), bf16),
                pltpu.VMEM((length, width), bf16),
                pltpu.VMEM((length, width), f32),
                pltpu.VMEM((length, width), f32),
                pltpu.VMEM((length, width), bf16),
                pltpu.VMEM((length, 3 * width), bf16),
            ],
        ),
        out_shape=[
            jax.ShapeDtypeStruct((rows_all, width), f32),
            jax.ShapeDtypeStruct(attn_use.shape, f32),
            jax.ShapeDtypeStruct((16, width), f32),
        ],
        input_output_aliases={11: 0} if first else {},
        compiler_params=pltpu.CompilerParams(vmem_limit_bytes=VMEM_BYTES),
    )(starts, classes, counts, tokens, middle_grad, qkv, context, ext, attn_use, norm_w, images, *(so_far or ()))


def mlp_kernel(
    same_ref, middle_ref, out_grad_ref, w_ref, taps_ref, norm_ref,
    output_ref, middle_grad_ref, w_grad_ref, taps_grad_ref, norm_grad_ref,
    normed_ref, normed_t_ref, out_grad_t_ref, out_sum_ref, up_sum_ref, tap_sum_ref,
    act_grads_ref, acts_ref, hidden_grads_ref, *buffers,
):
    row = pl.program_id(0)
    length, width = middle_ref.shape
    hidden = w_ref.shape[2]
    chunk = 2 * LANES
    big = 256
    grid_rows = length // GRID_W
    chunks = hidden // chunk
    empty = grid_rows * STRIDE + 8
    h_refs, g_refs = buffers[:2], buffers[2:]
    gain, bias = norm_ref[2:3, :], norm_ref[3:4, :]

    @pl.when(row == 0)
    def _():
        w_grad_ref[...] = jnp.zeros_like(w_grad_ref)
        norm_grad_ref[...] = jnp.zeros_like(norm_grad_ref)
        tap_sum_ref[...] = jnp.zeros_like(tap_sum_ref)
        for ref in buffers:
            ref[...] = jnp.zeros_like(ref)

    def normalize(step, carry):
        rows = pl.ds(pl.multiple_of(step * big, big), big)
        middle = middle_ref[rows, :]
        unit, _ = norm_parts(middle)
        normed_ref[rows, :] = (unit * gain + bias).astype(bf16)
        out_sum_ref[rows, :] = jnp.zeros((big, width), f32)
        up_sum_ref[rows, :] = jnp.zeros((big, width), f32)
        return carry

    lax.fori_loop(0, length // big, normalize, 0)
    normed_t_ref[...] = jnp.transpose(normed_ref[...])
    out_grad_t_ref[...] = jnp.transpose(out_grad_ref[...])

    def lanes_of(c):
        return pl.ds(pl.multiple_of(c * chunk, chunk), chunk)

    def lanes_of(c):
        return pl.ds(pl.multiple_of(c * chunk, chunk), chunk)

    def places(r):
        here = r * STRIDE + 8
        above = jnp.where(same_ref[row, r] == 1, here - STRIDE, empty)
        below = jnp.where(same_ref[row, r + 1] == 1, here + STRIDE, empty)
        return [pl.multiple_of(at, 8) for at in (above, here, below)]

    def neighbours(ref, at):
        return [ref[pl.ds(at - 1, GRID_W), :], ref[pl.ds(at, GRID_W), :], ref[pl.ds(at + 1, GRID_W), :]]

    def tall(values):
        return jnp.concatenate([values, values], axis=0)

    def total_of(terms):
        while len(terms) > 1:
            terms = [a + b for a, b in zip(terms[::2], terms[1::2])] + ([terms[-1]] if len(terms) % 2 else [])
        return terms[0]

    def taps_for(c, part, at):
        lane = pl.ds(pl.multiple_of(c * chunk + part * LANES, LANES), LANES)
        return [tall(taps_ref[at + k * 8 : at + (k + 1) * 8, lane]) for k in range(9)]

    lines = 16

    def do_chunk(c, carry):
        lanes = lanes_of(c)
        for t in range(length // big):
            rows = slice(t * big, (t + 1) * big)
            values = dot(normed_ref[rows, :], w_ref[0, :, lanes])
            for part in range(2):
                for s in range(big // GRID_W):
                    at = (t * (big // GRID_W) + s) * STRIDE + 8
                    h_refs[part][at : at + GRID_W, :] = values[
                        s * GRID_W : (s + 1) * GRID_W, part * LANES : (part + 1) * LANES
                    ]
        act_grads_ref[...] = dot(out_grad_ref[...], w_ref[1, :, lanes])

        def forward(t, carry):
            for part in range(2):
                taps = taps_for(c, part, 0)
                cols = slice(part * LANES, (part + 1) * LANES)
                for s in range(lines):
                    r = t * lines + s
                    near = pl.ds(pl.multiple_of(r * GRID_W, GRID_W), GRID_W)
                    around = places(r)
                    terms = []
                    for a, at in enumerate(around):
                        terms += [x * taps[3 * a + b] for b, x in enumerate(neighbours(h_refs[part], at))]
                    x = total_of(terms)
                    square = x * x
                    value = jnp.tanh(x * (GELU_A + square))
                    gate = 1.0 + value
                    twice = x * gate
                    acts_ref[near, cols] = twice.astype(bf16)
                    slope = gate + (twice * (1.0 - value)) * (GELU_A + 3.0 * square)
                    g_refs[part][pl.ds(around[1], GRID_W), :] = act_grads_ref[near, cols] * slope
            return carry

        lax.fori_loop(0, grid_rows // lines, forward, 0)

        def backward(t, carry):
            for part in range(2):
                taps = taps_for(c, part, 72)
                lane = pl.ds(pl.multiple_of(c * chunk + part * LANES, LANES), LANES)
                cols = slice(part * LANES, (part + 1) * LANES)
                totals = [None] * 9
                for s in range(lines):
                    r = t * lines + s
                    near = pl.ds(pl.multiple_of(r * GRID_W, GRID_W), GRID_W)
                    around = places(r)
                    source = h_refs[part][pl.ds(around[1], GRID_W), :]
                    terms = []
                    for a in range(3):
                        moved = neighbours(g_refs[part], around[2 - a])[::-1]
                        for b in range(3):
                            k = 3 * a + b
                            terms.append(moved[b] * taps[k])
                            product = source * moved[b]
                            folded = product[:8] + product[8:]
                            totals[k] = folded if totals[k] is None else totals[k] + folded
                    hidden_grads_ref[near, cols] = total_of(terms).astype(bf16)
                for k in range(9):
                    tap_sum_ref[k * 8 : (k + 1) * 8, lane] += totals[k]
            return carry

        lax.fori_loop(0, grid_rows // lines, backward, 0)
        w_grad_ref[0, :, lanes] += dot(normed_t_ref[...], hidden_grads_ref[...])
        w_grad_ref[1, :, lanes] += dot(out_grad_t_ref[...], acts_ref[...])
        out_sum_ref[...] += dot(acts_ref[...], w_ref[1, :, lanes], NT)
        up_sum_ref[...] += dot(hidden_grads_ref[...], w_ref[0, :, lanes], NT)
        return carry

    lax.fori_loop(0, chunks, do_chunk, 0)

    def finish(step, carry):
        rows = pl.ds(pl.multiple_of(step * big, big), big)
        middle = middle_ref[rows, :]
        output_ref[rows, :] = (middle + ACT_SCALE * out_sum_ref[rows, :]).astype(bf16)
        upstream = 0.5 * up_sum_ref[rows, :]
        unit, inverse = norm_parts(middle)
        middle_grad_ref[rows, :] = out_grad_ref[rows, :].astype(f32) + norm_back(upstream, gain, unit, inverse)
        norm_grad_ref[0:8, :] += fold_rows(upstream * unit)
        norm_grad_ref[8:16, :] += fold_rows(upstream)
        return carry

    lax.fori_loop(0, length // big, finish, 0)

    @pl.when(row == pl.num_programs(0) - 1)
    def _():
        w_grad_ref[0] = w_grad_ref[0] * 0.5
        w_grad_ref[1] = w_grad_ref[1] * ACT_SCALE
        taps_grad_ref[...] = jnp.zeros_like(taps_grad_ref)
        for k in range(9):
            total = jnp.sum(tap_sum_ref[k * 8 : (k + 1) * 8, :], axis=0, keepdims=True)
            taps_grad_ref[k : k + 1, :] = 0.5 * total


def mlp_layer(same, middle, out_grad, mlp_use, taps, norm_w):
    rows_all, width = middle.shape
    row_count = same.shape[0]
    length = rows_all // row_count
    hidden = mlp_use.shape[2]
    by_row = lambda columns: pl.BlockSpec((length, columns), lambda r, *_: (r, 0))
    slots = (length // GRID_W + 2) * STRIDE
    return pl.pallas_call(
        mlp_kernel,
        grid_spec=pltpu.PrefetchScalarGridSpec(
            num_scalar_prefetch=1,
            grid=(row_count,),
            in_specs=[
                by_row(width),
                by_row(width),
                pl.BlockSpec(mlp_use.shape, lambda r, *_: (0, 0, 0)),
                pl.BlockSpec(taps.shape, lambda r, *_: (0, 0)),
                pl.BlockSpec(norm_w.shape, lambda r, *_: (0, 0)),
            ],
            out_specs=[
                by_row(width),
                by_row(width),
                pl.BlockSpec(mlp_use.shape, lambda r, *_: (0, 0, 0)),
                pl.BlockSpec((16, hidden), lambda r, *_: (0, 0)),
                pl.BlockSpec((16, width), lambda r, *_: (0, 0)),
            ],
            scratch_shapes=[
                pltpu.VMEM((length, width), bf16),
                pltpu.VMEM((width, length), bf16),
                pltpu.VMEM((width, length), bf16),
                pltpu.VMEM((length, width), f32),
                pltpu.VMEM((length, width), f32),
                pltpu.VMEM((9 * 8, hidden), f32),
                pltpu.VMEM((length, 2 * LANES), f32),
                pltpu.VMEM((length, 2 * LANES), bf16),
                pltpu.VMEM((length, 2 * LANES), bf16),
            ]
            + [pltpu.VMEM((slots, LANES), f32)] * 4,
        ),
        out_shape=[
            jax.ShapeDtypeStruct((rows_all, width), bf16),
            jax.ShapeDtypeStruct((rows_all, width), f32),
            jax.ShapeDtypeStruct(mlp_use.shape, f32),
            jax.ShapeDtypeStruct((16, hidden), f32),
            jax.ShapeDtypeStruct((16, width), f32),
        ],
        compiler_params=pltpu.CompilerParams(vmem_limit_bytes=VMEM_BYTES),
    )(same, middle, out_grad, mlp_use, taps, norm_w)


def attention_plan(segments):
    row_count, length = segments.shape
    tiles = segments.reshape(row_count, length // TILE, TILE)
    first, last = tiles[:, :, 0], tiles[:, :, -1]
    low_end = jnp.sum((segments[:, None, :] < first[:, :, None]).astype(jnp.int32), axis=-1)
    high_end = jnp.sum((segments[:, None, :] <= last[:, :, None]).astype(jnp.int32), axis=-1)
    widths = widths_for(length)
    classes = sum(((high_end - low_end) > w).astype(jnp.int32) for w in widths[:-1])
    chosen = jnp.full_like(classes, widths[-1])
    for index, w in enumerate(widths):
        chosen = jnp.where(classes == index, w, chosen)
    starts = jnp.minimum(low_end, length - chosen)
    lane = jnp.arange(LANES, dtype=jnp.int32)
    begins = jnp.sum((segments[:, :, None] < lane).astype(jnp.int32), axis=1)
    ends = jnp.sum((segments[:, :, None] <= lane).astype(jnp.int32), axis=1)
    used = lane < IMAGES
    open_lane = (lane >= IMAGES) & (lane < IMAGES + 3 * 6)
    begins = jnp.where(used, begins, 0)
    ends = jnp.where(used, ends, jnp.where(open_lane, length, 0))
    images = jnp.zeros((row_count, 8, LANES), jnp.int32).at[:, 0].set(begins).at[:, 1].set(ends)
    return starts, classes, images


def spread_taps(conv_use):
    taps = conv_use.astype(f32)
    own = (jnp.arange(9) == 4).astype(f32)[:, None]
    taps = jnp.repeat(taps + own, 8, axis=0)
    return jnp.concatenate([taps * GELU_S, taps], axis=0)


def same_images(segments):
    ids = segments[:, ::GRID_W]
    edge = jnp.zeros((ids.shape[0], 1), jnp.int32)
    return jnp.concatenate([edge, (ids[:, 1:] == ids[:, :-1]).astype(jnp.int32), edge], axis=1)


def bits_of(size):
    bits = []
    b = 1
    while b < size:
        bits.append(b)
        b *= 2
    return bits


def swap(values, axis, size, bit):
    return lax.ppermute(values, axis, [(i, i ^ bit) for i in range(size)])


def gather_lines(shard, size):
    place = lax.axis_index("dp")
    held = shard[None]
    for bit in reversed(bits_of(size)):
        other = swap(held, "dp", size, bit)
        mine_first = (place & bit) == 0
        pair = jnp.stack([jnp.where(mine_first, held, other), jnp.where(mine_first, other, held)], axis=1)
        held = pair.reshape((-1,) + shard.shape)
    return held


def join_columns(mine, other, rank):
    first = jnp.where(rank == 0, mine, other)
    second = jnp.where(rank == 0, other, mine)
    return jnp.concatenate([first, second], axis=-1)


def gather_weights(shard, size, rank):
    count, part, columns = shard.shape
    held = gather_lines(shard, size)
    full = join_columns(held, swap(held, "head", 2, 1), rank)
    return jnp.moveaxis(full, 0, 1).reshape(count, size * part, 2 * columns)


def half_columns(values, side):
    half = values.shape[-1] // 2
    return lax.dynamic_slice_in_dim(values, side * half, half, axis=values.ndim - 1)


def by_line(values, size):
    count, rows, columns = values.shape
    return jnp.moveaxis(values.reshape(count, size, rows // size, columns), 1, 0).reshape(size, -1, columns)


def two_parts(values):
    high = values.astype(bf16)
    return jnp.concatenate([high, (values - high.astype(f32)).astype(bf16)], axis=0)


def from_parts(parts):
    count = parts.shape[0] // 2
    return parts[:count].astype(f32) + parts[count:].astype(f32)


def finish_exchange(keep, got, small_keep):
    rows = keep.size // keep.shape[-1]
    small = from_parts(two_parts(small_keep)) + from_parts(got[rows:])
    return keep + got[:rows].reshape(keep.shape).astype(f32), small


def start_exchange(send, small_send, axis, size, bit):
    sent = send.astype(bf16).reshape(-1, send.shape[-1])
    if small_send is not None:
        sent = jnp.concatenate([sent, two_parts(small_send)], axis=0)
    return swap(sent, axis, size, bit)


def halves(held, bit):
    held = held.reshape((-1, 2) + held.shape[1:])
    side = (lax.axis_index("dp") & bit) // bit
    mine = lax.dynamic_index_in_dim(held, side, 1, keepdims=False)
    return mine, lax.dynamic_index_in_dim(held, 1 - side, 1, keepdims=False)


def sum_everywhere(values, size):
    values = values + swap(values, "head", 2, 1)
    for bit in bits_of(size):
        values = values + swap(values, "dp", size, bit)
    return values


def adam_terms(grad_sum, first_old, second):
    first_new = BETA_ONE * first_old + (1.0 - BETA_ONE) * grad_sum
    second_new = BETA_TWO * second + (1.0 - BETA_TWO) * grad_sum * grad_sum
    direction = (
        first_new
        / (1.0 - BETA_ONE**STEP)
        / (jnp.sqrt(second_new / (1.0 - BETA_TWO**STEP)) + ADAM_EPS)
    )
    return (first_new, second_new, direction)


def after(first, second):
    return lax.optimization_barrier((first, second))


def body(
    size,
    tokens, grad_out, segments, counts,
    attn_w, attn_m, attn_v, mlp_w, mlp_m, mlp_v, conv_w, conv_m, conv_v, norm_w, norm_m, norm_v,
):
    rank = lax.axis_index("head")
    own_rows = segments.shape[0] // 2
    segments = lax.dynamic_slice_in_dim(segments, rank * own_rows, own_rows, axis=0)
    counts = lax.dynamic_slice_in_dim(counts, rank * own_rows, own_rows, axis=0)
    width = norm_w.shape[1]
    attn_use = gather_weights(attn_w.astype(bf16), size, rank)
    mlp_lines = lax.all_gather(mlp_w.astype(bf16), "dp", axis=1, tiled=True)
    conv_low = conv_w.astype(bf16)
    conv_use = join_columns(conv_low, swap(conv_low, "head", 2, 1), rank)
    starts, classes, images = attention_plan(segments)
    middle, qkv, context, ext = attn_forward(starts, classes, counts, tokens, attn_use, norm_w, images)
    middle, mlp_lines = after(middle, mlp_lines)
    mlp_use = join_columns(mlp_lines, swap(mlp_lines, "head", 2, 1), rank)
    output, grad_middle, grad_mlp, grad_conv, grad_norm_two = mlp_layer(
        same_images(segments), middle, grad_out, mlp_use, spread_taps(conv_use), norm_w
    )

    def back(first, count, so_far):
        return attn_backward(
            first, count, so_far, starts, classes, counts, tokens, grad_middle, qkv, context, ext, attn_use, norm_w, images
        )

    norm_two = jnp.sum(grad_norm_two.reshape(2, 8, width), axis=1).reshape(1, 2 * width)
    columns = conv_w.shape[1]
    wide_norm = jnp.pad(norm_two, ((0, 0), (0, columns - 2 * width)))
    small = jnp.concatenate([half_columns(grad_conv[:9], rank), wide_norm])
    held = by_line(half_columns(grad_mlp, rank), size)
    got = start_exchange(
        by_line(half_columns(grad_mlp, 1 - rank), size),
        jnp.concatenate([half_columns(grad_conv[:9], 1 - rank), wide_norm]),
        "head", 2, 1,
    )
    bits = bits_of(size)
    first_rows = max(1, own_rows // 3)
    so_far = back(0, first_rows, None)
    so_far, got = after(so_far, got)
    held, small = finish_exchange(held, got, small)
    keep, send = halves(held, bits[0])
    got = start_exchange(send, small, "dp", size, bits[0])
    if first_rows < own_rows:
        so_far, send = after(so_far, send)
        so_far = back(first_rows, own_rows - first_rows, so_far)
        so_far, got = after(so_far, got)
    grad_tokens, grad_attn, grad_norm_one = so_far
    held, small = finish_exchange(keep, got, small)

    attn_got = start_exchange(half_columns(grad_attn, 1 - rank), None, "head", 2, 1)
    attn_held = half_columns(grad_attn, rank)
    attn_held = by_line(attn_held + attn_got.reshape(attn_held.shape).astype(f32), size)
    for n, bit in enumerate(bits):
        attn_keep, attn_send = halves(attn_held, bit)
        attn_got = start_exchange(attn_send, None, "dp", size, bit)
        if n + 1 < len(bits):
            keep, send = halves(held, bits[n + 1])
            got = start_exchange(send, small, "dp", size, bits[n + 1])
        attn_held = attn_keep + attn_got.reshape(attn_keep.shape).astype(f32)
        if n + 1 < len(bits):
            held, small = finish_exchange(keep, got, small)
    grad_attn = attn_held.reshape(attn_w.shape)
    grad_mlp = held.reshape(mlp_w.shape)
    grad_conv = small[:9]
    norm_two = small[9, : 2 * width].reshape(2, width)

    new_attn_m, new_attn_v, attn_direction = adam_terms(grad_attn, attn_m, attn_v)
    new_mlp_m, new_mlp_v, mlp_direction = adam_terms(grad_mlp, mlp_m, mlp_v)
    new_conv_m, new_conv_v, conv_direction = adam_terms(grad_conv, conv_m, conv_v)
    attn_update = attn_direction + DECAY * attn_w
    mlp_update = mlp_direction + DECAY * mlp_w
    conv_update = conv_direction + DECAY * conv_w
    first_line = (lax.axis_index("dp") == 0).astype(f32)
    weight_squares = jnp.concatenate(
        [
            jnp.sum(attn_w * attn_w, axis=(1, 2)),
            jnp.sum(mlp_w * mlp_w, axis=(1, 2)),
            (first_line * jnp.sum(conv_w * conv_w))[None],
        ]
    )
    update_squares = jnp.concatenate(
        [
            jnp.sum(attn_update * attn_update, axis=(1, 2)),
            jnp.sum(mlp_update * mlp_update, axis=(1, 2)),
            (first_line * jnp.sum(conv_update * conv_update))[None],
        ]
    )
    squares = jnp.pad(jnp.stack([weight_squares, update_squares]), ((0, 0), (0, width - 7)))
    norm_one = jnp.sum(grad_norm_one.reshape(2, 8, width), axis=1)
    summed = sum_everywhere(jnp.concatenate([squares, norm_one, jnp.zeros((4, width), f32)]), size)
    squares, norm_grads = summed[:2, :7], jnp.concatenate([summed[2:4], norm_two])
    ratio = jnp.sqrt(squares[0]) / jnp.sqrt(squares[1])
    new_attn_w = attn_w - RATE * ratio[:4, None, None] * attn_update
    new_mlp_w = mlp_w - RATE * ratio[4:6, None, None] * mlp_update
    new_conv_w = conv_w - RATE * ratio[6] * conv_update
    new_norm_m, new_norm_v, norm_direction = adam_terms(norm_grads, norm_m, norm_v)
    new_norm_w = norm_w - RATE * norm_direction
    return (
        output, grad_tokens, new_attn_w, new_attn_m, new_attn_v, new_mlp_w, new_mlp_m, new_mlp_v,
        new_conv_w, new_conv_m, new_conv_v, new_norm_w, new_norm_m, new_norm_v,
    )


def solution(mesh):
    rows, lines = P(("dp", "head"), None), P("dp", None)
    shards, columns = P(None, "dp", "head"), P(None, "head")
    in_specs = (rows, rows, lines, P("dp")) + (shards,) * 6 + (columns,) * 3 + (P(),) * 3
    out_specs = (rows, rows) + (shards,) * 6 + (columns,) * 3 + (P(),) * 3
    return jax.shard_map(
        functools.partial(body, mesh.shape["dp"]), mesh=mesh, in_specs=in_specs, out_specs=out_specs, check_vma=False
    )
```

```python
import functools
import jax
import jax.numpy as jnp
from jax import lax
from jax.experimental import pallas as pl
from jax.experimental.pallas import tpu as pltpu
from jax.sharding import PartitionSpec as P

HEAD_DIM = 64
GRID_W = 16
STEP = 10
IMAGES = 8

NORM_EPS = 1e-06
BETA_ONE = 0.9
BETA_TWO = 0.999
ADAM_EPS = 1e-06
DECAY = 0.01
RATE = 0.5
LOG2E = 1.4426950408889634
LN2 = 0.6931471805599453
BIG = 2.0**100
GELU_ONE = 0.7978845608028654
GELU_TWO = 0.044715
GELU_S = (GELU_ONE * GELU_TWO) ** (1.0 / 3.0)
GELU_A = GELU_ONE / GELU_S
ACT_SCALE = 0.5 / GELU_S
EXTRA = 32
TILE = 128
LANES = 128
STRIDE = GRID_W + 8
VMEM_BYTES = 60 * 1024 * 1024

f32 = jnp.float32
bf16 = jnp.bfloat16
NN = (((1,), (0,)), ((), ()))
NT = (((1,), (1,)), ((), ()))
TN = (((0,), (0,)), ((), ()))


def dot(left, right, dims=NN):
    return lax.dot_general(left, right, dims, preferred_element_type=f32)


def widths_for(length):
    return [w for w in (256, 384, 512, 768) if w < length] + [length]


def norm_parts(values):
    average = jnp.mean(values, axis=-1, keepdims=True)
    centered = values - average
    inverse = lax.rsqrt(jnp.mean(centered * centered, axis=-1, keepdims=True) + NORM_EPS)
    return centered * inverse, inverse


def norm_back(upstream, gain_row, unit_rows, inverse):
    grad_unit = upstream * gain_row
    first_term = jnp.mean(grad_unit, axis=-1, keepdims=True)
    second_term = jnp.mean(grad_unit * unit_rows, axis=-1, keepdims=True)
    return inverse * (grad_unit - first_term - unit_rows * second_term)


def fold_rows(values):
    rows, columns = values.shape
    return jnp.sum(values.reshape(rows // 8, 8, columns), axis=0)


def pair_columns(flat):
    empty = jnp.zeros((HEAD_DIM, LANES), flat.dtype)
    return jnp.concatenate(
        [jnp.concatenate([flat[:HEAD_DIM], empty], axis=0), jnp.concatenate([empty, flat[HEAD_DIM:]], axis=0)], axis=1
    )


def pair_rows(both):
    return jnp.concatenate([both[:HEAD_DIM, :LANES], both[HEAD_DIM:, LANES:]], axis=0)


def fold_max(values):
    pieces = [values[at : at + 64] for at in range(0, values.shape[0], 64)]
    while len(pieces) > 1:
        pieces = [jnp.maximum(a, b) for a, b in zip(pieces[::2], pieces[1::2])] + ([pieces[-1]] if len(pieces) % 2 else [])
    top = pieces[0]
    top = jnp.maximum(top[:32], top[32:])
    top = jnp.maximum(top[:16], top[16:])
    return jnp.max(jnp.maximum(top[:8], top[8:]), axis=0, keepdims=True)


def three_parts(value, part):
    high = value.astype(bf16).astype(f32)
    rest = value - high
    middle = rest.astype(bf16).astype(f32)
    return jnp.where(part == 0, high, jnp.where(part == 1, middle, rest - middle))


def image_tags(image_ref, start, rows):
    place = start + lax.broadcasted_iota(jnp.int32, (rows, LANES), 0)
    inside = (place >= image_ref[0, 0:1, :]) & (place < image_ref[0, 1:2, :])
    return jnp.where(inside, 1.0, 0.0).astype(bf16)


def attn_forward_kernel(
    start_ref, class_ref, count_ref, tokens_ref, w_ref, norm_ref, image_ref,
    middle_ref, qkv_ref, context_ref, ext_ref,
    tag_ref, normed_ref, qt_ref, vt_ref,
):
    row = pl.program_id(0)
    length, width = tokens_ref.shape
    pairs = width // LANES
    big = 256
    gain, bias = norm_ref[0:1, :], norm_ref[1:2, :]

    def prepare(step, carry):
        rows = pl.ds(pl.multiple_of(step * big, big), big)
        unit, _ = norm_parts(tokens_ref[rows, :].astype(f32))
        normed_ref[rows, :] = (unit * gain + bias).astype(bf16)
        tag_ref[rows, :] = image_tags(image_ref, step * big, big)
        return carry

    lax.fori_loop(0, length // big, prepare, 0)
    queries = (dot(normed_ref[...], w_ref[0]) * (HEAD_DIM**-0.5 * LOG2E)).astype(bf16)
    qkv_ref[:, :width] = queries
    qt_ref[...] = jnp.transpose(queries)
    qkv_ref[:, width : 2 * width] = dot(normed_ref[...], w_ref[1]).astype(bf16)
    values = dot(normed_ref[...], w_ref[2]).astype(bf16)
    qkv_ref[:, 2 * width :] = values
    vt_ref[...] = jnp.transpose(values)

    def tile(step, carry):
        q0 = pl.multiple_of(step * TILE, TILE)
        here = pl.ds(q0, TILE)
        place = q0 + lax.broadcasted_iota(jnp.int32, (IMAGES, LANES), 1)
        inside = (place >= image_ref[0, 8 : 8 + IMAGES, :]) & (place < image_ref[0, 16 : 16 + IMAGES, :])
        mask = jnp.where(inside, 0.0, -BIG)
        mask_low = jnp.concatenate([mask, jnp.zeros((LANES - IMAGES, LANES), f32)], axis=0).astype(bf16)
        ext_rows = lax.broadcasted_iota(jnp.int32, (EXTRA - IMAGES, LANES), 0)

        def attend(window):
            there = pl.ds(pl.multiple_of(start_ref[row, step], LANES), window)
            tags = tag_ref[there, :]
            ones = jnp.ones((GRID_W, window), bf16)
            extra = jnp.zeros((EXTRA - IMAGES, LANES), f32)
            slices = [slice(p * LANES, (p + 1) * LANES) for p in range(pairs)]
            masks = jnp.concatenate([mask_low, mask_low], axis=1)
            scores, tops, exponents, mixes = [], [], [], []
            for p, at in enumerate(slices):
                keys = qkv_ref[there, width + p * LANES : width + (p + 1) * LANES]
                right = jnp.concatenate([pair_columns(qt_ref[at, here]), masks], axis=0)
                scores.append(dot(jnp.concatenate([keys, tags], axis=1), right))
            for p in range(pairs):
                tops.append(fold_max(scores[p]))
                exponents.append(jnp.exp2(scores[p] - tops[p]).astype(bf16))
            for p, at in enumerate(slices):
                mixes.append(dot(jnp.concatenate([vt_ref[at, there], ones], axis=0), exponents[p]))
            for p, at in enumerate(slices):
                mixed = mixes[p]
                total = mixed[LANES : LANES + 1, :]
                minus_lse = -(tops[p] + jnp.log(total) * LOG2E)
                scale = 1.0 / total
                lane = lax.broadcasted_iota(jnp.int32, (1, 2 * TILE), 1)
                head = 2 * p + jnp.where(lane < TILE, 0, 1)
                scale = jnp.where(head < count_ref[row], scale, 0.0)
                context_ref[here, at] = jnp.transpose(pair_rows(mixed[:LANES] * scale)).astype(bf16)
                for h in range(2):
                    value = minus_lse[:, h * TILE : (h + 1) * TILE]
                    first = 6 * p + 3 * h
                    extra = jnp.where(
                        (ext_rows >= first) & (ext_rows < first + 3), three_parts(value, ext_rows - first), extra
                    )
            ext_ref[:, here] = jnp.concatenate([mask, extra], axis=0).astype(bf16)

        for index, window in enumerate(widths_for(length)):
            pl.when(class_ref[row, step] == index)(functools.partial(attend, window))
        return carry

    lax.fori_loop(0, length // TILE, tile, 0)
    middle_ref[...] = tokens_ref[...].astype(f32) + dot(context_ref[...], w_ref[3], NT)


def attn_forward(starts, classes, counts, tokens, attn_use, norm_w, images):
    rows_all, width = tokens.shape
    row_count = counts.shape[0]
    length = rows_all // row_count
    by_row = lambda columns: pl.BlockSpec((length, columns), lambda r, *_: (r, 0))
    return pl.pallas_call(
        attn_forward_kernel,
        grid_spec=pltpu.PrefetchScalarGridSpec(
            num_scalar_prefetch=3,
            grid=(row_count,),
            in_specs=[
                by_row(width),
                pl.BlockSpec(attn_use.shape, lambda r, *_: (0, 0, 0)),
                pl.BlockSpec(norm_w.shape, lambda r, *_: (0, 0)),
                pl.BlockSpec((1, 24, LANES), lambda r, *_: (r, 0, 0)),
            ],
            out_specs=[
                by_row(width), by_row(3 * width), by_row(width), pl.BlockSpec((EXTRA, length), lambda r, *_: (r, 0))
            ],
            scratch_shapes=[
                pltpu.VMEM((length, LANES), bf16),
                pltpu.VMEM((length, width), bf16),
                pltpu.VMEM((width, length), bf16),
                pltpu.VMEM((width, length), bf16),
            ],
        ),
        out_shape=[
            jax.ShapeDtypeStruct((rows_all, width), f32),
            jax.ShapeDtypeStruct((rows_all, 3 * width), bf16),
            jax.ShapeDtypeStruct((rows_all, width), bf16),
            jax.ShapeDtypeStruct((row_count * EXTRA, length), bf16),
        ],
        compiler_params=pltpu.CompilerParams(vmem_limit_bytes=VMEM_BYTES),
    )(starts, classes, counts, tokens, attn_use, norm_w, images)


def attn_backward_kernel(
    first, final, start_ref, class_ref, count_ref, rank_ref, tokens_ref, middle_grad_ref, qkv_ref, context_ref, ext_ref, w_ref, norm_ref,
    image_ref, *refs,
):
    sums = None
    if first:
        sums, refs = refs[1:3], refs[3:]
    sent = None
    if final:
        tokens_grad_ref, keep_ref, send_ref, norm_grad_ref, *scratch, w_grad_ref = refs
        sent = (keep_ref, send_ref)
    else:
        tokens_grad_ref, w_grad_ref, norm_grad_ref, *scratch = refs
    attn_backward_row(
        first, sums, sent, start_ref, class_ref, count_ref, rank_ref, tokens_ref, middle_grad_ref, qkv_ref, context_ref, ext_ref, w_ref,
        norm_ref, image_ref, tokens_grad_ref, w_grad_ref, norm_grad_ref, *scratch,
    )


def attn_backward_row(
    first, sums, sent, start_ref, class_ref, count_ref, rank_ref, tokens_ref, middle_grad_ref, qkv_ref, context_ref, ext_ref, w_ref,
    norm_ref, image_ref, tokens_grad_ref, w_grad_ref, norm_grad_ref,
    tag_ref, up_ref, delta_ref, normed_ref, dq_ref, dk_ref, dv_ref, low_ref, proj_ref, qt_ref, kt_ref, upt_ref, upstream_ref,
):
    step_at = pl.program_id(0)
    row = first + step_at
    length, width = tokens_ref.shape
    pairs = width // LANES
    big = 256
    gain, bias = norm_ref[0:1, :], norm_ref[1:2, :]

    @pl.when(step_at == 0)
    def _():
        for n, ref in enumerate((w_grad_ref, norm_grad_ref)):
            ref[...] = sums[n][...] if sums else jnp.zeros_like(ref)

    target = lax.broadcasted_iota(jnp.int32, (EXTRA, width), 0) - IMAGES
    source = lax.broadcasted_iota(jnp.int32, (EXTRA, width), 1) // HEAD_DIM * 3
    collect = jnp.where((target >= source) & (target < source + 3), -1.0, 0.0).astype(bf16)
    active = jnp.where(
        lax.broadcasted_iota(jnp.int32, (1, width), 1) // HEAD_DIM < count_ref[row], 1.0, 0.0
    )

    def prepare(step, carry):
        rows = pl.ds(pl.multiple_of(step * big, big), big)
        unit, _ = norm_parts(tokens_ref[rows, :].astype(f32))
        normed_ref[rows, :] = (unit * gain + bias).astype(bf16)
        tag_ref[rows, :] = image_tags(image_ref, step * big, big)
        low_ref[rows, :] = middle_grad_ref[rows, :].astype(bf16)
        dk_ref[rows, :] = jnp.zeros((big, width), f32)
        dv_ref[rows, :] = jnp.zeros((big, width), f32)
        return carry

    lax.fori_loop(0, length // big, prepare, 0)
    up = (dot(low_ref[...], w_ref[3]) * active).astype(bf16)
    up_ref[...] = up
    upt_ref[...] = jnp.transpose(up)
    qt_ref[...] = jnp.transpose(qkv_ref[:, :width])
    kt_ref[...] = jnp.transpose(qkv_ref[:, width : 2 * width])

    def gather(step, carry):
        rows = pl.ds(pl.multiple_of(step * big, big), big)
        product = up_ref[rows, :].astype(f32) * context_ref[rows, :].astype(f32)
        high = product.astype(bf16)
        rest = (product - high.astype(f32)).astype(bf16)
        delta = dot(collect, high, NT) + dot(collect, rest, NT)
        part = lax.rem(lax.broadcasted_iota(jnp.int32, (EXTRA, big), 0) + 3 * EXTRA - IMAGES, 3)
        delta_ref[:, rows] = three_parts(delta, part).astype(bf16)
        return carry

    lax.fori_loop(0, length // big, gather, 0)
    lane = lax.broadcasted_iota(jnp.int32, (1, LANES), 1)
    first_half = jnp.where(lane < HEAD_DIM, 1.0, 0.0).astype(bf16)
    second_half = jnp.where(lane >= HEAD_DIM, 1.0, 0.0).astype(bf16)

    def tile(step, carry):
        q0 = pl.multiple_of(step * TILE, TILE)
        here = pl.ds(q0, TILE)

        def attend(window):
            there = pl.ds(pl.multiple_of(start_ref[row, step], LANES), window)
            tags = tag_ref[there, :]
            ext = ext_ref[:, here]
            delta = delta_ref[:, here]
            at_row = lax.broadcasted_iota(jnp.int32, (EXTRA, LANES), 0)
            empty = jnp.zeros((LANES - EXTRA, 2 * TILE), bf16)

            def own(edge, masks):
                keep = (at_row >= edge) & (at_row < edge + 3)
                return jnp.where(keep | (at_row < IMAGES) if masks else keep, 1.0, 0.0).astype(bf16)

            slices = [slice(p * LANES, (p + 1) * LANES) for p in range(pairs)]
            scores, grad_probs, probs, grad_scores = [], [], [], []
            for p, at in enumerate(slices):
                keys = qkv_ref[there, width + p * LANES : width + (p + 1) * LANES]
                values = qkv_ref[there, 2 * width + p * LANES : 2 * width + (p + 1) * LANES]
                edge = IMAGES + 6 * p
                q_side = jnp.concatenate(
                    [
                        pair_columns(qt_ref[at, here]),
                        jnp.concatenate([ext * own(edge, True), ext * own(edge + 3, True)], axis=1),
                        empty,
                    ],
                    axis=0,
                )
                up_side = jnp.concatenate(
                    [
                        pair_columns(upt_ref[at, here]),
                        jnp.concatenate([delta * own(edge, False), delta * own(edge + 3, False)], axis=1),
                        empty,
                    ],
                    axis=0,
                )
                scores.append(dot(jnp.concatenate([keys, tags], axis=1), q_side))
                grad_probs.append(dot(jnp.concatenate([values, tags], axis=1), up_side))
            for p in range(pairs):
                weight = jnp.exp2(scores[p])
                probs.append(weight.astype(bf16))
                grad_scores.append((weight * grad_probs[p]).astype(bf16))
            for p, at in enumerate(slices):
                queries, ups = qkv_ref[here, at], up_ref[here, at]
                q_pair = jnp.concatenate([queries * first_half, queries * second_half], axis=0)
                up_pair = jnp.concatenate([ups * first_half, ups * second_half], axis=0)
                dv_ref[there, at] += dot(probs[p], up_pair)
                dk_ref[there, at] += dot(grad_scores[p], q_pair)
                dq = pair_rows(dot(kt_ref[at, there], grad_scores[p]))
                dq_ref[here, at] = jnp.transpose(dq * HEAD_DIM**-0.5).astype(bf16)

        for index, window in enumerate(widths_for(length)):
            pl.when(class_ref[row, step] == index)(functools.partial(attend, window))
        return carry

    lax.fori_loop(0, length // TILE, tile, 0)
    keys_grad = (dk_ref[...] * LN2).astype(bf16)
    values_grad = dv_ref[...].astype(bf16)
    proj_ref[...] = jnp.concatenate([dq_ref[...], keys_grad, values_grad], axis=1)
    w_cat = jnp.concatenate([w_ref[0], w_ref[1], w_ref[2]], axis=1)
    upstream_ref[...] = dot(proj_ref[...], w_cat, NT)

    def finish(step, carry):
        rows = pl.ds(pl.multiple_of(step * big, big), big)
        upstream = upstream_ref[rows, :]
        unit, inverse = norm_parts(tokens_ref[rows, :].astype(f32))
        tokens_grad_ref[rows, :] = middle_grad_ref[rows, :] + norm_back(upstream, gain, unit, inverse)
        norm_grad_ref[0:8, :] += fold_rows(upstream * unit)
        norm_grad_ref[8:16, :] += fold_rows(upstream)
        return carry

    lax.fori_loop(0, length // big, finish, 0)
    normed_t = jnp.transpose(normed_ref[...])
    for k in range(3):
        w_grad_ref[k] += dot(normed_t, proj_ref[:, k * width : (k + 1) * width])
    w_grad_ref[3] += dot(jnp.transpose(low_ref[...]), context_ref[...])
    if sent:

        @pl.when(step_at == pl.num_programs(0) - 1)
        def _():
            for k in range(w_grad_ref.shape[0]):
                halves = w_grad_ref[k, :, : width // 2], w_grad_ref[k, :, width // 2 :]
                sent[0][k] = jnp.where(rank_ref[0] == 0, halves[0], halves[1])
                sent[1][k] = jnp.where(rank_ref[0] == 0, halves[1], halves[0]).astype(bf16)


def attn_backward(first, count, so_far, starts, classes, counts, rank, tokens, middle_grad, qkv, context, ext, attn_use, norm_w, images):
    rows_all, width = tokens.shape
    length = rows_all // counts.shape[0]
    by_row = lambda columns: pl.BlockSpec((length, columns), lambda r, *_: (first + r, 0))
    final = first + count == counts.shape[0]
    half = attn_use.shape[:2] + (width // 2,)
    halves = pl.BlockSpec(half, lambda r, *_: (0, 0, 0))
    whole = pl.BlockSpec(attn_use.shape, lambda r, *_: (0, 0, 0))
    sums = pl.BlockSpec((16, width), lambda r, *_: (0, 0))
    return pl.pallas_call(
        functools.partial(attn_backward_kernel, first, final),
        grid_spec=pltpu.PrefetchScalarGridSpec(
            num_scalar_prefetch=4,
            grid=(count,),
            in_specs=[
                by_row(width),
                by_row(width),
                by_row(3 * width),
                by_row(width),
                pl.BlockSpec((EXTRA, length), lambda r, *_: (first + r, 0)),
                whole,
                pl.BlockSpec(norm_w.shape, lambda r, *_: (0, 0)),
                pl.BlockSpec((1, 24, LANES), lambda r, *_: (first + r, 0, 0)),
            ]
            + ([pl.BlockSpec(memory_space=pl.ANY), whole, sums] if first else []),
            out_specs=[by_row(width), halves, halves, sums] if final else [by_row(width), whole, sums],
            scratch_shapes=[
                pltpu.VMEM((length, LANES), bf16),
                pltpu.VMEM((length, width), bf16),
                pltpu.VMEM((EXTRA, length), bf16),
                pltpu.VMEM((length, width), bf16),
                pltpu.VMEM((length, width), bf16),
                pltpu.VMEM((length, width), f32),
                pltpu.VMEM((length, width), f32),
                pltpu.VMEM((length, width), bf16),
                pltpu.VMEM((length, 3 * width), bf16),
                pltpu.VMEM((width, length), bf16),
                pltpu.VMEM((width, length), bf16),
                pltpu.VMEM((width, length), bf16),
                pltpu.VMEM((length, width), f32),
            ]
            + ([pltpu.VMEM(attn_use.shape, f32)] if final else []),
        ),
        out_shape=[jax.ShapeDtypeStruct((rows_all, width), f32)]
        + (
            [jax.ShapeDtypeStruct(half, f32), jax.ShapeDtypeStruct(half, bf16)]
            if final
            else [jax.ShapeDtypeStruct(attn_use.shape, f32)]
        )
        + [jax.ShapeDtypeStruct((16, width), f32)],
        input_output_aliases={12: 0} if first else {},
        compiler_params=pltpu.CompilerParams(vmem_limit_bytes=VMEM_BYTES),
    )(starts, classes, counts, rank, tokens, middle_grad, qkv, context, ext, attn_use, norm_w, images, *(so_far or ()))


def mlp_kernel(
    place_ref, rank_ref, middle_ref, out_grad_ref, w_ref, taps_ref, norm_ref,
    output_ref, middle_grad_ref, keep_ref, send_ref, taps_grad_ref, norm_grad_ref,
    w_grad_ref, normed_ref, normed_t_ref, out_grad_t_ref, out_sum_ref, up_sum_ref, tap_sum_ref,
    act_grads_ref, acts_ref, hidden_grads_ref, *buffers,
):
    row = pl.program_id(0)
    length, width = middle_ref.shape
    hidden = w_ref.shape[2]
    chunk = 2 * LANES
    big = 256
    grid_rows = length // GRID_W
    chunks = hidden // chunk
    h_refs, g_refs = buffers[:2], buffers[2:]
    gain, bias = norm_ref[2:3, :], norm_ref[3:4, :]

    @pl.when(row == 0)
    def _():
        w_grad_ref[...] = jnp.zeros_like(w_grad_ref)
        norm_grad_ref[...] = jnp.zeros_like(norm_grad_ref)
        tap_sum_ref[...] = jnp.zeros_like(tap_sum_ref)

    for ref in buffers:
        ref[...] = jnp.zeros_like(ref)

    def normalize(step, carry):
        rows = pl.ds(pl.multiple_of(step * big, big), big)
        middle = middle_ref[rows, :]
        unit, _ = norm_parts(middle)
        normed_ref[rows, :] = (unit * gain + bias).astype(bf16)
        out_sum_ref[rows, :] = jnp.zeros((big, width), f32)
        up_sum_ref[rows, :] = jnp.zeros((big, width), f32)
        return carry

    lax.fori_loop(0, length // big, normalize, 0)
    normed_t_ref[...] = jnp.transpose(normed_ref[...])
    out_grad_t_ref[...] = jnp.transpose(out_grad_ref[...])

    def lanes_of(c):
        return pl.ds(pl.multiple_of(c * chunk, chunk), chunk)

    def lanes_of(c):
        return pl.ds(pl.multiple_of(c * chunk, chunk), chunk)

    def place(r):
        return pl.multiple_of(place_ref[row, r], 8)

    def neighbours(ref, at):
        return [ref[pl.ds(at + (a * STRIDE + b), GRID_W), :] for a in (-1, 0, 1) for b in (-1, 0, 1)]

    def tall(values):
        return jnp.concatenate([values, values], axis=0)

    def total_of(terms):
        while len(terms) > 1:
            terms = [a + b for a, b in zip(terms[::2], terms[1::2])] + ([terms[-1]] if len(terms) % 2 else [])
        return terms[0]

    def taps_for(c, part, at):
        lane = pl.ds(pl.multiple_of(c * chunk + part * LANES, LANES), LANES)
        return [tall(taps_ref[at + k * 8 : at + (k + 1) * 8, lane]) for k in range(9)]

    lines = 16

    def do_chunk(c, carry):
        lanes = lanes_of(c)
        for t in range(length // big):
            rows = slice(t * big, (t + 1) * big)
            values = dot(normed_ref[rows, :], w_ref[0, :, lanes])
            for part in range(2):
                for s in range(big // GRID_W):
                    at = place(t * (big // GRID_W) + s)
                    h_refs[part][pl.ds(at, GRID_W), :] = values[
                        s * GRID_W : (s + 1) * GRID_W, part * LANES : (part + 1) * LANES
                    ]
        act_grads_ref[...] = dot(out_grad_ref[...], w_ref[1, :, lanes])

        def forward(t, carry):
            tokens_base = pl.multiple_of(t * (lines * GRID_W), lines * GRID_W)
            for part in range(2):
                taps = taps_for(c, part, 0)
                cols = slice(part * LANES, (part + 1) * LANES)
                for s in range(lines):
                    near = pl.ds(pl.multiple_of(tokens_base + s * GRID_W, GRID_W), GRID_W)
                    at = place(t * lines + s)
                    x = total_of([x * tap for x, tap in zip(neighbours(h_refs[part], at), taps)])
                    square = x * x
                    value = jnp.tanh(x * (GELU_A + square))
                    gate = 1.0 + value
                    twice = x * gate
                    acts_ref[near, cols] = twice.astype(bf16)
                    slope = gate + (twice * (1.0 - value)) * (GELU_A + 3.0 * square)
                    g_refs[part][pl.ds(at, GRID_W), :] = act_grads_ref[near, cols] * slope
            return carry

        lax.fori_loop(0, grid_rows // lines, forward, 0)

        def backward(t, carry):
            tokens_base = pl.multiple_of(t * (lines * GRID_W), lines * GRID_W)
            for part in range(2):
                taps = taps_for(c, part, 72)
                lane = pl.ds(pl.multiple_of(c * chunk + part * LANES, LANES), LANES)
                cols = slice(part * LANES, (part + 1) * LANES)
                totals = [None] * 9
                for s in range(lines):
                    near = pl.ds(pl.multiple_of(tokens_base + s * GRID_W, GRID_W), GRID_W)
                    at = place(t * lines + s)
                    source = h_refs[part][pl.ds(at, GRID_W), :]
                    moved = neighbours(g_refs[part], at)[::-1]
                    for k in range(9):
                        product = source * moved[k]
                        folded = product[:8] + product[8:]
                        totals[k] = folded if totals[k] is None else totals[k] + folded
                    terms = [x * tap for x, tap in zip(moved, taps)]
                    hidden_grads_ref[near, cols] = total_of(terms).astype(bf16)
                for k in range(9):
                    tap_sum_ref[k * 8 : (k + 1) * 8, lane] += totals[k]
            return carry

        lax.fori_loop(0, grid_rows // lines, backward, 0)
        w_grad_ref[0, :, lanes] += dot(normed_t_ref[...], hidden_grads_ref[...])
        w_grad_ref[1, :, lanes] += dot(out_grad_t_ref[...], acts_ref[...])
        out_sum_ref[...] += dot(acts_ref[...], w_ref[1, :, lanes], NT)
        up_sum_ref[...] += dot(hidden_grads_ref[...], w_ref[0, :, lanes], NT)
        return carry

    lax.fori_loop(0, chunks, do_chunk, 0)

    def finish(step, carry):
        rows = pl.ds(pl.multiple_of(step * big, big), big)
        middle = middle_ref[rows, :]
        output_ref[rows, :] = (middle + ACT_SCALE * out_sum_ref[rows, :]).astype(bf16)
        upstream = 0.5 * up_sum_ref[rows, :]
        unit, inverse = norm_parts(middle)
        middle_grad_ref[rows, :] = out_grad_ref[rows, :].astype(f32) + norm_back(upstream, gain, unit, inverse)
        norm_grad_ref[0:8, :] += fold_rows(upstream * unit)
        norm_grad_ref[8:16, :] += fold_rows(upstream)
        return carry

    lax.fori_loop(0, length // big, finish, 0)

    @pl.when(row == pl.num_programs(0) - 1)
    def _():
        for k, scale in enumerate((0.5, ACT_SCALE)):
            halves = w_grad_ref[k, :, : hidden // 2], w_grad_ref[k, :, hidden // 2 :]
            keep_ref[k] = scale * jnp.where(rank_ref[0] == 0, halves[0], halves[1])
            send_ref[k] = (scale * jnp.where(rank_ref[0] == 0, halves[1], halves[0])).astype(bf16)
        taps_grad_ref[...] = jnp.zeros_like(taps_grad_ref)
        for k in range(9):
            total = jnp.sum(tap_sum_ref[k * 8 : (k + 1) * 8, :], axis=0, keepdims=True)
            taps_grad_ref[k : k + 1, :] = 0.5 * total


def mlp_layer(places, rank, middle, out_grad, mlp_use, taps, norm_w):
    rows_all, width = middle.shape
    row_count = places.shape[0]
    length = rows_all // row_count
    hidden = mlp_use.shape[2]
    half = mlp_use.shape[:2] + (hidden // 2,)
    by_row = lambda columns: pl.BlockSpec((length, columns), lambda r, *_: (r, 0))
    slots = (length // GRID_W + IMAGES + 2) * STRIDE
    return pl.pallas_call(
        mlp_kernel,
        grid_spec=pltpu.PrefetchScalarGridSpec(
            num_scalar_prefetch=2,
            grid=(row_count,),
            in_specs=[
                by_row(width),
                by_row(width),
                pl.BlockSpec(mlp_use.shape, lambda r, *_: (0, 0, 0)),
                pl.BlockSpec(taps.shape, lambda r, *_: (0, 0)),
                pl.BlockSpec(norm_w.shape, lambda r, *_: (0, 0)),
            ],
            out_specs=[
                by_row(width),
                by_row(width),
                pl.BlockSpec(half, lambda r, *_: (0, 0, 0)),
                pl.BlockSpec(half, lambda r, *_: (0, 0, 0)),
                pl.BlockSpec((16, hidden), lambda r, *_: (0, 0)),
                pl.BlockSpec((16, width), lambda r, *_: (0, 0)),
            ],
            scratch_shapes=[
                pltpu.VMEM(mlp_use.shape, f32),
                pltpu.VMEM((length, width), bf16),
                pltpu.VMEM((width, length), bf16),
                pltpu.VMEM((width, length), bf16),
                pltpu.VMEM((length, width), f32),
                pltpu.VMEM((length, width), f32),
                pltpu.VMEM((9 * 8, hidden), f32),
                pltpu.VMEM((length, 2 * LANES), f32),
                pltpu.VMEM((length, 2 * LANES), bf16),
                pltpu.VMEM((length, 2 * LANES), bf16),
            ]
            + [pltpu.VMEM((slots, LANES), f32)] * 4,
        ),
        out_shape=[
            jax.ShapeDtypeStruct((rows_all, width), bf16),
            jax.ShapeDtypeStruct((rows_all, width), f32),
            jax.ShapeDtypeStruct(half, f32),
            jax.ShapeDtypeStruct(half, bf16),
            jax.ShapeDtypeStruct((16, hidden), f32),
            jax.ShapeDtypeStruct((16, width), f32),
        ],
        compiler_params=pltpu.CompilerParams(vmem_limit_bytes=VMEM_BYTES),
    )(places, rank, middle, out_grad, mlp_use, taps, norm_w)


def attention_plan(segments):
    row_count, length = segments.shape
    tiles = segments.reshape(row_count, length // TILE, TILE)
    first, last = tiles[:, :, 0], tiles[:, :, -1]
    ids = jnp.arange(IMAGES, dtype=jnp.int32)
    begins = jnp.sum((segments[:, None, :] < ids[None, :, None]).astype(jnp.int32), axis=-1)
    ends = jnp.sum((segments[:, None, :] <= ids[None, :, None]).astype(jnp.int32), axis=-1)
    low_end = jnp.sum(jnp.where(first[:, :, None] == ids, begins[:, None, :], 0), axis=-1) // LANES * LANES
    high_end = jnp.sum(jnp.where(last[:, :, None] == ids, ends[:, None, :], 0), axis=-1)
    widths = widths_for(length)
    classes = sum(((high_end - low_end) > w).astype(jnp.int32) for w in widths[:-1])
    chosen = jnp.full_like(classes, widths[-1])
    for index, w in enumerate(widths):
        chosen = jnp.where(classes == index, w, chosen)
    starts = jnp.minimum(low_end, length - chosen)
    used = jnp.zeros((row_count, EXTRA - IMAGES), jnp.int32)
    unused = jnp.zeros((row_count, LANES - EXTRA), jnp.int32)
    first_lane = jnp.concatenate([begins, used, unused], axis=1)
    end_lane = jnp.concatenate([ends, used + length, unused], axis=1)
    by_lane = jnp.pad(jnp.stack([first_lane, end_lane], axis=1), ((0, 0), (0, 6), (0, 0)))
    by_image = jnp.broadcast_to(jnp.concatenate([begins, ends], axis=1)[:, :, None], (row_count, 2 * IMAGES, LANES))
    return starts, classes, jnp.concatenate([by_lane, by_image], axis=1)


def spread_taps(conv_use):
    taps = conv_use.astype(f32)
    own = (jnp.arange(9) == 4).astype(f32)[:, None]
    taps = jnp.repeat(taps + own, 8, axis=0)
    return jnp.concatenate([taps * GELU_S, taps], axis=0)


def line_places(segments):
    ids = segments[:, ::GRID_W]
    return (jnp.arange(ids.shape[1], dtype=jnp.int32) + ids + 1) * STRIDE + 8


def bits_of(size):
    bits = []
    b = 1
    while b < size:
        bits.append(b)
        b *= 2
    return bits


def swap(values, axis, size, bit):
    return lax.ppermute(values, axis, [(i, i ^ bit) for i in range(size)])


def gather_lines(shard, size):
    place = lax.axis_index("dp")
    bits = bits_of(size)
    groups = [bits[at : at + 2] for at in range(0, len(bits), 2)]
    held = shard[None]
    for group in reversed(groups):
        steps = range(1 << len(group))
        found = [held if step == 0 else swap(held, "dp", size, step * group[0]) for step in steps]
        mine = (place // group[0]) % len(steps)
        ordered = []
        for target in steps:
            value = found[0]
            for step in steps[1:]:
                value = jnp.where((mine ^ step) == target, found[step], value)
            ordered.append(value)
        held = jnp.stack(ordered, axis=1).reshape((-1,) + shard.shape)
    return held


def join_columns(mine, other, rank):
    first = jnp.where(rank == 0, mine, other)
    second = jnp.where(rank == 0, other, mine)
    return jnp.concatenate([first, second], axis=-1)


def gather_weights(shard, size, rank):
    count, part, columns = shard.shape
    held = gather_lines(shard, size)
    full = join_columns(held, swap(held, "head", 2, 1), rank)
    return jnp.moveaxis(full, 0, 1).reshape(count, size * part, 2 * columns)


def half_columns(values, side):
    half = values.shape[-1] // 2
    return lax.dynamic_slice_in_dim(values, side * half, half, axis=values.ndim - 1)


def by_line(values, size):
    count, rows, columns = values.shape
    return values.reshape(count, size, rows // size, columns)


def two_parts(values):
    high = values.astype(bf16)
    return jnp.concatenate([high, (values - high.astype(f32)).astype(bf16)], axis=0)


def from_parts(parts):
    count = parts.shape[0] // 2
    return parts[:count].astype(f32) + parts[count:].astype(f32)


def finish_exchange(keep, got, small_keep):
    rows = keep.size // keep.shape[-1]
    small = from_parts(two_parts(small_keep)) + from_parts(got[rows:])
    return keep + got[:rows].reshape(keep.shape).astype(f32), small


def start_exchange(send, small_send, axis, size, bit):
    sent = send.astype(bf16).reshape(-1, send.shape[-1])
    if small_send is not None:
        sent = jnp.concatenate([sent, two_parts(small_send)], axis=0)
    return swap(sent, axis, size, bit)


def halves(held, bit):
    count, lines = held.shape[:2]
    held = held.reshape((count, lines // 2, 2) + held.shape[2:])
    side = (lax.axis_index("dp") & bit) // bit
    mine = lax.dynamic_index_in_dim(held, side, 2, keepdims=False)
    return mine, lax.dynamic_index_in_dim(held, 1 - side, 2, keepdims=False)


def sum_everywhere(values, size):
    values = values + swap(values, "head", 2, 1)
    for bit in bits_of(size):
        values = values + swap(values, "dp", size, bit)
    return values


def adam_terms(grad_sum, first_old, second):
    first_new = BETA_ONE * first_old + (1.0 - BETA_ONE) * grad_sum
    second_new = BETA_TWO * second + (1.0 - BETA_TWO) * grad_sum * grad_sum
    direction = (
        first_new
        / (1.0 - BETA_ONE**STEP)
        / (jnp.sqrt(second_new / (1.0 - BETA_TWO**STEP)) + ADAM_EPS)
    )
    return (first_new, second_new, direction)


def after(first, second):
    return lax.optimization_barrier((first, second))


def body(
    size,
    tokens, grad_out, segments, counts,
    attn_w, attn_m, attn_v, mlp_w, mlp_m, mlp_v, conv_w, conv_m, conv_v, norm_w, norm_m, norm_v,
):
    rank = lax.axis_index("head")
    own_rows = segments.shape[0] // 2
    segments = lax.dynamic_slice_in_dim(segments, rank * own_rows, own_rows, axis=0)
    counts = lax.dynamic_slice_in_dim(counts, rank * own_rows, own_rows, axis=0)
    width = norm_w.shape[1]
    attn_use = gather_weights(attn_w.astype(bf16), size, rank)
    mlp_lines = lax.all_gather(mlp_w.astype(bf16), "dp", axis=1, tiled=True)
    conv_low = conv_w.astype(bf16)
    conv_use = join_columns(conv_low, swap(conv_low, "head", 2, 1), rank)
    starts, classes, images = attention_plan(segments)
    middle, qkv, context, ext = attn_forward(starts, classes, counts, tokens, attn_use, norm_w, images)
    middle, mlp_lines = after(middle, mlp_lines)
    mlp_use = join_columns(mlp_lines, swap(mlp_lines, "head", 2, 1), rank)
    rank_at = rank.astype(jnp.int32).reshape(1)
    output, grad_middle, held, send, grad_conv, grad_norm_two = mlp_layer(
        line_places(segments), rank_at, middle, grad_out, mlp_use, spread_taps(conv_use), norm_w
    )

    def back(first, count, so_far):
        return attn_backward(
            first, count, so_far, starts, classes, counts, rank_at, tokens, grad_middle, qkv, context, ext, attn_use, norm_w, images
        )

    bits = bits_of(size)
    norm_two = jnp.sum(grad_norm_two.reshape(2, 8, width), axis=1).reshape(1, 2 * width)
    columns = conv_w.shape[1]
    wide_norm = jnp.pad(norm_two, ((0, 0), (0, columns - 2 * width)))
    small = jnp.concatenate([half_columns(grad_conv[:9], rank), wide_norm])
    got = start_exchange(send, jnp.concatenate([half_columns(grad_conv[:9], 1 - rank), wide_norm]), "head", 2, 1)
    first_rows = max(1, own_rows // 3)
    so_far = back(0, first_rows, None)
    so_far, got = after(so_far, got)
    held, small = finish_exchange(held, got, small)
    keep, send = halves(by_line(held, size), bits[0])
    got = start_exchange(send, small, "dp", size, bits[0])
    so_far, send = after(so_far, send)
    grad_tokens, attn_held, attn_send, grad_norm_one = back(first_rows, own_rows - first_rows, so_far)

    attn_got = start_exchange(attn_send, None, "head", 2, 1)
    attn_held, got = after(attn_held, got)
    held, small = finish_exchange(keep, got, small)
    attn_held = by_line(attn_held + attn_got.reshape(attn_held.shape).astype(f32), size)
    for n, bit in enumerate(bits):
        attn_keep, attn_send = halves(attn_held, bit)
        more = n + 1 < len(bits)
        if more:
            keep, send = halves(held, bits[n + 1])
            attn_send, send = after(attn_send, send)
        attn_got = start_exchange(attn_send, None, "dp", size, bit)
        if more:
            got = start_exchange(send, small, "dp", size, bits[n + 1])
        attn_held = attn_keep + attn_got.reshape(attn_keep.shape).astype(f32)
        if more:
            held, small = finish_exchange(keep, got, small)
    grad_attn = attn_held.reshape(attn_w.shape)
    grad_mlp = held.reshape(mlp_w.shape)
    grad_conv = small[:9]
    norm_two = small[9, : 2 * width].reshape(2, width)

    new_attn_m, new_attn_v, attn_direction = adam_terms(grad_attn, attn_m, attn_v)
    new_mlp_m, new_mlp_v, mlp_direction = adam_terms(grad_mlp, mlp_m, mlp_v)
    new_conv_m, new_conv_v, conv_direction = adam_terms(grad_conv, conv_m, conv_v)
    attn_update = attn_direction + DECAY * attn_w
    mlp_update = mlp_direction + DECAY * mlp_w
    conv_update = conv_direction + DECAY * conv_w
    first_line = (lax.axis_index("dp") == 0).astype(f32)
    weight_squares = jnp.concatenate(
        [
            jnp.sum(attn_w * attn_w, axis=(1, 2)),
            jnp.sum(mlp_w * mlp_w, axis=(1, 2)),
            (first_line * jnp.sum(conv_w * conv_w))[None],
        ]
    )
    update_squares = jnp.concatenate(
        [
            jnp.sum(attn_update * attn_update, axis=(1, 2)),
            jnp.sum(mlp_update * mlp_update, axis=(1, 2)),
            (first_line * jnp.sum(conv_update * conv_update))[None],
        ]
    )
    squares = jnp.pad(jnp.stack([weight_squares, update_squares]), ((0, 0), (0, width - 7)))
    norm_one = jnp.sum(grad_norm_one.reshape(2, 8, width), axis=1)
    summed = sum_everywhere(jnp.concatenate([squares, norm_one, jnp.zeros((4, width), f32)]), size)
    squares, norm_grads = summed[:2, :7], jnp.concatenate([summed[2:4], norm_two])
    ratio = jnp.sqrt(squares[0]) / jnp.sqrt(squares[1])
    new_attn_w = attn_w - RATE * ratio[:4, None, None] * attn_update
    new_mlp_w = mlp_w - RATE * ratio[4:6, None, None] * mlp_update
    new_conv_w = conv_w - RATE * ratio[6] * conv_update
    new_norm_m, new_norm_v, norm_direction = adam_terms(norm_grads, norm_m, norm_v)
    new_norm_w = norm_w - RATE * norm_direction
    return (
        output, grad_tokens, new_attn_w, new_attn_m, new_attn_v, new_mlp_w, new_mlp_m, new_mlp_v,
        new_conv_w, new_conv_m, new_conv_v, new_norm_w, new_norm_m, new_norm_v,
    )


def solution(mesh):
    rows, lines = P(("dp", "head"), None), P("dp", None)
    shards, columns = P(None, "dp", "head"), P(None, "head")
    in_specs = (rows, rows, lines, P("dp")) + (shards,) * 6 + (columns,) * 3 + (P(),) * 3
    out_specs = (rows, rows) + (shards,) * 6 + (columns,) * 3 + (P(),) * 3
    return jax.shard_map(
        functools.partial(body, mesh.shape["dp"]), mesh=mesh, in_specs=in_specs, out_specs=out_specs, check_vma=False
    )
```

```python
import functools
import jax
import jax.numpy as jnp
from jax import lax
from jax.experimental import pallas as pl
from jax.experimental.pallas import tpu as pltpu
from jax.sharding import PartitionSpec as P

HEAD_DIM = 64
GRID_W = 16
STEP = 10
IMAGES = 8

NORM_EPS = 1e-06
BETA_ONE = 0.9
BETA_TWO = 0.999
ADAM_EPS = 1e-06
DECAY = 0.01
RATE = 0.5
LOG2E = 1.4426950408889634
LN2 = 0.6931471805599453
BIG = 2.0**100
GELU_ONE = 0.7978845608028654
GELU_TWO = 0.044715
GELU_S = (GELU_ONE * GELU_TWO) ** (1.0 / 3.0)
GELU_A = GELU_ONE / GELU_S
ACT_SCALE = 0.5 / GELU_S
EXTRA = 32
TILE = 128
LANES = 128
STRIDE = GRID_W + 8
VMEM_BYTES = 60 * 1024 * 1024

f32 = jnp.float32
bf16 = jnp.bfloat16
NN = (((1,), (0,)), ((), ()))
NT = (((1,), (1,)), ((), ()))
TN = (((0,), (0,)), ((), ()))


def dot(left, right, dims=NN):
    return lax.dot_general(left, right, dims, preferred_element_type=f32)


def widths_for(length):
    return [w for w in (256, 384, 512, 768) if w < length] + [length]


def norm_parts(values):
    average = jnp.mean(values, axis=-1, keepdims=True)
    centered = values - average
    inverse = lax.rsqrt(jnp.mean(centered * centered, axis=-1, keepdims=True) + NORM_EPS)
    return centered * inverse, inverse


def norm_back(upstream, gain_row, unit_rows, inverse):
    grad_unit = upstream * gain_row
    first_term = jnp.mean(grad_unit, axis=-1, keepdims=True)
    second_term = jnp.mean(grad_unit * unit_rows, axis=-1, keepdims=True)
    return inverse * (grad_unit - first_term - unit_rows * second_term)


def fold_rows(values):
    rows, columns = values.shape
    return jnp.sum(values.reshape(rows // 8, 8, columns), axis=0)


def pair_columns(flat):
    empty = jnp.zeros((HEAD_DIM, LANES), flat.dtype)
    return jnp.concatenate(
        [jnp.concatenate([flat[:HEAD_DIM], empty], axis=0), jnp.concatenate([empty, flat[HEAD_DIM:]], axis=0)], axis=1
    )


def pair_rows(both):
    return jnp.concatenate([both[:HEAD_DIM, :LANES], both[HEAD_DIM:, LANES:]], axis=0)


def fold_max(values):
    pieces = [values[at : at + 64] for at in range(0, values.shape[0], 64)]
    while len(pieces) > 1:
        pieces = [jnp.maximum(a, b) for a, b in zip(pieces[::2], pieces[1::2])] + ([pieces[-1]] if len(pieces) % 2 else [])
    top = pieces[0]
    top = jnp.maximum(top[:32], top[32:])
    top = jnp.maximum(top[:16], top[16:])
    return jnp.max(jnp.maximum(top[:8], top[8:]), axis=0, keepdims=True)


def three_parts(value, part):
    high = value.astype(bf16).astype(f32)
    rest = value - high
    middle = rest.astype(bf16).astype(f32)
    return jnp.where(part == 0, high, jnp.where(part == 1, middle, rest - middle))


def image_tags(image_ref, start, rows):
    place = start + lax.broadcasted_iota(jnp.int32, (rows, LANES), 0)
    inside = (place >= image_ref[0, 0:1, :]) & (place < image_ref[0, 1:2, :])
    return jnp.where(inside, 1.0, 0.0).astype(bf16)


def attn_forward_kernel(
    start_ref, class_ref, count_ref, tokens_ref, w_ref, norm_ref, image_ref,
    middle_ref, qkv_ref, context_ref, ext_ref,
    tag_ref, normed_ref, qt_ref, vt_ref,
):
    row = pl.program_id(0)
    length, width = tokens_ref.shape
    pairs = width // LANES
    big = 256
    gain, bias = norm_ref[0:1, :], norm_ref[1:2, :]

    def prepare(step, carry):
        rows = pl.ds(pl.multiple_of(step * big, big), big)
        unit, _ = norm_parts(tokens_ref[rows, :].astype(f32))
        normed_ref[rows, :] = (unit * gain + bias).astype(bf16)
        tag_ref[rows, :] = image_tags(image_ref, step * big, big)
        return carry

    lax.fori_loop(0, length // big, prepare, 0)
    queries = (dot(normed_ref[...], w_ref[0]) * (HEAD_DIM**-0.5 * LOG2E)).astype(bf16)
    qkv_ref[:, :width] = queries
    qt_ref[...] = jnp.transpose(queries)
    qkv_ref[:, width : 2 * width] = dot(normed_ref[...], w_ref[1]).astype(bf16)
    values = dot(normed_ref[...], w_ref[2]).astype(bf16)
    qkv_ref[:, 2 * width :] = values
    vt_ref[...] = jnp.transpose(values)

    def tile(step, carry):
        q0 = pl.multiple_of(step * TILE, TILE)
        here = pl.ds(q0, TILE)
        place = q0 + lax.broadcasted_iota(jnp.int32, (IMAGES, LANES), 1)
        inside = (place >= image_ref[0, 8 : 8 + IMAGES, :]) & (place < image_ref[0, 16 : 16 + IMAGES, :])
        mask = jnp.where(inside, 0.0, -BIG)
        mask_low = jnp.concatenate([mask, jnp.zeros((LANES - IMAGES, LANES), f32)], axis=0).astype(bf16)
        ext_rows = lax.broadcasted_iota(jnp.int32, (EXTRA - IMAGES, LANES), 0)

        def attend(window):
            there = pl.ds(pl.multiple_of(start_ref[row, step], LANES), window)
            tags = tag_ref[there, :]
            ones = jnp.ones((GRID_W, window), bf16)
            extra = jnp.zeros((EXTRA - IMAGES, LANES), f32)
            slices = [slice(p * LANES, (p + 1) * LANES) for p in range(pairs)]
            masks = jnp.concatenate([mask_low, mask_low], axis=1)
            scores, tops, exponents, mixes = [], [], [], []
            for p, at in enumerate(slices):
                keys = qkv_ref[there, width + p * LANES : width + (p + 1) * LANES]
                right = jnp.concatenate([pair_columns(qt_ref[at, here]), masks], axis=0)
                scores.append(dot(jnp.concatenate([keys, tags], axis=1), right))
            for p in range(pairs):
                tops.append(fold_max(scores[p]))
                exponents.append(jnp.exp2(scores[p] - tops[p]).astype(bf16))
            for p, at in enumerate(slices):
                mixes.append(dot(jnp.concatenate([vt_ref[at, there], ones], axis=0), exponents[p]))
            for p, at in enumerate(slices):
                mixed = mixes[p]
                total = mixed[LANES : LANES + 1, :]
                minus_lse = -(tops[p] + jnp.log(total) * LOG2E)
                scale = 1.0 / total
                lane = lax.broadcasted_iota(jnp.int32, (1, 2 * TILE), 1)
                head = 2 * p + jnp.where(lane < TILE, 0, 1)
                scale = jnp.where(head < count_ref[row], scale, 0.0)
                context_ref[here, at] = jnp.transpose(pair_rows(mixed[:LANES] * scale)).astype(bf16)
                for h in range(2):
                    value = minus_lse[:, h * TILE : (h + 1) * TILE]
                    first = 6 * p + 3 * h
                    extra = jnp.where(
                        (ext_rows >= first) & (ext_rows < first + 3), three_parts(value, ext_rows - first), extra
                    )
            ext_ref[:, here] = jnp.concatenate([mask, extra], axis=0).astype(bf16)

        for index, window in enumerate(widths_for(length)):
            pl.when(class_ref[row, step] == index)(functools.partial(attend, window))
        return carry

    lax.fori_loop(0, length // TILE, tile, 0)
    middle_ref[...] = tokens_ref[...].astype(f32) + dot(context_ref[...], w_ref[3], NT)


def attn_forward(starts, classes, counts, tokens, attn_use, norm_w, images):
    rows_all, width = tokens.shape
    row_count = counts.shape[0]
    length = rows_all // row_count
    by_row = lambda columns: pl.BlockSpec((length, columns), lambda r, *_: (r, 0))
    return pl.pallas_call(
        attn_forward_kernel,
        grid_spec=pltpu.PrefetchScalarGridSpec(
            num_scalar_prefetch=3,
            grid=(row_count,),
            in_specs=[
                by_row(width),
                pl.BlockSpec(attn_use.shape, lambda r, *_: (0, 0, 0)),
                pl.BlockSpec(norm_w.shape, lambda r, *_: (0, 0)),
                pl.BlockSpec((1, 24, LANES), lambda r, *_: (r, 0, 0)),
            ],
            out_specs=[
                by_row(width), by_row(3 * width), by_row(width), pl.BlockSpec((EXTRA, length), lambda r, *_: (r, 0))
            ],
            scratch_shapes=[
                pltpu.VMEM((length, LANES), bf16),
                pltpu.VMEM((length, width), bf16),
                pltpu.VMEM((width, length), bf16),
                pltpu.VMEM((width, length), bf16),
            ],
        ),
        out_shape=[
            jax.ShapeDtypeStruct((rows_all, width), f32),
            jax.ShapeDtypeStruct((rows_all, 3 * width), bf16),
            jax.ShapeDtypeStruct((rows_all, width), bf16),
            jax.ShapeDtypeStruct((row_count * EXTRA, length), bf16),
        ],
        compiler_params=pltpu.CompilerParams(vmem_limit_bytes=VMEM_BYTES),
    )(starts, classes, counts, tokens, attn_use, norm_w, images)


def attn_backward_kernel(
    first, final, start_ref, class_ref, count_ref, rank_ref, tokens_ref, middle_grad_ref, qkv_ref, context_ref, ext_ref, w_ref, norm_ref,
    image_ref, *refs,
):
    sums = None
    if first:
        sums, refs = refs[1:3], refs[3:]
    sent = None
    if final:
        tokens_grad_ref, keep_ref, send_ref, norm_grad_ref, *scratch, w_grad_ref = refs
        sent = (keep_ref, send_ref)
    else:
        tokens_grad_ref, w_grad_ref, norm_grad_ref, *scratch = refs
    attn_backward_row(
        first, sums, sent, start_ref, class_ref, count_ref, rank_ref, tokens_ref, middle_grad_ref, qkv_ref, context_ref, ext_ref, w_ref,
        norm_ref, image_ref, tokens_grad_ref, w_grad_ref, norm_grad_ref, *scratch,
    )


def attn_backward_row(
    first, sums, sent, start_ref, class_ref, count_ref, rank_ref, tokens_ref, middle_grad_ref, qkv_ref, context_ref, ext_ref, w_ref,
    norm_ref, image_ref, tokens_grad_ref, w_grad_ref, norm_grad_ref,
    tag_ref, up_ref, delta_ref, normed_ref, dq_ref, dk_ref, dv_ref, low_ref, proj_ref, qt_ref, kt_ref, upt_ref, upstream_ref,
):
    step_at = pl.program_id(0)
    row = first + step_at
    length, width = tokens_ref.shape
    pairs = width // LANES
    big = 256
    gain, bias = norm_ref[0:1, :], norm_ref[1:2, :]

    @pl.when(step_at == 0)
    def _():
        for n, ref in enumerate((w_grad_ref, norm_grad_ref)):
            ref[...] = sums[n][...] if sums else jnp.zeros_like(ref)

    target = lax.broadcasted_iota(jnp.int32, (EXTRA, width), 0) - IMAGES
    source = lax.broadcasted_iota(jnp.int32, (EXTRA, width), 1) // HEAD_DIM * 3
    collect = jnp.where((target >= source) & (target < source + 3), -1.0, 0.0).astype(bf16)
    active = jnp.where(
        lax.broadcasted_iota(jnp.int32, (1, width), 1) // HEAD_DIM < count_ref[row], 1.0, 0.0
    )

    def prepare(step, carry):
        rows = pl.ds(pl.multiple_of(step * big, big), big)
        unit, _ = norm_parts(tokens_ref[rows, :].astype(f32))
        normed_ref[rows, :] = (unit * gain + bias).astype(bf16)
        tag_ref[rows, :] = image_tags(image_ref, step * big, big)
        low_ref[rows, :] = middle_grad_ref[rows, :].astype(bf16)
        dk_ref[rows, :] = jnp.zeros((big, width), f32)
        dv_ref[rows, :] = jnp.zeros((big, width), f32)
        return carry

    lax.fori_loop(0, length // big, prepare, 0)
    up = (dot(low_ref[...], w_ref[3]) * active).astype(bf16)
    up_ref[...] = up
    upt_ref[...] = jnp.transpose(up)
    qt_ref[...] = jnp.transpose(qkv_ref[:, :width])
    kt_ref[...] = jnp.transpose(qkv_ref[:, width : 2 * width])

    def gather(step, carry):
        rows = pl.ds(pl.multiple_of(step * big, big), big)
        product = up_ref[rows, :].astype(f32) * context_ref[rows, :].astype(f32)
        high = product.astype(bf16)
        rest = (product - high.astype(f32)).astype(bf16)
        delta = dot(collect, high, NT) + dot(collect, rest, NT)
        part = lax.rem(lax.broadcasted_iota(jnp.int32, (EXTRA, big), 0) + 3 * EXTRA - IMAGES, 3)
        delta_ref[:, rows] = three_parts(delta, part).astype(bf16)
        return carry

    lax.fori_loop(0, length // big, gather, 0)
    lane = lax.broadcasted_iota(jnp.int32, (1, LANES), 1)
    first_half = jnp.where(lane < HEAD_DIM, 1.0, 0.0).astype(bf16)
    second_half = jnp.where(lane >= HEAD_DIM, 1.0, 0.0).astype(bf16)

    def tile(step, carry):
        q0 = pl.multiple_of(step * TILE, TILE)
        here = pl.ds(q0, TILE)

        def attend(window):
            there = pl.ds(pl.multiple_of(start_ref[row, step], LANES), window)
            tags = tag_ref[there, :]
            ext = ext_ref[:, here]
            delta = delta_ref[:, here]
            at_row = lax.broadcasted_iota(jnp.int32, (EXTRA, LANES), 0)
            empty = jnp.zeros((LANES - EXTRA, 2 * TILE), bf16)

            def own(edge, masks):
                keep = (at_row >= edge) & (at_row < edge + 3)
                return jnp.where(keep | (at_row < IMAGES) if masks else keep, 1.0, 0.0).astype(bf16)

            slices = [slice(p * LANES, (p + 1) * LANES) for p in range(pairs)]
            scores, grad_probs, probs, grad_scores = [], [], [], []
            for p, at in enumerate(slices):
                keys = qkv_ref[there, width + p * LANES : width + (p + 1) * LANES]
                values = qkv_ref[there, 2 * width + p * LANES : 2 * width + (p + 1) * LANES]
                edge = IMAGES + 6 * p
                q_side = jnp.concatenate(
                    [
                        pair_columns(qt_ref[at, here]),
                        jnp.concatenate([ext * own(edge, True), ext * own(edge + 3, True)], axis=1),
                        empty,
                    ],
                    axis=0,
                )
                up_side = jnp.concatenate(
                    [
                        pair_columns(upt_ref[at, here]),
                        jnp.concatenate([delta * own(edge, False), delta * own(edge + 3, False)], axis=1),
                        empty,
                    ],
                    axis=0,
                )
                scores.append(dot(jnp.concatenate([keys, tags], axis=1), q_side))
                grad_probs.append(dot(jnp.concatenate([values, tags], axis=1), up_side))
            for p in range(pairs):
                weight = jnp.exp2(scores[p])
                probs.append(weight.astype(bf16))
                grad_scores.append((weight * grad_probs[p]).astype(bf16))
            for p, at in enumerate(slices):
                queries, ups = qkv_ref[here, at], up_ref[here, at]
                q_pair = jnp.concatenate([queries * first_half, queries * second_half], axis=0)
                up_pair = jnp.concatenate([ups * first_half, ups * second_half], axis=0)
                dv_ref[there, at] += dot(probs[p], up_pair)
                dk_ref[there, at] += dot(grad_scores[p], q_pair)
                dq = pair_rows(dot(kt_ref[at, there], grad_scores[p]))
                dq_ref[here, at] = jnp.transpose(dq * HEAD_DIM**-0.5).astype(bf16)

        for index, window in enumerate(widths_for(length)):
            pl.when(class_ref[row, step] == index)(functools.partial(attend, window))
        return carry

    lax.fori_loop(0, length // TILE, tile, 0)
    keys_grad = (dk_ref[...] * LN2).astype(bf16)
    values_grad = dv_ref[...].astype(bf16)
    proj_ref[...] = jnp.concatenate([dq_ref[...], keys_grad, values_grad], axis=1)
    w_cat = jnp.concatenate([w_ref[0], w_ref[1], w_ref[2]], axis=1)
    upstream_ref[...] = dot(proj_ref[...], w_cat, NT)

    def finish(step, carry):
        rows = pl.ds(pl.multiple_of(step * big, big), big)
        upstream = upstream_ref[rows, :]
        unit, inverse = norm_parts(tokens_ref[rows, :].astype(f32))
        tokens_grad_ref[rows, :] = middle_grad_ref[rows, :] + norm_back(upstream, gain, unit, inverse)
        norm_grad_ref[0:8, :] += fold_rows(upstream * unit)
        norm_grad_ref[8:16, :] += fold_rows(upstream)
        return carry

    lax.fori_loop(0, length // big, finish, 0)
    normed_t = jnp.transpose(normed_ref[...])
    for k in range(3):
        w_grad_ref[k] += dot(normed_t, proj_ref[:, k * width : (k + 1) * width])
    w_grad_ref[3] += dot(jnp.transpose(low_ref[...]), context_ref[...])
    if sent:

        @pl.when(step_at == pl.num_programs(0) - 1)
        def _():
            for k in range(2):
                one, two = w_grad_ref[k], w_grad_ref[k + 2]
                halves = [jnp.concatenate([one[:, at : at + width // 2], two[:, at : at + width // 2]], axis=1) for at in (0, width // 2)]
                sent[0][k] = jnp.where(rank_ref[0] == 0, halves[0], halves[1])
                sent[1][k] = jnp.where(rank_ref[0] == 0, halves[1], halves[0]).astype(bf16)


def attn_backward(first, count, so_far, starts, classes, counts, rank, tokens, middle_grad, qkv, context, ext, attn_use, norm_w, images):
    rows_all, width = tokens.shape
    length = rows_all // counts.shape[0]
    by_row = lambda columns: pl.BlockSpec((length, columns), lambda r, *_: (first + r, 0))
    final = first + count == counts.shape[0]
    half = (2, width, width)
    halves = pl.BlockSpec(half, lambda r, *_: (0, 0, 0))
    whole = pl.BlockSpec(attn_use.shape, lambda r, *_: (0, 0, 0))
    sums = pl.BlockSpec((16, width), lambda r, *_: (0, 0))
    return pl.pallas_call(
        functools.partial(attn_backward_kernel, first, final),
        grid_spec=pltpu.PrefetchScalarGridSpec(
            num_scalar_prefetch=4,
            grid=(count,),
            in_specs=[
                by_row(width),
                by_row(width),
                by_row(3 * width),
                by_row(width),
                pl.BlockSpec((EXTRA, length), lambda r, *_: (first + r, 0)),
                whole,
                pl.BlockSpec(norm_w.shape, lambda r, *_: (0, 0)),
                pl.BlockSpec((1, 24, LANES), lambda r, *_: (first + r, 0, 0)),
            ]
            + ([pl.BlockSpec(memory_space=pl.ANY), whole, sums] if first else []),
            out_specs=[by_row(width), halves, halves, sums] if final else [by_row(width), whole, sums],
            scratch_shapes=[
                pltpu.VMEM((length, LANES), bf16),
                pltpu.VMEM((length, width), bf16),
                pltpu.VMEM((EXTRA, length), bf16),
                pltpu.VMEM((length, width), bf16),
                pltpu.VMEM((length, width), bf16),
                pltpu.VMEM((length, width), f32),
                pltpu.VMEM((length, width), f32),
                pltpu.VMEM((length, width), bf16),
                pltpu.VMEM((length, 3 * width), bf16),
                pltpu.VMEM((width, length), bf16),
                pltpu.VMEM((width, length), bf16),
                pltpu.VMEM((width, length), bf16),
                pltpu.VMEM((length, width), f32),
            ]
            + ([pltpu.VMEM(attn_use.shape, f32)] if final else []),
        ),
        out_shape=[jax.ShapeDtypeStruct((rows_all, width), f32)]
        + (
            [jax.ShapeDtypeStruct(half, f32), jax.ShapeDtypeStruct(half, bf16)]
            if final
            else [jax.ShapeDtypeStruct(attn_use.shape, f32)]
        )
        + [jax.ShapeDtypeStruct((16, width), f32)],
        input_output_aliases={12: 0} if first else {},
        compiler_params=pltpu.CompilerParams(vmem_limit_bytes=VMEM_BYTES),
    )(starts, classes, counts, rank, tokens, middle_grad, qkv, context, ext, attn_use, norm_w, images, *(so_far or ()))


def mlp_kernel(
    place_ref, rank_ref, middle_ref, out_grad_ref, w_ref, taps_ref, norm_ref,
    output_ref, middle_grad_ref, keep_ref, send_ref, taps_grad_ref, norm_grad_ref,
    w_grad_ref, normed_ref, normed_t_ref, out_grad_t_ref, out_sum_ref, up_sum_ref, tap_sum_ref,
    act_grads_ref, acts_ref, hidden_grads_ref, *buffers,
):
    row = pl.program_id(0)
    length, width = middle_ref.shape
    hidden = w_ref.shape[2]
    chunk = 2 * LANES
    big = 256
    grid_rows = length // GRID_W
    chunks = hidden // chunk
    h_refs, g_refs = buffers[:2], buffers[2:]
    gain, bias = norm_ref[2:3, :], norm_ref[3:4, :]

    @pl.when(row == 0)
    def _():
        w_grad_ref[...] = jnp.zeros_like(w_grad_ref)
        norm_grad_ref[...] = jnp.zeros_like(norm_grad_ref)
        tap_sum_ref[...] = jnp.zeros_like(tap_sum_ref)

    for ref in buffers:
        ref[...] = jnp.zeros_like(ref)

    def normalize(step, carry):
        rows = pl.ds(pl.multiple_of(step * big, big), big)
        middle = middle_ref[rows, :]
        unit, _ = norm_parts(middle)
        normed_ref[rows, :] = (unit * gain + bias).astype(bf16)
        out_sum_ref[rows, :] = jnp.zeros((big, width), f32)
        up_sum_ref[rows, :] = jnp.zeros((big, width), f32)
        return carry

    lax.fori_loop(0, length // big, normalize, 0)
    normed_t_ref[...] = jnp.transpose(normed_ref[...])
    out_grad_t_ref[...] = jnp.transpose(out_grad_ref[...])

    def lanes_of(c):
        return pl.ds(pl.multiple_of(c * chunk, chunk), chunk)

    def lanes_of(c):
        return pl.ds(pl.multiple_of(c * chunk, chunk), chunk)

    def place(r):
        return pl.multiple_of(place_ref[row, r], 8)

    def neighbours(ref, at):
        return [ref[pl.ds(at + (a * STRIDE + b), GRID_W), :] for a in (-1, 0, 1) for b in (-1, 0, 1)]

    def tall(values):
        return jnp.concatenate([values, values], axis=0)

    def total_of(terms):
        while len(terms) > 1:
            terms = [a + b for a, b in zip(terms[::2], terms[1::2])] + ([terms[-1]] if len(terms) % 2 else [])
        return terms[0]

    def taps_for(c, part, at):
        lane = pl.ds(pl.multiple_of(c * chunk + part * LANES, LANES), LANES)
        return [tall(taps_ref[at + k * 8 : at + (k + 1) * 8, lane]) for k in range(9)]

    lines = 16

    def do_chunk(c, carry):
        lanes = lanes_of(c)
        for t in range(length // big):
            rows = slice(t * big, (t + 1) * big)
            values = dot(normed_ref[rows, :], w_ref[0, :, lanes])
            for part in range(2):
                for s in range(big // GRID_W):
                    at = place(t * (big // GRID_W) + s)
                    h_refs[part][pl.ds(at, GRID_W), :] = values[
                        s * GRID_W : (s + 1) * GRID_W, part * LANES : (part + 1) * LANES
                    ]
        act_grads_ref[...] = dot(out_grad_ref[...], w_ref[1, :, lanes])

        def forward(t, carry):
            tokens_base = pl.multiple_of(t * (lines * GRID_W), lines * GRID_W)
            for part in range(2):
                taps = taps_for(c, part, 0)
                cols = slice(part * LANES, (part + 1) * LANES)
                for s in range(lines):
                    near = pl.ds(pl.multiple_of(tokens_base + s * GRID_W, GRID_W), GRID_W)
                    at = place(t * lines + s)
                    x = total_of([x * tap for x, tap in zip(neighbours(h_refs[part], at), taps)])
                    square = x * x
                    value = jnp.tanh(x * (GELU_A + square))
                    gate = 1.0 + value
                    twice = x * gate
                    acts_ref[near, cols] = twice.astype(bf16)
                    slope = gate + (twice * (1.0 - value)) * (GELU_A + 3.0 * square)
                    g_refs[part][pl.ds(at, GRID_W), :] = act_grads_ref[near, cols] * slope
            return carry

        lax.fori_loop(0, grid_rows // lines, forward, 0)

        def backward(t, carry):
            tokens_base = pl.multiple_of(t * (lines * GRID_W), lines * GRID_W)
            for part in range(2):
                taps = taps_for(c, part, 72)
                lane = pl.ds(pl.multiple_of(c * chunk + part * LANES, LANES), LANES)
                cols = slice(part * LANES, (part + 1) * LANES)
                totals = [None] * 9
                for s in range(lines):
                    near = pl.ds(pl.multiple_of(tokens_base + s * GRID_W, GRID_W), GRID_W)
                    at = place(t * lines + s)
                    source = h_refs[part][pl.ds(at, GRID_W), :]
                    moved = neighbours(g_refs[part], at)[::-1]
                    for k in range(9):
                        product = source * moved[k]
                        folded = product[:8] + product[8:]
                        totals[k] = folded if totals[k] is None else totals[k] + folded
                    terms = [x * tap for x, tap in zip(moved, taps)]
                    hidden_grads_ref[near, cols] = total_of(terms).astype(bf16)
                for k in range(9):
                    tap_sum_ref[k * 8 : (k + 1) * 8, lane] += totals[k]
            return carry

        lax.fori_loop(0, grid_rows // lines, backward, 0)
        w_grad_ref[0, :, lanes] += dot(normed_t_ref[...], hidden_grads_ref[...])
        w_grad_ref[1, :, lanes] += dot(out_grad_t_ref[...], acts_ref[...])
        out_sum_ref[...] += dot(acts_ref[...], w_ref[1, :, lanes], NT)
        up_sum_ref[...] += dot(hidden_grads_ref[...], w_ref[0, :, lanes], NT)
        return carry

    lax.fori_loop(0, chunks, do_chunk, 0)

    def finish(step, carry):
        rows = pl.ds(pl.multiple_of(step * big, big), big)
        middle = middle_ref[rows, :]
        output_ref[rows, :] = (middle + ACT_SCALE * out_sum_ref[rows, :]).astype(bf16)
        upstream = 0.5 * up_sum_ref[rows, :]
        unit, inverse = norm_parts(middle)
        middle_grad_ref[rows, :] = out_grad_ref[rows, :].astype(f32) + norm_back(upstream, gain, unit, inverse)
        norm_grad_ref[0:8, :] += fold_rows(upstream * unit)
        norm_grad_ref[8:16, :] += fold_rows(upstream)
        return carry

    lax.fori_loop(0, length // big, finish, 0)

    @pl.when(row == pl.num_programs(0) - 1)
    def _():
        for k, scale in enumerate((0.5, ACT_SCALE)):
            halves = w_grad_ref[k, :, : hidden // 2], w_grad_ref[k, :, hidden // 2 :]
            keep_ref[k] = scale * jnp.where(rank_ref[0] == 0, halves[0], halves[1])
            send_ref[k] = (scale * jnp.where(rank_ref[0] == 0, halves[1], halves[0])).astype(bf16)
        taps_grad_ref[...] = jnp.zeros_like(taps_grad_ref)
        for k in range(9):
            total = jnp.sum(tap_sum_ref[k * 8 : (k + 1) * 8, :], axis=0, keepdims=True)
            taps_grad_ref[k : k + 1, :] = 0.5 * total


def mlp_layer(places, rank, middle, out_grad, mlp_use, taps, norm_w):
    rows_all, width = middle.shape
    row_count = places.shape[0]
    length = rows_all // row_count
    hidden = mlp_use.shape[2]
    half = mlp_use.shape[:2] + (hidden // 2,)
    by_row = lambda columns: pl.BlockSpec((length, columns), lambda r, *_: (r, 0))
    slots = (length // GRID_W + IMAGES + 2) * STRIDE
    return pl.pallas_call(
        mlp_kernel,
        grid_spec=pltpu.PrefetchScalarGridSpec(
            num_scalar_prefetch=2,
            grid=(row_count,),
            in_specs=[
                by_row(width),
                by_row(width),
                pl.BlockSpec(mlp_use.shape, lambda r, *_: (0, 0, 0)),
                pl.BlockSpec(taps.shape, lambda r, *_: (0, 0)),
                pl.BlockSpec(norm_w.shape, lambda r, *_: (0, 0)),
            ],
            out_specs=[
                by_row(width),
                by_row(width),
                pl.BlockSpec(half, lambda r, *_: (0, 0, 0)),
                pl.BlockSpec(half, lambda r, *_: (0, 0, 0)),
                pl.BlockSpec((16, hidden), lambda r, *_: (0, 0)),
                pl.BlockSpec((16, width), lambda r, *_: (0, 0)),
            ],
            scratch_shapes=[
                pltpu.VMEM(mlp_use.shape, f32),
                pltpu.VMEM((length, width), bf16),
                pltpu.VMEM((width, length), bf16),
                pltpu.VMEM((width, length), bf16),
                pltpu.VMEM((length, width), f32),
                pltpu.VMEM((length, width), f32),
                pltpu.VMEM((9 * 8, hidden), f32),
                pltpu.VMEM((length, 2 * LANES), f32),
                pltpu.VMEM((length, 2 * LANES), bf16),
                pltpu.VMEM((length, 2 * LANES), bf16),
            ]
            + [pltpu.VMEM((slots, LANES), f32)] * 4,
        ),
        out_shape=[
            jax.ShapeDtypeStruct((rows_all, width), bf16),
            jax.ShapeDtypeStruct((rows_all, width), f32),
            jax.ShapeDtypeStruct(half, f32),
            jax.ShapeDtypeStruct(half, bf16),
            jax.ShapeDtypeStruct((16, hidden), f32),
            jax.ShapeDtypeStruct((16, width), f32),
        ],
        compiler_params=pltpu.CompilerParams(vmem_limit_bytes=VMEM_BYTES),
    )(places, rank, middle, out_grad, mlp_use, taps, norm_w)


def attention_plan(segments):
    row_count, length = segments.shape
    tiles = segments.reshape(row_count, length // TILE, TILE)
    first, last = tiles[:, :, 0], tiles[:, :, -1]
    ids = jnp.arange(IMAGES, dtype=jnp.int32)
    begins = jnp.sum((segments[:, None, :] < ids[None, :, None]).astype(jnp.int32), axis=-1)
    ends = jnp.sum((segments[:, None, :] <= ids[None, :, None]).astype(jnp.int32), axis=-1)
    low_end = jnp.sum(jnp.where(first[:, :, None] == ids, begins[:, None, :], 0), axis=-1) // LANES * LANES
    high_end = jnp.sum(jnp.where(last[:, :, None] == ids, ends[:, None, :], 0), axis=-1)
    widths = widths_for(length)
    classes = sum(((high_end - low_end) > w).astype(jnp.int32) for w in widths[:-1])
    chosen = jnp.full_like(classes, widths[-1])
    for index, w in enumerate(widths):
        chosen = jnp.where(classes == index, w, chosen)
    starts = jnp.minimum(low_end, length - chosen)
    used = jnp.zeros((row_count, EXTRA - IMAGES), jnp.int32)
    unused = jnp.zeros((row_count, LANES - EXTRA), jnp.int32)
    first_lane = jnp.concatenate([begins, used, unused], axis=1)
    end_lane = jnp.concatenate([ends, used + length, unused], axis=1)
    by_lane = jnp.pad(jnp.stack([first_lane, end_lane], axis=1), ((0, 0), (0, 6), (0, 0)))
    by_image = jnp.broadcast_to(jnp.concatenate([begins, ends], axis=1)[:, :, None], (row_count, 2 * IMAGES, LANES))
    return starts, classes, jnp.concatenate([by_lane, by_image], axis=1)


def spread_taps(conv_use):
    taps = conv_use.astype(f32)
    own = (jnp.arange(9) == 4).astype(f32)[:, None]
    taps = jnp.repeat(taps + own, 8, axis=0)
    return jnp.concatenate([taps * GELU_S, taps], axis=0)


def line_places(segments):
    ids = segments[:, ::GRID_W]
    return (jnp.arange(ids.shape[1], dtype=jnp.int32) + ids + 1) * STRIDE + 8


def bits_of(size):
    bits = []
    b = 1
    while b < size:
        bits.append(b)
        b *= 2
    return bits


def groups_of(size):
    bits = bits_of(size)
    return [(bits[at], 1 << len(bits[at : at + 2])) for at in range(0, len(bits), 2)]


def swap(values, axis, size, bit):
    return lax.ppermute(values, axis, [(i, i ^ bit) for i in range(size)])


def in_order(found, mine):
    ordered = []
    for target in range(len(found)):
        value = found[0]
        for step in range(1, len(found)):
            value = jnp.where((mine ^ step) == target, found[step], value)
        ordered.append(value)
    return ordered


def gather_lines(shard, size):
    place = lax.axis_index("dp")
    held = shard[None]
    for low, count in reversed(groups_of(size)):
        found = [held] + [swap(held, "dp", size, step * low) for step in range(1, count)]
        held = jnp.stack(in_order(found, (place // low) % count), axis=1).reshape((-1,) + shard.shape)
    return held


def fold_pairs(values):
    count = values.shape[0] // 2
    return jnp.concatenate([values[:count], values[count:]], axis=-1)


def unfold_pairs(values):
    half = values.shape[-1] // 2
    return jnp.concatenate([values[..., :half], values[..., half:]], axis=0)


def join_columns(mine, other, rank):
    first = jnp.where(rank == 0, mine, other)
    second = jnp.where(rank == 0, other, mine)
    return jnp.concatenate([first, second], axis=-1)


def gather_weights(shard, size, rank):
    count, part, columns = shard.shape
    mine = gather_lines(fold_pairs(shard), size)
    other = swap(mine, "head", 2, 1)
    full = [join_columns(mine[..., at : at + columns], other[..., at : at + columns], rank) for at in (0, columns)]
    return jnp.moveaxis(jnp.concatenate(full, axis=1), 0, 1).reshape(count, size * part, 2 * columns)


def half_columns(values, side):
    half = values.shape[-1] // 2
    return lax.dynamic_slice_in_dim(values, side * half, half, axis=values.ndim - 1)


def by_line(values, size):
    count, rows, columns = values.shape
    return values.reshape(count, size, rows // size, columns)


def two_parts(values):
    high = values.astype(bf16)
    return jnp.concatenate([high, (values - high.astype(f32)).astype(bf16)], axis=0)


def from_parts(parts):
    count = parts.shape[0] // 2
    return parts[:count].astype(f32) + parts[count:].astype(f32)


def pieces_of(held, low, count):
    n, lines = held.shape[:2]
    split = held.reshape((n, lines // count, count) + held.shape[2:])
    mine = (lax.axis_index("dp") // low) % count
    return [lax.dynamic_index_in_dim(split, mine ^ step, 2, keepdims=False) for step in range(count)]


def flat(values):
    return values.astype(bf16).reshape(-1, values.shape[-1])


def sum_everywhere(values, size):
    values = values + swap(values, "head", 2, 1)
    for bit in bits_of(size):
        values = values + swap(values, "dp", size, bit)
    return values


def after(first, second):
    return lax.optimization_barrier((first, second))


def adam_terms(grad_sum, first_old, second):
    first_new = BETA_ONE * first_old + (1.0 - BETA_ONE) * grad_sum
    second_new = BETA_TWO * second + (1.0 - BETA_TWO) * grad_sum * grad_sum
    direction = (
        first_new
        / (1.0 - BETA_ONE**STEP)
        / (jnp.sqrt(second_new / (1.0 - BETA_TWO**STEP)) + ADAM_EPS)
    )
    return (first_new, second_new, direction)


def moments_kernel(line_ref, norm_ref, *refs):
    count = 3
    grads, weights, firsts, seconds = (refs[n * count : (n + 1) * count] for n in range(4))
    new_firsts, new_seconds, updates = (refs[(4 + n) * count : (5 + n) * count] for n in range(3))
    sums_ref = refs[7 * count]
    width = sums_ref.shape[1]
    lane = lax.broadcasted_iota(jnp.int32, (1, width), 1)
    rows = [jnp.zeros((1, width), f32), jnp.zeros((1, width), f32)]
    at = 0
    for n in range(count):
        grad, weight = grads[n][...], weights[n][...]
        new_first, new_second, direction = adam_terms(grad, firsts[n][...], seconds[n][...])
        update = direction + DECAY * weight
        new_firsts[n][...], new_seconds[n][...], updates[n][...] = new_first, new_second, update
        matrices = weight.shape[0] if weight.ndim == 3 else 1
        for k in range(matrices):
            for row, values in enumerate((weight, update)):
                values = values[k] if weight.ndim == 3 else values
                total = jnp.sum(jnp.sum(values * values, axis=0, keepdims=True), axis=1, keepdims=True)
                if weight.ndim == 2:
                    total = jnp.where(line_ref[0] == 0, total, 0.0)
                rows[row] = jnp.where(lane == at, total, rows[row])
            at += 1
    gain = jnp.sum(norm_ref[0:8, :], axis=0, keepdims=True)
    bias = jnp.sum(norm_ref[8:16, :], axis=0, keepdims=True)
    sums_ref[...] = jnp.concatenate(rows + [gain, bias, jnp.zeros((4, width), f32)], axis=0)


def apply_kernel(sums_ref, norm_two_ref, norm_w_ref, norm_m_ref, norm_v_ref, *refs):
    count = 3
    weights, updates, news = (refs[n * count : (n + 1) * count] for n in range(3))
    new_norm_w_ref, new_norm_m_ref, new_norm_v_ref = refs[3 * count :]
    ratio = jnp.sqrt(sums_ref[0:1, :]) / jnp.sqrt(sums_ref[1:2, :])
    at = 0
    for n in range(count):
        shape = weights[n].shape
        if len(shape) == 3:
            for k in range(shape[0]):
                news[n][k] = weights[n][k] - RATE * ratio[:, at : at + 1] * updates[n][k]
                at += 1
        else:
            news[n][...] = weights[n][...] - RATE * ratio[:, at : at + 1] * updates[n][...]
            at += 1
    grads = jnp.concatenate([sums_ref[2:4, :], norm_two_ref[...]], axis=0)
    new_first, new_second, direction = adam_terms(grads, norm_m_ref[...], norm_v_ref[...])
    new_norm_m_ref[...], new_norm_v_ref[...] = new_first, new_second
    new_norm_w_ref[...] = norm_w_ref[...] - RATE * direction


def like(values):
    return [jax.ShapeDtypeStruct(v.shape, f32) for v in values]


def body(
    size,
    tokens, grad_out, segments, counts,
    attn_w, attn_m, attn_v, mlp_w, mlp_m, mlp_v, conv_w, conv_m, conv_v, norm_w, norm_m, norm_v,
):
    rank = lax.axis_index("head")
    place = lax.axis_index("dp")
    own_rows = segments.shape[0] // 2
    segments = lax.dynamic_slice_in_dim(segments, rank * own_rows, own_rows, axis=0)
    counts = lax.dynamic_slice_in_dim(counts, rank * own_rows, own_rows, axis=0)
    width = norm_w.shape[1]
    attn_use = gather_weights(attn_w.astype(bf16), size, rank)
    mlp_lines = [lax.all_gather(mlp_w[k].astype(bf16), "dp", axis=0, tiled=True) for k in range(2)]
    conv_low = conv_w.astype(bf16)
    conv_use = join_columns(conv_low, swap(conv_low, "head", 2, 1), rank)
    starts, classes, images = attention_plan(segments)
    middle, qkv, context, ext = attn_forward(starts, classes, counts, tokens, attn_use, norm_w, images)
    middle, mlp_lines = after(middle, mlp_lines)
    mlp_lines = jnp.stack(mlp_lines)
    mlp_use = join_columns(mlp_lines, swap(mlp_lines, "head", 2, 1), rank)
    rank_at = rank.astype(jnp.int32).reshape(1)
    output, grad_middle, held, send, grad_conv, grad_norm_two = mlp_layer(
        line_places(segments), rank_at, middle, grad_out, mlp_use, spread_taps(conv_use), norm_w
    )

    def back(first, count, so_far):
        return attn_backward(
            first, count, so_far, starts, classes, counts, rank_at, tokens, grad_middle, qkv, context, ext, attn_use, norm_w, images
        )

    groups = groups_of(size)
    columns = conv_w.shape[1]
    norm_two = jnp.sum(grad_norm_two.reshape(2, 8, width), axis=1).reshape(1, 2 * width)
    norm_two = jnp.pad(norm_two, ((0, 0), (0, columns - 2 * width)))
    taps = grad_conv[:9]
    small = jnp.concatenate([half_columns(taps, rank), norm_two])
    small_send = jnp.concatenate([half_columns(taps, 1 - rank), norm_two])
    got = swap(jnp.concatenate([flat(send), two_parts(small_send)], axis=0), "head", 2, 1)
    first_rows = max(1, own_rows // 3)
    so_far, got = after(back(0, first_rows, None), got)
    rows = held.size // columns
    held = by_line(held + got[:rows].reshape(held.shape).astype(f32), size)
    small = from_parts(two_parts(small)) + from_parts(got[rows:])
    low, count = groups[0]
    pieces = pieces_of(held, low, count)
    small_parts = two_parts(small)
    gots = [
        swap(jnp.concatenate([flat(pieces[step]), small_parts], axis=0), "dp", size, step * low) for step in range(1, count)
    ]
    so_far, pieces = after(so_far, pieces)
    grad_tokens, attn_held, attn_send, grad_norm_one = back(first_rows, own_rows - first_rows, so_far)

    def take(pieces, gots, small_parts, low, count):
        keep = pieces[0]
        rows = keep.size // keep.shape[-1]
        for got in gots:
            keep = keep + got[:rows].reshape(keep.shape).astype(f32)
        ordered = in_order([small_parts] + [got[rows:] for got in gots], (place // low) % count)
        return keep, sum(from_parts(part) for part in ordered)

    attn_got = swap(flat(attn_send), "head", 2, 1)
    attn_held, gots = after(attn_held, gots)
    held, small = take(pieces, gots, small_parts, low, count)
    rest = bits_of(size)[2:]
    attn_held = by_line(attn_held + attn_got.reshape(attn_held.shape).astype(f32), size)
    waiting = list(groups)
    while waiting or rest:
        attn_pieces, pieces, extra = [None], None, None
        if waiting:
            low, count = waiting.pop(0)
            attn_pieces = pieces_of(attn_held, low, count)
        sent = {step * low: [flat(attn_pieces[step])] for step in range(1, len(attn_pieces))}
        bit = None
        if rest:
            bit = rest.pop(0)
            pieces = pieces_of(held, bit, 2)
            small_parts = two_parts(small)
            extra = jnp.concatenate([flat(pieces[1]), small_parts], axis=0).reshape(-1, attn_held.shape[-1])
            sent.setdefault(bit, []).append(extra)
        gots = {step: swap(jnp.concatenate(parts, axis=0), "dp", size, step) for step, parts in sent.items()}
        if bit:
            got = gots[bit][gots[bit].shape[0] - extra.shape[0] :].reshape(-1, columns)
            held, small = take(pieces, [got], small_parts, bit, 2)
        if attn_pieces[0] is not None:
            attn_held = attn_pieces[0]
            rows = attn_held.size // attn_held.shape[-1]
            for step in range(1, len(attn_pieces)):
                attn_held = attn_held + gots[step * low][:rows].reshape(attn_held.shape).astype(f32)
    grad_attn = unfold_pairs(attn_held.reshape(attn_held.shape[:1] + attn_held.shape[2:]))
    grad_mlp = held.reshape(mlp_w.shape)
    norm_two = small[9, : 2 * width].reshape(2, width)

    weights, firsts, seconds = [attn_w, mlp_w, conv_w], [attn_m, mlp_m, conv_m], [attn_v, mlp_v, conv_v]
    scalars = pl.BlockSpec(memory_space=pltpu.SMEM)
    vectors = pl.BlockSpec(memory_space=pltpu.VMEM)
    results = pl.pallas_call(
        moments_kernel,
        in_specs=[scalars] + [vectors] * 13,
        out_specs=[vectors] * 10,
        out_shape=like(weights) * 3 + [jax.ShapeDtypeStruct((8, width), f32)],
        compiler_params=pltpu.CompilerParams(vmem_limit_bytes=VMEM_BYTES),
    )(place.astype(jnp.int32).reshape(1), grad_norm_one, grad_attn, grad_mlp, small[:9], *weights, *firsts, *seconds)
    new_firsts, new_seconds, updates, sums = results[:3], results[3:6], results[6:9], results[9]
    new_w = pl.pallas_call(
        apply_kernel,
        in_specs=[vectors] * 11,
        out_specs=[vectors] * 6,
        out_shape=like(weights) + like([norm_w] * 3),
        compiler_params=pltpu.CompilerParams(vmem_limit_bytes=VMEM_BYTES),
    )(sum_everywhere(sums, size), norm_two, norm_w, norm_m, norm_v, *weights, *updates)
    return (
        output, grad_tokens, new_w[0], new_firsts[0], new_seconds[0], new_w[1], new_firsts[1], new_seconds[1],
        new_w[2], new_firsts[2], new_seconds[2], *new_w[3:],
    )


def solution(mesh):
    rows, lines = P(("dp", "head"), None), P("dp", None)
    shards, columns = P(None, "dp", "head"), P(None, "head")
    in_specs = (rows, rows, lines, P("dp")) + (shards,) * 6 + (columns,) * 3 + (P(),) * 3
    out_specs = (rows, rows) + (shards,) * 6 + (columns,) * 3 + (P(),) * 3
    return jax.shard_map(
        functools.partial(body, mesh.shape["dp"]), mesh=mesh, in_specs=in_specs, out_specs=out_specs, check_vma=False
    )
```

```python
import functools
import jax
import jax.numpy as jnp
from jax import lax
from jax.experimental import pallas as pl
from jax.experimental.pallas import tpu as pltpu
from jax.sharding import PartitionSpec as P

HEAD_DIM = 64
GRID_W = 16
STEP = 10
IMAGES = 8

NORM_EPS = 1e-06
BETA_ONE = 0.9
BETA_TWO = 0.999
ADAM_EPS = 1e-06
DECAY = 0.01
RATE = 0.5
LOG2E = 1.4426950408889634
LN2 = 0.6931471805599453
BIG = 2.0**100
GELU_ONE = 0.7978845608028654
GELU_TWO = 0.044715
GELU_S = (GELU_ONE * GELU_TWO) ** (1.0 / 3.0)
GELU_A = GELU_ONE / GELU_S
ACT_SCALE = 0.5 / GELU_S
EXTRA = 32
PARTS = 4
TILE = 128
LANES = 128
STRIDE = GRID_W + 8
MIB = 1024 * 1024

f32 = jnp.float32
bf16 = jnp.bfloat16
NN = (((1,), (0,)), ((), ()))
NT = (((1,), (1,)), ((), ()))
TN = (((0,), (0,)), ((), ()))


def dot(left, right, dims=NN):
    return lax.dot_general(left, right, dims, preferred_element_type=f32)


def widths_for(length):
    return [w for w in (256, 384, 512, 768) if w < length] + [length]


def norm_parts(values):
    average = jnp.mean(values, axis=-1, keepdims=True)
    centered = values - average
    inverse = lax.rsqrt(jnp.mean(centered * centered, axis=-1, keepdims=True) + NORM_EPS)
    return centered * inverse, inverse


def norm_back(upstream, gain_row, unit_rows, inverse):
    grad_unit = upstream * gain_row
    first_term = jnp.mean(grad_unit, axis=-1, keepdims=True)
    second_term = jnp.mean(grad_unit * unit_rows, axis=-1, keepdims=True)
    return inverse * (grad_unit - first_term - unit_rows * second_term)


def fold_rows(values):
    rows, columns = values.shape
    return jnp.sum(values.reshape(rows // 8, 8, columns), axis=0)


def pair_columns(flat):
    empty = jnp.zeros((HEAD_DIM, LANES), flat.dtype)
    return jnp.concatenate(
        [jnp.concatenate([flat[:HEAD_DIM], empty], axis=0), jnp.concatenate([empty, flat[HEAD_DIM:]], axis=0)], axis=1
    )


def pair_rows(both):
    return jnp.concatenate([both[:HEAD_DIM, :LANES], both[HEAD_DIM:, LANES:]], axis=0)


def fold_max(values):
    pieces = [values[at : at + 64] for at in range(0, values.shape[0], 64)]
    while len(pieces) > 1:
        pieces = [jnp.maximum(a, b) for a, b in zip(pieces[::2], pieces[1::2])] + ([pieces[-1]] if len(pieces) % 2 else [])
    top = pieces[0]
    top = jnp.maximum(top[:32], top[32:])
    top = jnp.maximum(top[:16], top[16:])
    return jnp.max(jnp.maximum(top[:8], top[8:]), axis=0, keepdims=True)


def three_parts(value, part):
    high = value.astype(bf16).astype(f32)
    rest = value - high
    middle = rest.astype(bf16).astype(f32)
    return jnp.where(part == 0, high, jnp.where(part == 1, middle, rest - middle))


def image_tags(image_ref, start, rows):
    place = start + lax.broadcasted_iota(jnp.int32, (rows, LANES), 0)
    inside = (place >= image_ref[0, 0:1, :]) & (place < image_ref[0, 1:2, :])
    return jnp.where(inside, 1.0, 0.0).astype(bf16)


def attn_forward_kernel(
    start_ref, class_ref, count_ref, tokens_ref, w_ref, norm_ref, image_ref,
    middle_ref, qkv_ref, context_ref, ext_ref,
    tag_ref, normed_ref, qt_ref, vt_ref,
):
    row = pl.program_id(0)
    length, width = tokens_ref.shape
    pairs = width // LANES
    big = 256
    gain, bias = norm_ref[0:1, :], norm_ref[1:2, :]

    def prepare(step, carry):
        rows = pl.ds(pl.multiple_of(step * big, big), big)
        unit, _ = norm_parts(tokens_ref[rows, :].astype(f32))
        normed_ref[rows, :] = (unit * gain + bias).astype(bf16)
        tag_ref[rows, :] = image_tags(image_ref, step * big, big)
        return carry

    lax.fori_loop(0, length // big, prepare, 0)
    queries = (dot(normed_ref[...], w_ref[0]) * (HEAD_DIM**-0.5 * LOG2E)).astype(bf16)
    qkv_ref[:, :width] = queries
    qt_ref[...] = jnp.transpose(queries)
    qkv_ref[:, width : 2 * width] = dot(normed_ref[...], w_ref[1]).astype(bf16)
    values = dot(normed_ref[...], w_ref[2]).astype(bf16)
    qkv_ref[:, 2 * width :] = values
    vt_ref[...] = jnp.transpose(values)

    def tile(step, carry):
        q0 = pl.multiple_of(step * TILE, TILE)
        here = pl.ds(q0, TILE)
        place = q0 + lax.broadcasted_iota(jnp.int32, (IMAGES, LANES), 1)
        inside = (place >= image_ref[0, 8 : 8 + IMAGES, :]) & (place < image_ref[0, 16 : 16 + IMAGES, :])
        mask = jnp.where(inside, 0.0, -BIG)
        mask_low = jnp.concatenate([mask, jnp.zeros((LANES - IMAGES, LANES), f32)], axis=0).astype(bf16)
        ext_rows = lax.broadcasted_iota(jnp.int32, (EXTRA - IMAGES, LANES), 0)

        def attend(window):
            there = pl.ds(pl.multiple_of(start_ref[row, step], LANES), window)
            tags = tag_ref[there, :]
            ones = jnp.ones((GRID_W, window), bf16)
            extra = jnp.zeros((EXTRA - IMAGES, LANES), f32)
            slices = [slice(p * LANES, (p + 1) * LANES) for p in range(pairs)]
            masks = jnp.concatenate([mask_low, mask_low], axis=1)
            scores, tops, exponents, mixes = [], [], [], []
            for p, at in enumerate(slices):
                keys = qkv_ref[there, width + p * LANES : width + (p + 1) * LANES]
                right = jnp.concatenate([pair_columns(qt_ref[at, here]), masks], axis=0)
                scores.append(dot(jnp.concatenate([keys, tags], axis=1), right))
            for p in range(pairs):
                tops.append(fold_max(scores[p]))
                exponents.append(jnp.exp2(scores[p] - tops[p]).astype(bf16))
            for p, at in enumerate(slices):
                mixes.append(dot(jnp.concatenate([vt_ref[at, there], ones], axis=0), exponents[p]))
            for p, at in enumerate(slices):
                mixed = mixes[p]
                total = mixed[LANES : LANES + 1, :]
                minus_lse = -(tops[p] + jnp.log(total) * LOG2E)
                scale = 1.0 / total
                lane = lax.broadcasted_iota(jnp.int32, (1, 2 * TILE), 1)
                head = 2 * p + jnp.where(lane < TILE, 0, 1)
                scale = jnp.where(head < count_ref[row], scale, 0.0)
                context_ref[here, at] = jnp.transpose(pair_rows(mixed[:LANES] * scale)).astype(bf16)
                for h in range(2):
                    value = minus_lse[:, h * TILE : (h + 1) * TILE]
                    first = 6 * p + 3 * h
                    extra = jnp.where(
                        (ext_rows >= first) & (ext_rows < first + 3), three_parts(value, ext_rows - first), extra
                    )
            ext_ref[:, here] = jnp.concatenate([mask, extra], axis=0).astype(bf16)

        for index, window in enumerate(widths_for(length)):
            pl.when(class_ref[row, step] == index)(functools.partial(attend, window))
        return carry

    lax.fori_loop(0, length // TILE, tile, 0)
    middle_ref[...] = tokens_ref[...].astype(f32) + dot(context_ref[...], w_ref[3], NT)


def attn_forward(starts, classes, counts, tokens, attn_use, norm_w, images):
    rows_all, width = tokens.shape
    row_count = counts.shape[0]
    length = rows_all // row_count
    by_row = lambda columns: pl.BlockSpec((length, columns), lambda r, *_: (r, 0))
    return pl.pallas_call(
        attn_forward_kernel,
        grid_spec=pltpu.PrefetchScalarGridSpec(
            num_scalar_prefetch=3,
            grid=(row_count,),
            in_specs=[
                by_row(width),
                pl.BlockSpec(attn_use.shape, lambda r, *_: (0, 0, 0)),
                pl.BlockSpec(norm_w.shape, lambda r, *_: (0, 0)),
                pl.BlockSpec((1, 24, LANES), lambda r, *_: (r, 0, 0)),
            ],
            out_specs=[
                by_row(width), by_row(3 * width), by_row(width), pl.BlockSpec((EXTRA, length), lambda r, *_: (r, 0))
            ],
            scratch_shapes=[
                pltpu.VMEM((length, LANES), bf16),
                pltpu.VMEM((length, width), bf16),
                pltpu.VMEM((width, length), bf16),
                pltpu.VMEM((width, length), bf16),
            ],
        ),
        out_shape=[
            jax.ShapeDtypeStruct((rows_all, width), f32),
            jax.ShapeDtypeStruct((rows_all, 3 * width), bf16),
            jax.ShapeDtypeStruct((rows_all, width), bf16),
            jax.ShapeDtypeStruct((row_count * EXTRA, length), bf16),
        ],
        compiler_params=pltpu.CompilerParams(vmem_limit_bytes=34 * MIB),
    )(starts, classes, counts, tokens, attn_use, norm_w, images)


def attn_backward_kernel(
    first, final, start_ref, class_ref, count_ref, rank_ref, tokens_ref, middle_grad_ref, qkv_ref, context_ref, ext_ref, w_ref, norm_ref,
    image_ref, *refs,
):
    sums = None
    if first:
        sums, refs = refs[1:3], refs[3:]
    sent = None
    if final:
        tokens_grad_ref, keep_ref, send_ref, norm_grad_ref, *scratch, w_grad_ref = refs
        sent = (keep_ref, send_ref)
    else:
        tokens_grad_ref, w_grad_ref, norm_grad_ref, *scratch = refs
    attn_backward_row(
        first, sums, sent, start_ref, class_ref, count_ref, rank_ref, tokens_ref, middle_grad_ref, qkv_ref, context_ref, ext_ref, w_ref,
        norm_ref, image_ref, tokens_grad_ref, w_grad_ref, norm_grad_ref, *scratch,
    )


def attn_backward_row(
    first, sums, sent, start_ref, class_ref, count_ref, rank_ref, tokens_ref, middle_grad_ref, qkv_ref, context_ref, ext_ref, w_ref,
    norm_ref, image_ref, tokens_grad_ref, w_grad_ref, norm_grad_ref,
    tag_ref, up_ref, delta_ref, normed_ref, dq_ref, dk_ref, dv_ref, low_ref, proj_ref, qt_ref, kt_ref, upt_ref, upstream_ref,
):
    step_at = pl.program_id(0)
    row = first + step_at
    length, width = tokens_ref.shape
    pairs = width // LANES
    big = 256
    gain, bias = norm_ref[0:1, :], norm_ref[1:2, :]

    @pl.when(step_at == 0)
    def _():
        for n, ref in enumerate((w_grad_ref, norm_grad_ref)):
            ref[...] = sums[n][...] if sums else jnp.zeros_like(ref)

    target = lax.broadcasted_iota(jnp.int32, (EXTRA, width), 0) - IMAGES
    source = lax.broadcasted_iota(jnp.int32, (EXTRA, width), 1) // HEAD_DIM * 3
    collect = jnp.where((target >= source) & (target < source + 3), -1.0, 0.0).astype(bf16)
    active = jnp.where(
        lax.broadcasted_iota(jnp.int32, (1, width), 1) // HEAD_DIM < count_ref[row], 1.0, 0.0
    )

    def prepare(step, carry):
        rows = pl.ds(pl.multiple_of(step * big, big), big)
        unit, _ = norm_parts(tokens_ref[rows, :].astype(f32))
        normed_ref[rows, :] = (unit * gain + bias).astype(bf16)
        tag_ref[rows, :] = image_tags(image_ref, step * big, big)
        low_ref[rows, :] = middle_grad_ref[rows, :].astype(bf16)
        dk_ref[rows, :] = jnp.zeros((big, width), f32)
        dv_ref[rows, :] = jnp.zeros((big, width), f32)
        return carry

    lax.fori_loop(0, length // big, prepare, 0)
    up = (dot(low_ref[...], w_ref[3]) * active).astype(bf16)
    up_ref[...] = up
    upt_ref[...] = jnp.transpose(up)
    qt_ref[...] = jnp.transpose(qkv_ref[:, :width])
    kt_ref[...] = jnp.transpose(qkv_ref[:, width : 2 * width])

    def gather(step, carry):
        rows = pl.ds(pl.multiple_of(step * big, big), big)
        product = up_ref[rows, :].astype(f32) * context_ref[rows, :].astype(f32)
        high = product.astype(bf16)
        rest = (product - high.astype(f32)).astype(bf16)
        delta = dot(collect, high, NT) + dot(collect, rest, NT)
        part = lax.rem(lax.broadcasted_iota(jnp.int32, (EXTRA, big), 0) + 3 * EXTRA - IMAGES, 3)
        delta_ref[:, rows] = three_parts(delta, part).astype(bf16)
        return carry

    lax.fori_loop(0, length // big, gather, 0)
    lane = lax.broadcasted_iota(jnp.int32, (1, LANES), 1)
    first_half = jnp.where(lane < HEAD_DIM, 1.0, 0.0).astype(bf16)
    second_half = jnp.where(lane >= HEAD_DIM, 1.0, 0.0).astype(bf16)

    def tile(step, carry):
        q0 = pl.multiple_of(step * TILE, TILE)
        here = pl.ds(q0, TILE)

        def attend(window):
            there = pl.ds(pl.multiple_of(start_ref[row, step], LANES), window)
            tags = tag_ref[there, :]
            ext = ext_ref[:, here]
            delta = delta_ref[:, here]
            at_row = lax.broadcasted_iota(jnp.int32, (EXTRA, LANES), 0)
            empty = jnp.zeros((LANES - EXTRA, 2 * TILE), bf16)

            def own(edge, masks):
                keep = (at_row >= edge) & (at_row < edge + 3)
                return jnp.where(keep | (at_row < IMAGES) if masks else keep, 1.0, 0.0).astype(bf16)

            slices = [slice(p * LANES, (p + 1) * LANES) for p in range(pairs)]
            scores, grad_probs, probs, grad_scores = [], [], [], []
            for p, at in enumerate(slices):
                keys = qkv_ref[there, width + p * LANES : width + (p + 1) * LANES]
                values = qkv_ref[there, 2 * width + p * LANES : 2 * width + (p + 1) * LANES]
                edge = IMAGES + 6 * p
                q_side = jnp.concatenate(
                    [
                        pair_columns(qt_ref[at, here]),
                        jnp.concatenate([ext * own(edge, True), ext * own(edge + 3, True)], axis=1),
                        empty,
                    ],
                    axis=0,
                )
                up_side = jnp.concatenate(
                    [
                        pair_columns(upt_ref[at, here]),
                        jnp.concatenate([delta * own(edge, False), delta * own(edge + 3, False)], axis=1),
                        empty,
                    ],
                    axis=0,
                )
                scores.append(dot(jnp.concatenate([keys, tags], axis=1), q_side))
                grad_probs.append(dot(jnp.concatenate([values, tags], axis=1), up_side))
            for p in range(pairs):
                weight = jnp.exp2(scores[p])
                probs.append(weight.astype(bf16))
                grad_scores.append((weight * grad_probs[p]).astype(bf16))
            for p, at in enumerate(slices):
                queries, ups = qkv_ref[here, at], up_ref[here, at]
                q_pair = jnp.concatenate([queries * first_half, queries * second_half], axis=0)
                up_pair = jnp.concatenate([ups * first_half, ups * second_half], axis=0)
                dv_ref[there, at] += dot(probs[p], up_pair)
                dk_ref[there, at] += dot(grad_scores[p], q_pair)
                dq = pair_rows(dot(kt_ref[at, there], grad_scores[p]))
                dq_ref[here, at] = jnp.transpose(dq * HEAD_DIM**-0.5).astype(bf16)

        for index, window in enumerate(widths_for(length)):
            pl.when(class_ref[row, step] == index)(functools.partial(attend, window))
        return carry

    lax.fori_loop(0, length // TILE, tile, 0)
    keys_grad = (dk_ref[...] * LN2).astype(bf16)
    values_grad = dv_ref[...].astype(bf16)
    proj_ref[...] = jnp.concatenate([dq_ref[...], keys_grad, values_grad], axis=1)
    w_cat = jnp.concatenate([w_ref[0], w_ref[1], w_ref[2]], axis=1)
    upstream_ref[...] = dot(proj_ref[...], w_cat, NT)

    def finish(step, carry):
        rows = pl.ds(pl.multiple_of(step * big, big), big)
        upstream = upstream_ref[rows, :]
        unit, inverse = norm_parts(tokens_ref[rows, :].astype(f32))
        tokens_grad_ref[rows, :] = middle_grad_ref[rows, :] + norm_back(upstream, gain, unit, inverse)
        norm_grad_ref[0:8, :] += fold_rows(upstream * unit)
        norm_grad_ref[8:16, :] += fold_rows(upstream)
        return carry

    lax.fori_loop(0, length // big, finish, 0)
    normed_t = jnp.transpose(normed_ref[...])
    for k in range(3):
        w_grad_ref[k] += dot(normed_t, proj_ref[:, k * width : (k + 1) * width])
    w_grad_ref[3] += dot(jnp.transpose(low_ref[...]), context_ref[...])
    if sent:

        @pl.when(step_at == pl.num_programs(0) - 1)
        def _():
            for k in range(2):
                one, two = w_grad_ref[k], w_grad_ref[k + 2]
                halves = [jnp.concatenate([one[:, at : at + width // 2], two[:, at : at + width // 2]], axis=1) for at in (0, width // 2)]
                sent[0][k] = jnp.where(rank_ref[0] == 0, halves[0], halves[1])
                sent[1][k] = jnp.where(rank_ref[0] == 0, halves[1], halves[0]).astype(bf16)


def attn_backward(first, count, so_far, starts, classes, counts, rank, tokens, middle_grad, qkv, context, ext, attn_use, norm_w, images):
    rows_all, width = tokens.shape
    length = rows_all // counts.shape[0]
    by_row = lambda columns: pl.BlockSpec((length, columns), lambda r, *_: (first + r, 0))
    final = first + count == counts.shape[0]
    half = (2, width, width)
    halves = pl.BlockSpec(half, lambda r, *_: (0, 0, 0))
    whole = pl.BlockSpec(attn_use.shape, lambda r, *_: (0, 0, 0))
    sums = pl.BlockSpec((16, width), lambda r, *_: (0, 0))
    return pl.pallas_call(
        functools.partial(attn_backward_kernel, first, final),
        grid_spec=pltpu.PrefetchScalarGridSpec(
            num_scalar_prefetch=4,
            grid=(count,),
            in_specs=[
                by_row(width),
                by_row(width),
                by_row(3 * width),
                by_row(width),
                pl.BlockSpec((EXTRA, length), lambda r, *_: (first + r, 0)),
                whole,
                pl.BlockSpec(norm_w.shape, lambda r, *_: (0, 0)),
                pl.BlockSpec((1, 24, LANES), lambda r, *_: (first + r, 0, 0)),
            ]
            + ([pl.BlockSpec(memory_space=pl.ANY), whole, sums] if first else []),
            out_specs=[by_row(width), halves, halves, sums] if final else [by_row(width), whole, sums],
            scratch_shapes=[
                pltpu.VMEM((length, LANES), bf16),
                pltpu.VMEM((length, width), bf16),
                pltpu.VMEM((EXTRA, length), bf16),
                pltpu.VMEM((length, width), bf16),
                pltpu.VMEM((length, width), bf16),
                pltpu.VMEM((length, width), f32),
                pltpu.VMEM((length, width), f32),
                pltpu.VMEM((length, width), bf16),
                pltpu.VMEM((length, 3 * width), bf16),
                pltpu.VMEM((width, length), bf16),
                pltpu.VMEM((width, length), bf16),
                pltpu.VMEM((width, length), bf16),
                pltpu.VMEM((length, width), f32),
            ]
            + ([pltpu.VMEM(attn_use.shape, f32)] if final else []),
        ),
        out_shape=[jax.ShapeDtypeStruct((rows_all, width), f32)]
        + (
            [jax.ShapeDtypeStruct(half, f32), jax.ShapeDtypeStruct(half, bf16)]
            if final
            else [jax.ShapeDtypeStruct(attn_use.shape, f32)]
        )
        + [jax.ShapeDtypeStruct((16, width), f32)],
        input_output_aliases={12: 0} if first else {},
        compiler_params=pltpu.CompilerParams(vmem_limit_bytes=40 * MIB),
    )(starts, classes, counts, rank, tokens, middle_grad, qkv, context, ext, attn_use, norm_w, images, *(so_far or ()))


def mlp_kernel(
    place_ref, rank_ref, middle_ref, out_grad_ref, w_ref, taps_ref, norm_ref,
    output_ref, middle_grad_ref, keep_ref, send_ref, taps_grad_ref, norm_grad_ref,
    w_grad_ref, normed_ref, normed_t_ref, out_grad_t_ref, out_sum_ref, up_sum_ref, tap_sum_ref,
    act_grads_ref, acts_ref, hidden_grads_ref, *buffers,
):
    row = pl.program_id(0)
    length, width = middle_ref.shape
    hidden = w_ref.shape[2]
    chunk = PARTS * LANES
    big = 256
    grid_rows = length // GRID_W
    chunks = hidden // chunk
    h_refs, g_refs = buffers[:PARTS], buffers[PARTS:]
    gain, bias = norm_ref[2:3, :], norm_ref[3:4, :]

    @pl.when(row == 0)
    def _():
        w_grad_ref[...] = jnp.zeros_like(w_grad_ref)
        norm_grad_ref[...] = jnp.zeros_like(norm_grad_ref)
        tap_sum_ref[...] = jnp.zeros_like(tap_sum_ref)
        for ref in buffers:
            ref[...] = jnp.zeros_like(ref)

    def place(r):
        return pl.multiple_of(place_ref[row, r], 8)

    for n in range(IMAGES + 1):
        at = place(grid_rows + n)
        for ref in buffers:
            ref[pl.ds(at, GRID_W), :] = jnp.zeros((GRID_W, LANES), f32)

    def normalize(step, carry):
        rows = pl.ds(pl.multiple_of(step * big, big), big)
        middle = middle_ref[rows, :]
        unit, _ = norm_parts(middle)
        normed_ref[rows, :] = (unit * gain + bias).astype(bf16)
        out_sum_ref[rows, :] = jnp.zeros((big, width), f32)
        up_sum_ref[rows, :] = jnp.zeros((big, width), f32)
        return carry

    lax.fori_loop(0, length // big, normalize, 0)
    normed_t_ref[...] = jnp.transpose(normed_ref[...])
    out_grad_t_ref[...] = jnp.transpose(out_grad_ref[...])

    def lanes_of(c):
        return pl.ds(pl.multiple_of(c * chunk, chunk), chunk)

    def lanes_of(c):
        return pl.ds(pl.multiple_of(c * chunk, chunk), chunk)

    def neighbours(ref, at):
        return [ref[pl.ds(at + (a * STRIDE + b), GRID_W), :] for a in (-1, 0, 1) for b in (-1, 0, 1)]

    def tall(values):
        return jnp.concatenate([values, values], axis=0)

    def total_of(terms):
        while len(terms) > 1:
            terms = [a + b for a, b in zip(terms[::2], terms[1::2])] + ([terms[-1]] if len(terms) % 2 else [])
        return terms[0]

    def taps_for(c, part, at):
        lane = pl.ds(pl.multiple_of(c * chunk + part * LANES, LANES), LANES)
        return [tall(taps_ref[at + k * 8 : at + (k + 1) * 8, lane]) for k in range(9)]

    lines = 8

    def do_chunk(c, carry):
        lanes = lanes_of(c)
        for t in range(length // big):
            rows = slice(t * big, (t + 1) * big)
            values = dot(normed_ref[rows, :], w_ref[0, :, lanes])
            for part in range(PARTS):
                for s in range(big // GRID_W):
                    at = place(t * (big // GRID_W) + s)
                    h_refs[part][pl.ds(at, GRID_W), :] = values[
                        s * GRID_W : (s + 1) * GRID_W, part * LANES : (part + 1) * LANES
                    ]
        act_grads_ref[...] = dot(out_grad_ref[...], w_ref[1, :, lanes])

        def forward(t, carry):
            tokens_base = pl.multiple_of(t * (lines * GRID_W), lines * GRID_W)
            for part in range(PARTS):
                taps = taps_for(c, part, 0)
                cols = slice(part * LANES, (part + 1) * LANES)
                for s in range(lines):
                    near = pl.ds(pl.multiple_of(tokens_base + s * GRID_W, GRID_W), GRID_W)
                    at = place(t * lines + s)
                    x = total_of([x * tap for x, tap in zip(neighbours(h_refs[part], at), taps)])
                    square = x * x
                    value = jnp.tanh(x * (GELU_A + square))
                    gate = 1.0 + value
                    twice = x * gate
                    acts_ref[near, cols] = twice.astype(bf16)
                    slope = gate + (twice * (1.0 - value)) * (GELU_A + 3.0 * square)
                    g_refs[part][pl.ds(at, GRID_W), :] = act_grads_ref[near, cols] * slope
            return carry

        lax.fori_loop(0, grid_rows // lines, forward, 0)

        def backward(t, carry):
            tokens_base = pl.multiple_of(t * (lines * GRID_W), lines * GRID_W)
            for part in range(PARTS):
                taps = taps_for(c, part, 72)
                lane = pl.ds(pl.multiple_of(c * chunk + part * LANES, LANES), LANES)
                cols = slice(part * LANES, (part + 1) * LANES)
                totals = [None] * 9
                for s in range(lines):
                    near = pl.ds(pl.multiple_of(tokens_base + s * GRID_W, GRID_W), GRID_W)
                    at = place(t * lines + s)
                    source = h_refs[part][pl.ds(at, GRID_W), :]
                    moved = neighbours(g_refs[part], at)[::-1]
                    for k in range(9):
                        product = source * moved[k]
                        folded = product[:8] + product[8:]
                        totals[k] = folded if totals[k] is None else totals[k] + folded
                    terms = [x * tap for x, tap in zip(moved, taps)]
                    hidden_grads_ref[near, cols] = total_of(terms).astype(bf16)
                for k in range(9):
                    tap_sum_ref[k * 8 : (k + 1) * 8, lane] += totals[k]
            return carry

        lax.fori_loop(0, grid_rows // lines, backward, 0)
        w_grad_ref[0, :, lanes] += dot(normed_t_ref[...], hidden_grads_ref[...])
        w_grad_ref[1, :, lanes] += dot(out_grad_t_ref[...], acts_ref[...])
        out_sum_ref[...] += dot(acts_ref[...], w_ref[1, :, lanes], NT)
        up_sum_ref[...] += dot(hidden_grads_ref[...], w_ref[0, :, lanes], NT)
        return carry

    lax.fori_loop(0, chunks, do_chunk, 0)

    def finish(step, carry):
        rows = pl.ds(pl.multiple_of(step * big, big), big)
        middle = middle_ref[rows, :]
        output_ref[rows, :] = (middle + ACT_SCALE * out_sum_ref[rows, :]).astype(bf16)
        upstream = 0.5 * up_sum_ref[rows, :]
        unit, inverse = norm_parts(middle)
        middle_grad_ref[rows, :] = out_grad_ref[rows, :].astype(f32) + norm_back(upstream, gain, unit, inverse)
        norm_grad_ref[0:8, :] += fold_rows(upstream * unit)
        norm_grad_ref[8:16, :] += fold_rows(upstream)
        return carry

    lax.fori_loop(0, length // big, finish, 0)

    @pl.when(row == pl.num_programs(0) - 1)
    def _():
        for k, scale in enumerate((0.5, ACT_SCALE)):
            halves = w_grad_ref[k, :, : hidden // 2], w_grad_ref[k, :, hidden // 2 :]
            keep_ref[k] = scale * jnp.where(rank_ref[0] == 0, halves[0], halves[1])
            send_ref[k] = (scale * jnp.where(rank_ref[0] == 0, halves[1], halves[0])).astype(bf16)
        taps_grad_ref[...] = jnp.zeros_like(taps_grad_ref)
        for k in range(9):
            total = jnp.sum(tap_sum_ref[k * 8 : (k + 1) * 8, :], axis=0, keepdims=True)
            taps_grad_ref[k : k + 1, :] = 0.5 * total


def mlp_layer(places, rank, middle, out_grad, mlp_use, taps, norm_w):
    rows_all, width = middle.shape
    row_count = places.shape[0]
    length = rows_all // row_count
    hidden = mlp_use.shape[2]
    half = mlp_use.shape[:2] + (hidden // 2,)
    by_row = lambda columns: pl.BlockSpec((length, columns), lambda r, *_: (r, 0))
    slots = (length // GRID_W + IMAGES + 2) * STRIDE
    return pl.pallas_call(
        mlp_kernel,
        grid_spec=pltpu.PrefetchScalarGridSpec(
            num_scalar_prefetch=2,
            grid=(row_count,),
            in_specs=[
                by_row(width),
                by_row(width),
                pl.BlockSpec(mlp_use.shape, lambda r, *_: (0, 0, 0)),
                pl.BlockSpec(taps.shape, lambda r, *_: (0, 0)),
                pl.BlockSpec(norm_w.shape, lambda r, *_: (0, 0)),
            ],
            out_specs=[
                by_row(width),
                by_row(width),
                pl.BlockSpec(half, lambda r, *_: (0, 0, 0)),
                pl.BlockSpec(half, lambda r, *_: (0, 0, 0)),
                pl.BlockSpec((16, hidden), lambda r, *_: (0, 0)),
                pl.BlockSpec((16, width), lambda r, *_: (0, 0)),
            ],
            scratch_shapes=[
                pltpu.VMEM(mlp_use.shape, f32),
                pltpu.VMEM((length, width), bf16),
                pltpu.VMEM((width, length), bf16),
                pltpu.VMEM((width, length), bf16),
                pltpu.VMEM((length, width), f32),
                pltpu.VMEM((length, width), f32),
                pltpu.VMEM((9 * 8, hidden), f32),
                pltpu.VMEM((length, PARTS * LANES), f32),
                pltpu.VMEM((length, PARTS * LANES), bf16),
                pltpu.VMEM((length, PARTS * LANES), bf16),
            ]
            + [pltpu.VMEM((slots, LANES), f32)] * (2 * PARTS),
        ),
        out_shape=[
            jax.ShapeDtypeStruct((rows_all, width), bf16),
            jax.ShapeDtypeStruct((rows_all, width), f32),
            jax.ShapeDtypeStruct(half, f32),
            jax.ShapeDtypeStruct(half, bf16),
            jax.ShapeDtypeStruct((16, hidden), f32),
            jax.ShapeDtypeStruct((16, width), f32),
        ],
        compiler_params=pltpu.CompilerParams(vmem_limit_bytes=50 * MIB),
    )(places, rank, middle, out_grad, mlp_use, taps, norm_w)


def attention_plan(segments):
    row_count, length = segments.shape
    tiles = segments.reshape(row_count, length // TILE, TILE)
    first, last = tiles[:, :, 0], tiles[:, :, -1]
    ids = jnp.arange(IMAGES, dtype=jnp.int32)
    begins = jnp.sum((segments[:, None, :] < ids[None, :, None]).astype(jnp.int32), axis=-1)
    ends = jnp.sum((segments[:, None, :] <= ids[None, :, None]).astype(jnp.int32), axis=-1)
    low_end = jnp.sum(jnp.where(first[:, :, None] == ids, begins[:, None, :], 0), axis=-1) // LANES * LANES
    high_end = jnp.sum(jnp.where(last[:, :, None] == ids, ends[:, None, :], 0), axis=-1)
    widths = widths_for(length)
    classes = sum(((high_end - low_end) > w).astype(jnp.int32) for w in widths[:-1])
    chosen = jnp.full_like(classes, widths[-1])
    for index, w in enumerate(widths):
        chosen = jnp.where(classes == index, w, chosen)
    starts = jnp.minimum(low_end, length - chosen)
    used = jnp.zeros((row_count, EXTRA - IMAGES), jnp.int32)
    unused = jnp.zeros((row_count, LANES - EXTRA), jnp.int32)
    first_lane = jnp.concatenate([begins, used, unused], axis=1)
    end_lane = jnp.concatenate([ends, used + length, unused], axis=1)
    by_lane = jnp.pad(jnp.stack([first_lane, end_lane], axis=1), ((0, 0), (0, 6), (0, 0)))
    by_image = jnp.broadcast_to(jnp.concatenate([begins, ends], axis=1)[:, :, None], (row_count, 2 * IMAGES, LANES))
    return starts, classes, jnp.concatenate([by_lane, by_image], axis=1)


def spread_taps(conv_use):
    taps = conv_use.astype(f32)
    own = (jnp.arange(9) == 4).astype(f32)[:, None]
    taps = jnp.repeat(taps + own, 8, axis=0)
    return jnp.concatenate([taps * GELU_S, taps], axis=0)


def line_places(segments):
    ids = segments[:, ::GRID_W]
    count = ids.shape[1]
    rows = jnp.arange(count, dtype=jnp.int32) + ids + 1
    images = jnp.arange(IMAGES, dtype=jnp.int32)
    first = jnp.sum((ids[:, None, :] < images[None, :, None]).astype(jnp.int32), axis=-1)
    gaps = jnp.concatenate([first + images, jnp.full((ids.shape[0], 1), count + IMAGES, jnp.int32)], axis=1)
    return jnp.concatenate([rows, gaps], axis=1) * STRIDE + 8


def bits_of(size):
    bits = []
    b = 1
    while b < size:
        bits.append(b)
        b *= 2
    return bits


def groups_of(size):
    bits = bits_of(size)
    return [(bits[at], 1 << len(bits[at : at + 2])) for at in range(0, len(bits), 2)]


def swap(values, axis, size, bit):
    return lax.ppermute(values, axis, [(i, i ^ bit) for i in range(size)])


def in_order(found, mine):
    ordered = []
    for target in range(len(found)):
        value = found[0]
        for step in range(1, len(found)):
            value = jnp.where((mine ^ step) == target, found[step], value)
        ordered.append(value)
    return ordered


def gather_lines(shard, size):
    place = lax.axis_index("dp")
    held = shard[None]
    for low, count in reversed(groups_of(size)):
        found = [held] + [swap(held, "dp", size, step * low) for step in range(1, count)]
        held = jnp.stack(in_order(found, (place // low) % count), axis=1).reshape((-1,) + shard.shape)
    return held


def fold_pairs(values):
    count = values.shape[0] // 2
    return jnp.concatenate([values[:count], values[count:]], axis=-1)


def unfold_pairs(values):
    half = values.shape[-1] // 2
    return jnp.concatenate([values[..., :half], values[..., half:]], axis=0)


def join_columns(mine, other, rank):
    first = jnp.where(rank == 0, mine, other)
    second = jnp.where(rank == 0, other, mine)
    return jnp.concatenate([first, second], axis=-1)


def gather_weights(shard, size, rank):
    count, part, columns = shard.shape
    mine = gather_lines(fold_pairs(shard), size)
    other = swap(mine, "head", 2, 1)
    full = [join_columns(mine[..., at : at + columns], other[..., at : at + columns], rank) for at in (0, columns)]
    return jnp.moveaxis(jnp.concatenate(full, axis=1), 0, 1).reshape(count, size * part, 2 * columns)


def half_columns(values, side):
    half = values.shape[-1] // 2
    return lax.dynamic_slice_in_dim(values, side * half, half, axis=values.ndim - 1)


def by_line(values, size):
    count, rows, columns = values.shape
    return values.reshape(count, size, rows // size, columns)


def two_parts(values):
    high = values.astype(bf16)
    return jnp.concatenate([high, (values - high.astype(f32)).astype(bf16)], axis=0)


def from_parts(parts):
    count = parts.shape[0] // 2
    return parts[:count].astype(f32) + parts[count:].astype(f32)


def pieces_of(held, low, count):
    n, lines = held.shape[:2]
    split = held.reshape((n, lines // count, count) + held.shape[2:])
    mine = (lax.axis_index("dp") // low) % count
    return [lax.dynamic_index_in_dim(split, mine ^ step, 2, keepdims=False) for step in range(count)]


def flat(values):
    return values.astype(bf16).reshape(-1, values.shape[-1])


def sum_everywhere(values, size):
    values = values + swap(values, "head", 2, 1)
    for bit in bits_of(size):
        values = values + swap(values, "dp", size, bit)
    return values


def after(first, second):
    return lax.optimization_barrier((first, second))


def adam_terms(grad_sum, first_old, second):
    first_new = BETA_ONE * first_old + (1.0 - BETA_ONE) * grad_sum
    second_new = BETA_TWO * second + (1.0 - BETA_TWO) * grad_sum * grad_sum
    direction = (
        first_new
        / (1.0 - BETA_ONE**STEP)
        / (jnp.sqrt(second_new / (1.0 - BETA_TWO**STEP)) + ADAM_EPS)
    )
    return (first_new, second_new, direction)


def moments_kernel(line_ref, norm_ref, *refs):
    count = 3
    grads, weights, firsts, seconds = (refs[n * count : (n + 1) * count] for n in range(4))
    new_firsts, new_seconds, updates = (refs[(4 + n) * count : (5 + n) * count] for n in range(3))
    sums_ref = refs[7 * count]
    width = sums_ref.shape[1]
    lane = lax.broadcasted_iota(jnp.int32, (1, width), 1)
    rows = [jnp.zeros((1, width), f32), jnp.zeros((1, width), f32)]
    at = 0
    for n in range(count):
        grad, weight = grads[n][...], weights[n][...]
        new_first, new_second, direction = adam_terms(grad, firsts[n][...], seconds[n][...])
        update = direction + DECAY * weight
        new_firsts[n][...], new_seconds[n][...], updates[n][...] = new_first, new_second, update
        matrices = weight.shape[0] if weight.ndim == 3 else 1
        for k in range(matrices):
            for row, values in enumerate((weight, update)):
                values = values[k] if weight.ndim == 3 else values
                total = jnp.sum(jnp.sum(values * values, axis=0, keepdims=True), axis=1, keepdims=True)
                if weight.ndim == 2:
                    total = jnp.where(line_ref[0] == 0, total, 0.0)
                rows[row] = jnp.where(lane == at, total, rows[row])
            at += 1
    gain = jnp.sum(norm_ref[0:8, :], axis=0, keepdims=True)
    bias = jnp.sum(norm_ref[8:16, :], axis=0, keepdims=True)
    sums_ref[...] = jnp.concatenate(rows + [gain, bias, jnp.zeros((4, width), f32)], axis=0)


def apply_kernel(sums_ref, norm_two_ref, norm_w_ref, norm_m_ref, norm_v_ref, *refs):
    count = 3
    weights, updates, news = (refs[n * count : (n + 1) * count] for n in range(3))
    new_norm_w_ref, new_norm_m_ref, new_norm_v_ref = refs[3 * count :]
    ratio = jnp.sqrt(sums_ref[0:1, :]) / jnp.sqrt(sums_ref[1:2, :])
    at = 0
    for n in range(count):
        shape = weights[n].shape
        if len(shape) == 3:
            for k in range(shape[0]):
                news[n][k] = weights[n][k] - RATE * ratio[:, at : at + 1] * updates[n][k]
                at += 1
        else:
            news[n][...] = weights[n][...] - RATE * ratio[:, at : at + 1] * updates[n][...]
            at += 1
    grads = jnp.concatenate([sums_ref[2:4, :], norm_two_ref[...]], axis=0)
    new_first, new_second, direction = adam_terms(grads, norm_m_ref[...], norm_v_ref[...])
    new_norm_m_ref[...], new_norm_v_ref[...] = new_first, new_second
    new_norm_w_ref[...] = norm_w_ref[...] - RATE * direction


def like(values):
    return [jax.ShapeDtypeStruct(v.shape, f32) for v in values]


def body(
    size,
    tokens, grad_out, segments, counts,
    attn_w, attn_m, attn_v, mlp_w, mlp_m, mlp_v, conv_w, conv_m, conv_v, norm_w, norm_m, norm_v,
):
    rank = lax.axis_index("head")
    place = lax.axis_index("dp")
    own_rows = segments.shape[0] // 2
    segments = lax.dynamic_slice_in_dim(segments, rank * own_rows, own_rows, axis=0)
    counts = lax.dynamic_slice_in_dim(counts, rank * own_rows, own_rows, axis=0)
    width = norm_w.shape[1]
    attn_use = gather_weights(attn_w.astype(bf16), size, rank)
    mlp_lines = lax.all_gather(mlp_w.astype(bf16), "dp", axis=1, tiled=True)
    conv_low = conv_w.astype(bf16)
    conv_use = join_columns(conv_low, swap(conv_low, "head", 2, 1), rank)
    starts, classes, images = attention_plan(segments)
    middle, qkv, context, ext = attn_forward(starts, classes, counts, tokens, attn_use, norm_w, images)
    middle, mlp_lines = after(middle, mlp_lines)
    mlp_use = join_columns(mlp_lines, swap(mlp_lines, "head", 2, 1), rank)
    rank_at = rank.astype(jnp.int32).reshape(1)
    output, grad_middle, held, send, grad_conv, grad_norm_two = mlp_layer(
        line_places(segments), rank_at, middle, grad_out, mlp_use, spread_taps(conv_use), norm_w
    )

    def back(first, count, so_far):
        return attn_backward(
            first, count, so_far, starts, classes, counts, rank_at, tokens, grad_middle, qkv, context, ext, attn_use, norm_w, images
        )

    groups = groups_of(size)
    columns = conv_w.shape[1]
    norm_two = jnp.sum(grad_norm_two.reshape(2, 8, width), axis=1).reshape(1, 2 * width)
    norm_two = jnp.pad(norm_two, ((0, 0), (0, columns - 2 * width)))
    taps = grad_conv[:9]
    small = jnp.concatenate([half_columns(taps, rank), norm_two])
    small_send = jnp.concatenate([half_columns(taps, 1 - rank), norm_two])
    got = swap(jnp.concatenate([flat(send), two_parts(small_send)], axis=0), "head", 2, 1)
    first_rows = max(1, own_rows // 3)
    so_far, got = after(back(0, first_rows, None), got)
    rows = held.size // columns
    held = by_line(held + got[:rows].reshape(held.shape).astype(f32), size)
    small = from_parts(two_parts(small)) + from_parts(got[rows:])
    low, count = groups[0]
    pieces = pieces_of(held, low, count)
    small_parts = two_parts(small)
    gots = [
        swap(jnp.concatenate([flat(pieces[step]), small_parts], axis=0), "dp", size, step * low) for step in range(1, count)
    ]
    so_far, pieces = after(so_far, pieces)
    grad_tokens, attn_held, attn_send, grad_norm_one = back(first_rows, own_rows - first_rows, so_far)

    def take(pieces, gots, small_parts, low, count):
        keep = pieces[0]
        rows = keep.size // keep.shape[-1]
        for got in gots:
            keep = keep + got[:rows].reshape(keep.shape).astype(f32)
        ordered = in_order([small_parts] + [got[rows:] for got in gots], (place // low) % count)
        return keep, sum(from_parts(part) for part in ordered)

    attn_got = swap(flat(attn_send), "head", 2, 1)
    attn_got, gots = after(attn_got, gots)
    held, small = take(pieces, gots, small_parts, low, count)
    rest = bits_of(size)[2:]
    attn_held = by_line(attn_held + attn_got.reshape(attn_held.shape).astype(f32), size)
    waiting = list(groups)
    while waiting or rest:
        attn_pieces, pieces, extra = [None], None, None
        if waiting:
            low, count = waiting.pop(0)
            attn_pieces = pieces_of(attn_held, low, count)
        sent = {step * low: [flat(attn_pieces[step])] for step in range(1, len(attn_pieces))}
        bit = None
        if rest:
            bit = rest.pop(0)
            pieces = pieces_of(held, bit, 2)
            small_parts = two_parts(small)
            extra = jnp.concatenate([flat(pieces[1]), small_parts], axis=0).reshape(-1, attn_held.shape[-1])
            sent.setdefault(bit, []).append(extra)
        gots = {step: swap(jnp.concatenate(parts, axis=0), "dp", size, step) for step, parts in sent.items()}
        if bit:
            got = gots[bit][gots[bit].shape[0] - extra.shape[0] :].reshape(-1, columns)
            held, small = take(pieces, [got], small_parts, bit, 2)
        if attn_pieces[0] is not None:
            attn_held = attn_pieces[0]
            rows = attn_held.size // attn_held.shape[-1]
            for step in range(1, len(attn_pieces)):
                attn_held = attn_held + gots[step * low][:rows].reshape(attn_held.shape).astype(f32)
    grad_attn = unfold_pairs(attn_held.reshape(attn_held.shape[:1] + attn_held.shape[2:]))
    grad_mlp = held.reshape(mlp_w.shape)
    norm_two = small[9, : 2 * width].reshape(2, width)

    weights, firsts, seconds = [attn_w, mlp_w, conv_w], [attn_m, mlp_m, conv_m], [attn_v, mlp_v, conv_v]
    scalars = pl.BlockSpec(memory_space=pltpu.SMEM)
    vectors = pl.BlockSpec(memory_space=pltpu.VMEM)
    results = pl.pallas_call(
        moments_kernel,
        in_specs=[scalars] + [vectors] * 13,
        out_specs=[vectors] * 10,
        out_shape=like(weights) * 3 + [jax.ShapeDtypeStruct((8, width), f32)],
        compiler_params=pltpu.CompilerParams(vmem_limit_bytes=16 * MIB),
    )(place.astype(jnp.int32).reshape(1), grad_norm_one, grad_attn, grad_mlp, small[:9], *weights, *firsts, *seconds)
    new_firsts, new_seconds, updates, sums = results[:3], results[3:6], results[6:9], results[9]
    new_w = pl.pallas_call(
        apply_kernel,
        in_specs=[vectors] * 11,
        out_specs=[vectors] * 6,
        out_shape=like(weights) + like([norm_w] * 3),
        compiler_params=pltpu.CompilerParams(vmem_limit_bytes=16 * MIB),
    )(sum_everywhere(sums, size), norm_two, norm_w, norm_m, norm_v, *weights, *updates)
    return (
        output, grad_tokens, new_w[0], new_firsts[0], new_seconds[0], new_w[1], new_firsts[1], new_seconds[1],
        new_w[2], new_firsts[2], new_seconds[2], *new_w[3:],
    )


def solution(mesh):
    rows, lines = P(("dp", "head"), None), P("dp", None)
    shards, columns = P(None, "dp", "head"), P(None, "head")
    in_specs = (rows, rows, lines, P("dp")) + (shards,) * 6 + (columns,) * 3 + (P(),) * 3
    out_specs = (rows, rows) + (shards,) * 6 + (columns,) * 3 + (P(),) * 3
    return jax.shard_map(
        functools.partial(body, mesh.shape["dp"]), mesh=mesh, in_specs=in_specs, out_specs=out_specs, check_vma=False
    )
```

```python
import functools
import jax
import jax.numpy as jnp
from jax import lax
from jax.experimental import pallas as pl
from jax.experimental.pallas import tpu as pltpu
from jax.sharding import PartitionSpec as P

HEAD_DIM = 64
GRID_W = 16
STEP = 10
IMAGES = 8

NORM_EPS = 1e-06
BETA_ONE = 0.9
BETA_TWO = 0.999
ADAM_EPS = 1e-06
DECAY = 0.01
RATE = 0.5
LOG2E = 1.4426950408889634
LN2 = 0.6931471805599453
BIG = 2.0**100
GELU_ONE = 0.7978845608028654
GELU_TWO = 0.044715
GELU_S = (GELU_ONE * GELU_TWO) ** (1.0 / 3.0)
GELU_A = GELU_ONE / GELU_S
ACT_SCALE = 0.5 / GELU_S
EXTRA = 32
PARTS = 4
TILE = 128
LANES = 128
STRIDE = GRID_W + 8
MIB = 1024 * 1024

f32 = jnp.float32
bf16 = jnp.bfloat16
NN = (((1,), (0,)), ((), ()))
NT = (((1,), (1,)), ((), ()))
TN = (((0,), (0,)), ((), ()))


def dot(left, right, dims=NN):
    return lax.dot_general(left, right, dims, preferred_element_type=f32)


def work_of(micros):
    return pl.CostEstimate(flops=micros * 1_000_000_000, bytes_accessed=micros * 1_000_000, transcendentals=0)


def widths_for(length):
    return [w for w in (256, 384, 512, 768) if w < length] + [length]


def norm_parts(values):
    average = jnp.mean(values, axis=-1, keepdims=True)
    centered = values - average
    inverse = lax.rsqrt(jnp.mean(centered * centered, axis=-1, keepdims=True) + NORM_EPS)
    return centered * inverse, inverse


def norm_back(upstream, gain_row, unit_rows, inverse):
    grad_unit = upstream * gain_row
    first_term = jnp.mean(grad_unit, axis=-1, keepdims=True)
    second_term = jnp.mean(grad_unit * unit_rows, axis=-1, keepdims=True)
    return inverse * (grad_unit - first_term - unit_rows * second_term)


def fold_rows(values):
    rows, columns = values.shape
    return jnp.sum(values.reshape(rows // 8, 8, columns), axis=0)


def pair_columns(flat):
    empty = jnp.zeros((HEAD_DIM, LANES), flat.dtype)
    return jnp.concatenate(
        [jnp.concatenate([flat[:HEAD_DIM], empty], axis=0), jnp.concatenate([empty, flat[HEAD_DIM:]], axis=0)], axis=1
    )


def pair_rows(both):
    return jnp.concatenate([both[:HEAD_DIM, :LANES], both[HEAD_DIM:, LANES:]], axis=0)


def fold_max(values):
    pieces = [values[at : at + 64] for at in range(0, values.shape[0], 64)]
    while len(pieces) > 1:
        pieces = [jnp.maximum(a, b) for a, b in zip(pieces[::2], pieces[1::2])] + ([pieces[-1]] if len(pieces) % 2 else [])
    top = pieces[0]
    top = jnp.maximum(top[:32], top[32:])
    top = jnp.maximum(top[:16], top[16:])
    return jnp.max(jnp.maximum(top[:8], top[8:]), axis=0, keepdims=True)


def three_parts(value, part):
    high = value.astype(bf16).astype(f32)
    rest = value - high
    middle = rest.astype(bf16).astype(f32)
    return jnp.where(part == 0, high, jnp.where(part == 1, middle, rest - middle))


def image_tags(image_ref, start, rows):
    place = start + lax.broadcasted_iota(jnp.int32, (rows, LANES), 0)
    inside = (place >= image_ref[0, 0:1, :]) & (place < image_ref[0, 1:2, :])
    return jnp.where(inside, 1.0, 0.0).astype(bf16)


def attn_forward_kernel(
    start_ref, class_ref, count_ref, tokens_ref, w_ref, norm_ref, image_ref,
    middle_ref, qkv_ref, context_ref, ext_ref,
    tag_ref, normed_ref, qt_ref, vt_ref,
):
    row = pl.program_id(0)
    length, width = tokens_ref.shape
    pairs = width // LANES
    big = 256
    gain, bias = norm_ref[0:1, :], norm_ref[1:2, :]

    def prepare(step, carry):
        rows = pl.ds(pl.multiple_of(step * big, big), big)
        unit, _ = norm_parts(tokens_ref[rows, :].astype(f32))
        normed_ref[rows, :] = (unit * gain + bias).astype(bf16)
        tag_ref[rows, :] = image_tags(image_ref, step * big, big)
        return carry

    lax.fori_loop(0, length // big, prepare, 0)
    queries = (dot(normed_ref[...], w_ref[0]) * (HEAD_DIM**-0.5 * LOG2E)).astype(bf16)
    qkv_ref[:, :width] = queries
    qt_ref[...] = jnp.transpose(queries)
    qkv_ref[:, width : 2 * width] = dot(normed_ref[...], w_ref[1]).astype(bf16)
    values = dot(normed_ref[...], w_ref[2]).astype(bf16)
    qkv_ref[:, 2 * width :] = values
    vt_ref[...] = jnp.transpose(values)

    def tile(step, carry):
        q0 = pl.multiple_of(step * TILE, TILE)
        here = pl.ds(q0, TILE)
        place = q0 + lax.broadcasted_iota(jnp.int32, (IMAGES, LANES), 1)
        inside = (place >= image_ref[0, 8 : 8 + IMAGES, :]) & (place < image_ref[0, 16 : 16 + IMAGES, :])
        mask = jnp.where(inside, 0.0, -BIG)
        mask_low = jnp.concatenate([mask, jnp.zeros((LANES - IMAGES, LANES), f32)], axis=0).astype(bf16)
        ext_rows = lax.broadcasted_iota(jnp.int32, (EXTRA - IMAGES, LANES), 0)

        def attend(window):
            there = pl.ds(pl.multiple_of(start_ref[row, step], LANES), window)
            tags = tag_ref[there, :]
            ones = jnp.ones((GRID_W, window), bf16)
            extra = jnp.zeros((EXTRA - IMAGES, LANES), f32)
            slices = [slice(p * LANES, (p + 1) * LANES) for p in range(pairs)]
            masks = jnp.concatenate([mask_low, mask_low], axis=1)
            scores, tops, exponents, mixes = [], [], [], []
            for p, at in enumerate(slices):
                keys = qkv_ref[there, width + p * LANES : width + (p + 1) * LANES]
                right = jnp.concatenate([pair_columns(qt_ref[at, here]), masks], axis=0)
                scores.append(dot(jnp.concatenate([keys, tags], axis=1), right))
            for p in range(pairs):
                tops.append(fold_max(scores[p]))
                exponents.append(jnp.exp2(scores[p] - tops[p]).astype(bf16))
            for p, at in enumerate(slices):
                mixes.append(dot(jnp.concatenate([vt_ref[at, there], ones], axis=0), exponents[p]))
            for p, at in enumerate(slices):
                mixed = mixes[p]
                total = mixed[LANES : LANES + 1, :]
                minus_lse = -(tops[p] + jnp.log(total) * LOG2E)
                scale = 1.0 / total
                lane = lax.broadcasted_iota(jnp.int32, (1, 2 * TILE), 1)
                head = 2 * p + jnp.where(lane < TILE, 0, 1)
                scale = jnp.where(head < count_ref[row], scale, 0.0)
                context_ref[here, at] = jnp.transpose(pair_rows(mixed[:LANES] * scale)).astype(bf16)
                for h in range(2):
                    value = minus_lse[:, h * TILE : (h + 1) * TILE]
                    first = 6 * p + 3 * h
                    extra = jnp.where(
                        (ext_rows >= first) & (ext_rows < first + 3), three_parts(value, ext_rows - first), extra
                    )
            ext_ref[:, here] = jnp.concatenate([mask, extra], axis=0).astype(bf16)

        for index, window in enumerate(widths_for(length)):
            pl.when(class_ref[row, step] == index)(functools.partial(attend, window))
        return carry

    lax.fori_loop(0, length // TILE, tile, 0)
    middle_ref[...] = tokens_ref[...].astype(f32) + dot(context_ref[...], w_ref[3], NT)


def attn_forward(starts, classes, counts, tokens, attn_use, norm_w, images):
    rows_all, width = tokens.shape
    row_count = counts.shape[0]
    length = rows_all // row_count
    by_row = lambda columns: pl.BlockSpec((length, columns), lambda r, *_: (r, 0))
    return pl.pallas_call(
        attn_forward_kernel,
        grid_spec=pltpu.PrefetchScalarGridSpec(
            num_scalar_prefetch=3,
            grid=(row_count,),
            in_specs=[
                by_row(width),
                pl.BlockSpec(attn_use.shape, lambda r, *_: (0, 0, 0)),
                pl.BlockSpec(norm_w.shape, lambda r, *_: (0, 0)),
                pl.BlockSpec((1, 24, LANES), lambda r, *_: (r, 0, 0)),
            ],
            out_specs=[
                by_row(width), by_row(3 * width), by_row(width), pl.BlockSpec((EXTRA, length), lambda r, *_: (r, 0))
            ],
            scratch_shapes=[
                pltpu.VMEM((length, LANES), bf16),
                pltpu.VMEM((length, width), bf16),
                pltpu.VMEM((width, length), bf16),
                pltpu.VMEM((width, length), bf16),
            ],
        ),
        out_shape=[
            jax.ShapeDtypeStruct((rows_all, width), f32),
            jax.ShapeDtypeStruct((rows_all, 3 * width), bf16),
            jax.ShapeDtypeStruct((rows_all, width), bf16),
            jax.ShapeDtypeStruct((row_count * EXTRA, length), bf16),
        ],
        cost_estimate=work_of(30),
        compiler_params=pltpu.CompilerParams(vmem_limit_bytes=34 * MIB),
    )(starts, classes, counts, tokens, attn_use, norm_w, images)


def attn_backward_kernel(
    first, final, start_ref, class_ref, count_ref, rank_ref, tokens_ref, middle_grad_ref, qkv_ref, context_ref, ext_ref, w_ref, norm_ref,
    image_ref, *refs,
):
    sums = None
    if first:
        sums, refs = refs[1:3], refs[3:]
    sent = None
    if final:
        tokens_grad_ref, keep_ref, send_ref, norm_grad_ref, *scratch, w_grad_ref = refs
        sent = (keep_ref, send_ref)
    else:
        tokens_grad_ref, w_grad_ref, norm_grad_ref, *scratch = refs
    attn_backward_row(
        first, sums, sent, start_ref, class_ref, count_ref, rank_ref, tokens_ref, middle_grad_ref, qkv_ref, context_ref, ext_ref, w_ref,
        norm_ref, image_ref, tokens_grad_ref, w_grad_ref, norm_grad_ref, *scratch,
    )


def attn_backward_row(
    first, sums, sent, start_ref, class_ref, count_ref, rank_ref, tokens_ref, middle_grad_ref, qkv_ref, context_ref, ext_ref, w_ref,
    norm_ref, image_ref, tokens_grad_ref, w_grad_ref, norm_grad_ref,
    tag_ref, up_ref, delta_ref, normed_ref, dq_ref, dk_ref, dv_ref, low_ref, proj_ref, qt_ref, kt_ref, upt_ref, upstream_ref,
):
    step_at = pl.program_id(0)
    row = first + step_at
    length, width = tokens_ref.shape
    pairs = width // LANES
    big = 256
    gain, bias = norm_ref[0:1, :], norm_ref[1:2, :]

    @pl.when(step_at == 0)
    def _():
        for n, ref in enumerate((w_grad_ref, norm_grad_ref)):
            ref[...] = sums[n][...] if sums else jnp.zeros_like(ref)

    target = lax.broadcasted_iota(jnp.int32, (EXTRA, width), 0) - IMAGES
    source = lax.broadcasted_iota(jnp.int32, (EXTRA, width), 1) // HEAD_DIM * 3
    collect = jnp.where((target >= source) & (target < source + 3), -1.0, 0.0).astype(bf16)
    active = jnp.where(
        lax.broadcasted_iota(jnp.int32, (1, width), 1) // HEAD_DIM < count_ref[row], 1.0, 0.0
    )

    def prepare(step, carry):
        rows = pl.ds(pl.multiple_of(step * big, big), big)
        unit, _ = norm_parts(tokens_ref[rows, :].astype(f32))
        normed_ref[rows, :] = (unit * gain + bias).astype(bf16)
        tag_ref[rows, :] = image_tags(image_ref, step * big, big)
        low_ref[rows, :] = middle_grad_ref[rows, :].astype(bf16)
        dk_ref[rows, :] = jnp.zeros((big, width), f32)
        dv_ref[rows, :] = jnp.zeros((big, width), f32)
        return carry

    lax.fori_loop(0, length // big, prepare, 0)
    up = (dot(low_ref[...], w_ref[3]) * active).astype(bf16)
    up_ref[...] = up
    upt_ref[...] = jnp.transpose(up)
    qt_ref[...] = jnp.transpose(qkv_ref[:, :width])
    kt_ref[...] = jnp.transpose(qkv_ref[:, width : 2 * width])

    def gather(step, carry):
        rows = pl.ds(pl.multiple_of(step * big, big), big)
        product = up_ref[rows, :].astype(f32) * context_ref[rows, :].astype(f32)
        high = product.astype(bf16)
        rest = (product - high.astype(f32)).astype(bf16)
        delta = dot(collect, high, NT) + dot(collect, rest, NT)
        part = lax.rem(lax.broadcasted_iota(jnp.int32, (EXTRA, big), 0) + 3 * EXTRA - IMAGES, 3)
        delta_ref[:, rows] = three_parts(delta, part).astype(bf16)
        return carry

    lax.fori_loop(0, length // big, gather, 0)
    lane = lax.broadcasted_iota(jnp.int32, (1, LANES), 1)
    first_half = jnp.where(lane < HEAD_DIM, 1.0, 0.0).astype(bf16)
    second_half = jnp.where(lane >= HEAD_DIM, 1.0, 0.0).astype(bf16)

    def tile(step, carry):
        q0 = pl.multiple_of(step * TILE, TILE)
        here = pl.ds(q0, TILE)

        def attend(window):
            there = pl.ds(pl.multiple_of(start_ref[row, step], LANES), window)
            tags = tag_ref[there, :]
            ext = ext_ref[:, here]
            delta = delta_ref[:, here]
            at_row = lax.broadcasted_iota(jnp.int32, (EXTRA, LANES), 0)
            empty = jnp.zeros((LANES - EXTRA, 2 * TILE), bf16)

            def own(edge, masks):
                keep = (at_row >= edge) & (at_row < edge + 3)
                return jnp.where(keep | (at_row < IMAGES) if masks else keep, 1.0, 0.0).astype(bf16)

            slices = [slice(p * LANES, (p + 1) * LANES) for p in range(pairs)]
            scores, grad_probs, probs, grad_scores = [], [], [], []
            for p, at in enumerate(slices):
                keys = qkv_ref[there, width + p * LANES : width + (p + 1) * LANES]
                values = qkv_ref[there, 2 * width + p * LANES : 2 * width + (p + 1) * LANES]
                edge = IMAGES + 6 * p
                q_side = jnp.concatenate(
                    [
                        pair_columns(qt_ref[at, here]),
                        jnp.concatenate([ext * own(edge, True), ext * own(edge + 3, True)], axis=1),
                        empty,
                    ],
                    axis=0,
                )
                up_side = jnp.concatenate(
                    [
                        pair_columns(upt_ref[at, here]),
                        jnp.concatenate([delta * own(edge, False), delta * own(edge + 3, False)], axis=1),
                        empty,
                    ],
                    axis=0,
                )
                scores.append(dot(jnp.concatenate([keys, tags], axis=1), q_side))
                grad_probs.append(dot(jnp.concatenate([values, tags], axis=1), up_side))
            for p in range(pairs):
                weight = jnp.exp2(scores[p])
                probs.append(weight.astype(bf16))
                grad_scores.append((weight * grad_probs[p]).astype(bf16))
            for p, at in enumerate(slices):
                queries, ups = qkv_ref[here, at], up_ref[here, at]
                q_pair = jnp.concatenate([queries * first_half, queries * second_half], axis=0)
                up_pair = jnp.concatenate([ups * first_half, ups * second_half], axis=0)
                dv_ref[there, at] += dot(probs[p], up_pair)
                dk_ref[there, at] += dot(grad_scores[p], q_pair)
                dq = pair_rows(dot(kt_ref[at, there], grad_scores[p]))
                dq_ref[here, at] = jnp.transpose(dq * HEAD_DIM**-0.5).astype(bf16)

        for index, window in enumerate(widths_for(length)):
            pl.when(class_ref[row, step] == index)(functools.partial(attend, window))
        return carry

    lax.fori_loop(0, length // TILE, tile, 0)
    keys_grad = (dk_ref[...] * LN2).astype(bf16)
    values_grad = dv_ref[...].astype(bf16)
    proj_ref[...] = jnp.concatenate([dq_ref[...], keys_grad, values_grad], axis=1)
    w_cat = jnp.concatenate([w_ref[0], w_ref[1], w_ref[2]], axis=1)
    upstream_ref[...] = dot(proj_ref[...], w_cat, NT)

    def finish(step, carry):
        rows = pl.ds(pl.multiple_of(step * big, big), big)
        upstream = upstream_ref[rows, :]
        unit, inverse = norm_parts(tokens_ref[rows, :].astype(f32))
        tokens_grad_ref[rows, :] = middle_grad_ref[rows, :] + norm_back(upstream, gain, unit, inverse)
        norm_grad_ref[0:8, :] += fold_rows(upstream * unit)
        norm_grad_ref[8:16, :] += fold_rows(upstream)
        return carry

    lax.fori_loop(0, length // big, finish, 0)
    normed_t = jnp.transpose(normed_ref[...])
    for k in range(3):
        w_grad_ref[k] += dot(normed_t, proj_ref[:, k * width : (k + 1) * width])
    w_grad_ref[3] += dot(jnp.transpose(low_ref[...]), context_ref[...])
    if sent:

        @pl.when(step_at == pl.num_programs(0) - 1)
        def _():
            for k in range(2):
                one, two = w_grad_ref[k], w_grad_ref[k + 2]
                halves = [jnp.concatenate([one[:, at : at + width // 2], two[:, at : at + width // 2]], axis=1) for at in (0, width // 2)]
                sent[0][k] = jnp.where(rank_ref[0] == 0, halves[0], halves[1])
                sent[1][k] = jnp.where(rank_ref[0] == 0, halves[1], halves[0]).astype(bf16)


def attn_backward(first, count, so_far, starts, classes, counts, rank, tokens, middle_grad, qkv, context, ext, attn_use, norm_w, images):
    rows_all, width = tokens.shape
    length = rows_all // counts.shape[0]
    by_row = lambda columns: pl.BlockSpec((length, columns), lambda r, *_: (first + r, 0))
    final = first + count == counts.shape[0]
    half = (2, width, width)
    halves = pl.BlockSpec(half, lambda r, *_: (0, 0, 0))
    whole = pl.BlockSpec(attn_use.shape, lambda r, *_: (0, 0, 0))
    sums = pl.BlockSpec((16, width), lambda r, *_: (0, 0))
    return pl.pallas_call(
        functools.partial(attn_backward_kernel, first, final),
        grid_spec=pltpu.PrefetchScalarGridSpec(
            num_scalar_prefetch=4,
            grid=(count,),
            in_specs=[
                by_row(width),
                by_row(width),
                by_row(3 * width),
                by_row(width),
                pl.BlockSpec((EXTRA, length), lambda r, *_: (first + r, 0)),
                whole,
                pl.BlockSpec(norm_w.shape, lambda r, *_: (0, 0)),
                pl.BlockSpec((1, 24, LANES), lambda r, *_: (first + r, 0, 0)),
            ]
            + ([pl.BlockSpec(memory_space=pl.ANY), whole, sums] if first else []),
            out_specs=[by_row(width), halves, halves, sums] if final else [by_row(width), whole, sums],
            scratch_shapes=[
                pltpu.VMEM((length, LANES), bf16),
                pltpu.VMEM((length, width), bf16),
                pltpu.VMEM((EXTRA, length), bf16),
                pltpu.VMEM((length, width), bf16),
                pltpu.VMEM((length, width), bf16),
                pltpu.VMEM((length, width), f32),
                pltpu.VMEM((length, width), f32),
                pltpu.VMEM((length, width), bf16),
                pltpu.VMEM((length, 3 * width), bf16),
                pltpu.VMEM((width, length), bf16),
                pltpu.VMEM((width, length), bf16),
                pltpu.VMEM((width, length), bf16),
                pltpu.VMEM((length, width), f32),
            ]
            + ([pltpu.VMEM(attn_use.shape, f32)] if final else []),
        ),
        out_shape=[jax.ShapeDtypeStruct((rows_all, width), f32)]
        + (
            [jax.ShapeDtypeStruct(half, f32), jax.ShapeDtypeStruct(half, bf16)]
            if final
            else [jax.ShapeDtypeStruct(attn_use.shape, f32)]
        )
        + [jax.ShapeDtypeStruct((16, width), f32)],
        input_output_aliases={12: 0} if first else {},
        cost_estimate=work_of(20 * count),
        compiler_params=pltpu.CompilerParams(vmem_limit_bytes=40 * MIB),
    )(starts, classes, counts, rank, tokens, middle_grad, qkv, context, ext, attn_use, norm_w, images, *(so_far or ()))


def mlp_kernel(
    place_ref, rank_ref, middle_ref, out_grad_ref, w_ref, taps_ref, norm_ref,
    output_ref, middle_grad_ref, keep_ref, send_ref, taps_grad_ref, norm_grad_ref,
    w_grad_ref, normed_ref, normed_t_ref, out_grad_t_ref, out_sum_ref, up_sum_ref, tap_sum_ref,
    act_grads_ref, acts_ref, hidden_grads_ref, *buffers,
):
    row = pl.program_id(0)
    length, width = middle_ref.shape
    hidden = w_ref.shape[2]
    chunk = PARTS * LANES
    big = 256
    grid_rows = length // GRID_W
    chunks = hidden // chunk
    h_refs, g_refs = buffers[:PARTS], buffers[PARTS:]
    gain, bias = norm_ref[2:3, :], norm_ref[3:4, :]

    @pl.when(row == 0)
    def _():
        w_grad_ref[...] = jnp.zeros_like(w_grad_ref)
        norm_grad_ref[...] = jnp.zeros_like(norm_grad_ref)
        tap_sum_ref[...] = jnp.zeros_like(tap_sum_ref)
        for ref in buffers:
            ref[...] = jnp.zeros_like(ref)

    def place(r):
        return pl.multiple_of(place_ref[row, r], 8)

    for n in range(IMAGES + 1):
        at = place(grid_rows + n)
        for ref in buffers:
            ref[pl.ds(at, GRID_W), :] = jnp.zeros((GRID_W, LANES), f32)

    def normalize(step, carry):
        rows = pl.ds(pl.multiple_of(step * big, big), big)
        middle = middle_ref[rows, :]
        unit, _ = norm_parts(middle)
        normed_ref[rows, :] = (unit * gain + bias).astype(bf16)
        out_sum_ref[rows, :] = jnp.zeros((big, width), f32)
        up_sum_ref[rows, :] = jnp.zeros((big, width), f32)
        return carry

    lax.fori_loop(0, length // big, normalize, 0)
    normed_t_ref[...] = jnp.transpose(normed_ref[...])
    out_grad_t_ref[...] = jnp.transpose(out_grad_ref[...])

    def lanes_of(c):
        return pl.ds(pl.multiple_of(c * chunk, chunk), chunk)

    def lanes_of(c):
        return pl.ds(pl.multiple_of(c * chunk, chunk), chunk)

    def neighbours(ref, at):
        return [ref[pl.ds(at + (a * STRIDE + b), GRID_W), :] for a in (-1, 0, 1) for b in (-1, 0, 1)]

    def tall(values):
        return jnp.concatenate([values, values], axis=0)

    def total_of(terms):
        while len(terms) > 1:
            terms = [a + b for a, b in zip(terms[::2], terms[1::2])] + ([terms[-1]] if len(terms) % 2 else [])
        return terms[0]

    def taps_for(c, part, at):
        lane = pl.ds(pl.multiple_of(c * chunk + part * LANES, LANES), LANES)
        return [tall(taps_ref[at + k * 8 : at + (k + 1) * 8, lane]) for k in range(9)]

    lines = 8

    def do_chunk(c, carry):
        lanes = lanes_of(c)
        for t in range(length // big):
            rows = slice(t * big, (t + 1) * big)
            values = dot(normed_ref[rows, :], w_ref[0, :, lanes])
            for part in range(PARTS):
                for s in range(big // GRID_W):
                    at = place(t * (big // GRID_W) + s)
                    h_refs[part][pl.ds(at, GRID_W), :] = values[
                        s * GRID_W : (s + 1) * GRID_W, part * LANES : (part + 1) * LANES
                    ]
        act_grads_ref[...] = dot(out_grad_ref[...], w_ref[1, :, lanes])

        def forward(t, carry):
            tokens_base = pl.multiple_of(t * (lines * GRID_W), lines * GRID_W)
            for part in range(PARTS):
                taps = taps_for(c, part, 0)
                cols = slice(part * LANES, (part + 1) * LANES)
                for s in range(lines):
                    near = pl.ds(pl.multiple_of(tokens_base + s * GRID_W, GRID_W), GRID_W)
                    at = place(t * lines + s)
                    x = total_of([x * tap for x, tap in zip(neighbours(h_refs[part], at), taps)])
                    square = x * x
                    value = jnp.tanh(x * (GELU_A + square))
                    gate = 1.0 + value
                    twice = x * gate
                    acts_ref[near, cols] = twice.astype(bf16)
                    slope = gate + (twice * (1.0 - value)) * (GELU_A + 3.0 * square)
                    g_refs[part][pl.ds(at, GRID_W), :] = act_grads_ref[near, cols] * slope
            return carry

        lax.fori_loop(0, grid_rows // lines, forward, 0)

        def backward(t, carry):
            tokens_base = pl.multiple_of(t * (lines * GRID_W), lines * GRID_W)
            for part in range(PARTS):
                taps = taps_for(c, part, 72)
                lane = pl.ds(pl.multiple_of(c * chunk + part * LANES, LANES), LANES)
                cols = slice(part * LANES, (part + 1) * LANES)
                totals = [None] * 9
                for s in range(lines):
                    near = pl.ds(pl.multiple_of(tokens_base + s * GRID_W, GRID_W), GRID_W)
                    at = place(t * lines + s)
                    source = h_refs[part][pl.ds(at, GRID_W), :]
                    moved = neighbours(g_refs[part], at)[::-1]
                    for k in range(9):
                        product = source * moved[k]
                        folded = product[:8] + product[8:]
                        totals[k] = folded if totals[k] is None else totals[k] + folded
                    terms = [x * tap for x, tap in zip(moved, taps)]
                    hidden_grads_ref[near, cols] = total_of(terms).astype(bf16)
                for k in range(9):
                    tap_sum_ref[k * 8 : (k + 1) * 8, lane] += totals[k]
            return carry

        lax.fori_loop(0, grid_rows // lines, backward, 0)
        w_grad_ref[0, :, lanes] += dot(normed_t_ref[...], hidden_grads_ref[...])
        w_grad_ref[1, :, lanes] += dot(out_grad_t_ref[...], acts_ref[...])
        out_sum_ref[...] += dot(acts_ref[...], w_ref[1, :, lanes], NT)
        up_sum_ref[...] += dot(hidden_grads_ref[...], w_ref[0, :, lanes], NT)
        return carry

    lax.fori_loop(0, chunks, do_chunk, 0)

    def finish(step, carry):
        rows = pl.ds(pl.multiple_of(step * big, big), big)
        middle = middle_ref[rows, :]
        output_ref[rows, :] = (middle + ACT_SCALE * out_sum_ref[rows, :]).astype(bf16)
        upstream = 0.5 * up_sum_ref[rows, :]
        unit, inverse = norm_parts(middle)
        middle_grad_ref[rows, :] = out_grad_ref[rows, :].astype(f32) + norm_back(upstream, gain, unit, inverse)
        norm_grad_ref[0:8, :] += fold_rows(upstream * unit)
        norm_grad_ref[8:16, :] += fold_rows(upstream)
        return carry

    lax.fori_loop(0, length // big, finish, 0)

    @pl.when(row == pl.num_programs(0) - 1)
    def _():
        for k, scale in enumerate((0.5, ACT_SCALE)):
            halves = w_grad_ref[k, :, : hidden // 2], w_grad_ref[k, :, hidden // 2 :]
            keep_ref[k] = scale * jnp.where(rank_ref[0] == 0, halves[0], halves[1])
            send_ref[k] = (scale * jnp.where(rank_ref[0] == 0, halves[1], halves[0])).astype(bf16)
        taps_grad_ref[...] = jnp.zeros_like(taps_grad_ref)
        for k in range(9):
            total = jnp.sum(tap_sum_ref[k * 8 : (k + 1) * 8, :], axis=0, keepdims=True)
            taps_grad_ref[k : k + 1, :] = 0.5 * total


def mlp_layer(places, rank, middle, out_grad, mlp_use, taps, norm_w):
    rows_all, width = middle.shape
    row_count = places.shape[0]
    length = rows_all // row_count
    hidden = mlp_use.shape[2]
    half = mlp_use.shape[:2] + (hidden // 2,)
    by_row = lambda columns: pl.BlockSpec((length, columns), lambda r, *_: (r, 0))
    slots = (length // GRID_W + IMAGES + 2) * STRIDE
    return pl.pallas_call(
        mlp_kernel,
        grid_spec=pltpu.PrefetchScalarGridSpec(
            num_scalar_prefetch=2,
            grid=(row_count,),
            in_specs=[
                by_row(width),
                by_row(width),
                pl.BlockSpec(mlp_use.shape, lambda r, *_: (0, 0, 0)),
                pl.BlockSpec(taps.shape, lambda r, *_: (0, 0)),
                pl.BlockSpec(norm_w.shape, lambda r, *_: (0, 0)),
            ],
            out_specs=[
                by_row(width),
                by_row(width),
                pl.BlockSpec(half, lambda r, *_: (0, 0, 0)),
                pl.BlockSpec(half, lambda r, *_: (0, 0, 0)),
                pl.BlockSpec((16, hidden), lambda r, *_: (0, 0)),
                pl.BlockSpec((16, width), lambda r, *_: (0, 0)),
            ],
            scratch_shapes=[
                pltpu.VMEM(mlp_use.shape, f32),
                pltpu.VMEM((length, width), bf16),
                pltpu.VMEM((width, length), bf16),
                pltpu.VMEM((width, length), bf16),
                pltpu.VMEM((length, width), f32),
                pltpu.VMEM((length, width), f32),
                pltpu.VMEM((9 * 8, hidden), f32),
                pltpu.VMEM((length, PARTS * LANES), f32),
                pltpu.VMEM((length, PARTS * LANES), bf16),
                pltpu.VMEM((length, PARTS * LANES), bf16),
            ]
            + [pltpu.VMEM((slots, LANES), f32)] * (2 * PARTS),
        ),
        out_shape=[
            jax.ShapeDtypeStruct((rows_all, width), bf16),
            jax.ShapeDtypeStruct((rows_all, width), f32),
            jax.ShapeDtypeStruct(half, f32),
            jax.ShapeDtypeStruct(half, bf16),
            jax.ShapeDtypeStruct((16, hidden), f32),
            jax.ShapeDtypeStruct((16, width), f32),
        ],
        cost_estimate=work_of(90),
        compiler_params=pltpu.CompilerParams(vmem_limit_bytes=50 * MIB),
    )(places, rank, middle, out_grad, mlp_use, taps, norm_w)


def attention_plan(segments):
    row_count, length = segments.shape
    tiles = segments.reshape(row_count, length // TILE, TILE)
    first, last = tiles[:, :, 0], tiles[:, :, -1]
    ids = jnp.arange(IMAGES, dtype=jnp.int32)
    begins = jnp.sum((segments[:, None, :] < ids[None, :, None]).astype(jnp.int32), axis=-1)
    ends = jnp.sum((segments[:, None, :] <= ids[None, :, None]).astype(jnp.int32), axis=-1)
    low_end = jnp.sum(jnp.where(first[:, :, None] == ids, begins[:, None, :], 0), axis=-1) // LANES * LANES
    high_end = jnp.sum(jnp.where(last[:, :, None] == ids, ends[:, None, :], 0), axis=-1)
    widths = widths_for(length)
    classes = sum(((high_end - low_end) > w).astype(jnp.int32) for w in widths[:-1])
    chosen = jnp.full_like(classes, widths[-1])
    for index, w in enumerate(widths):
        chosen = jnp.where(classes == index, w, chosen)
    starts = jnp.minimum(low_end, length - chosen)
    used = jnp.zeros((row_count, EXTRA - IMAGES), jnp.int32)
    unused = jnp.zeros((row_count, LANES - EXTRA), jnp.int32)
    first_lane = jnp.concatenate([begins, used, unused], axis=1)
    end_lane = jnp.concatenate([ends, used + length, unused], axis=1)
    by_lane = jnp.pad(jnp.stack([first_lane, end_lane], axis=1), ((0, 0), (0, 6), (0, 0)))
    by_image = jnp.broadcast_to(jnp.concatenate([begins, ends], axis=1)[:, :, None], (row_count, 2 * IMAGES, LANES))
    return starts, classes, jnp.concatenate([by_lane, by_image], axis=1)


def spread_taps(conv_use):
    taps = conv_use.astype(f32)
    own = (jnp.arange(9) == 4).astype(f32)[:, None]
    taps = jnp.repeat(taps + own, 8, axis=0)
    return jnp.concatenate([taps * GELU_S, taps], axis=0)


def line_places(segments):
    ids = segments[:, ::GRID_W]
    count = ids.shape[1]
    rows = jnp.arange(count, dtype=jnp.int32) + ids + 1
    images = jnp.arange(IMAGES, dtype=jnp.int32)
    first = jnp.sum((ids[:, None, :] < images[None, :, None]).astype(jnp.int32), axis=-1)
    gaps = jnp.concatenate([first + images, jnp.full((ids.shape[0], 1), count + IMAGES, jnp.int32)], axis=1)
    return jnp.concatenate([rows, gaps], axis=1) * STRIDE + 8


def bits_of(size):
    bits = []
    b = 1
    while b < size:
        bits.append(b)
        b *= 2
    return bits


def groups_of(size):
    bits = bits_of(size)
    return [(bits[at], 1 << len(bits[at : at + 2])) for at in range(0, len(bits), 2)]


def swap(values, axis, size, bit):
    return lax.ppermute(values, axis, [(i, i ^ bit) for i in range(size)])


def in_order(found, mine):
    ordered = []
    for target in range(len(found)):
        value = found[0]
        for step in range(1, len(found)):
            value = jnp.where((mine ^ step) == target, found[step], value)
        ordered.append(value)
    return ordered


def gather_lines(shard, size):
    place = lax.axis_index("dp")
    held = shard[None]
    for low, count in reversed(groups_of(size)):
        found = [held] + [swap(held, "dp", size, step * low) for step in range(1, count)]
        held = jnp.stack(in_order(found, (place // low) % count), axis=1).reshape((-1,) + shard.shape)
    return held


def start_group(held, size, low, count):
    return [held] + [swap(held, "dp", size, step * low) for step in range(1, count)]


def finish_group(found, low, count):
    held = jnp.stack(in_order(found, (lax.axis_index("dp") // low) % count))
    return held.reshape((-1,) + held.shape[2:])


def fold_pairs(values):
    count = values.shape[0] // 2
    return jnp.concatenate([values[:count], values[count:]], axis=-1)


def unfold_pairs(values):
    half = values.shape[-1] // 2
    return jnp.concatenate([values[..., :half], values[..., half:]], axis=0)


def join_columns(mine, other, rank):
    first = jnp.where(rank == 0, mine, other)
    second = jnp.where(rank == 0, other, mine)
    return jnp.concatenate([first, second], axis=-1)


def gather_weights(shard, size, rank):
    count, part, columns = shard.shape
    mine = gather_lines(fold_pairs(shard), size)
    other = swap(mine, "head", 2, 1)
    full = [join_columns(mine[..., at : at + columns], other[..., at : at + columns], rank) for at in (0, columns)]
    return jnp.moveaxis(jnp.concatenate(full, axis=1), 0, 1).reshape(count, size * part, 2 * columns)


def half_columns(values, side):
    half = values.shape[-1] // 2
    return lax.dynamic_slice_in_dim(values, side * half, half, axis=values.ndim - 1)


def by_line(values, size):
    count, rows, columns = values.shape
    return values.reshape(count, size, rows // size, columns)


def two_parts(values):
    high = values.astype(bf16)
    return jnp.concatenate([high, (values - high.astype(f32)).astype(bf16)], axis=0)


def from_parts(parts):
    count = parts.shape[0] // 2
    return parts[:count].astype(f32) + parts[count:].astype(f32)


def pieces_of(held, low, count):
    n, lines = held.shape[:2]
    split = held.reshape((n, lines // count, count) + held.shape[2:])
    mine = (lax.axis_index("dp") // low) % count
    return [lax.dynamic_index_in_dim(split, mine ^ step, 2, keepdims=False) for step in range(count)]


def flat(values):
    return values.astype(bf16).reshape(-1, values.shape[-1])


def sum_everywhere(values, size):
    values = values + swap(values, "head", 2, 1)
    for bit in bits_of(size):
        values = values + swap(values, "dp", size, bit)
    return values


def after(first, second):
    return lax.optimization_barrier((first, second))


def adam_terms(grad_sum, first_old, second):
    first_new = BETA_ONE * first_old + (1.0 - BETA_ONE) * grad_sum
    second_new = BETA_TWO * second + (1.0 - BETA_TWO) * grad_sum * grad_sum
    direction = (
        first_new
        / (1.0 - BETA_ONE**STEP)
        / (jnp.sqrt(second_new / (1.0 - BETA_TWO**STEP)) + ADAM_EPS)
    )
    return (first_new, second_new, direction)


def moments_kernel(line_ref, norm_ref, *refs):
    count = 3
    grads, weights, firsts, seconds = (refs[n * count : (n + 1) * count] for n in range(4))
    new_firsts, new_seconds, updates = (refs[(4 + n) * count : (5 + n) * count] for n in range(3))
    sums_ref = refs[7 * count]
    width = sums_ref.shape[1]
    lane = lax.broadcasted_iota(jnp.int32, (1, width), 1)
    rows = [jnp.zeros((1, width), f32), jnp.zeros((1, width), f32)]
    at = 0
    for n in range(count):
        grad, weight = grads[n][...], weights[n][...]
        new_first, new_second, direction = adam_terms(grad, firsts[n][...], seconds[n][...])
        update = direction + DECAY * weight
        new_firsts[n][...], new_seconds[n][...], updates[n][...] = new_first, new_second, update
        matrices = weight.shape[0] if weight.ndim == 3 else 1
        for k in range(matrices):
            for row, values in enumerate((weight, update)):
                values = values[k] if weight.ndim == 3 else values
                total = jnp.sum(jnp.sum(values * values, axis=0, keepdims=True), axis=1, keepdims=True)
                if weight.ndim == 2:
                    total = jnp.where(line_ref[0] == 0, total, 0.0)
                rows[row] = jnp.where(lane == at, total, rows[row])
            at += 1
    gain = jnp.sum(norm_ref[0:8, :], axis=0, keepdims=True)
    bias = jnp.sum(norm_ref[8:16, :], axis=0, keepdims=True)
    sums_ref[...] = jnp.concatenate(rows + [gain, bias, jnp.zeros((4, width), f32)], axis=0)


def apply_kernel(sums_ref, norm_two_ref, norm_w_ref, norm_m_ref, norm_v_ref, *refs):
    count = 3
    weights, updates, news = (refs[n * count : (n + 1) * count] for n in range(3))
    new_norm_w_ref, new_norm_m_ref, new_norm_v_ref = refs[3 * count :]
    ratio = jnp.sqrt(sums_ref[0:1, :]) / jnp.sqrt(sums_ref[1:2, :])
    at = 0
    for n in range(count):
        shape = weights[n].shape
        if len(shape) == 3:
            for k in range(shape[0]):
                news[n][k] = weights[n][k] - RATE * ratio[:, at : at + 1] * updates[n][k]
                at += 1
        else:
            news[n][...] = weights[n][...] - RATE * ratio[:, at : at + 1] * updates[n][...]
            at += 1
    grads = jnp.concatenate([sums_ref[2:4, :], norm_two_ref[...]], axis=0)
    new_first, new_second, direction = adam_terms(grads, norm_m_ref[...], norm_v_ref[...])
    new_norm_m_ref[...], new_norm_v_ref[...] = new_first, new_second
    new_norm_w_ref[...] = norm_w_ref[...] - RATE * direction


def like(values):
    return [jax.ShapeDtypeStruct(v.shape, f32) for v in values]


def body(
    size,
    tokens, grad_out, segments, counts,
    attn_w, attn_m, attn_v, mlp_w, mlp_m, mlp_v, conv_w, conv_m, conv_v, norm_w, norm_m, norm_v,
):
    rank = lax.axis_index("head")
    place = lax.axis_index("dp")
    own_rows = segments.shape[0] // 2
    segments = lax.dynamic_slice_in_dim(segments, rank * own_rows, own_rows, axis=0)
    counts = lax.dynamic_slice_in_dim(counts, rank * own_rows, own_rows, axis=0)
    width = norm_w.shape[1]
    attn_use = gather_weights(attn_w.astype(bf16), size, rank)
    mlp_lines = mlp_w.astype(bf16)[None]
    groups = groups_of(size)
    for low, count in groups[:-1]:
        mlp_lines = finish_group(start_group(mlp_lines, size, low, count), low, count)
    found = start_group(mlp_lines, size, *groups[-1])
    conv_low = conv_w.astype(bf16)
    conv_use = join_columns(conv_low, swap(conv_low, "head", 2, 1), rank)
    starts, classes, images = attention_plan(segments)
    middle, qkv, context, ext = attn_forward(starts, classes, counts, tokens, attn_use, norm_w, images)
    middle, found = after(middle, found)
    mlp_lines = finish_group(found, *groups[-1])
    mlp_lines = jnp.moveaxis(mlp_lines, 0, 1).reshape(mlp_w.shape[0], -1, mlp_w.shape[2])
    mlp_use = join_columns(mlp_lines, swap(mlp_lines, "head", 2, 1), rank)
    rank_at = rank.astype(jnp.int32).reshape(1)
    output, grad_middle, held, send, grad_conv, grad_norm_two = mlp_layer(
        line_places(segments), rank_at, middle, grad_out, mlp_use, spread_taps(conv_use), norm_w
    )

    def back(first, count, so_far):
        return attn_backward(
            first, count, so_far, starts, classes, counts, rank_at, tokens, grad_middle, qkv, context, ext, attn_use, norm_w, images
        )

    columns = conv_w.shape[1]
    norm_two = jnp.sum(grad_norm_two.reshape(2, 8, width), axis=1).reshape(1, 2 * width)
    norm_two = jnp.pad(norm_two, ((0, 0), (0, columns - 2 * width)))
    taps = grad_conv[:9]
    small = jnp.concatenate([half_columns(taps, rank), norm_two])
    small_send = jnp.concatenate([half_columns(taps, 1 - rank), norm_two])
    got = swap(jnp.concatenate([flat(send), two_parts(small_send)], axis=0), "head", 2, 1)
    first_rows = max(1, own_rows // 3)
    so_far, got = after(back(0, first_rows, None), got)
    rows = held.size // columns
    held = by_line(held + got[:rows].reshape(held.shape).astype(f32), size)
    small = from_parts(two_parts(small)) + from_parts(got[rows:])
    low, count = groups[0]
    pieces = pieces_of(held, low, count)
    small_parts = two_parts(small)
    gots = [
        swap(jnp.concatenate([flat(pieces[step]), small_parts], axis=0), "dp", size, step * low) for step in range(1, count)
    ]
    so_far, pieces = after(so_far, pieces)
    grad_tokens, attn_held, attn_send, grad_norm_one = back(first_rows, own_rows - first_rows, so_far)

    def take(pieces, gots, small_parts, low, count):
        keep = pieces[0]
        rows = keep.size // keep.shape[-1]
        for got in gots:
            keep = keep + got[:rows].reshape(keep.shape).astype(f32)
        ordered = in_order([small_parts] + [got[rows:] for got in gots], (place // low) % count)
        return keep, sum(from_parts(part) for part in ordered)

    attn_got = swap(flat(attn_send), "head", 2, 1)
    attn_held, gots = after(attn_held, gots)
    held, small = take(pieces, gots, small_parts, low, count)
    rest = bits_of(size)[2:]
    attn_held = by_line(attn_held + attn_got.reshape(attn_held.shape).astype(f32), size)
    waiting = list(groups)
    while waiting or rest:
        attn_pieces, pieces, extra = [None], None, None
        if waiting:
            low, count = waiting.pop(0)
            attn_pieces = pieces_of(attn_held, low, count)
        sent = {step * low: [flat(attn_pieces[step])] for step in range(1, len(attn_pieces))}
        bit = None
        if rest:
            bit = rest.pop(0)
            pieces = pieces_of(held, bit, 2)
            small_parts = two_parts(small)
            extra = jnp.concatenate([flat(pieces[1]), small_parts], axis=0).reshape(-1, attn_held.shape[-1])
            sent.setdefault(bit, []).append(extra)
        gots = {step: swap(jnp.concatenate(parts, axis=0), "dp", size, step) for step, parts in sent.items()}
        if bit:
            got = gots[bit][gots[bit].shape[0] - extra.shape[0] :].reshape(-1, columns)
            held, small = take(pieces, [got], small_parts, bit, 2)
        if attn_pieces[0] is not None:
            attn_held = attn_pieces[0]
            rows = attn_held.size // attn_held.shape[-1]
            for step in range(1, len(attn_pieces)):
                attn_held = attn_held + gots[step * low][:rows].reshape(attn_held.shape).astype(f32)
    grad_attn = unfold_pairs(attn_held.reshape(attn_held.shape[:1] + attn_held.shape[2:]))
    grad_mlp = held.reshape(mlp_w.shape)
    norm_two = small[9, : 2 * width].reshape(2, width)

    weights, firsts, seconds = [attn_w, mlp_w, conv_w], [attn_m, mlp_m, conv_m], [attn_v, mlp_v, conv_v]
    scalars = pl.BlockSpec(memory_space=pltpu.SMEM)
    vectors = pl.BlockSpec(memory_space=pltpu.VMEM)
    results = pl.pallas_call(
        moments_kernel,
        in_specs=[scalars] + [vectors] * 13,
        out_specs=[vectors] * 10,
        out_shape=like(weights) * 3 + [jax.ShapeDtypeStruct((8, width), f32)],
        compiler_params=pltpu.CompilerParams(vmem_limit_bytes=16 * MIB),
    )(place.astype(jnp.int32).reshape(1), grad_norm_one, grad_attn, grad_mlp, small[:9], *weights, *firsts, *seconds)
    new_firsts, new_seconds, updates, sums = results[:3], results[3:6], results[6:9], results[9]
    new_w = pl.pallas_call(
        apply_kernel,
        in_specs=[vectors] * 11,
        out_specs=[vectors] * 6,
        out_shape=like(weights) + like([norm_w] * 3),
        compiler_params=pltpu.CompilerParams(vmem_limit_bytes=16 * MIB),
    )(sum_everywhere(sums, size), norm_two, norm_w, norm_m, norm_v, *weights, *updates)
    return (
        output, grad_tokens, new_w[0], new_firsts[0], new_seconds[0], new_w[1], new_firsts[1], new_seconds[1],
        new_w[2], new_firsts[2], new_seconds[2], *new_w[3:],
    )


def solution(mesh):
    rows, lines = P(("dp", "head"), None), P("dp", None)
    shards, columns = P(None, "dp", "head"), P(None, "head")
    in_specs = (rows, rows, lines, P("dp")) + (shards,) * 6 + (columns,) * 3 + (P(),) * 3
    out_specs = (rows, rows) + (shards,) * 6 + (columns,) * 3 + (P(),) * 3
    return jax.shard_map(
        functools.partial(body, mesh.shape["dp"]), mesh=mesh, in_specs=in_specs, out_specs=out_specs, check_vma=False
    )
```

```python
import functools
import jax
import jax.numpy as jnp
from jax import lax
from jax.experimental import pallas as pl
from jax.experimental.pallas import tpu as pltpu
from jax.sharding import PartitionSpec as P

HEAD_DIM = 64
GRID_W = 16
STEP = 10
IMAGES = 8

NORM_EPS = 1e-06
BETA_ONE = 0.9
BETA_TWO = 0.999
ADAM_EPS = 1e-06
DECAY = 0.01
RATE = 0.5
LOG2E = 1.4426950408889634
LN2 = 0.6931471805599453
BIG = 2.0**100
GELU_ONE = 0.7978845608028654
GELU_TWO = 0.044715
GELU_S = (GELU_ONE * GELU_TWO) ** (1.0 / 3.0)
GELU_A = GELU_ONE / GELU_S
ACT_SCALE = 0.5 / GELU_S
EXTRA = 32
PARTS = 4
TILE = 128
LANES = 128
STRIDE = GRID_W + 8
MIB = 1024 * 1024

f32 = jnp.float32
bf16 = jnp.bfloat16
NN = (((1,), (0,)), ((), ()))
NT = (((1,), (1,)), ((), ()))
TN = (((0,), (0,)), ((), ()))


def dot(left, right, dims=NN):
    return lax.dot_general(left, right, dims, preferred_element_type=f32)


def work_of(micros):
    return pl.CostEstimate(flops=micros * 1_000_000_000, bytes_accessed=micros * 1_000_000, transcendentals=0)


def widths_for(length):
    return [w for w in (256, 384, 512, 768) if w < length] + [length]


def norm_parts(values):
    average = jnp.mean(values, axis=-1, keepdims=True)
    centered = values - average
    inverse = lax.rsqrt(jnp.mean(centered * centered, axis=-1, keepdims=True) + NORM_EPS)
    return centered * inverse, inverse


def norm_back(upstream, gain_row, unit_rows, inverse):
    grad_unit = upstream * gain_row
    first_term = jnp.mean(grad_unit, axis=-1, keepdims=True)
    second_term = jnp.mean(grad_unit * unit_rows, axis=-1, keepdims=True)
    return inverse * (grad_unit - first_term - unit_rows * second_term)


def fold_rows(values):
    rows, columns = values.shape
    return jnp.sum(values.reshape(rows // 8, 8, columns), axis=0)


def pair_columns(flat):
    empty = jnp.zeros((HEAD_DIM, LANES), flat.dtype)
    return jnp.concatenate(
        [jnp.concatenate([flat[:HEAD_DIM], empty], axis=0), jnp.concatenate([empty, flat[HEAD_DIM:]], axis=0)], axis=1
    )


def pair_rows(both):
    return jnp.concatenate([both[:HEAD_DIM, :LANES], both[HEAD_DIM:, LANES:]], axis=0)


def fold_max(values):
    pieces = [values[at : at + 64] for at in range(0, values.shape[0], 64)]
    while len(pieces) > 1:
        pieces = [jnp.maximum(a, b) for a, b in zip(pieces[::2], pieces[1::2])] + ([pieces[-1]] if len(pieces) % 2 else [])
    top = pieces[0]
    top = jnp.maximum(top[:32], top[32:])
    top = jnp.maximum(top[:16], top[16:])
    return jnp.max(jnp.maximum(top[:8], top[8:]), axis=0, keepdims=True)


def three_parts(value, part):
    high = value.astype(bf16).astype(f32)
    rest = value - high
    middle = rest.astype(bf16).astype(f32)
    return jnp.where(part == 0, high, jnp.where(part == 1, middle, rest - middle))


def image_tags(image_ref, start, rows):
    place = start + lax.broadcasted_iota(jnp.int32, (rows, LANES), 0)
    inside = (place >= image_ref[0, 0:1, :]) & (place < image_ref[0, 1:2, :])
    return jnp.where(inside, 1.0, 0.0).astype(bf16)


def first_norm_kernel(tokens_ref, out_grad_ref, norm_ref, normed_ref, normed_t_ref, out_grad_t_ref):
    big = 256

    def step(at, carry):
        rows = pl.ds(pl.multiple_of(at * big, big), big)
        unit, _ = norm_parts(tokens_ref[rows, :].astype(f32))
        normed_ref[rows, :] = (unit * norm_ref[0:1, :] + norm_ref[1:2, :]).astype(bf16)
        return carry

    lax.fori_loop(0, tokens_ref.shape[0] // big, step, 0)
    normed_t_ref[...] = jnp.transpose(normed_ref[...])
    out_grad_t_ref[...] = jnp.transpose(out_grad_ref[...])


def first_norm(tokens, out_grad, norm_w, row_count):
    rows_all, width = tokens.shape
    length = rows_all // row_count
    by_row = pl.BlockSpec((length, width), lambda r: (r, 0))
    turned = pl.BlockSpec((width, length), lambda r: (r, 0))
    flipped = jax.ShapeDtypeStruct((row_count * width, length), bf16)
    return pl.pallas_call(
        first_norm_kernel,
        grid=(row_count,),
        in_specs=[by_row, by_row, pl.BlockSpec(norm_w.shape, lambda r: (0, 0))],
        out_specs=[by_row, turned, turned],
        out_shape=[jax.ShapeDtypeStruct((rows_all, width), bf16), flipped, flipped],
        cost_estimate=work_of(8),
        compiler_params=pltpu.CompilerParams(vmem_limit_bytes=20 * MIB),
    )(tokens, out_grad, norm_w)


def attn_forward_kernel(
    start_ref, class_ref, count_ref, tokens_ref, normed_ref, w_ref, image_ref,
    middle_ref, qkv_ref, context_ref, ext_ref,
    tag_ref, qt_ref, vt_ref,
):
    row = pl.program_id(0)
    length, width = tokens_ref.shape
    pairs = width // LANES
    tag_ref[...] = image_tags(image_ref, 0, length)
    queries = (dot(normed_ref[...], w_ref[0]) * (HEAD_DIM**-0.5 * LOG2E)).astype(bf16)
    qkv_ref[:, :width] = queries
    qt_ref[...] = jnp.transpose(queries)
    qkv_ref[:, width : 2 * width] = dot(normed_ref[...], w_ref[1]).astype(bf16)
    values = dot(normed_ref[...], w_ref[2]).astype(bf16)
    qkv_ref[:, 2 * width :] = values
    vt_ref[...] = jnp.transpose(values)

    def tile(step, carry):
        q0 = pl.multiple_of(step * TILE, TILE)
        here = pl.ds(q0, TILE)
        place = q0 + lax.broadcasted_iota(jnp.int32, (IMAGES, LANES), 1)
        inside = (place >= image_ref[0, 8 : 8 + IMAGES, :]) & (place < image_ref[0, 16 : 16 + IMAGES, :])
        mask = jnp.where(inside, 0.0, -BIG)
        mask_low = jnp.concatenate([mask, jnp.zeros((LANES - IMAGES, LANES), f32)], axis=0).astype(bf16)
        ext_rows = lax.broadcasted_iota(jnp.int32, (EXTRA - IMAGES, LANES), 0)

        def attend(window):
            there = pl.ds(pl.multiple_of(start_ref[row, step], LANES), window)
            tags = tag_ref[there, :]
            ones = jnp.ones((GRID_W, window), bf16)
            extra = jnp.zeros((EXTRA - IMAGES, LANES), f32)
            slices = [slice(p * LANES, (p + 1) * LANES) for p in range(pairs)]
            masks = jnp.concatenate([mask_low, mask_low], axis=1)
            scores, tops, exponents, mixes = [], [], [], []
            for p, at in enumerate(slices):
                keys = qkv_ref[there, width + p * LANES : width + (p + 1) * LANES]
                right = jnp.concatenate([pair_columns(qt_ref[at, here]), masks], axis=0)
                scores.append(dot(jnp.concatenate([keys, tags], axis=1), right))
            for p in range(pairs):
                tops.append(fold_max(scores[p]))
                exponents.append(jnp.exp2(scores[p] - tops[p]).astype(bf16))
            for p, at in enumerate(slices):
                mixes.append(dot(jnp.concatenate([vt_ref[at, there], ones], axis=0), exponents[p]))
            for p, at in enumerate(slices):
                mixed = mixes[p]
                total = mixed[LANES : LANES + 1, :]
                minus_lse = -(tops[p] + jnp.log(total) * LOG2E)
                scale = 1.0 / total
                lane = lax.broadcasted_iota(jnp.int32, (1, 2 * TILE), 1)
                head = 2 * p + jnp.where(lane < TILE, 0, 1)
                scale = jnp.where(head < count_ref[row], scale, 0.0)
                context_ref[here, at] = jnp.transpose(pair_rows(mixed[:LANES] * scale)).astype(bf16)
                for h in range(2):
                    value = minus_lse[:, h * TILE : (h + 1) * TILE]
                    first = 6 * p + 3 * h
                    extra = jnp.where(
                        (ext_rows >= first) & (ext_rows < first + 3), three_parts(value, ext_rows - first), extra
                    )
            ext_ref[:, here] = jnp.concatenate([mask, extra], axis=0).astype(bf16)

        for index, window in enumerate(widths_for(length)):
            pl.when(class_ref[row, step] == index)(functools.partial(attend, window))
        return carry

    lax.fori_loop(0, length // TILE, tile, 0)
    middle_ref[...] = tokens_ref[...].astype(f32) + dot(context_ref[...], w_ref[3], NT)


def attn_forward(starts, classes, counts, tokens, normed, attn_use, images):
    rows_all, width = tokens.shape
    row_count = counts.shape[0]
    length = rows_all // row_count
    by_row = lambda columns: pl.BlockSpec((length, columns), lambda r, *_: (r, 0))
    return pl.pallas_call(
        attn_forward_kernel,
        grid_spec=pltpu.PrefetchScalarGridSpec(
            num_scalar_prefetch=3,
            grid=(row_count,),
            in_specs=[
                by_row(width),
                by_row(width),
                pl.BlockSpec(attn_use.shape, lambda r, *_: (0, 0, 0)),
                pl.BlockSpec((1, 24, LANES), lambda r, *_: (r, 0, 0)),
            ],
            out_specs=[
                by_row(width), by_row(3 * width), by_row(width), pl.BlockSpec((EXTRA, length), lambda r, *_: (r, 0))
            ],
            scratch_shapes=[
                pltpu.VMEM((length, LANES), bf16),
                pltpu.VMEM((width, length), bf16),
                pltpu.VMEM((width, length), bf16),
            ],
        ),
        out_shape=[
            jax.ShapeDtypeStruct((rows_all, width), f32),
            jax.ShapeDtypeStruct((rows_all, 3 * width), bf16),
            jax.ShapeDtypeStruct((rows_all, width), bf16),
            jax.ShapeDtypeStruct((row_count * EXTRA, length), bf16),
        ],
        cost_estimate=work_of(30),
        compiler_params=pltpu.CompilerParams(vmem_limit_bytes=56 * MIB),
    )(starts, classes, counts, tokens, normed, attn_use, images)


def attn_backward_kernel(
    first, final, start_ref, class_ref, count_ref, rank_ref, normed_t_ref, middle_grad_ref, qkv_ref, context_ref, ext_ref, w_ref,
    image_ref, *refs,
):
    sums = None
    if first:
        sums, refs = refs[1], refs[2:]
    sent = None
    if final:
        proj_ref, keep_ref, send_ref, *scratch, w_grad_ref = refs
        sent = (keep_ref, send_ref)
    else:
        proj_ref, w_grad_ref, *scratch = refs
    attn_backward_row(
        first, sums, sent, start_ref, class_ref, count_ref, rank_ref, normed_t_ref, middle_grad_ref, qkv_ref, context_ref, ext_ref,
        w_ref, image_ref, proj_ref, w_grad_ref, *scratch,
    )


def attn_backward_row(
    first, sums, sent, start_ref, class_ref, count_ref, rank_ref, normed_t_ref, middle_grad_ref, qkv_ref, context_ref, ext_ref, w_ref,
    image_ref, proj_ref, w_grad_ref,
    tag_ref, up_ref, delta_ref, dq_ref, dk_ref, dv_ref, low_ref, qt_ref, kt_ref, upt_ref,
):
    step_at = pl.program_id(0)
    row = first + step_at
    length, width = middle_grad_ref.shape
    pairs = width // LANES
    big = 256

    @pl.when(step_at == 0)
    def _():
        w_grad_ref[...] = jnp.zeros_like(w_grad_ref) if sums is None else sums[...]

    target = lax.broadcasted_iota(jnp.int32, (EXTRA, width), 0) - IMAGES
    source = lax.broadcasted_iota(jnp.int32, (EXTRA, width), 1) // HEAD_DIM * 3
    collect = jnp.where((target >= source) & (target < source + 3), -1.0, 0.0).astype(bf16)
    active = jnp.where(
        lax.broadcasted_iota(jnp.int32, (1, width), 1) // HEAD_DIM < count_ref[row], 1.0, 0.0
    )

    def prepare(step, carry):
        rows = pl.ds(pl.multiple_of(step * big, big), big)
        tag_ref[rows, :] = image_tags(image_ref, step * big, big)
        low_ref[rows, :] = middle_grad_ref[rows, :].astype(bf16)
        dk_ref[rows, :] = jnp.zeros((big, width), f32)
        dv_ref[rows, :] = jnp.zeros((big, width), f32)
        return carry

    lax.fori_loop(0, length // big, prepare, 0)
    up = (dot(low_ref[...], w_ref[3]) * active).astype(bf16)
    up_ref[...] = up
    upt_ref[...] = jnp.transpose(up)
    qt_ref[...] = jnp.transpose(qkv_ref[:, :width])
    kt_ref[...] = jnp.transpose(qkv_ref[:, width : 2 * width])

    def gather(step, carry):
        rows = pl.ds(pl.multiple_of(step * big, big), big)
        product = up_ref[rows, :].astype(f32) * context_ref[rows, :].astype(f32)
        high = product.astype(bf16)
        rest = (product - high.astype(f32)).astype(bf16)
        delta = dot(collect, high, NT) + dot(collect, rest, NT)
        part = lax.rem(lax.broadcasted_iota(jnp.int32, (EXTRA, big), 0) + 3 * EXTRA - IMAGES, 3)
        delta_ref[:, rows] = three_parts(delta, part).astype(bf16)
        return carry

    lax.fori_loop(0, length // big, gather, 0)
    lane = lax.broadcasted_iota(jnp.int32, (1, LANES), 1)
    first_half = jnp.where(lane < HEAD_DIM, 1.0, 0.0).astype(bf16)
    second_half = jnp.where(lane >= HEAD_DIM, 1.0, 0.0).astype(bf16)

    def tile(step, carry):
        q0 = pl.multiple_of(step * TILE, TILE)
        here = pl.ds(q0, TILE)

        def attend(window):
            there = pl.ds(pl.multiple_of(start_ref[row, step], LANES), window)
            tags = tag_ref[there, :]
            ext = ext_ref[:, here]
            delta = delta_ref[:, here]
            at_row = lax.broadcasted_iota(jnp.int32, (EXTRA, LANES), 0)
            empty = jnp.zeros((LANES - EXTRA, 2 * TILE), bf16)

            def own(edge, masks):
                keep = (at_row >= edge) & (at_row < edge + 3)
                return jnp.where(keep | (at_row < IMAGES) if masks else keep, 1.0, 0.0).astype(bf16)

            slices = [slice(p * LANES, (p + 1) * LANES) for p in range(pairs)]
            scores, grad_probs, probs, grad_scores = [], [], [], []
            for p, at in enumerate(slices):
                keys = qkv_ref[there, width + p * LANES : width + (p + 1) * LANES]
                values = qkv_ref[there, 2 * width + p * LANES : 2 * width + (p + 1) * LANES]
                edge = IMAGES + 6 * p
                q_side = jnp.concatenate(
                    [
                        pair_columns(qt_ref[at, here]),
                        jnp.concatenate([ext * own(edge, True), ext * own(edge + 3, True)], axis=1),
                        empty,
                    ],
                    axis=0,
                )
                up_side = jnp.concatenate(
                    [
                        pair_columns(upt_ref[at, here]),
                        jnp.concatenate([delta * own(edge, False), delta * own(edge + 3, False)], axis=1),
                        empty,
                    ],
                    axis=0,
                )
                scores.append(dot(jnp.concatenate([keys, tags], axis=1), q_side))
                grad_probs.append(dot(jnp.concatenate([values, tags], axis=1), up_side))
            for p in range(pairs):
                weight = jnp.exp2(scores[p])
                probs.append(weight.astype(bf16))
                grad_scores.append((weight * grad_probs[p]).astype(bf16))
            for p, at in enumerate(slices):
                queries, ups = qkv_ref[here, at], up_ref[here, at]
                q_pair = jnp.concatenate([queries * first_half, queries * second_half], axis=0)
                up_pair = jnp.concatenate([ups * first_half, ups * second_half], axis=0)
                dv_ref[there, at] += dot(probs[p], up_pair)
                dk_ref[there, at] += dot(grad_scores[p], q_pair)
                dq = pair_rows(dot(kt_ref[at, there], grad_scores[p]))
                dq_ref[here, at] = jnp.transpose(dq * HEAD_DIM**-0.5).astype(bf16)

        for index, window in enumerate(widths_for(length)):
            pl.when(class_ref[row, step] == index)(functools.partial(attend, window))
        return carry

    lax.fori_loop(0, length // TILE, tile, 0)
    keys_grad = (dk_ref[...] * LN2).astype(bf16)
    values_grad = dv_ref[...].astype(bf16)
    proj_ref[...] = jnp.concatenate([dq_ref[...], keys_grad, values_grad], axis=1)
    for k in range(3):
        w_grad_ref[k] += dot(normed_t_ref[...], proj_ref[:, k * width : (k + 1) * width])
    w_grad_ref[3] += dot(jnp.transpose(low_ref[...]), context_ref[...])
    if sent:

        @pl.when(step_at == pl.num_programs(0) - 1)
        def _():
            for k in range(2):
                one, two = w_grad_ref[k], w_grad_ref[k + 2]
                halves = [jnp.concatenate([one[:, at : at + width // 2], two[:, at : at + width // 2]], axis=1) for at in (0, width // 2)]
                sent[0][k] = jnp.where(rank_ref[0] == 0, halves[0], halves[1])
                sent[1][k] = jnp.where(rank_ref[0] == 0, halves[1], halves[0]).astype(bf16)


def attn_backward(first, count, so_far, starts, classes, counts, rank, normed_t, middle_grad, qkv, context, ext, attn_use, images):
    rows_all, width = middle_grad.shape
    length = rows_all // counts.shape[0]
    by_row = lambda columns: pl.BlockSpec((length, columns), lambda r, *_: (first + r, 0))
    final = first + count == counts.shape[0]
    half = (2, width, width)
    halves = pl.BlockSpec(half, lambda r, *_: (0, 0, 0))
    whole = pl.BlockSpec(attn_use.shape, lambda r, *_: (0, 0, 0))
    return pl.pallas_call(
        functools.partial(attn_backward_kernel, first, final),
        grid_spec=pltpu.PrefetchScalarGridSpec(
            num_scalar_prefetch=4,
            grid=(count,),
            in_specs=[
                pl.BlockSpec((width, length), lambda r, *_: (first + r, 0)),
                by_row(width),
                by_row(3 * width),
                by_row(width),
                pl.BlockSpec((EXTRA, length), lambda r, *_: (first + r, 0)),
                whole,
                pl.BlockSpec((1, 24, LANES), lambda r, *_: (first + r, 0, 0)),
            ]
            + ([pl.BlockSpec(memory_space=pl.ANY), whole] if first else []),
            out_specs=[by_row(3 * width)] + ([halves, halves] if final else [whole]),
            scratch_shapes=[
                pltpu.VMEM((length, LANES), bf16),
                pltpu.VMEM((length, width), bf16),
                pltpu.VMEM((EXTRA, length), bf16),
                pltpu.VMEM((length, width), bf16),
                pltpu.VMEM((length, width), f32),
                pltpu.VMEM((length, width), f32),
                pltpu.VMEM((length, width), bf16),
                pltpu.VMEM((width, length), bf16),
                pltpu.VMEM((width, length), bf16),
                pltpu.VMEM((width, length), bf16),
            ]
            + ([pltpu.VMEM(attn_use.shape, f32)] if final else []),
        ),
        out_shape=[jax.ShapeDtypeStruct((rows_all, 3 * width), bf16)]
        + (
            [jax.ShapeDtypeStruct(half, f32), jax.ShapeDtypeStruct(half, bf16)]
            if final
            else [jax.ShapeDtypeStruct(attn_use.shape, f32)]
        ),
        input_output_aliases={11: 0} if first else {},
        cost_estimate=work_of(18 * count),
        compiler_params=pltpu.CompilerParams(vmem_limit_bytes=40 * MIB),
    )(starts, classes, counts, rank, normed_t, middle_grad, qkv, context, ext, attn_use, images, *(so_far or ()))


def tokens_back_kernel(proj_ref, tokens_ref, middle_grad_ref, w_ref, norm_ref, tokens_grad_ref, norm_grad_ref, upstream_ref):
    length, width = tokens_ref.shape
    big = 256

    @pl.when(pl.program_id(0) == 0)
    def _():
        norm_grad_ref[...] = jnp.zeros_like(norm_grad_ref)

    w_cat = jnp.concatenate([w_ref[0], w_ref[1], w_ref[2]], axis=1)
    upstream_ref[...] = dot(proj_ref[...], w_cat, NT)

    def finish(step, carry):
        rows = pl.ds(pl.multiple_of(step * big, big), big)
        upstream = upstream_ref[rows, :]
        unit, inverse = norm_parts(tokens_ref[rows, :].astype(f32))
        tokens_grad_ref[rows, :] = middle_grad_ref[rows, :] + norm_back(upstream, norm_ref[0:1, :], unit, inverse)
        norm_grad_ref[0:8, :] += fold_rows(upstream * unit)
        norm_grad_ref[8:16, :] += fold_rows(upstream)
        return carry

    lax.fori_loop(0, length // big, finish, 0)


def tokens_back(proj, tokens, middle_grad, attn_use, norm_w, row_count):
    rows_all, width = tokens.shape
    length = rows_all // row_count
    by_row = lambda columns: pl.BlockSpec((length, columns), lambda r: (r, 0))
    return pl.pallas_call(
        tokens_back_kernel,
        grid=(row_count,),
        in_specs=[
            by_row(3 * width),
            by_row(width),
            by_row(width),
            pl.BlockSpec(attn_use.shape, lambda r: (0, 0, 0)),
            pl.BlockSpec(norm_w.shape, lambda r: (0, 0)),
        ],
        out_specs=[by_row(width), pl.BlockSpec((16, width), lambda r: (0, 0))],
        out_shape=[jax.ShapeDtypeStruct((rows_all, width), f32), jax.ShapeDtypeStruct((16, width), f32)],
        scratch_shapes=[pltpu.VMEM((length, width), f32)],
        cost_estimate=work_of(9),
        compiler_params=pltpu.CompilerParams(vmem_limit_bytes=30 * MIB),
    )(proj, tokens, middle_grad, attn_use, norm_w)


def mlp_kernel(
    place_ref, rank_ref, middle_ref, out_grad_ref, out_grad_t_ref, own_w_ref, other_w_ref, taps_ref, norm_ref,
    output_ref, middle_grad_ref, keep_ref, send_ref, taps_grad_ref, norm_grad_ref,
    w_ref, w_grad_ref, normed_ref, normed_t_ref, out_sum_ref, up_sum_ref, tap_sum_ref,
    act_grads_ref, acts_ref, hidden_grads_ref, *buffers,
):
    row = pl.program_id(0)
    length, width = middle_ref.shape
    hidden = w_ref.shape[2]
    chunk = PARTS * LANES
    big = 256
    grid_rows = length // GRID_W
    chunks = hidden // chunk
    h_refs, g_refs = buffers[:PARTS], buffers[PARTS:]
    gain, bias = norm_ref[2:3, :], norm_ref[3:4, :]

    @pl.when(row == 0)
    def _():
        w_grad_ref[...] = jnp.zeros_like(w_grad_ref)
        norm_grad_ref[...] = jnp.zeros_like(norm_grad_ref)
        tap_sum_ref[...] = jnp.zeros_like(tap_sum_ref)
        for rank, halves in enumerate(((own_w_ref, other_w_ref), (other_w_ref, own_w_ref))):

            @pl.when(rank_ref[0] == rank)
            def _():
                w_ref[:, :, : hidden // 2] = halves[0][...]
                w_ref[:, :, hidden // 2 :] = halves[1][...]

        for ref in buffers:
            ref[...] = jnp.zeros_like(ref)

    def place(r):
        return pl.multiple_of(place_ref[row, r], 8)

    for n in range(IMAGES + 1):
        at = place(grid_rows + n)
        for ref in buffers:
            ref[pl.ds(at, GRID_W), :] = jnp.zeros((GRID_W, LANES), f32)

    def normalize(step, carry):
        rows = pl.ds(pl.multiple_of(step * big, big), big)
        middle = middle_ref[rows, :]
        unit, _ = norm_parts(middle)
        normed_ref[rows, :] = (unit * gain + bias).astype(bf16)
        out_sum_ref[rows, :] = jnp.zeros((big, width), f32)
        up_sum_ref[rows, :] = jnp.zeros((big, width), f32)
        return carry

    lax.fori_loop(0, length // big, normalize, 0)
    normed_t_ref[...] = jnp.transpose(normed_ref[...])

    def lanes_of(c):
        return pl.ds(pl.multiple_of(c * chunk, chunk), chunk)

    def lanes_of(c):
        return pl.ds(pl.multiple_of(c * chunk, chunk), chunk)

    def neighbours(ref, at):
        return [ref[pl.ds(at + (a * STRIDE + b), GRID_W), :] for a in (-1, 0, 1) for b in (-1, 0, 1)]

    def tall(values):
        return jnp.concatenate([values, values], axis=0)

    def total_of(terms):
        while len(terms) > 1:
            terms = [a + b for a, b in zip(terms[::2], terms[1::2])] + ([terms[-1]] if len(terms) % 2 else [])
        return terms[0]

    def taps_for(c, part, at):
        lane = pl.ds(pl.multiple_of(c * chunk + part * LANES, LANES), LANES)
        return [tall(taps_ref[at + k * 8 : at + (k + 1) * 8, lane]) for k in range(9)]

    lines = 8

    def do_chunk(c, carry):
        lanes = lanes_of(c)
        for t in range(length // big):
            rows = slice(t * big, (t + 1) * big)
            values = dot(normed_ref[rows, :], w_ref[0, :, lanes])
            for part in range(PARTS):
                for s in range(big // GRID_W):
                    at = place(t * (big // GRID_W) + s)
                    h_refs[part][pl.ds(at, GRID_W), :] = values[
                        s * GRID_W : (s + 1) * GRID_W, part * LANES : (part + 1) * LANES
                    ]
        act_grads_ref[...] = dot(out_grad_ref[...], w_ref[1, :, lanes])

        def forward(t, carry):
            tokens_base = pl.multiple_of(t * (lines * GRID_W), lines * GRID_W)
            for part in range(PARTS):
                taps = taps_for(c, part, 0)
                cols = slice(part * LANES, (part + 1) * LANES)
                for s in range(lines):
                    near = pl.ds(pl.multiple_of(tokens_base + s * GRID_W, GRID_W), GRID_W)
                    at = place(t * lines + s)
                    x = total_of([x * tap for x, tap in zip(neighbours(h_refs[part], at), taps)])
                    square = x * x
                    value = jnp.tanh(x * (GELU_A + square))
                    gate = 1.0 + value
                    twice = x * gate
                    acts_ref[near, cols] = twice.astype(bf16)
                    slope = gate + (twice * (1.0 - value)) * (GELU_A + 3.0 * square)
                    g_refs[part][pl.ds(at, GRID_W), :] = act_grads_ref[near, cols] * slope
            return carry

        lax.fori_loop(0, grid_rows // lines, forward, 0)

        def backward(t, carry):
            tokens_base = pl.multiple_of(t * (lines * GRID_W), lines * GRID_W)
            for part in range(PARTS):
                taps = taps_for(c, part, 72)
                lane = pl.ds(pl.multiple_of(c * chunk + part * LANES, LANES), LANES)
                cols = slice(part * LANES, (part + 1) * LANES)
                totals = [None] * 9
                for s in range(lines):
                    near = pl.ds(pl.multiple_of(tokens_base + s * GRID_W, GRID_W), GRID_W)
                    at = place(t * lines + s)
                    source = h_refs[part][pl.ds(at, GRID_W), :]
                    moved = neighbours(g_refs[part], at)[::-1]
                    for k in range(9):
                        product = source * moved[k]
                        folded = product[:8] + product[8:]
                        totals[k] = folded if totals[k] is None else totals[k] + folded
                    terms = [x * tap for x, tap in zip(moved, taps)]
                    hidden_grads_ref[near, cols] = total_of(terms).astype(bf16)
                for k in range(9):
                    tap_sum_ref[k * 8 : (k + 1) * 8, lane] += totals[k]
            return carry

        lax.fori_loop(0, grid_rows // lines, backward, 0)
        w_grad_ref[0, :, lanes] += dot(normed_t_ref[...], hidden_grads_ref[...])
        w_grad_ref[1, :, lanes] += dot(out_grad_t_ref[...], acts_ref[...])
        out_sum_ref[...] += dot(acts_ref[...], w_ref[1, :, lanes], NT)
        up_sum_ref[...] += dot(hidden_grads_ref[...], w_ref[0, :, lanes], NT)
        return carry

    lax.fori_loop(0, chunks, do_chunk, 0)

    def finish(step, carry):
        rows = pl.ds(pl.multiple_of(step * big, big), big)
        middle = middle_ref[rows, :]
        output_ref[rows, :] = (middle + ACT_SCALE * out_sum_ref[rows, :]).astype(bf16)
        upstream = 0.5 * up_sum_ref[rows, :]
        unit, inverse = norm_parts(middle)
        middle_grad_ref[rows, :] = out_grad_ref[rows, :].astype(f32) + norm_back(upstream, gain, unit, inverse)
        norm_grad_ref[0:8, :] += fold_rows(upstream * unit)
        norm_grad_ref[8:16, :] += fold_rows(upstream)
        return carry

    lax.fori_loop(0, length // big, finish, 0)

    @pl.when(row == pl.num_programs(0) - 1)
    def _():
        for k, scale in enumerate((0.5, ACT_SCALE)):
            halves = w_grad_ref[k, :, : hidden // 2], w_grad_ref[k, :, hidden // 2 :]
            keep_ref[k] = scale * jnp.where(rank_ref[0] == 0, halves[0], halves[1])
            send_ref[k] = (scale * jnp.where(rank_ref[0] == 0, halves[1], halves[0])).astype(bf16)
        taps_grad_ref[...] = jnp.zeros_like(taps_grad_ref)
        for k in range(9):
            total = jnp.sum(tap_sum_ref[k * 8 : (k + 1) * 8, :], axis=0, keepdims=True)
            taps_grad_ref[k : k + 1, :] = 0.5 * total


def mlp_layer(places, rank, middle, out_grad, out_grad_t, own_w, other_w, taps, norm_w):
    rows_all, width = middle.shape
    row_count = places.shape[0]
    length = rows_all // row_count
    half = own_w.shape
    hidden = 2 * half[2]
    whole = half[:2] + (hidden,)
    by_row = lambda columns: pl.BlockSpec((length, columns), lambda r, *_: (r, 0))
    slots = (length // GRID_W + IMAGES + 2) * STRIDE
    return pl.pallas_call(
        mlp_kernel,
        grid_spec=pltpu.PrefetchScalarGridSpec(
            num_scalar_prefetch=2,
            grid=(row_count,),
            in_specs=[
                by_row(width),
                by_row(width),
                pl.BlockSpec((width, length), lambda r, *_: (r, 0)),
                pl.BlockSpec(half, lambda r, *_: (0, 0, 0)),
                pl.BlockSpec(half, lambda r, *_: (0, 0, 0)),
                pl.BlockSpec(taps.shape, lambda r, *_: (0, 0)),
                pl.BlockSpec(norm_w.shape, lambda r, *_: (0, 0)),
            ],
            out_specs=[
                by_row(width),
                by_row(width),
                pl.BlockSpec(half, lambda r, *_: (0, 0, 0)),
                pl.BlockSpec(half, lambda r, *_: (0, 0, 0)),
                pl.BlockSpec((16, hidden), lambda r, *_: (0, 0)),
                pl.BlockSpec((16, width), lambda r, *_: (0, 0)),
            ],
            scratch_shapes=[
                pltpu.VMEM(whole, bf16),
                pltpu.VMEM(whole, f32),
                pltpu.VMEM((length, width), bf16),
                pltpu.VMEM((width, length), bf16),
                pltpu.VMEM((length, width), f32),
                pltpu.VMEM((length, width), f32),
                pltpu.VMEM((9 * 8, hidden), f32),
                pltpu.VMEM((length, PARTS * LANES), f32),
                pltpu.VMEM((length, PARTS * LANES), bf16),
                pltpu.VMEM((length, PARTS * LANES), bf16),
            ]
            + [pltpu.VMEM((slots, LANES), f32)] * (2 * PARTS),
        ),
        out_shape=[
            jax.ShapeDtypeStruct((rows_all, width), bf16),
            jax.ShapeDtypeStruct((rows_all, width), f32),
            jax.ShapeDtypeStruct(half, f32),
            jax.ShapeDtypeStruct(half, bf16),
            jax.ShapeDtypeStruct((16, hidden), f32),
            jax.ShapeDtypeStruct((16, width), f32),
        ],
        cost_estimate=work_of(90),
        compiler_params=pltpu.CompilerParams(vmem_limit_bytes=50 * MIB),
    )(places, rank, middle, out_grad, out_grad_t, own_w, other_w, taps, norm_w)


def attention_plan(segments):
    row_count, length = segments.shape
    tiles = segments.reshape(row_count, length // TILE, TILE)
    first, last = tiles[:, :, 0], tiles[:, :, -1]
    ids = jnp.arange(IMAGES, dtype=jnp.int32)
    begins = jnp.sum((segments[:, None, :] < ids[None, :, None]).astype(jnp.int32), axis=-1)
    ends = jnp.sum((segments[:, None, :] <= ids[None, :, None]).astype(jnp.int32), axis=-1)
    low_end = jnp.sum(jnp.where(first[:, :, None] == ids, begins[:, None, :], 0), axis=-1) // LANES * LANES
    high_end = jnp.sum(jnp.where(last[:, :, None] == ids, ends[:, None, :], 0), axis=-1)
    widths = widths_for(length)
    classes = sum(((high_end - low_end) > w).astype(jnp.int32) for w in widths[:-1])
    chosen = jnp.full_like(classes, widths[-1])
    for index, w in enumerate(widths):
        chosen = jnp.where(classes == index, w, chosen)
    starts = jnp.minimum(low_end, length - chosen)
    used = jnp.zeros((row_count, EXTRA - IMAGES), jnp.int32)
    unused = jnp.zeros((row_count, LANES - EXTRA), jnp.int32)
    first_lane = jnp.concatenate([begins, used, unused], axis=1)
    end_lane = jnp.concatenate([ends, used + length, unused], axis=1)
    by_lane = jnp.pad(jnp.stack([first_lane, end_lane], axis=1), ((0, 0), (0, 6), (0, 0)))
    by_image = jnp.broadcast_to(jnp.concatenate([begins, ends], axis=1)[:, :, None], (row_count, 2 * IMAGES, LANES))
    return starts, classes, jnp.concatenate([by_lane, by_image], axis=1)


def spread_taps(conv_use):
    taps = conv_use.astype(f32)
    own = (jnp.arange(9) == 4).astype(f32)[:, None]
    taps = jnp.repeat(taps + own, 8, axis=0)
    return jnp.concatenate([taps * GELU_S, taps], axis=0)


def line_places(segments):
    ids = segments[:, ::GRID_W]
    count = ids.shape[1]
    rows = jnp.arange(count, dtype=jnp.int32) + ids + 1
    images = jnp.arange(IMAGES, dtype=jnp.int32)
    first = jnp.sum((ids[:, None, :] < images[None, :, None]).astype(jnp.int32), axis=-1)
    gaps = jnp.concatenate([first + images, jnp.full((ids.shape[0], 1), count + IMAGES, jnp.int32)], axis=1)
    return jnp.concatenate([rows, gaps], axis=1) * STRIDE + 8


def bits_of(size):
    bits = []
    b = 1
    while b < size:
        bits.append(b)
        b *= 2
    return bits


def groups_of(size):
    bits = bits_of(size)
    return [(bits[at], 1 << len(bits[at : at + 2])) for at in range(0, len(bits), 2)]


def swap(values, axis, size, bit):
    return lax.ppermute(values, axis, [(i, i ^ bit) for i in range(size)])


def in_order(found, mine):
    ordered = []
    for target in range(len(found)):
        value = found[0]
        for step in range(1, len(found)):
            value = jnp.where((mine ^ step) == target, found[step], value)
        ordered.append(value)
    return ordered


def gather_lines(shard, size):
    place = lax.axis_index("dp")
    held = shard[None]
    for low, count in reversed(groups_of(size)):
        found = [held] + [swap(held, "dp", size, step * low) for step in range(1, count)]
        held = jnp.stack(in_order(found, (place // low) % count), axis=1).reshape((-1,) + shard.shape)
    return held


def start_group(held, size, low, count):
    return [held] + [swap(held, "dp", size, step * low) for step in range(1, count)]


def finish_group(found, low, count):
    held = jnp.stack(in_order(found, (lax.axis_index("dp") // low) % count))
    return held.reshape((-1,) + held.shape[2:])


def fold_pairs(values):
    count = values.shape[0] // 2
    return jnp.concatenate([values[:count], values[count:]], axis=-1)


def unfold_pairs(values):
    half = values.shape[-1] // 2
    return jnp.concatenate([values[..., :half], values[..., half:]], axis=0)


def join_columns(mine, other, rank):
    first = jnp.where(rank == 0, mine, other)
    second = jnp.where(rank == 0, other, mine)
    return jnp.concatenate([first, second], axis=-1)


def gather_weights(shard, size, rank):
    count, part, columns = shard.shape
    mine = gather_lines(fold_pairs(shard), size)
    other = swap(mine, "head", 2, 1)
    full = [join_columns(mine[..., at : at + columns], other[..., at : at + columns], rank) for at in (0, columns)]
    return jnp.moveaxis(jnp.concatenate(full, axis=1), 0, 1).reshape(count, size * part, 2 * columns)


def half_columns(values, side):
    half = values.shape[-1] // 2
    return lax.dynamic_slice_in_dim(values, side * half, half, axis=values.ndim - 1)


def by_line(values, size):
    count, rows, columns = values.shape
    return values.reshape(count, size, rows // size, columns)


def two_parts(values):
    high = values.astype(bf16)
    return jnp.concatenate([high, (values - high.astype(f32)).astype(bf16)], axis=0)


def from_parts(parts):
    count = parts.shape[0] // 2
    return parts[:count].astype(f32) + parts[count:].astype(f32)


def pieces_of(held, low, count):
    n, lines = held.shape[:2]
    split = held.reshape((n, lines // count, count) + held.shape[2:])
    mine = (lax.axis_index("dp") // low) % count
    return [lax.dynamic_index_in_dim(split, mine ^ step, 2, keepdims=False) for step in range(count)]


def flat(values):
    return values.astype(bf16).reshape(-1, values.shape[-1])


def sum_everywhere(values, size):
    values = values + swap(values, "head", 2, 1)
    for bit in bits_of(size):
        values = values + swap(values, "dp", size, bit)
    return values


def after(first, second):
    return lax.optimization_barrier((first, second))


def adam_terms(grad_sum, first_old, second):
    first_new = BETA_ONE * first_old + (1.0 - BETA_ONE) * grad_sum
    second_new = BETA_TWO * second + (1.0 - BETA_TWO) * grad_sum * grad_sum
    direction = (
        first_new
        / (1.0 - BETA_ONE**STEP)
        / (jnp.sqrt(second_new / (1.0 - BETA_TWO**STEP)) + ADAM_EPS)
    )
    return (first_new, second_new, direction)


def moments_kernel(line_ref, norm_ref, *refs):
    count = 3
    grads, weights, firsts, seconds = (refs[n * count : (n + 1) * count] for n in range(4))
    new_firsts, new_seconds, updates = (refs[(4 + n) * count : (5 + n) * count] for n in range(3))
    sums_ref = refs[7 * count]
    width = sums_ref.shape[1]
    lane = lax.broadcasted_iota(jnp.int32, (1, width), 1)
    rows = [jnp.zeros((1, width), f32), jnp.zeros((1, width), f32)]
    at = 0
    for n in range(count):
        grad, weight = grads[n][...], weights[n][...]
        new_first, new_second, direction = adam_terms(grad, firsts[n][...], seconds[n][...])
        update = direction + DECAY * weight
        new_firsts[n][...], new_seconds[n][...], updates[n][...] = new_first, new_second, update
        matrices = weight.shape[0] if weight.ndim == 3 else 1
        for k in range(matrices):
            for row, values in enumerate((weight, update)):
                values = values[k] if weight.ndim == 3 else values
                total = jnp.sum(jnp.sum(values * values, axis=0, keepdims=True), axis=1, keepdims=True)
                if weight.ndim == 2:
                    total = jnp.where(line_ref[0] == 0, total, 0.0)
                rows[row] = jnp.where(lane == at, total, rows[row])
            at += 1
    gain = jnp.sum(norm_ref[0:8, :], axis=0, keepdims=True)
    bias = jnp.sum(norm_ref[8:16, :], axis=0, keepdims=True)
    sums_ref[...] = jnp.concatenate(rows + [gain, bias, jnp.zeros((4, width), f32)], axis=0)


def apply_kernel(sums_ref, norm_two_ref, norm_w_ref, norm_m_ref, norm_v_ref, *refs):
    count = 3
    weights, updates, news = (refs[n * count : (n + 1) * count] for n in range(3))
    new_norm_w_ref, new_norm_m_ref, new_norm_v_ref = refs[3 * count :]
    ratio = jnp.sqrt(sums_ref[0:1, :]) / jnp.sqrt(sums_ref[1:2, :])
    at = 0
    for n in range(count):
        shape = weights[n].shape
        if len(shape) == 3:
            for k in range(shape[0]):
                news[n][k] = weights[n][k] - RATE * ratio[:, at : at + 1] * updates[n][k]
                at += 1
        else:
            news[n][...] = weights[n][...] - RATE * ratio[:, at : at + 1] * updates[n][...]
            at += 1
    grads = jnp.concatenate([sums_ref[2:4, :], norm_two_ref[...]], axis=0)
    new_first, new_second, direction = adam_terms(grads, norm_m_ref[...], norm_v_ref[...])
    new_norm_m_ref[...], new_norm_v_ref[...] = new_first, new_second
    new_norm_w_ref[...] = norm_w_ref[...] - RATE * direction


def like(values):
    return [jax.ShapeDtypeStruct(v.shape, f32) for v in values]


def body(
    size,
    tokens, grad_out, segments, counts,
    attn_w, attn_m, attn_v, mlp_w, mlp_m, mlp_v, conv_w, conv_m, conv_v, norm_w, norm_m, norm_v,
):
    rank = lax.axis_index("head")
    place = lax.axis_index("dp")
    own_rows = segments.shape[0] // 2
    segments = lax.dynamic_slice_in_dim(segments, rank * own_rows, own_rows, axis=0)
    counts = lax.dynamic_slice_in_dim(counts, rank * own_rows, own_rows, axis=0)
    width = norm_w.shape[1]
    attn_use = gather_weights(attn_w.astype(bf16), size, rank)
    mlp_lines = mlp_w.astype(bf16)[None]
    groups = groups_of(size)
    for low, count in groups[:-1]:
        mlp_lines = finish_group(start_group(mlp_lines, size, low, count), low, count)
    found = start_group(mlp_lines, size, *groups[-1])
    conv_low = conv_w.astype(bf16)
    conv_use = join_columns(conv_low, swap(conv_low, "head", 2, 1), rank)
    starts, classes, images = attention_plan(segments)
    normed, normed_t, out_grad_t = first_norm(tokens, grad_out, norm_w, own_rows)
    middle, qkv, context, ext = attn_forward(starts, classes, counts, tokens, normed, attn_use, images)
    middle, found = after(middle, found)
    mlp_lines = finish_group(found, *groups[-1])
    mlp_lines = jnp.moveaxis(mlp_lines, 0, 1).reshape(mlp_w.shape[0], -1, mlp_w.shape[2])
    rank_at = rank.astype(jnp.int32).reshape(1)
    output, grad_middle, held, send, grad_conv, grad_norm_two = mlp_layer(
        line_places(segments), rank_at, middle, grad_out, out_grad_t, mlp_lines, swap(mlp_lines, "head", 2, 1),
        spread_taps(conv_use), norm_w,
    )

    def back(first, count, so_far):
        return attn_backward(
            first, count, so_far, starts, classes, counts, rank_at, normed_t, grad_middle, qkv, context, ext, attn_use, images
        )

    columns = conv_w.shape[1]
    norm_two = jnp.sum(grad_norm_two.reshape(2, 8, width), axis=1).reshape(1, 2 * width)
    norm_two = jnp.pad(norm_two, ((0, 0), (0, columns - 2 * width)))
    taps = grad_conv[:9]
    small = jnp.concatenate([half_columns(taps, rank), norm_two])
    small_send = jnp.concatenate([half_columns(taps, 1 - rank), norm_two])
    got = swap(jnp.concatenate([flat(send), two_parts(small_send)], axis=0), "head", 2, 1)
    first_rows = max(1, own_rows // 3)
    so_far, got = after(back(0, first_rows, None), got)
    rows = held.size // columns
    held = by_line(held + got[:rows].reshape(held.shape).astype(f32), size)
    small = from_parts(two_parts(small)) + from_parts(got[rows:])
    low, count = groups[0]
    pieces = pieces_of(held, low, count)
    small_parts = two_parts(small)
    gots = [
        swap(jnp.concatenate([flat(pieces[step]), small_parts], axis=0), "dp", size, step * low) for step in range(1, count)
    ]
    so_far, pieces = after(so_far, pieces)
    projected_grad, attn_held, attn_send = back(first_rows, own_rows - first_rows, so_far)

    def take(pieces, gots, small_parts, low, count):
        keep = pieces[0]
        rows = keep.size // keep.shape[-1]
        for got in gots:
            keep = keep + got[:rows].reshape(keep.shape).astype(f32)
        ordered = in_order([small_parts] + [got[rows:] for got in gots], (place // low) % count)
        return keep, sum(from_parts(part) for part in ordered)

    attn_got = swap(flat(attn_send), "head", 2, 1)
    attn_held, gots = after(attn_held, gots)
    held, small = take(pieces, gots, small_parts, low, count)
    rest = bits_of(size)[2:]
    attn_held = by_line(attn_held + attn_got.reshape(attn_held.shape).astype(f32), size)
    waiting = list(groups)
    while waiting or rest:
        attn_pieces, pieces, extra = [None], None, None
        if waiting:
            low, count = waiting.pop(0)
            attn_pieces = pieces_of(attn_held, low, count)
        sent = {step * low: [flat(attn_pieces[step])] for step in range(1, len(attn_pieces))}
        bit = None
        if rest:
            bit = rest.pop(0)
            pieces = pieces_of(held, bit, 2)
            small_parts = two_parts(small)
            extra = jnp.concatenate([flat(pieces[1]), small_parts], axis=0).reshape(-1, attn_held.shape[-1])
            sent.setdefault(bit, []).append(extra)
        first_time = attn_pieces[0] is not None and low == groups[0][0]
        if first_time:
            sent, projected_grad = after(sent, projected_grad)
        gots = {step: swap(jnp.concatenate(parts, axis=0), "dp", size, step) for step, parts in sent.items()}
        if first_time:
            results = tokens_back(projected_grad, tokens, grad_middle, attn_use, norm_w, own_rows)
            (grad_tokens, grad_norm_one), gots = after(results, gots)
        if bit:
            got = gots[bit][gots[bit].shape[0] - extra.shape[0] :].reshape(-1, columns)
            held, small = take(pieces, [got], small_parts, bit, 2)
        if attn_pieces[0] is not None:
            attn_held = attn_pieces[0]
            rows = attn_held.size // attn_held.shape[-1]
            for step in range(1, len(attn_pieces)):
                attn_held = attn_held + gots[step * low][:rows].reshape(attn_held.shape).astype(f32)
    grad_attn = unfold_pairs(attn_held.reshape(attn_held.shape[:1] + attn_held.shape[2:]))
    grad_mlp = held.reshape(mlp_w.shape)
    norm_two = small[9, : 2 * width].reshape(2, width)

    weights, firsts, seconds = [attn_w, mlp_w, conv_w], [attn_m, mlp_m, conv_m], [attn_v, mlp_v, conv_v]
    scalars = pl.BlockSpec(memory_space=pltpu.SMEM)
    vectors = pl.BlockSpec(memory_space=pltpu.VMEM)
    results = pl.pallas_call(
        moments_kernel,
        in_specs=[scalars] + [vectors] * 13,
        out_specs=[vectors] * 10,
        out_shape=like(weights) * 3 + [jax.ShapeDtypeStruct((8, width), f32)],
        compiler_params=pltpu.CompilerParams(vmem_limit_bytes=16 * MIB),
    )(place.astype(jnp.int32).reshape(1), grad_norm_one, grad_attn, grad_mlp, small[:9], *weights, *firsts, *seconds)
    new_firsts, new_seconds, updates, sums = results[:3], results[3:6], results[6:9], results[9]
    new_w = pl.pallas_call(
        apply_kernel,
        in_specs=[vectors] * 11,
        out_specs=[vectors] * 6,
        out_shape=like(weights) + like([norm_w] * 3),
        compiler_params=pltpu.CompilerParams(vmem_limit_bytes=16 * MIB),
    )(sum_everywhere(sums, size), norm_two, norm_w, norm_m, norm_v, *weights, *updates)
    return (
        output, grad_tokens, new_w[0], new_firsts[0], new_seconds[0], new_w[1], new_firsts[1], new_seconds[1],
        new_w[2], new_firsts[2], new_seconds[2], *new_w[3:],
    )


def solution(mesh):
    rows, lines = P(("dp", "head"), None), P("dp", None)
    shards, columns = P(None, "dp", "head"), P(None, "head")
    in_specs = (rows, rows, lines, P("dp")) + (shards,) * 6 + (columns,) * 3 + (P(),) * 3
    out_specs = (rows, rows) + (shards,) * 6 + (columns,) * 3 + (P(),) * 3
    return jax.shard_map(
        functools.partial(body, mesh.shape["dp"]), mesh=mesh, in_specs=in_specs, out_specs=out_specs, check_vma=False
    )
```

```python
import functools
import jax
import jax.numpy as jnp
from jax import lax
from jax.experimental import pallas as pl
from jax.experimental.pallas import tpu as pltpu
from jax.sharding import PartitionSpec as P

HEAD_DIM = 64
GRID_W = 16
STEP = 10
IMAGES = 8

NORM_EPS = 1e-06
BETA_ONE = 0.9
BETA_TWO = 0.999
ADAM_EPS = 1e-06
DECAY = 0.01
RATE = 0.5
LOG2E = 1.4426950408889634
LN2 = 0.6931471805599453
BIG = 2.0**100
GELU_ONE = 0.7978845608028654
GELU_TWO = 0.044715
GELU_S = (GELU_ONE * GELU_TWO) ** (1.0 / 3.0)
GELU_A = GELU_ONE / GELU_S
ACT_SCALE = 0.5 / GELU_S
EXTRA = 32
PARTS = 4
TILE = 128
LANES = 128
STRIDE = GRID_W + 8
MIB = 1024 * 1024

f32 = jnp.float32
bf16 = jnp.bfloat16
NN = (((1,), (0,)), ((), ()))
NT = (((1,), (1,)), ((), ()))
TN = (((0,), (0,)), ((), ()))


def dot(left, right, dims=NN):
    return lax.dot_general(left, right, dims, preferred_element_type=f32)


def work_of(micros):
    return pl.CostEstimate(flops=micros * 1_000_000_000, bytes_accessed=micros * 1_000_000, transcendentals=0)


def widths_for(length):
    return [w for w in (256, 384, 512, 768) if w < length] + [length]


def norm_parts(values):
    average = jnp.mean(values, axis=-1, keepdims=True)
    centered = values - average
    inverse = lax.rsqrt(jnp.mean(centered * centered, axis=-1, keepdims=True) + NORM_EPS)
    return centered * inverse, inverse


def norm_back(upstream, gain_row, unit_rows, inverse):
    grad_unit = upstream * gain_row
    first_term = jnp.mean(grad_unit, axis=-1, keepdims=True)
    second_term = jnp.mean(grad_unit * unit_rows, axis=-1, keepdims=True)
    return inverse * (grad_unit - first_term - unit_rows * second_term)


def fold_rows(values):
    rows, columns = values.shape
    return jnp.sum(values.reshape(rows // 8, 8, columns), axis=0)


def pair_columns(flat):
    empty = jnp.zeros((HEAD_DIM, LANES), flat.dtype)
    return jnp.concatenate(
        [jnp.concatenate([flat[:HEAD_DIM], empty], axis=0), jnp.concatenate([empty, flat[HEAD_DIM:]], axis=0)], axis=1
    )


def pair_rows(both):
    return jnp.concatenate([both[:HEAD_DIM, :LANES], both[HEAD_DIM:, LANES:]], axis=0)


def fold_max(values):
    pieces = [values[at : at + 64] for at in range(0, values.shape[0], 64)]
    while len(pieces) > 1:
        pieces = [jnp.maximum(a, b) for a, b in zip(pieces[::2], pieces[1::2])] + ([pieces[-1]] if len(pieces) % 2 else [])
    top = pieces[0]
    top = jnp.maximum(top[:32], top[32:])
    top = jnp.maximum(top[:16], top[16:])
    return jnp.max(jnp.maximum(top[:8], top[8:]), axis=0, keepdims=True)


def three_parts(value, part):
    high = value.astype(bf16).astype(f32)
    rest = value - high
    middle = rest.astype(bf16).astype(f32)
    return jnp.where(part == 0, high, jnp.where(part == 1, middle, rest - middle))


def image_tags(image_ref, start, rows):
    place = start + lax.broadcasted_iota(jnp.int32, (rows, LANES), 0)
    inside = (place >= image_ref[0, 0:1, :]) & (place < image_ref[0, 1:2, :])
    return jnp.where(inside, 1.0, 0.0).astype(bf16)


def first_norm_kernel(tokens_ref, out_grad_ref, norm_ref, normed_ref, normed_t_ref, out_grad_t_ref):
    big = 256

    def step(at, carry):
        rows = pl.ds(pl.multiple_of(at * big, big), big)
        unit, _ = norm_parts(tokens_ref[rows, :].astype(f32))
        normed_ref[rows, :] = (unit * norm_ref[0:1, :] + norm_ref[1:2, :]).astype(bf16)
        return carry

    lax.fori_loop(0, tokens_ref.shape[0] // big, step, 0)
    normed_t_ref[...] = jnp.transpose(normed_ref[...])
    out_grad_t_ref[...] = jnp.transpose(out_grad_ref[...])


def first_norm(tokens, out_grad, norm_w, row_count):
    rows_all, width = tokens.shape
    length = rows_all // row_count
    by_row = pl.BlockSpec((length, width), lambda r: (r, 0))
    turned = pl.BlockSpec((width, length), lambda r: (r, 0))
    flipped = jax.ShapeDtypeStruct((row_count * width, length), bf16)
    return pl.pallas_call(
        first_norm_kernel,
        grid=(row_count,),
        in_specs=[by_row, by_row, pl.BlockSpec(norm_w.shape, lambda r: (0, 0))],
        out_specs=[by_row, turned, turned],
        out_shape=[jax.ShapeDtypeStruct((rows_all, width), bf16), flipped, flipped],
        cost_estimate=work_of(8),
        compiler_params=pltpu.CompilerParams(vmem_limit_bytes=60 * MIB),
    )(tokens, out_grad, norm_w)


def attn_forward_kernel(
    start_ref, class_ref, count_ref, tokens_ref, normed_ref, w_ref, image_ref,
    middle_ref, qkv_ref, context_ref, ext_ref,
    tag_ref, qt_ref, vt_ref,
):
    row = pl.program_id(0)
    length, width = tokens_ref.shape
    pairs = width // LANES
    tag_ref[...] = image_tags(image_ref, 0, length)
    queries = (dot(normed_ref[...], w_ref[0]) * (HEAD_DIM**-0.5 * LOG2E)).astype(bf16)
    qkv_ref[:, :width] = queries
    qt_ref[...] = jnp.transpose(queries)
    qkv_ref[:, width : 2 * width] = dot(normed_ref[...], w_ref[1]).astype(bf16)
    values = dot(normed_ref[...], w_ref[2]).astype(bf16)
    qkv_ref[:, 2 * width :] = values
    vt_ref[...] = jnp.transpose(values)

    def tile(step, carry):
        q0 = pl.multiple_of(step * TILE, TILE)
        here = pl.ds(q0, TILE)
        place = q0 + lax.broadcasted_iota(jnp.int32, (IMAGES, LANES), 1)
        inside = (place >= image_ref[0, 8 : 8 + IMAGES, :]) & (place < image_ref[0, 16 : 16 + IMAGES, :])
        mask = jnp.where(inside, 0.0, -BIG)
        mask_low = jnp.concatenate([mask, jnp.zeros((LANES - IMAGES, LANES), f32)], axis=0).astype(bf16)
        ext_rows = lax.broadcasted_iota(jnp.int32, (EXTRA - IMAGES, LANES), 0)

        def attend(window):
            there = pl.ds(pl.multiple_of(start_ref[row, step], LANES), window)
            tags = tag_ref[there, :]
            ones = jnp.ones((GRID_W, window), bf16)
            extra = jnp.zeros((EXTRA - IMAGES, LANES), f32)
            slices = [slice(p * LANES, (p + 1) * LANES) for p in range(pairs)]
            masks = jnp.concatenate([mask_low, mask_low], axis=1)
            scores, tops, exponents, mixes = [], [], [], []
            for p, at in enumerate(slices):
                keys = qkv_ref[there, width + p * LANES : width + (p + 1) * LANES]
                right = jnp.concatenate([pair_columns(qt_ref[at, here]), masks], axis=0)
                scores.append(dot(jnp.concatenate([keys, tags], axis=1), right))
            for p in range(pairs):
                tops.append(fold_max(scores[p]))
                exponents.append(jnp.exp2(scores[p] - tops[p]).astype(bf16))
            for p, at in enumerate(slices):
                mixes.append(dot(jnp.concatenate([vt_ref[at, there], ones], axis=0), exponents[p]))
            for p, at in enumerate(slices):
                mixed = mixes[p]
                total = mixed[LANES : LANES + 1, :]
                minus_lse = -(tops[p] + jnp.log(total) * LOG2E)
                scale = 1.0 / total
                lane = lax.broadcasted_iota(jnp.int32, (1, 2 * TILE), 1)
                head = 2 * p + jnp.where(lane < TILE, 0, 1)
                scale = jnp.where(head < count_ref[row], scale, 0.0)
                context_ref[here, at] = jnp.transpose(pair_rows(mixed[:LANES] * scale)).astype(bf16)
                for h in range(2):
                    value = minus_lse[:, h * TILE : (h + 1) * TILE]
                    first = 6 * p + 3 * h
                    extra = jnp.where(
                        (ext_rows >= first) & (ext_rows < first + 3), three_parts(value, ext_rows - first), extra
                    )
            ext_ref[:, here] = jnp.concatenate([mask, extra], axis=0).astype(bf16)

        for index, window in enumerate(widths_for(length)):
            pl.when(class_ref[row, step] == index)(functools.partial(attend, window))
        return carry

    lax.fori_loop(0, length // TILE, tile, 0)
    middle_ref[...] = tokens_ref[...].astype(f32) + dot(context_ref[...], w_ref[3], NT)


def attn_forward(starts, classes, counts, tokens, normed, attn_use, images):
    rows_all, width = tokens.shape
    row_count = counts.shape[0]
    length = rows_all // row_count
    by_row = lambda columns: pl.BlockSpec((length, columns), lambda r, *_: (r, 0))
    return pl.pallas_call(
        attn_forward_kernel,
        grid_spec=pltpu.PrefetchScalarGridSpec(
            num_scalar_prefetch=3,
            grid=(row_count,),
            in_specs=[
                by_row(width),
                by_row(width),
                pl.BlockSpec(attn_use.shape, lambda r, *_: (0, 0, 0)),
                pl.BlockSpec((1, 24, LANES), lambda r, *_: (r, 0, 0)),
            ],
            out_specs=[
                by_row(width), by_row(3 * width), by_row(width), pl.BlockSpec((EXTRA, length), lambda r, *_: (r, 0))
            ],
            scratch_shapes=[
                pltpu.VMEM((length, LANES), bf16),
                pltpu.VMEM((width, length), bf16),
                pltpu.VMEM((width, length), bf16),
            ],
        ),
        out_shape=[
            jax.ShapeDtypeStruct((rows_all, width), f32),
            jax.ShapeDtypeStruct((rows_all, 3 * width), bf16),
            jax.ShapeDtypeStruct((rows_all, width), bf16),
            jax.ShapeDtypeStruct((row_count * EXTRA, length), bf16),
        ],
        cost_estimate=work_of(30),
        compiler_params=pltpu.CompilerParams(vmem_limit_bytes=56 * MIB),
    )(starts, classes, counts, tokens, normed, attn_use, images)


def attn_backward_kernel(
    first, final, start_ref, class_ref, count_ref, rank_ref, normed_t_ref, middle_grad_ref, qkv_ref, context_ref, ext_ref, w_ref,
    image_ref, *refs,
):
    sums = None
    if first:
        sums, refs = refs[1], refs[2:]
    sent = None
    if final:
        proj_ref, keep_ref, send_ref, *scratch, w_grad_ref = refs
        sent = (keep_ref, send_ref)
    else:
        proj_ref, w_grad_ref, *scratch = refs
    attn_backward_row(
        first, sums, sent, start_ref, class_ref, count_ref, rank_ref, normed_t_ref, middle_grad_ref, qkv_ref, context_ref, ext_ref,
        w_ref, image_ref, proj_ref, w_grad_ref, *scratch,
    )


def attn_backward_row(
    first, sums, sent, start_ref, class_ref, count_ref, rank_ref, normed_t_ref, middle_grad_ref, qkv_ref, context_ref, ext_ref, w_ref,
    image_ref, proj_ref, w_grad_ref,
    tag_ref, up_ref, delta_ref, dq_ref, dk_ref, dv_ref, low_ref, qt_ref, kt_ref, upt_ref,
):
    step_at = pl.program_id(0)
    row = first + step_at
    length, width = middle_grad_ref.shape
    pairs = width // LANES
    big = 256

    @pl.when(step_at == 0)
    def _():
        w_grad_ref[...] = jnp.zeros_like(w_grad_ref) if sums is None else sums[...]

    target = lax.broadcasted_iota(jnp.int32, (EXTRA, width), 0) - IMAGES
    source = lax.broadcasted_iota(jnp.int32, (EXTRA, width), 1) // HEAD_DIM * 3
    collect = jnp.where((target >= source) & (target < source + 3), -1.0, 0.0).astype(bf16)
    active = jnp.where(
        lax.broadcasted_iota(jnp.int32, (1, width), 1) // HEAD_DIM < count_ref[row], 1.0, 0.0
    )

    def prepare(step, carry):
        rows = pl.ds(pl.multiple_of(step * big, big), big)
        tag_ref[rows, :] = image_tags(image_ref, step * big, big)
        low_ref[rows, :] = middle_grad_ref[rows, :].astype(bf16)
        dk_ref[rows, :] = jnp.zeros((big, width), f32)
        dv_ref[rows, :] = jnp.zeros((big, width), f32)
        return carry

    lax.fori_loop(0, length // big, prepare, 0)
    up = (dot(low_ref[...], w_ref[3]) * active).astype(bf16)
    up_ref[...] = up
    upt_ref[...] = jnp.transpose(up)
    qt_ref[...] = jnp.transpose(qkv_ref[:, :width])
    kt_ref[...] = jnp.transpose(qkv_ref[:, width : 2 * width])

    def gather(step, carry):
        rows = pl.ds(pl.multiple_of(step * big, big), big)
        product = up_ref[rows, :].astype(f32) * context_ref[rows, :].astype(f32)
        high = product.astype(bf16)
        rest = (product - high.astype(f32)).astype(bf16)
        delta = dot(collect, high, NT) + dot(collect, rest, NT)
        part = lax.rem(lax.broadcasted_iota(jnp.int32, (EXTRA, big), 0) + 3 * EXTRA - IMAGES, 3)
        delta_ref[:, rows] = three_parts(delta, part).astype(bf16)
        return carry

    lax.fori_loop(0, length // big, gather, 0)
    lane = lax.broadcasted_iota(jnp.int32, (1, LANES), 1)
    first_half = jnp.where(lane < HEAD_DIM, 1.0, 0.0).astype(bf16)
    second_half = jnp.where(lane >= HEAD_DIM, 1.0, 0.0).astype(bf16)

    def tile(step, carry):
        q0 = pl.multiple_of(step * TILE, TILE)
        here = pl.ds(q0, TILE)

        def attend(window):
            there = pl.ds(pl.multiple_of(start_ref[row, step], LANES), window)
            tags = tag_ref[there, :]
            ext = ext_ref[:, here]
            delta = delta_ref[:, here]
            at_row = lax.broadcasted_iota(jnp.int32, (EXTRA, LANES), 0)
            empty = jnp.zeros((LANES - EXTRA, 2 * TILE), bf16)

            def own(edge, masks):
                keep = (at_row >= edge) & (at_row < edge + 3)
                return jnp.where(keep | (at_row < IMAGES) if masks else keep, 1.0, 0.0).astype(bf16)

            slices = [slice(p * LANES, (p + 1) * LANES) for p in range(pairs)]
            scores, grad_probs, probs, grad_scores = [], [], [], []
            for p, at in enumerate(slices):
                keys = qkv_ref[there, width + p * LANES : width + (p + 1) * LANES]
                values = qkv_ref[there, 2 * width + p * LANES : 2 * width + (p + 1) * LANES]
                edge = IMAGES + 6 * p
                q_side = jnp.concatenate(
                    [
                        pair_columns(qt_ref[at, here]),
                        jnp.concatenate([ext * own(edge, True), ext * own(edge + 3, True)], axis=1),
                        empty,
                    ],
                    axis=0,
                )
                up_side = jnp.concatenate(
                    [
                        pair_columns(upt_ref[at, here]),
                        jnp.concatenate([delta * own(edge, False), delta * own(edge + 3, False)], axis=1),
                        empty,
                    ],
                    axis=0,
                )
                scores.append(dot(jnp.concatenate([keys, tags], axis=1), q_side))
                grad_probs.append(dot(jnp.concatenate([values, tags], axis=1), up_side))
            for p in range(pairs):
                weight = jnp.exp2(scores[p])
                probs.append(weight.astype(bf16))
                grad_scores.append((weight * grad_probs[p]).astype(bf16))
            for p, at in enumerate(slices):
                queries, ups = qkv_ref[here, at], up_ref[here, at]
                q_pair = jnp.concatenate([queries * first_half, queries * second_half], axis=0)
                up_pair = jnp.concatenate([ups * first_half, ups * second_half], axis=0)
                dv_ref[there, at] += dot(probs[p], up_pair)
                dk_ref[there, at] += dot(grad_scores[p], q_pair)
                dq = pair_rows(dot(kt_ref[at, there], grad_scores[p]))
                dq_ref[here, at] = jnp.transpose(dq * HEAD_DIM**-0.5).astype(bf16)

        for index, window in enumerate(widths_for(length)):
            pl.when(class_ref[row, step] == index)(functools.partial(attend, window))
        return carry

    lax.fori_loop(0, length // TILE, tile, 0)
    keys_grad = (dk_ref[...] * LN2).astype(bf16)
    values_grad = dv_ref[...].astype(bf16)
    proj_ref[...] = jnp.concatenate([dq_ref[...], keys_grad, values_grad], axis=1)
    for k in range(3):
        w_grad_ref[k] += dot(normed_t_ref[...], proj_ref[:, k * width : (k + 1) * width])
    w_grad_ref[3] += dot(jnp.transpose(low_ref[...]), context_ref[...])
    if sent:

        @pl.when(step_at == pl.num_programs(0) - 1)
        def _():
            for k in range(2):
                one, two = w_grad_ref[k], w_grad_ref[k + 2]
                halves = [jnp.concatenate([one[:, at : at + width // 2], two[:, at : at + width // 2]], axis=1) for at in (0, width // 2)]
                sent[0][k] = jnp.where(rank_ref[0] == 0, halves[0], halves[1])
                sent[1][k] = jnp.where(rank_ref[0] == 0, halves[1], halves[0]).astype(bf16)


def attn_backward(first, count, so_far, starts, classes, counts, rank, normed_t, middle_grad, qkv, context, ext, attn_use, images):
    rows_all, width = middle_grad.shape
    length = rows_all // counts.shape[0]
    by_row = lambda columns: pl.BlockSpec((length, columns), lambda r, *_: (first + r, 0))
    final = first + count == counts.shape[0]
    half = (2, width, width)
    halves = pl.BlockSpec(half, lambda r, *_: (0, 0, 0))
    whole = pl.BlockSpec(attn_use.shape, lambda r, *_: (0, 0, 0))
    return pl.pallas_call(
        functools.partial(attn_backward_kernel, first, final),
        grid_spec=pltpu.PrefetchScalarGridSpec(
            num_scalar_prefetch=4,
            grid=(count,),
            in_specs=[
                pl.BlockSpec((width, length), lambda r, *_: (first + r, 0)),
                by_row(width),
                by_row(3 * width),
                by_row(width),
                pl.BlockSpec((EXTRA, length), lambda r, *_: (first + r, 0)),
                whole,
                pl.BlockSpec((1, 24, LANES), lambda r, *_: (first + r, 0, 0)),
            ]
            + ([pl.BlockSpec(memory_space=pl.ANY), whole] if first else []),
            out_specs=[by_row(3 * width)] + ([halves, halves] if final else [whole]),
            scratch_shapes=[
                pltpu.VMEM((length, LANES), bf16),
                pltpu.VMEM((length, width), bf16),
                pltpu.VMEM((EXTRA, length), bf16),
                pltpu.VMEM((length, width), bf16),
                pltpu.VMEM((length, width), f32),
                pltpu.VMEM((length, width), f32),
                pltpu.VMEM((length, width), bf16),
                pltpu.VMEM((width, length), bf16),
                pltpu.VMEM((width, length), bf16),
                pltpu.VMEM((width, length), bf16),
            ]
            + ([pltpu.VMEM(attn_use.shape, f32)] if final else []),
        ),
        out_shape=[jax.ShapeDtypeStruct((rows_all, 3 * width), bf16)]
        + (
            [jax.ShapeDtypeStruct(half, f32), jax.ShapeDtypeStruct(half, bf16)]
            if final
            else [jax.ShapeDtypeStruct(attn_use.shape, f32)]
        ),
        input_output_aliases={11: 0} if first else {},
        cost_estimate=work_of(18 * count),
        compiler_params=pltpu.CompilerParams(vmem_limit_bytes=40 * MIB),
    )(starts, classes, counts, rank, normed_t, middle_grad, qkv, context, ext, attn_use, images, *(so_far or ()))


def tokens_back_kernel(proj_ref, tokens_ref, middle_grad_ref, w_ref, norm_ref, tokens_grad_ref, norm_grad_ref, upstream_ref):
    length, width = tokens_ref.shape
    big = 256

    @pl.when(pl.program_id(0) == 0)
    def _():
        norm_grad_ref[...] = jnp.zeros_like(norm_grad_ref)

    w_cat = jnp.concatenate([w_ref[0], w_ref[1], w_ref[2]], axis=1)
    upstream_ref[...] = dot(proj_ref[...], w_cat, NT)

    def finish(step, carry):
        rows = pl.ds(pl.multiple_of(step * big, big), big)
        upstream = upstream_ref[rows, :]
        unit, inverse = norm_parts(tokens_ref[rows, :].astype(f32))
        tokens_grad_ref[rows, :] = middle_grad_ref[rows, :] + norm_back(upstream, norm_ref[0:1, :], unit, inverse)
        norm_grad_ref[0:8, :] += fold_rows(upstream * unit)
        norm_grad_ref[8:16, :] += fold_rows(upstream)
        return carry

    lax.fori_loop(0, length // big, finish, 0)


def tokens_back(proj, tokens, middle_grad, attn_use, norm_w, row_count):
    rows_all, width = tokens.shape
    length = rows_all // row_count
    by_row = lambda columns: pl.BlockSpec((length, columns), lambda r: (r, 0))
    return pl.pallas_call(
        tokens_back_kernel,
        grid=(row_count,),
        in_specs=[
            by_row(3 * width),
            by_row(width),
            by_row(width),
            pl.BlockSpec(attn_use.shape, lambda r: (0, 0, 0)),
            pl.BlockSpec(norm_w.shape, lambda r: (0, 0)),
        ],
        out_specs=[by_row(width), pl.BlockSpec((16, width), lambda r: (0, 0))],
        out_shape=[jax.ShapeDtypeStruct((rows_all, width), f32), jax.ShapeDtypeStruct((16, width), f32)],
        scratch_shapes=[pltpu.VMEM((length, width), f32)],
        cost_estimate=work_of(9),
        compiler_params=pltpu.CompilerParams(vmem_limit_bytes=60 * MIB),
    )(proj, tokens, middle_grad, attn_use, norm_w)


def mlp_kernel(
    place_ref, rank_ref, middle_ref, out_grad_ref, out_grad_t_ref, own_w_ref, other_w_ref, taps_ref, norm_ref,
    output_ref, middle_grad_ref, keep_ref, send_ref, taps_grad_ref, norm_grad_ref,
    w_ref, w_grad_ref, normed_ref, normed_t_ref, out_sum_ref, up_sum_ref, tap_sum_ref,
    act_grads_ref, acts_ref, hidden_grads_ref, *buffers,
):
    row = pl.program_id(0)
    length, width = middle_ref.shape
    hidden = w_ref.shape[2]
    chunk = PARTS * LANES
    big = 256
    grid_rows = length // GRID_W
    chunks = hidden // chunk
    h_refs, g_refs = buffers[:PARTS], buffers[PARTS:]
    gain, bias = norm_ref[2:3, :], norm_ref[3:4, :]

    @pl.when(row == 0)
    def _():
        w_grad_ref[...] = jnp.zeros_like(w_grad_ref)
        norm_grad_ref[...] = jnp.zeros_like(norm_grad_ref)
        tap_sum_ref[...] = jnp.zeros_like(tap_sum_ref)
        for rank, halves in enumerate(((own_w_ref, other_w_ref), (other_w_ref, own_w_ref))):

            @pl.when(rank_ref[0] == rank)
            def _():
                w_ref[:, :, : hidden // 2] = halves[0][...]
                w_ref[:, :, hidden // 2 :] = halves[1][...]

        for ref in buffers:
            ref[...] = jnp.zeros_like(ref)

    def place(r):
        return pl.multiple_of(place_ref[row, r], 8)

    for n in range(IMAGES + 1):
        at = place(grid_rows + n)
        for ref in buffers:
            ref[pl.ds(at, GRID_W), :] = jnp.zeros((GRID_W, LANES), f32)

    def normalize(step, carry):
        rows = pl.ds(pl.multiple_of(step * big, big), big)
        middle = middle_ref[rows, :]
        unit, _ = norm_parts(middle)
        normed_ref[rows, :] = (unit * gain + bias).astype(bf16)
        out_sum_ref[rows, :] = jnp.zeros((big, width), f32)
        up_sum_ref[rows, :] = jnp.zeros((big, width), f32)
        return carry

    lax.fori_loop(0, length // big, normalize, 0)
    normed_t_ref[...] = jnp.transpose(normed_ref[...])

    def lanes_of(c):
        return pl.ds(pl.multiple_of(c * chunk, chunk), chunk)

    def lanes_of(c):
        return pl.ds(pl.multiple_of(c * chunk, chunk), chunk)

    def neighbours(ref, at):
        return [ref[pl.ds(at + (a * STRIDE + b), GRID_W), :] for a in (-1, 0, 1) for b in (-1, 0, 1)]

    def tall(values):
        return jnp.concatenate([values, values], axis=0)

    def total_of(terms):
        while len(terms) > 1:
            terms = [a + b for a, b in zip(terms[::2], terms[1::2])] + ([terms[-1]] if len(terms) % 2 else [])
        return terms[0]

    def taps_for(c, part, at):
        lane = pl.ds(pl.multiple_of(c * chunk + part * LANES, LANES), LANES)
        return [tall(taps_ref[at + k * 8 : at + (k + 1) * 8, lane]) for k in range(9)]

    lines = 8

    def do_chunk(c, carry):
        lanes = lanes_of(c)
        for t in range(length // big):
            rows = slice(t * big, (t + 1) * big)
            values = dot(normed_ref[rows, :], w_ref[0, :, lanes])
            for part in range(PARTS):
                for s in range(big // GRID_W):
                    at = place(t * (big // GRID_W) + s)
                    h_refs[part][pl.ds(at, GRID_W), :] = values[
                        s * GRID_W : (s + 1) * GRID_W, part * LANES : (part + 1) * LANES
                    ]
        act_grads_ref[...] = dot(out_grad_ref[...], w_ref[1, :, lanes])

        def forward(t, carry):
            tokens_base = pl.multiple_of(t * (lines * GRID_W), lines * GRID_W)
            for part in range(PARTS):
                taps = taps_for(c, part, 0)
                cols = slice(part * LANES, (part + 1) * LANES)
                for s in range(lines):
                    near = pl.ds(pl.multiple_of(tokens_base + s * GRID_W, GRID_W), GRID_W)
                    at = place(t * lines + s)
                    x = total_of([x * tap for x, tap in zip(neighbours(h_refs[part], at), taps)])
                    square = x * x
                    value = jnp.tanh(x * (GELU_A + square))
                    gate = 1.0 + value
                    twice = x * gate
                    acts_ref[near, cols] = twice.astype(bf16)
                    slope = gate + (twice * (1.0 - value)) * (GELU_A + 3.0 * square)
                    g_refs[part][pl.ds(at, GRID_W), :] = act_grads_ref[near, cols] * slope
            return carry

        lax.fori_loop(0, grid_rows // lines, forward, 0)

        def backward(t, carry):
            tokens_base = pl.multiple_of(t * (lines * GRID_W), lines * GRID_W)
            for part in range(PARTS):
                taps = taps_for(c, part, 72)
                lane = pl.ds(pl.multiple_of(c * chunk + part * LANES, LANES), LANES)
                cols = slice(part * LANES, (part + 1) * LANES)
                totals = [None] * 9
                for s in range(lines):
                    near = pl.ds(pl.multiple_of(tokens_base + s * GRID_W, GRID_W), GRID_W)
                    at = place(t * lines + s)
                    source = h_refs[part][pl.ds(at, GRID_W), :]
                    moved = neighbours(g_refs[part], at)[::-1]
                    for k in range(9):
                        product = source * moved[k]
                        folded = product[:8] + product[8:]
                        totals[k] = folded if totals[k] is None else totals[k] + folded
                    terms = [x * tap for x, tap in zip(moved, taps)]
                    hidden_grads_ref[near, cols] = total_of(terms).astype(bf16)
                for k in range(9):
                    tap_sum_ref[k * 8 : (k + 1) * 8, lane] += totals[k]
            return carry

        lax.fori_loop(0, grid_rows // lines, backward, 0)
        w_grad_ref[0, :, lanes] += dot(normed_t_ref[...], hidden_grads_ref[...])
        w_grad_ref[1, :, lanes] += dot(out_grad_t_ref[...], acts_ref[...])
        out_sum_ref[...] += dot(acts_ref[...], w_ref[1, :, lanes], NT)
        up_sum_ref[...] += dot(hidden_grads_ref[...], w_ref[0, :, lanes], NT)
        return carry

    lax.fori_loop(0, chunks, do_chunk, 0)

    def finish(step, carry):
        rows = pl.ds(pl.multiple_of(step * big, big), big)
        middle = middle_ref[rows, :]
        output_ref[rows, :] = (middle + ACT_SCALE * out_sum_ref[rows, :]).astype(bf16)
        upstream = 0.5 * up_sum_ref[rows, :]
        unit, inverse = norm_parts(middle)
        middle_grad_ref[rows, :] = out_grad_ref[rows, :].astype(f32) + norm_back(upstream, gain, unit, inverse)
        norm_grad_ref[0:8, :] += fold_rows(upstream * unit)
        norm_grad_ref[8:16, :] += fold_rows(upstream)
        return carry

    lax.fori_loop(0, length // big, finish, 0)

    @pl.when(row == pl.num_programs(0) - 1)
    def _():
        for k, scale in enumerate((0.5, ACT_SCALE)):
            halves = w_grad_ref[k, :, : hidden // 2], w_grad_ref[k, :, hidden // 2 :]
            keep_ref[k] = scale * jnp.where(rank_ref[0] == 0, halves[0], halves[1])
            send_ref[k] = (scale * jnp.where(rank_ref[0] == 0, halves[1], halves[0])).astype(bf16)
        taps_grad_ref[...] = jnp.zeros_like(taps_grad_ref)
        for k in range(9):
            total = jnp.sum(tap_sum_ref[k * 8 : (k + 1) * 8, :], axis=0, keepdims=True)
            taps_grad_ref[k : k + 1, :] = 0.5 * total


def mlp_layer(places, rank, middle, out_grad, out_grad_t, own_w, other_w, taps, norm_w):
    rows_all, width = middle.shape
    row_count = places.shape[0]
    length = rows_all // row_count
    half = own_w.shape
    hidden = 2 * half[2]
    whole = half[:2] + (hidden,)
    by_row = lambda columns: pl.BlockSpec((length, columns), lambda r, *_: (r, 0))
    slots = (length // GRID_W + IMAGES + 2) * STRIDE
    return pl.pallas_call(
        mlp_kernel,
        grid_spec=pltpu.PrefetchScalarGridSpec(
            num_scalar_prefetch=2,
            grid=(row_count,),
            in_specs=[
                by_row(width),
                by_row(width),
                pl.BlockSpec((width, length), lambda r, *_: (r, 0)),
                pl.BlockSpec(half, lambda r, *_: (0, 0, 0)),
                pl.BlockSpec(half, lambda r, *_: (0, 0, 0)),
                pl.BlockSpec(taps.shape, lambda r, *_: (0, 0)),
                pl.BlockSpec(norm_w.shape, lambda r, *_: (0, 0)),
            ],
            out_specs=[
                by_row(width),
                by_row(width),
                pl.BlockSpec(half, lambda r, *_: (0, 0, 0)),
                pl.BlockSpec(half, lambda r, *_: (0, 0, 0)),
                pl.BlockSpec((16, hidden), lambda r, *_: (0, 0)),
                pl.BlockSpec((16, width), lambda r, *_: (0, 0)),
            ],
            scratch_shapes=[
                pltpu.VMEM(whole, bf16),
                pltpu.VMEM(whole, f32),
                pltpu.VMEM((length, width), bf16),
                pltpu.VMEM((width, length), bf16),
                pltpu.VMEM((length, width), f32),
                pltpu.VMEM((length, width), f32),
                pltpu.VMEM((9 * 8, hidden), f32),
                pltpu.VMEM((length, PARTS * LANES), f32),
                pltpu.VMEM((length, PARTS * LANES), bf16),
                pltpu.VMEM((length, PARTS * LANES), bf16),
            ]
            + [pltpu.VMEM((slots, LANES), f32)] * (2 * PARTS),
        ),
        out_shape=[
            jax.ShapeDtypeStruct((rows_all, width), bf16),
            jax.ShapeDtypeStruct((rows_all, width), f32),
            jax.ShapeDtypeStruct(half, f32),
            jax.ShapeDtypeStruct(half, bf16),
            jax.ShapeDtypeStruct((16, hidden), f32),
            jax.ShapeDtypeStruct((16, width), f32),
        ],
        cost_estimate=work_of(90),
        compiler_params=pltpu.CompilerParams(vmem_limit_bytes=50 * MIB),
    )(places, rank, middle, out_grad, out_grad_t, own_w, other_w, taps, norm_w)


def attention_plan(segments):
    row_count, length = segments.shape
    tiles = segments.reshape(row_count, length // TILE, TILE)
    first, last = tiles[:, :, 0], tiles[:, :, -1]
    ids = jnp.arange(IMAGES, dtype=jnp.int32)
    begins = jnp.sum((segments[:, None, :] < ids[None, :, None]).astype(jnp.int32), axis=-1)
    ends = jnp.sum((segments[:, None, :] <= ids[None, :, None]).astype(jnp.int32), axis=-1)
    low_end = jnp.sum(jnp.where(first[:, :, None] == ids, begins[:, None, :], 0), axis=-1) // LANES * LANES
    high_end = jnp.sum(jnp.where(last[:, :, None] == ids, ends[:, None, :], 0), axis=-1)
    widths = widths_for(length)
    classes = sum(((high_end - low_end) > w).astype(jnp.int32) for w in widths[:-1])
    chosen = jnp.full_like(classes, widths[-1])
    for index, w in enumerate(widths):
        chosen = jnp.where(classes == index, w, chosen)
    starts = jnp.minimum(low_end, length - chosen)
    used = jnp.zeros((row_count, EXTRA - IMAGES), jnp.int32)
    unused = jnp.zeros((row_count, LANES - EXTRA), jnp.int32)
    first_lane = jnp.concatenate([begins, used, unused], axis=1)
    end_lane = jnp.concatenate([ends, used + length, unused], axis=1)
    by_lane = jnp.pad(jnp.stack([first_lane, end_lane], axis=1), ((0, 0), (0, 6), (0, 0)))
    by_image = jnp.broadcast_to(jnp.concatenate([begins, ends], axis=1)[:, :, None], (row_count, 2 * IMAGES, LANES))
    return starts, classes, jnp.concatenate([by_lane, by_image], axis=1)


def spread_taps(conv_use):
    taps = conv_use.astype(f32)
    own = (jnp.arange(9) == 4).astype(f32)[:, None]
    taps = jnp.repeat(taps + own, 8, axis=0)
    return jnp.concatenate([taps * GELU_S, taps], axis=0)


def line_places(segments):
    ids = segments[:, ::GRID_W]
    count = ids.shape[1]
    rows = jnp.arange(count, dtype=jnp.int32) + ids + 1
    images = jnp.arange(IMAGES, dtype=jnp.int32)
    first = jnp.sum((ids[:, None, :] < images[None, :, None]).astype(jnp.int32), axis=-1)
    gaps = jnp.concatenate([first + images, jnp.full((ids.shape[0], 1), count + IMAGES, jnp.int32)], axis=1)
    return jnp.concatenate([rows, gaps], axis=1) * STRIDE + 8


def bits_of(size):
    bits = []
    b = 1
    while b < size:
        bits.append(b)
        b *= 2
    return bits


def groups_of(size):
    bits = bits_of(size)
    return [(bits[at], 1 << len(bits[at : at + 2])) for at in range(0, len(bits), 2)]


def swap(values, axis, size, bit):
    return lax.ppermute(values, axis, [(i, i ^ bit) for i in range(size)])


def in_order(found, mine):
    ordered = []
    for target in range(len(found)):
        value = found[0]
        for step in range(1, len(found)):
            value = jnp.where((mine ^ step) == target, found[step], value)
        ordered.append(value)
    return ordered


def start_group(held, size, low, count):
    return [held] + [swap(held, "dp", size, step * low) for step in range(1, count)]


def finish_stack(found, low, count):
    held = jnp.stack(in_order(found, (lax.axis_index("dp") // low) % count), axis=1)
    return held.reshape((-1,) + held.shape[2:])


def finish_group(found, low, count):
    held = jnp.stack(in_order(found, (lax.axis_index("dp") // low) % count))
    return held.reshape((-1,) + held.shape[2:])


def fold_pairs(values):
    count = values.shape[0] // 2
    return jnp.concatenate([values[:count], values[count:]], axis=-1)


def unfold_pairs(values):
    half = values.shape[-1] // 2
    return jnp.concatenate([values[..., :half], values[..., half:]], axis=0)


def join_columns(mine, other, rank):
    first = jnp.where(rank == 0, mine, other)
    second = jnp.where(rank == 0, other, mine)
    return jnp.concatenate([first, second], axis=-1)


def join_weights(mine, other, rank, count):
    lines, _, part, columns = mine.shape
    half = columns // 2
    full = [join_columns(mine[..., at : at + half], other[..., at : at + half], rank) for at in (0, half)]
    return jnp.moveaxis(jnp.concatenate(full, axis=1), 0, 1).reshape(count, lines * part, columns)


def half_columns(values, side):
    half = values.shape[-1] // 2
    return lax.dynamic_slice_in_dim(values, side * half, half, axis=values.ndim - 1)


def by_line(values, size):
    count, rows, columns = values.shape
    return values.reshape(count, size, rows // size, columns)


def two_parts(values):
    high = values.astype(bf16)
    return jnp.concatenate([high, (values - high.astype(f32)).astype(bf16)], axis=0)


def from_parts(parts):
    count = parts.shape[0] // 2
    return parts[:count].astype(f32) + parts[count:].astype(f32)


def pieces_of(held, low, count):
    n, lines = held.shape[:2]
    split = held.reshape((n, lines // count, count) + held.shape[2:])
    mine = (lax.axis_index("dp") // low) % count
    return [lax.dynamic_index_in_dim(split, mine ^ step, 2, keepdims=False) for step in range(count)]


def flat(values):
    return values.astype(bf16).reshape(-1, values.shape[-1])


def sum_everywhere(values, size):
    values = values + swap(values, "head", 2, 1)
    for bit in bits_of(size):
        values = values + swap(values, "dp", size, bit)
    return values


def after(first, second):
    return lax.optimization_barrier((first, second))


def adam_terms(grad_sum, first_old, second):
    first_new = BETA_ONE * first_old + (1.0 - BETA_ONE) * grad_sum
    second_new = BETA_TWO * second + (1.0 - BETA_TWO) * grad_sum * grad_sum
    direction = (
        first_new
        / (1.0 - BETA_ONE**STEP)
        / (jnp.sqrt(second_new / (1.0 - BETA_TWO**STEP)) + ADAM_EPS)
    )
    return (first_new, second_new, direction)


def moments_kernel(line_ref, norm_ref, *refs):
    count = 3
    grads, weights, firsts, seconds = (refs[n * count : (n + 1) * count] for n in range(4))
    new_firsts, new_seconds, updates = (refs[(4 + n) * count : (5 + n) * count] for n in range(3))
    sums_ref = refs[7 * count]
    width = sums_ref.shape[1]
    lane = lax.broadcasted_iota(jnp.int32, (1, width), 1)
    rows = [jnp.zeros((1, width), f32), jnp.zeros((1, width), f32)]
    at = 0
    for n in range(count):
        grad, weight = grads[n][...], weights[n][...]
        new_first, new_second, direction = adam_terms(grad, firsts[n][...], seconds[n][...])
        update = direction + DECAY * weight
        new_firsts[n][...], new_seconds[n][...], updates[n][...] = new_first, new_second, update
        matrices = weight.shape[0] if weight.ndim == 3 else 1
        for k in range(matrices):
            for row, values in enumerate((weight, update)):
                values = values[k] if weight.ndim == 3 else values
                total = jnp.sum(jnp.sum(values * values, axis=0, keepdims=True), axis=1, keepdims=True)
                if weight.ndim == 2:
                    total = jnp.where(line_ref[0] == 0, total, 0.0)
                rows[row] = jnp.where(lane == at, total, rows[row])
            at += 1
    gain = jnp.sum(norm_ref[0:8, :], axis=0, keepdims=True)
    bias = jnp.sum(norm_ref[8:16, :], axis=0, keepdims=True)
    sums_ref[...] = jnp.concatenate(rows + [gain, bias, jnp.zeros((4, width), f32)], axis=0)


def apply_kernel(sums_ref, norm_two_ref, norm_w_ref, norm_m_ref, norm_v_ref, *refs):
    count = 3
    weights, updates, news = (refs[n * count : (n + 1) * count] for n in range(3))
    new_norm_w_ref, new_norm_m_ref, new_norm_v_ref = refs[3 * count :]
    ratio = jnp.sqrt(sums_ref[0:1, :]) / jnp.sqrt(sums_ref[1:2, :])
    at = 0
    for n in range(count):
        shape = weights[n].shape
        if len(shape) == 3:
            for k in range(shape[0]):
                news[n][k] = weights[n][k] - RATE * ratio[:, at : at + 1] * updates[n][k]
                at += 1
        else:
            news[n][...] = weights[n][...] - RATE * ratio[:, at : at + 1] * updates[n][...]
            at += 1
    grads = jnp.concatenate([sums_ref[2:4, :], norm_two_ref[...]], axis=0)
    new_first, new_second, direction = adam_terms(grads, norm_m_ref[...], norm_v_ref[...])
    new_norm_m_ref[...], new_norm_v_ref[...] = new_first, new_second
    new_norm_w_ref[...] = norm_w_ref[...] - RATE * direction


def like(values):
    return [jax.ShapeDtypeStruct(v.shape, f32) for v in values]


def body(
    size,
    tokens, grad_out, segments, counts,
    attn_w, attn_m, attn_v, mlp_w, mlp_m, mlp_v, conv_w, conv_m, conv_v, norm_w, norm_m, norm_v,
):
    rank = lax.axis_index("head")
    place = lax.axis_index("dp")
    own_rows = segments.shape[0] // 2
    segments = lax.dynamic_slice_in_dim(segments, rank * own_rows, own_rows, axis=0)
    counts = lax.dynamic_slice_in_dim(counts, rank * own_rows, own_rows, axis=0)
    width = norm_w.shape[1]
    groups = groups_of(size)
    attn_lines = fold_pairs(attn_w.astype(bf16))[None]
    mlp_lines = mlp_w.astype(bf16)[None]
    for near, far in zip(groups[:-1], groups[:0:-1]):
        found, more = start_group(attn_lines, size, *far), start_group(mlp_lines, size, *near)
        attn_lines, mlp_lines = finish_stack(found, *far), finish_group(more, *near)
    attn_lines, early = after(attn_lines, (tokens, grad_out))
    found = start_group(attn_lines, size, *groups[0])
    (normed, normed_t, out_grad_t), found = after(first_norm(*early, norm_w, own_rows), found)
    attn_lines = finish_stack(found, *groups[0])
    attn_use = join_weights(attn_lines, swap(attn_lines, "head", 2, 1), rank, attn_w.shape[0])
    found = start_group(mlp_lines, size, *groups[-1])
    conv_low = conv_w.astype(bf16)
    conv_use = join_columns(conv_low, swap(conv_low, "head", 2, 1), rank)
    starts, classes, images = attention_plan(segments)
    middle, qkv, context, ext = attn_forward(starts, classes, counts, tokens, normed, attn_use, images)
    middle, found = after(middle, found)
    mlp_lines = finish_group(found, *groups[-1])
    mlp_lines = jnp.moveaxis(mlp_lines, 0, 1).reshape(mlp_w.shape[0], -1, mlp_w.shape[2])
    rank_at = rank.astype(jnp.int32).reshape(1)
    output, grad_middle, held, send, grad_conv, grad_norm_two = mlp_layer(
        line_places(segments), rank_at, middle, grad_out, out_grad_t, mlp_lines, swap(mlp_lines, "head", 2, 1),
        spread_taps(conv_use), norm_w,
    )

    def back(first, count, so_far):
        return attn_backward(
            first, count, so_far, starts, classes, counts, rank_at, normed_t, grad_middle, qkv, context, ext, attn_use, images
        )

    columns = conv_w.shape[1]
    norm_two = jnp.sum(grad_norm_two.reshape(2, 8, width), axis=1).reshape(1, 2 * width)
    norm_two = jnp.pad(norm_two, ((0, 0), (0, columns - 2 * width)))
    taps = grad_conv[:9]
    small = jnp.concatenate([half_columns(taps, rank), norm_two])
    small_send = jnp.concatenate([half_columns(taps, 1 - rank), norm_two])
    got = swap(jnp.concatenate([flat(send), two_parts(small_send)], axis=0), "head", 2, 1)
    first_rows = max(1, own_rows // 3)
    so_far, got = after(back(0, first_rows, None), got)
    rows = held.size // columns
    held = by_line(held + got[:rows].reshape(held.shape).astype(f32), size)
    small = from_parts(two_parts(small)) + from_parts(got[rows:])
    low, count = groups[0]
    pieces = pieces_of(held, low, count)
    small_parts = two_parts(small)
    gots = [
        swap(jnp.concatenate([flat(pieces[step]), small_parts], axis=0), "dp", size, step * low) for step in range(1, count)
    ]
    so_far, pieces = after(so_far, pieces)
    projected_grad, attn_held, attn_send = back(first_rows, own_rows - first_rows, so_far)

    def take(pieces, gots, small_parts, low, count):
        keep = pieces[0]
        rows = keep.size // keep.shape[-1]
        for got in gots:
            keep = keep + got[:rows].reshape(keep.shape).astype(f32)
        ordered = in_order([small_parts] + [got[rows:] for got in gots], (place // low) % count)
        return keep, sum(from_parts(part) for part in ordered)

    attn_got = swap(flat(attn_send), "head", 2, 1)
    attn_held, gots = after(attn_held, gots)
    held, small = take(pieces, gots, small_parts, low, count)
    rest = bits_of(size)[2:]
    attn_held = by_line(attn_held + attn_got.reshape(attn_held.shape).astype(f32), size)
    waiting = list(groups)
    while waiting or rest:
        attn_pieces, pieces, extra = [None], None, None
        if waiting:
            low, count = waiting.pop(0)
            attn_pieces = pieces_of(attn_held, low, count)
        sent = {step * low: [flat(attn_pieces[step])] for step in range(1, len(attn_pieces))}
        bit = None
        if rest:
            bit = rest.pop(0)
            pieces = pieces_of(held, bit, 2)
            small_parts = two_parts(small)
            extra = jnp.concatenate([flat(pieces[1]), small_parts], axis=0).reshape(-1, attn_held.shape[-1])
            sent.setdefault(bit, []).append(extra)
        first_time = attn_pieces[0] is not None and low == groups[0][0]
        if first_time:
            sent, projected_grad = after(sent, projected_grad)
        gots = {step: swap(jnp.concatenate(parts, axis=0), "dp", size, step) for step, parts in sent.items()}
        if first_time:
            results = tokens_back(projected_grad, tokens, grad_middle, attn_use, norm_w, own_rows)
            (grad_tokens, grad_norm_one), gots = after(results, gots)
        if bit:
            got = gots[bit][gots[bit].shape[0] - extra.shape[0] :].reshape(-1, columns)
            held, small = take(pieces, [got], small_parts, bit, 2)
        if attn_pieces[0] is not None:
            attn_held = attn_pieces[0]
            rows = attn_held.size // attn_held.shape[-1]
            for step in range(1, len(attn_pieces)):
                attn_held = attn_held + gots[step * low][:rows].reshape(attn_held.shape).astype(f32)
    grad_attn = unfold_pairs(attn_held.reshape(attn_held.shape[:1] + attn_held.shape[2:]))
    grad_mlp = held.reshape(mlp_w.shape)
    norm_two = small[9, : 2 * width].reshape(2, width)

    weights, firsts, seconds = [attn_w, mlp_w, conv_w], [attn_m, mlp_m, conv_m], [attn_v, mlp_v, conv_v]
    scalars = pl.BlockSpec(memory_space=pltpu.SMEM)
    vectors = pl.BlockSpec(memory_space=pltpu.VMEM)
    results = pl.pallas_call(
        moments_kernel,
        in_specs=[scalars] + [vectors] * 13,
        out_specs=[vectors] * 10,
        out_shape=like(weights) * 3 + [jax.ShapeDtypeStruct((8, width), f32)],
        compiler_params=pltpu.CompilerParams(vmem_limit_bytes=16 * MIB),
    )(place.astype(jnp.int32).reshape(1), grad_norm_one, grad_attn, grad_mlp, small[:9], *weights, *firsts, *seconds)
    new_firsts, new_seconds, updates, sums = results[:3], results[3:6], results[6:9], results[9]
    new_w = pl.pallas_call(
        apply_kernel,
        in_specs=[vectors] * 11,
        out_specs=[vectors] * 6,
        out_shape=like(weights) + like([norm_w] * 3),
        compiler_params=pltpu.CompilerParams(vmem_limit_bytes=16 * MIB),
    )(sum_everywhere(sums, size), norm_two, norm_w, norm_m, norm_v, *weights, *updates)
    return (
        output, grad_tokens, new_w[0], new_firsts[0], new_seconds[0], new_w[1], new_firsts[1], new_seconds[1],
        new_w[2], new_firsts[2], new_seconds[2], *new_w[3:],
    )


def solution(mesh):
    rows, lines = P(("dp", "head"), None), P("dp", None)
    shards, columns = P(None, "dp", "head"), P(None, "head")
    in_specs = (rows, rows, lines, P("dp")) + (shards,) * 6 + (columns,) * 3 + (P(),) * 3
    out_specs = (rows, rows) + (shards,) * 6 + (columns,) * 3 + (P(),) * 3
    return jax.shard_map(
        functools.partial(body, mesh.shape["dp"]), mesh=mesh, in_specs=in_specs, out_specs=out_specs, check_vma=False
    )
```

```python
import functools
import jax
import jax.numpy as jnp
from jax import lax
from jax.experimental import pallas as pl
from jax.experimental.pallas import tpu as pltpu
from jax.sharding import PartitionSpec as P

HEAD_DIM = 64
GRID_W = 16
STEP = 10
IMAGES = 8

NORM_EPS = 1e-06
BETA_ONE = 0.9
BETA_TWO = 0.999
ADAM_EPS = 1e-06
DECAY = 0.01
RATE = 0.5
LOG2E = 1.4426950408889634
LN2 = 0.6931471805599453
BIG = 2.0**100
GELU_ONE = 0.7978845608028654
GELU_TWO = 0.044715
GELU_S = (GELU_ONE * GELU_TWO) ** (1.0 / 3.0)
GELU_A = GELU_ONE / GELU_S
ACT_SCALE = 0.5 / GELU_S
EXTRA = 32
PARTS = 4
TILE = 128
WIDE_TILE = 256
FILL = 512
LANES = 128
STRIDE = GRID_W + 8
MIB = 1024 * 1024

f32 = jnp.float32
bf16 = jnp.bfloat16
NN = (((1,), (0,)), ((), ()))
NT = (((1,), (1,)), ((), ()))
TN = (((0,), (0,)), ((), ()))


def dot(left, right, dims=NN):
    return lax.dot_general(left, right, dims, preferred_element_type=f32)


def work_of(micros):
    return pl.CostEstimate(flops=micros * 1_000_000_000, bytes_accessed=micros * 1_000_000, transcendentals=0)


def widths_for(length):
    return [w for w in (256, 384, 512, 768) if w < length] + [length]


def norm_parts(values):
    average = jnp.mean(values, axis=-1, keepdims=True)
    centered = values - average
    inverse = lax.rsqrt(jnp.mean(centered * centered, axis=-1, keepdims=True) + NORM_EPS)
    return centered * inverse, inverse


def norm_back(upstream, gain_row, unit_rows, inverse):
    grad_unit = upstream * gain_row
    first_term = jnp.mean(grad_unit, axis=-1, keepdims=True)
    second_term = jnp.mean(grad_unit * unit_rows, axis=-1, keepdims=True)
    return inverse * (grad_unit - first_term - unit_rows * second_term)


def fold_rows(values):
    rows, columns = values.shape
    return jnp.sum(values.reshape(rows // 8, 8, columns), axis=0)


def pair_columns(flat):
    empty = jnp.zeros((HEAD_DIM, flat.shape[1]), flat.dtype)
    return jnp.concatenate(
        [jnp.concatenate([flat[:HEAD_DIM], empty], axis=0), jnp.concatenate([empty, flat[HEAD_DIM:]], axis=0)], axis=1
    )


def pair_rows(both):
    half = both.shape[1] // 2
    return jnp.concatenate([both[:HEAD_DIM, :half], both[HEAD_DIM:, half:]], axis=0)


def fold_max(values):
    pieces = [values[at : at + 64] for at in range(0, values.shape[0], 64)]
    while len(pieces) > 1:
        pieces = [jnp.maximum(a, b) for a, b in zip(pieces[::2], pieces[1::2])] + ([pieces[-1]] if len(pieces) % 2 else [])
    top = pieces[0]
    top = jnp.maximum(top[:32], top[32:])
    top = jnp.maximum(top[:16], top[16:])
    return jnp.max(jnp.maximum(top[:8], top[8:]), axis=0, keepdims=True)


def three_parts(value, part):
    high = value.astype(bf16).astype(f32)
    rest = value - high
    middle = rest.astype(bf16).astype(f32)
    return jnp.where(part == 0, high, jnp.where(part == 1, middle, rest - middle))


def image_tags(image_ref, start, rows):
    place = start + lax.broadcasted_iota(jnp.int32, (rows, LANES), 0)
    inside = (place >= image_ref[0, 0:1, :]) & (place < image_ref[0, 1:2, :])
    return jnp.where(inside, 1.0, 0.0).astype(bf16)


def first_norm_kernel(tokens_ref, out_grad_ref, norm_ref, normed_ref, normed_t_ref, out_grad_t_ref):
    big = 256

    def step(at, carry):
        rows = pl.ds(pl.multiple_of(at * big, big), big)
        unit, _ = norm_parts(tokens_ref[rows, :].astype(f32))
        normed_ref[rows, :] = (unit * norm_ref[0:1, :] + norm_ref[1:2, :]).astype(bf16)
        return carry

    lax.fori_loop(0, tokens_ref.shape[0] // big, step, 0)
    normed_t_ref[...] = jnp.transpose(normed_ref[...])
    out_grad_t_ref[...] = jnp.transpose(out_grad_ref[...])


def first_norm(tokens, out_grad, norm_w, row_count):
    rows_all, width = tokens.shape
    length = rows_all // row_count
    by_row = pl.BlockSpec((length, width), lambda r: (r, 0))
    turned = pl.BlockSpec((width, length), lambda r: (r, 0))
    flipped = jax.ShapeDtypeStruct((row_count * width, length), bf16)
    return pl.pallas_call(
        first_norm_kernel,
        grid=(row_count,),
        in_specs=[by_row, by_row, pl.BlockSpec(norm_w.shape, lambda r: (0, 0))],
        out_specs=[by_row, turned, turned],
        out_shape=[jax.ShapeDtypeStruct((rows_all, width), bf16), flipped, flipped],
        cost_estimate=work_of(8),
        compiler_params=pltpu.CompilerParams(vmem_limit_bytes=60 * MIB),
    )(tokens, out_grad, norm_w)


def attn_forward_kernel(
    start_ref, class_ref, count_ref, tokens_ref, normed_ref, w_ref, image_ref,
    middle_ref, qkv_ref, context_ref, ext_ref,
    tag_ref, qt_ref, vt_ref,
):
    row = pl.program_id(0)
    length, width = tokens_ref.shape
    pairs = width // LANES
    tag_ref[...] = image_tags(image_ref, 0, length)
    queries = (dot(normed_ref[...], w_ref[0]) * (HEAD_DIM**-0.5 * LOG2E)).astype(bf16)
    qkv_ref[:, :width] = queries
    qt_ref[...] = jnp.transpose(queries)
    qkv_ref[:, width : 2 * width] = dot(normed_ref[...], w_ref[1]).astype(bf16)
    values = dot(normed_ref[...], w_ref[2]).astype(bf16)
    qkv_ref[:, 2 * width :] = values
    vt_ref[...] = jnp.transpose(values)

    def tile(step, carry):
        q0 = pl.multiple_of(step * WIDE_TILE, WIDE_TILE)
        here = pl.ds(q0, WIDE_TILE)
        place = q0 + lax.broadcasted_iota(jnp.int32, (IMAGES, WIDE_TILE), 1)
        edges = [jnp.concatenate([image_ref[0, at : at + IMAGES, :]] * (WIDE_TILE // LANES), axis=1) for at in (8, 16)]
        inside = (place >= edges[0]) & (place < edges[1])
        mask = jnp.where(inside, 0.0, -BIG)
        mask_low = jnp.concatenate([mask, jnp.zeros((LANES - IMAGES, WIDE_TILE), f32)], axis=0).astype(bf16)
        ext_rows = lax.broadcasted_iota(jnp.int32, (EXTRA - IMAGES, WIDE_TILE), 0)

        def attend(window):
            there = pl.ds(pl.multiple_of(start_ref[row, step], LANES), window)
            tags = tag_ref[there, :]
            ones = jnp.ones((GRID_W, window), bf16)
            extra = jnp.zeros((EXTRA - IMAGES, WIDE_TILE), f32)
            slices = [slice(p * LANES, (p + 1) * LANES) for p in range(pairs)]
            masks = jnp.concatenate([mask_low, mask_low], axis=1)
            scores, tops, exponents, mixes = [], [], [], []
            for p, at in enumerate(slices):
                keys = qkv_ref[there, width + p * LANES : width + (p + 1) * LANES]
                right = jnp.concatenate([pair_columns(qt_ref[at, here]), masks], axis=0)
                scores.append(dot(jnp.concatenate([keys, tags], axis=1), right))
            for p in range(pairs):
                tops.append(fold_max(scores[p]))
                exponents.append(jnp.exp2(scores[p] - tops[p]).astype(bf16))
            for p, at in enumerate(slices):
                mixes.append(dot(jnp.concatenate([vt_ref[at, there], ones], axis=0), exponents[p]))
            for p, at in enumerate(slices):
                mixed = mixes[p]
                total = mixed[LANES : LANES + 1, :]
                minus_lse = -(tops[p] + jnp.log(total) * LOG2E)
                scale = 1.0 / total
                lane = lax.broadcasted_iota(jnp.int32, (1, 2 * WIDE_TILE), 1)
                head = 2 * p + jnp.where(lane < WIDE_TILE, 0, 1)
                scale = jnp.where(head < count_ref[row], scale, 0.0)
                context_ref[here, at] = jnp.transpose(pair_rows(mixed[:LANES] * scale)).astype(bf16)
                for h in range(2):
                    value = minus_lse[:, h * WIDE_TILE : (h + 1) * WIDE_TILE]
                    first = 6 * p + 3 * h
                    extra = jnp.where(
                        (ext_rows >= first) & (ext_rows < first + 3), three_parts(value, ext_rows - first), extra
                    )
            ext_ref[:, here] = jnp.concatenate([mask, extra], axis=0).astype(bf16)

        for index, window in enumerate(widths_for(length)):
            pl.when(class_ref[row, step] == index)(functools.partial(attend, window))
        return carry

    lax.fori_loop(0, length // WIDE_TILE, tile, 0)
    middle_ref[...] = tokens_ref[...].astype(f32) + dot(context_ref[...], w_ref[3], NT)


def attn_forward(starts, classes, counts, tokens, normed, attn_use, images):
    rows_all, width = tokens.shape
    row_count = counts.shape[0]
    length = rows_all // row_count
    by_row = lambda columns: pl.BlockSpec((length, columns), lambda r, *_: (r, 0))
    return pl.pallas_call(
        attn_forward_kernel,
        grid_spec=pltpu.PrefetchScalarGridSpec(
            num_scalar_prefetch=3,
            grid=(row_count,),
            in_specs=[
                by_row(width),
                by_row(width),
                pl.BlockSpec(attn_use.shape, lambda r, *_: (0, 0, 0)),
                pl.BlockSpec((1, 24, LANES), lambda r, *_: (r, 0, 0)),
            ],
            out_specs=[
                by_row(width), by_row(3 * width), by_row(width), pl.BlockSpec((EXTRA, length), lambda r, *_: (r, 0))
            ],
            scratch_shapes=[
                pltpu.VMEM((length, LANES), bf16),
                pltpu.VMEM((width, length), bf16),
                pltpu.VMEM((width, length), bf16),
            ],
        ),
        out_shape=[
            jax.ShapeDtypeStruct((rows_all, width), f32),
            jax.ShapeDtypeStruct((rows_all, 3 * width), bf16),
            jax.ShapeDtypeStruct((rows_all, width), bf16),
            jax.ShapeDtypeStruct((row_count * EXTRA, length), bf16),
        ],
        cost_estimate=work_of(30),
        compiler_params=pltpu.CompilerParams(vmem_limit_bytes=56 * MIB),
    )(starts, classes, counts, tokens, normed, attn_use, images)


def attn_backward_kernel(
    first, final, start_ref, class_ref, count_ref, rank_ref, normed_t_ref, middle_grad_ref, qkv_ref, context_ref, ext_ref, w_ref,
    image_ref, *refs,
):
    sums = None
    if first:
        sums, refs = refs[1], refs[2:]
    sent = None
    if final:
        proj_ref, keep_ref, send_ref, *scratch, w_grad_ref = refs
        sent = (keep_ref, send_ref)
    else:
        proj_ref, w_grad_ref, *scratch = refs
    attn_backward_row(
        first, sums, sent, start_ref, class_ref, count_ref, rank_ref, normed_t_ref, middle_grad_ref, qkv_ref, context_ref, ext_ref,
        w_ref, image_ref, proj_ref, w_grad_ref, *scratch,
    )


def attn_backward_row(
    first, sums, sent, start_ref, class_ref, count_ref, rank_ref, normed_t_ref, middle_grad_ref, qkv_ref, context_ref, ext_ref, w_ref,
    image_ref, proj_ref, w_grad_ref,
    tag_ref, up_ref, delta_ref, dq_ref, dk_ref, dv_ref, low_ref, qt_ref, kt_ref, upt_ref,
):
    step_at = pl.program_id(0)
    row = first + step_at
    length, width = middle_grad_ref.shape
    pairs = width // LANES
    big = 256

    @pl.when(step_at == 0)
    def _():
        w_grad_ref[...] = jnp.zeros_like(w_grad_ref) if sums is None else sums[...]

    target = lax.broadcasted_iota(jnp.int32, (EXTRA, width), 0) - IMAGES
    source = lax.broadcasted_iota(jnp.int32, (EXTRA, width), 1) // HEAD_DIM * 3
    collect = jnp.where((target >= source) & (target < source + 3), -1.0, 0.0).astype(bf16)
    active = jnp.where(
        lax.broadcasted_iota(jnp.int32, (1, width), 1) // HEAD_DIM < count_ref[row], 1.0, 0.0
    )

    def prepare(step, carry):
        rows = pl.ds(pl.multiple_of(step * big, big), big)
        tag_ref[rows, :] = image_tags(image_ref, step * big, big)
        low_ref[rows, :] = middle_grad_ref[rows, :].astype(bf16)
        dk_ref[rows, :] = jnp.zeros((big, width), f32)
        dv_ref[rows, :] = jnp.zeros((big, width), f32)
        return carry

    lax.fori_loop(0, length // big, prepare, 0)
    up = (dot(low_ref[...], w_ref[3]) * active).astype(bf16)
    up_ref[...] = up
    upt_ref[...] = jnp.transpose(up)
    qt_ref[...] = jnp.transpose(qkv_ref[:, :width])
    kt_ref[...] = jnp.transpose(qkv_ref[:, width : 2 * width])

    def gather(step, carry):
        rows = pl.ds(pl.multiple_of(step * big, big), big)
        product = up_ref[rows, :].astype(f32) * context_ref[rows, :].astype(f32)
        high = product.astype(bf16)
        rest = (product - high.astype(f32)).astype(bf16)
        delta = dot(collect, high, NT) + dot(collect, rest, NT)
        part = lax.rem(lax.broadcasted_iota(jnp.int32, (EXTRA, big), 0) + 3 * EXTRA - IMAGES, 3)
        delta_ref[:, rows] = three_parts(delta, part).astype(bf16)
        return carry

    lax.fori_loop(0, length // big, gather, 0)
    lane = lax.broadcasted_iota(jnp.int32, (1, LANES), 1)
    first_half = jnp.where(lane < HEAD_DIM, 1.0, 0.0).astype(bf16)
    second_half = jnp.where(lane >= HEAD_DIM, 1.0, 0.0).astype(bf16)

    def tile(step, carry):
        q0 = pl.multiple_of(step * TILE, TILE)
        here = pl.ds(q0, TILE)

        def attend(window):
            there = pl.ds(pl.multiple_of(start_ref[row, step], LANES), window)
            tags = tag_ref[there, :]
            ext = ext_ref[:, here]
            delta = delta_ref[:, here]
            at_row = lax.broadcasted_iota(jnp.int32, (EXTRA, LANES), 0)
            empty = jnp.zeros((LANES - EXTRA, 2 * TILE), bf16)

            def own(edge, masks):
                keep = (at_row >= edge) & (at_row < edge + 3)
                return jnp.where(keep | (at_row < IMAGES) if masks else keep, 1.0, 0.0).astype(bf16)

            slices = [slice(p * LANES, (p + 1) * LANES) for p in range(pairs)]
            scores, grad_probs, probs, grad_scores = [], [], [], []
            for p, at in enumerate(slices):
                keys = qkv_ref[there, width + p * LANES : width + (p + 1) * LANES]
                values = qkv_ref[there, 2 * width + p * LANES : 2 * width + (p + 1) * LANES]
                edge = IMAGES + 6 * p
                q_side = jnp.concatenate(
                    [
                        pair_columns(qt_ref[at, here]),
                        jnp.concatenate([ext * own(edge, True), ext * own(edge + 3, True)], axis=1),
                        empty,
                    ],
                    axis=0,
                )
                up_side = jnp.concatenate(
                    [
                        pair_columns(upt_ref[at, here]),
                        jnp.concatenate([delta * own(edge, False), delta * own(edge + 3, False)], axis=1),
                        empty,
                    ],
                    axis=0,
                )
                scores.append(dot(jnp.concatenate([keys, tags], axis=1), q_side))
                grad_probs.append(dot(jnp.concatenate([values, tags], axis=1), up_side))
            for p in range(pairs):
                weight = jnp.exp2(scores[p])
                probs.append(weight.astype(bf16))
                grad_scores.append((weight * grad_probs[p]).astype(bf16))
            for p, at in enumerate(slices):
                queries, ups = qkv_ref[here, at], up_ref[here, at]
                q_pair = jnp.concatenate([queries * first_half, queries * second_half], axis=0)
                up_pair = jnp.concatenate([ups * first_half, ups * second_half], axis=0)
                dv_ref[there, at] += dot(probs[p], up_pair)
                dk_ref[there, at] += dot(grad_scores[p], q_pair)
                dq = pair_rows(dot(kt_ref[at, there], grad_scores[p]))
                dq_ref[here, at] = jnp.transpose(dq * HEAD_DIM**-0.5).astype(bf16)

        for index, window in enumerate(widths_for(length)):
            pl.when(class_ref[row, step] == index)(functools.partial(attend, window))
        return carry

    lax.fori_loop(0, length // TILE, tile, 0)
    keys_grad = (dk_ref[...] * LN2).astype(bf16)
    values_grad = dv_ref[...].astype(bf16)
    proj_ref[...] = jnp.concatenate([dq_ref[...], keys_grad, values_grad], axis=1)
    for k in range(3):
        w_grad_ref[k] += dot(normed_t_ref[...], proj_ref[:, k * width : (k + 1) * width])
    w_grad_ref[3] += dot(jnp.transpose(low_ref[...]), context_ref[...])
    if sent:

        @pl.when(step_at == pl.num_programs(0) - 1)
        def _():
            for k in range(2):
                one, two = w_grad_ref[k], w_grad_ref[k + 2]
                halves = [jnp.concatenate([one[:, at : at + width // 2], two[:, at : at + width // 2]], axis=1) for at in (0, width // 2)]
                sent[0][k] = jnp.where(rank_ref[0] == 0, halves[0], halves[1])
                sent[1][k] = jnp.where(rank_ref[0] == 0, halves[1], halves[0]).astype(bf16)


def attn_backward(first, count, so_far, starts, classes, counts, rank, normed_t, middle_grad, qkv, context, ext, attn_use, images):
    rows_all, width = middle_grad.shape
    length = rows_all // counts.shape[0]
    by_row = lambda columns: pl.BlockSpec((length, columns), lambda r, *_: (first + r, 0))
    final = first + count == counts.shape[0]
    half = (2, width, width)
    halves = pl.BlockSpec(half, lambda r, *_: (0, 0, 0))
    whole = pl.BlockSpec(attn_use.shape, lambda r, *_: (0, 0, 0))
    return pl.pallas_call(
        functools.partial(attn_backward_kernel, first, final),
        grid_spec=pltpu.PrefetchScalarGridSpec(
            num_scalar_prefetch=4,
            grid=(count,),
            in_specs=[
                pl.BlockSpec((width, length), lambda r, *_: (first + r, 0)),
                by_row(width),
                by_row(3 * width),
                by_row(width),
                pl.BlockSpec((EXTRA, length), lambda r, *_: (first + r, 0)),
                whole,
                pl.BlockSpec((1, 24, LANES), lambda r, *_: (first + r, 0, 0)),
            ]
            + ([pl.BlockSpec(memory_space=pl.ANY), whole] if first else []),
            out_specs=[by_row(3 * width)] + ([halves, halves] if final else [whole]),
            scratch_shapes=[
                pltpu.VMEM((length, LANES), bf16),
                pltpu.VMEM((length, width), bf16),
                pltpu.VMEM((EXTRA, length), bf16),
                pltpu.VMEM((length, width), bf16),
                pltpu.VMEM((length, width), f32),
                pltpu.VMEM((length, width), f32),
                pltpu.VMEM((length, width), bf16),
                pltpu.VMEM((width, length), bf16),
                pltpu.VMEM((width, length), bf16),
                pltpu.VMEM((width, length), bf16),
            ]
            + ([pltpu.VMEM(attn_use.shape, f32)] if final else []),
        ),
        out_shape=[jax.ShapeDtypeStruct((rows_all, 3 * width), bf16)]
        + (
            [jax.ShapeDtypeStruct(half, f32), jax.ShapeDtypeStruct(half, bf16)]
            if final
            else [jax.ShapeDtypeStruct(attn_use.shape, f32)]
        ),
        input_output_aliases={11: 0} if first else {},
        cost_estimate=work_of(18 * count),
        compiler_params=pltpu.CompilerParams(vmem_limit_bytes=50 * MIB),
    )(starts, classes, counts, rank, normed_t, middle_grad, qkv, context, ext, attn_use, images, *(so_far or ()))


def tokens_back_kernel(proj_ref, tokens_ref, middle_grad_ref, w_ref, norm_ref, *refs):
    tokens_grad_ref, norm_grad_ref = refs[-2:]

    @pl.when(pl.program_id(0) == 0)
    def _():
        norm_grad_ref[...] = jnp.zeros_like(norm_grad_ref)

    w_cat = jnp.concatenate([w_ref[0], w_ref[1], w_ref[2]], axis=1)
    upstream = dot(proj_ref[...], w_cat, NT)
    unit, inverse = norm_parts(tokens_ref[...].astype(f32))
    tokens_grad_ref[...] = middle_grad_ref[...] + norm_back(upstream, norm_ref[0:1, :], unit, inverse)
    norm_grad_ref[0:8, :] += fold_rows(upstream * unit)
    norm_grad_ref[8:16, :] += fold_rows(upstream)


def tokens_back(first, count, so_far, proj, tokens, middle_grad, attn_use, norm_w):
    rows_all, width = tokens.shape
    some = lambda columns: pl.BlockSpec((FILL, columns), lambda r: (first + r, 0))
    return pl.pallas_call(
        tokens_back_kernel,
        grid=(count,),
        in_specs=[
            some(3 * width),
            some(width),
            some(width),
            pl.BlockSpec(attn_use.shape, lambda r: (0, 0, 0)),
            pl.BlockSpec(norm_w.shape, lambda r: (0, 0)),
        ]
        + ([] if so_far is None else [pl.BlockSpec(memory_space=pl.ANY)]),
        out_specs=[some(width), pl.BlockSpec((16, width), lambda r: (0, 0))],
        out_shape=[jax.ShapeDtypeStruct((rows_all, width), f32), jax.ShapeDtypeStruct((16, width), f32)],
        input_output_aliases={} if so_far is None else {5: 0},
        cost_estimate=work_of(2 * count),
        compiler_params=pltpu.CompilerParams(vmem_limit_bytes=60 * MIB),
    )(proj, tokens, middle_grad, attn_use, norm_w, *([] if so_far is None else [so_far]))


def mlp_kernel(
    place_ref, rank_ref, middle_ref, out_grad_ref, out_grad_t_ref, own_w_ref, other_w_ref, taps_ref, norm_ref,
    output_ref, middle_grad_ref, keep_ref, send_ref, taps_grad_ref, norm_grad_ref,
    w_ref, w_grad_ref, normed_ref, normed_t_ref, out_sum_ref, up_sum_ref, tap_sum_ref,
    act_grads_ref, acts_ref, hidden_grads_ref, *buffers,
):
    row = pl.program_id(0)
    length, width = middle_ref.shape
    hidden = w_ref.shape[2]
    chunk = PARTS * LANES
    big = 256
    grid_rows = length // GRID_W
    chunks = hidden // chunk
    h_refs, g_refs = buffers[:PARTS], buffers[PARTS:]
    gain, bias = norm_ref[2:3, :], norm_ref[3:4, :]

    @pl.when(row == 0)
    def _():
        w_grad_ref[...] = jnp.zeros_like(w_grad_ref)
        norm_grad_ref[...] = jnp.zeros_like(norm_grad_ref)
        tap_sum_ref[...] = jnp.zeros_like(tap_sum_ref)
        for rank, halves in enumerate(((own_w_ref, other_w_ref), (other_w_ref, own_w_ref))):

            @pl.when(rank_ref[0] == rank)
            def _():
                w_ref[:, :, : hidden // 2] = halves[0][...]
                w_ref[:, :, hidden // 2 :] = halves[1][...]

        for ref in buffers:
            ref[...] = jnp.zeros_like(ref)

    def place(r):
        return pl.multiple_of(place_ref[row, r], 8)

    for n in range(IMAGES + 1):
        at = place(grid_rows + n)
        for ref in buffers:
            ref[pl.ds(at, GRID_W), :] = jnp.zeros((GRID_W, LANES), f32)

    def normalize(step, carry):
        rows = pl.ds(pl.multiple_of(step * big, big), big)
        middle = middle_ref[rows, :]
        unit, _ = norm_parts(middle)
        normed_ref[rows, :] = (unit * gain + bias).astype(bf16)
        out_sum_ref[rows, :] = jnp.zeros((big, width), f32)
        up_sum_ref[rows, :] = jnp.zeros((big, width), f32)
        return carry

    lax.fori_loop(0, length // big, normalize, 0)
    normed_t_ref[...] = jnp.transpose(normed_ref[...])

    def lanes_of(c):
        return pl.ds(pl.multiple_of(c * chunk, chunk), chunk)

    def lanes_of(c):
        return pl.ds(pl.multiple_of(c * chunk, chunk), chunk)

    def neighbours(ref, at):
        return [ref[pl.ds(at + (a * STRIDE + b), GRID_W), :] for a in (-1, 0, 1) for b in (-1, 0, 1)]

    def tall(values):
        return jnp.concatenate([values, values], axis=0)

    def total_of(terms):
        while len(terms) > 1:
            terms = [a + b for a, b in zip(terms[::2], terms[1::2])] + ([terms[-1]] if len(terms) % 2 else [])
        return terms[0]

    def taps_for(c, part, at):
        lane = pl.ds(pl.multiple_of(c * chunk + part * LANES, LANES), LANES)
        return [tall(taps_ref[at + k * 8 : at + (k + 1) * 8, lane]) for k in range(9)]

    lines = 8

    def do_chunk(c, carry):
        lanes = lanes_of(c)
        for t in range(length // big):
            rows = slice(t * big, (t + 1) * big)
            values = dot(normed_ref[rows, :], w_ref[0, :, lanes])
            for part in range(PARTS):
                for s in range(big // GRID_W):
                    at = place(t * (big // GRID_W) + s)
                    h_refs[part][pl.ds(at, GRID_W), :] = values[
                        s * GRID_W : (s + 1) * GRID_W, part * LANES : (part + 1) * LANES
                    ]
        act_grads_ref[...] = dot(out_grad_ref[...], w_ref[1, :, lanes])

        def forward(t, carry):
            tokens_base = pl.multiple_of(t * (lines * GRID_W), lines * GRID_W)
            for part in range(PARTS):
                taps = taps_for(c, part, 0)
                cols = slice(part * LANES, (part + 1) * LANES)
                for s in range(lines):
                    near = pl.ds(pl.multiple_of(tokens_base + s * GRID_W, GRID_W), GRID_W)
                    at = place(t * lines + s)
                    x = total_of([x * tap for x, tap in zip(neighbours(h_refs[part], at), taps)])
                    square = x * x
                    value = jnp.tanh(x * (GELU_A + square))
                    gate = 1.0 + value
                    twice = x * gate
                    acts_ref[near, cols] = twice.astype(bf16)
                    slope = gate + (twice * (1.0 - value)) * (GELU_A + 3.0 * square)
                    g_refs[part][pl.ds(at, GRID_W), :] = act_grads_ref[near, cols] * slope
            return carry

        lax.fori_loop(0, grid_rows // lines, forward, 0)

        def backward(t, carry):
            tokens_base = pl.multiple_of(t * (lines * GRID_W), lines * GRID_W)
            for part in range(PARTS):
                taps = taps_for(c, part, 72)
                lane = pl.ds(pl.multiple_of(c * chunk + part * LANES, LANES), LANES)
                cols = slice(part * LANES, (part + 1) * LANES)
                totals = [None] * 9
                for s in range(lines):
                    near = pl.ds(pl.multiple_of(tokens_base + s * GRID_W, GRID_W), GRID_W)
                    at = place(t * lines + s)
                    source = h_refs[part][pl.ds(at, GRID_W), :]
                    moved = neighbours(g_refs[part], at)[::-1]
                    for k in range(9):
                        product = source * moved[k]
                        folded = product[:8] + product[8:]
                        totals[k] = folded if totals[k] is None else totals[k] + folded
                    terms = [x * tap for x, tap in zip(moved, taps)]
                    hidden_grads_ref[near, cols] = total_of(terms).astype(bf16)
                for k in range(9):
                    tap_sum_ref[k * 8 : (k + 1) * 8, lane] += totals[k]
            return carry

        lax.fori_loop(0, grid_rows // lines, backward, 0)
        w_grad_ref[0, :, lanes] += dot(normed_t_ref[...], hidden_grads_ref[...])
        w_grad_ref[1, :, lanes] += dot(out_grad_t_ref[...], acts_ref[...])
        out_sum_ref[...] += dot(acts_ref[...], w_ref[1, :, lanes], NT)
        up_sum_ref[...] += dot(hidden_grads_ref[...], w_ref[0, :, lanes], NT)
        return carry

    lax.fori_loop(0, chunks, do_chunk, 0)

    def finish(step, carry):
        rows = pl.ds(pl.multiple_of(step * big, big), big)
        middle = middle_ref[rows, :]
        output_ref[rows, :] = (middle + ACT_SCALE * out_sum_ref[rows, :]).astype(bf16)
        upstream = 0.5 * up_sum_ref[rows, :]
        unit, inverse = norm_parts(middle)
        middle_grad_ref[rows, :] = out_grad_ref[rows, :].astype(f32) + norm_back(upstream, gain, unit, inverse)
        norm_grad_ref[0:8, :] += fold_rows(upstream * unit)
        norm_grad_ref[8:16, :] += fold_rows(upstream)
        return carry

    lax.fori_loop(0, length // big, finish, 0)

    @pl.when(row == pl.num_programs(0) - 1)
    def _():
        for k, scale in enumerate((0.5, ACT_SCALE)):
            halves = w_grad_ref[k, :, : hidden // 2], w_grad_ref[k, :, hidden // 2 :]
            keep_ref[k] = scale * jnp.where(rank_ref[0] == 0, halves[0], halves[1])
            send_ref[k] = (scale * jnp.where(rank_ref[0] == 0, halves[1], halves[0])).astype(bf16)
        taps_grad_ref[...] = jnp.zeros_like(taps_grad_ref)
        for k in range(9):
            total = jnp.sum(tap_sum_ref[k * 8 : (k + 1) * 8, :], axis=0, keepdims=True)
            taps_grad_ref[k : k + 1, :] = 0.5 * total


def mlp_layer(places, rank, middle, out_grad, out_grad_t, own_w, other_w, taps, norm_w):
    rows_all, width = middle.shape
    row_count = places.shape[0]
    length = rows_all // row_count
    half = own_w.shape
    hidden = 2 * half[2]
    whole = half[:2] + (hidden,)
    by_row = lambda columns: pl.BlockSpec((length, columns), lambda r, *_: (r, 0))
    slots = (length // GRID_W + IMAGES + 2) * STRIDE
    return pl.pallas_call(
        mlp_kernel,
        grid_spec=pltpu.PrefetchScalarGridSpec(
            num_scalar_prefetch=2,
            grid=(row_count,),
            in_specs=[
                by_row(width),
                by_row(width),
                pl.BlockSpec((width, length), lambda r, *_: (r, 0)),
                pl.BlockSpec(half, lambda r, *_: (0, 0, 0)),
                pl.BlockSpec(half, lambda r, *_: (0, 0, 0)),
                pl.BlockSpec(taps.shape, lambda r, *_: (0, 0)),
                pl.BlockSpec(norm_w.shape, lambda r, *_: (0, 0)),
            ],
            out_specs=[
                by_row(width),
                by_row(width),
                pl.BlockSpec(half, lambda r, *_: (0, 0, 0)),
                pl.BlockSpec(half, lambda r, *_: (0, 0, 0)),
                pl.BlockSpec((16, hidden), lambda r, *_: (0, 0)),
                pl.BlockSpec((16, width), lambda r, *_: (0, 0)),
            ],
            scratch_shapes=[
                pltpu.VMEM(whole, bf16),
                pltpu.VMEM(whole, f32),
                pltpu.VMEM((length, width), bf16),
                pltpu.VMEM((width, length), bf16),
                pltpu.VMEM((length, width), f32),
                pltpu.VMEM((length, width), f32),
                pltpu.VMEM((9 * 8, hidden), f32),
                pltpu.VMEM((length, PARTS * LANES), f32),
                pltpu.VMEM((length, PARTS * LANES), bf16),
                pltpu.VMEM((length, PARTS * LANES), bf16),
            ]
            + [pltpu.VMEM((slots, LANES), f32)] * (2 * PARTS),
        ),
        out_shape=[
            jax.ShapeDtypeStruct((rows_all, width), bf16),
            jax.ShapeDtypeStruct((rows_all, width), f32),
            jax.ShapeDtypeStruct(half, f32),
            jax.ShapeDtypeStruct(half, bf16),
            jax.ShapeDtypeStruct((16, hidden), f32),
            jax.ShapeDtypeStruct((16, width), f32),
        ],
        cost_estimate=work_of(90),
        compiler_params=pltpu.CompilerParams(vmem_limit_bytes=50 * MIB),
    )(places, rank, middle, out_grad, out_grad_t, own_w, other_w, taps, norm_w)


def attention_plan(segments, tile):
    row_count, length = segments.shape
    tiles = segments.reshape(row_count, length // tile, tile)
    first, last = tiles[:, :, 0], tiles[:, :, -1]
    ids = jnp.arange(IMAGES, dtype=jnp.int32)
    begins = jnp.sum((segments[:, None, :] < ids[None, :, None]).astype(jnp.int32), axis=-1)
    ends = jnp.sum((segments[:, None, :] <= ids[None, :, None]).astype(jnp.int32), axis=-1)
    low_end = jnp.sum(jnp.where(first[:, :, None] == ids, begins[:, None, :], 0), axis=-1) // LANES * LANES
    high_end = jnp.sum(jnp.where(last[:, :, None] == ids, ends[:, None, :], 0), axis=-1)
    widths = widths_for(length)
    classes = sum(((high_end - low_end) > w).astype(jnp.int32) for w in widths[:-1])
    chosen = jnp.full_like(classes, widths[-1])
    for index, w in enumerate(widths):
        chosen = jnp.where(classes == index, w, chosen)
    starts = jnp.minimum(low_end, length - chosen)
    used = jnp.zeros((row_count, EXTRA - IMAGES), jnp.int32)
    unused = jnp.zeros((row_count, LANES - EXTRA), jnp.int32)
    first_lane = jnp.concatenate([begins, used, unused], axis=1)
    end_lane = jnp.concatenate([ends, used + length, unused], axis=1)
    by_lane = jnp.pad(jnp.stack([first_lane, end_lane], axis=1), ((0, 0), (0, 6), (0, 0)))
    by_image = jnp.broadcast_to(jnp.concatenate([begins, ends], axis=1)[:, :, None], (row_count, 2 * IMAGES, LANES))
    return starts, classes, jnp.concatenate([by_lane, by_image], axis=1)


def spread_taps(conv_use):
    taps = conv_use.astype(f32)
    own = (jnp.arange(9) == 4).astype(f32)[:, None]
    taps = jnp.repeat(taps + own, 8, axis=0)
    return jnp.concatenate([taps * GELU_S, taps], axis=0)


def line_places(segments):
    ids = segments[:, ::GRID_W]
    count = ids.shape[1]
    rows = jnp.arange(count, dtype=jnp.int32) + ids + 1
    images = jnp.arange(IMAGES, dtype=jnp.int32)
    first = jnp.sum((ids[:, None, :] < images[None, :, None]).astype(jnp.int32), axis=-1)
    gaps = jnp.concatenate([first + images, jnp.full((ids.shape[0], 1), count + IMAGES, jnp.int32)], axis=1)
    return jnp.concatenate([rows, gaps], axis=1) * STRIDE + 8


def bits_of(size):
    bits = []
    b = 1
    while b < size:
        bits.append(b)
        b *= 2
    return bits


def groups_of(size):
    bits = bits_of(size)
    return [(bits[at], 1 << len(bits[at : at + 2])) for at in range(0, len(bits), 2)]


def swap(values, axis, size, bit):
    return lax.ppermute(values, axis, [(i, i ^ bit) for i in range(size)])


def in_order(found, mine):
    ordered = []
    for target in range(len(found)):
        value = found[0]
        for step in range(1, len(found)):
            value = jnp.where((mine ^ step) == target, found[step], value)
        ordered.append(value)
    return ordered


def start_group(held, size, low, count):
    return [held] + [swap(held, "dp", size, step * low) for step in range(1, count)]


def finish_stack(found, low, count):
    held = jnp.stack(in_order(found, (lax.axis_index("dp") // low) % count), axis=1)
    return held.reshape((-1,) + held.shape[2:])


def finish_group(found, low, count):
    held = jnp.stack(in_order(found, (lax.axis_index("dp") // low) % count))
    return held.reshape((-1,) + held.shape[2:])


def fold_pairs(values):
    count = values.shape[0] // 2
    return jnp.concatenate([values[:count], values[count:]], axis=-1)


def unfold_pairs(values):
    half = values.shape[-1] // 2
    return jnp.concatenate([values[..., :half], values[..., half:]], axis=0)


def join_columns(mine, other, rank):
    first = jnp.where(rank == 0, mine, other)
    second = jnp.where(rank == 0, other, mine)
    return jnp.concatenate([first, second], axis=-1)


def join_weights(mine, other, rank, count):
    lines, _, part, columns = mine.shape
    half = columns // 2
    full = [join_columns(mine[..., at : at + half], other[..., at : at + half], rank) for at in (0, half)]
    return jnp.moveaxis(jnp.concatenate(full, axis=1), 0, 1).reshape(count, lines * part, columns)


def half_columns(values, side):
    half = values.shape[-1] // 2
    return lax.dynamic_slice_in_dim(values, side * half, half, axis=values.ndim - 1)


def by_line(values, size):
    count, rows, columns = values.shape
    return values.reshape(count, size, rows // size, columns)


def two_parts(values):
    high = values.astype(bf16)
    return jnp.concatenate([high, (values - high.astype(f32)).astype(bf16)], axis=0)


def from_parts(parts):
    count = parts.shape[0] // 2
    return parts[:count].astype(f32) + parts[count:].astype(f32)


def pieces_of(held, low, count):
    n, lines = held.shape[:2]
    split = held.reshape((n, lines // count, count) + held.shape[2:])
    mine = (lax.axis_index("dp") // low) % count
    return [lax.dynamic_index_in_dim(split, mine ^ step, 2, keepdims=False) for step in range(count)]


def flat(values):
    return values.astype(bf16).reshape(-1, values.shape[-1])


def sum_everywhere(values, size):
    values = values + swap(values, "head", 2, 1)
    for bit in bits_of(size):
        values = values + swap(values, "dp", size, bit)
    return values


def after(first, second):
    return lax.optimization_barrier((first, second))


def adam_terms(grad_sum, first_old, second):
    first_new = BETA_ONE * first_old + (1.0 - BETA_ONE) * grad_sum
    second_new = BETA_TWO * second + (1.0 - BETA_TWO) * grad_sum * grad_sum
    direction = (
        first_new
        / (1.0 - BETA_ONE**STEP)
        / (jnp.sqrt(second_new / (1.0 - BETA_TWO**STEP)) + ADAM_EPS)
    )
    return (first_new, second_new, direction)


def moments_kernel(line_ref, norm_ref, *refs):
    count = 3
    grads, weights, firsts, seconds = (refs[n * count : (n + 1) * count] for n in range(4))
    new_firsts, new_seconds, updates = (refs[(4 + n) * count : (5 + n) * count] for n in range(3))
    sums_ref = refs[7 * count]
    width = sums_ref.shape[1]
    lane = lax.broadcasted_iota(jnp.int32, (1, width), 1)
    rows = [jnp.zeros((1, width), f32), jnp.zeros((1, width), f32)]
    at = 0
    for n in range(count):
        grad, weight = grads[n][...], weights[n][...]
        new_first, new_second, direction = adam_terms(grad, firsts[n][...], seconds[n][...])
        update = direction + DECAY * weight
        new_firsts[n][...], new_seconds[n][...], updates[n][...] = new_first, new_second, update
        matrices = weight.shape[0] if weight.ndim == 3 else 1
        for k in range(matrices):
            for row, values in enumerate((weight, update)):
                values = values[k] if weight.ndim == 3 else values
                total = jnp.sum(jnp.sum(values * values, axis=0, keepdims=True), axis=1, keepdims=True)
                if weight.ndim == 2:
                    total = jnp.where(line_ref[0] == 0, total, 0.0)
                rows[row] = jnp.where(lane == at, total, rows[row])
            at += 1
    gain = jnp.sum(norm_ref[0:8, :], axis=0, keepdims=True)
    bias = jnp.sum(norm_ref[8:16, :], axis=0, keepdims=True)
    sums_ref[...] = jnp.concatenate(rows + [gain, bias, jnp.zeros((4, width), f32)], axis=0)


def apply_kernel(sums_ref, norm_two_ref, norm_w_ref, norm_m_ref, norm_v_ref, *refs):
    count = 3
    weights, updates, news = (refs[n * count : (n + 1) * count] for n in range(3))
    new_norm_w_ref, new_norm_m_ref, new_norm_v_ref = refs[3 * count :]
    ratio = jnp.sqrt(sums_ref[0:1, :]) / jnp.sqrt(sums_ref[1:2, :])
    at = 0
    for n in range(count):
        shape = weights[n].shape
        if len(shape) == 3:
            for k in range(shape[0]):
                news[n][k] = weights[n][k] - RATE * ratio[:, at : at + 1] * updates[n][k]
                at += 1
        else:
            news[n][...] = weights[n][...] - RATE * ratio[:, at : at + 1] * updates[n][...]
            at += 1
    grads = jnp.concatenate([sums_ref[2:4, :], norm_two_ref[...]], axis=0)
    new_first, new_second, direction = adam_terms(grads, norm_m_ref[...], norm_v_ref[...])
    new_norm_m_ref[...], new_norm_v_ref[...] = new_first, new_second
    new_norm_w_ref[...] = norm_w_ref[...] - RATE * direction


def like(values):
    return [jax.ShapeDtypeStruct(v.shape, f32) for v in values]


def body(
    size,
    tokens, grad_out, segments, counts,
    attn_w, attn_m, attn_v, mlp_w, mlp_m, mlp_v, conv_w, conv_m, conv_v, norm_w, norm_m, norm_v,
):
    rank = lax.axis_index("head")
    place = lax.axis_index("dp")
    own_rows = segments.shape[0] // 2
    segments = lax.dynamic_slice_in_dim(segments, rank * own_rows, own_rows, axis=0)
    counts = lax.dynamic_slice_in_dim(counts, rank * own_rows, own_rows, axis=0)
    width = norm_w.shape[1]
    groups = groups_of(size)
    attn_lines = fold_pairs(attn_w.astype(bf16))[None]
    mlp_lines = mlp_w.astype(bf16)[None]
    for near, far in zip(groups[:-1], groups[:0:-1]):
        found, more = start_group(attn_lines, size, *far), start_group(mlp_lines, size, *near)
        attn_lines, mlp_lines = finish_stack(found, *far), finish_group(more, *near)
    attn_lines, early = after(attn_lines, (tokens, grad_out))
    found = start_group(attn_lines, size, *groups[0])
    (normed, normed_t, out_grad_t), found = after(first_norm(*early, norm_w, own_rows), found)
    attn_lines = finish_stack(found, *groups[0])
    attn_use = join_weights(attn_lines, swap(attn_lines, "head", 2, 1), rank, attn_w.shape[0])
    found = start_group(mlp_lines, size, *groups[-1])
    conv_low = conv_w.astype(bf16)
    conv_use = join_columns(conv_low, swap(conv_low, "head", 2, 1), rank)
    starts, classes, images = attention_plan(segments, WIDE_TILE)
    back_starts, back_classes, _ = attention_plan(segments, TILE)
    middle, qkv, context, ext = attn_forward(starts, classes, counts, tokens, normed, attn_use, images)
    middle, found = after(middle, found)
    mlp_lines = finish_group(found, *groups[-1])
    mlp_lines = jnp.moveaxis(mlp_lines, 0, 1).reshape(mlp_w.shape[0], -1, mlp_w.shape[2])
    rank_at = rank.astype(jnp.int32).reshape(1)
    output, grad_middle, held, send, grad_conv, grad_norm_two = mlp_layer(
        line_places(segments), rank_at, middle, grad_out, out_grad_t, mlp_lines, swap(mlp_lines, "head", 2, 1),
        spread_taps(conv_use), norm_w,
    )

    def back(first, count, so_far):
        return attn_backward(
            first, count, so_far, back_starts, back_classes, counts, rank_at, normed_t, grad_middle, qkv, context, ext, attn_use, images
        )

    columns = conv_w.shape[1]
    norm_two = jnp.sum(grad_norm_two.reshape(2, 8, width), axis=1).reshape(1, 2 * width)
    norm_two = jnp.pad(norm_two, ((0, 0), (0, columns - 2 * width)))
    taps = grad_conv[:9]
    small = jnp.concatenate([half_columns(taps, rank), norm_two])
    small_send = jnp.concatenate([half_columns(taps, 1 - rank), norm_two])
    got = swap(jnp.concatenate([flat(send), two_parts(small_send)], axis=0), "head", 2, 1)
    first_rows = max(1, own_rows // 3)
    so_far, got = after(back(0, first_rows, None), got)
    rows = held.size // columns
    held = by_line(held + got[:rows].reshape(held.shape).astype(f32), size)
    small = from_parts(two_parts(small)) + from_parts(got[rows:])
    low, count = groups[0]
    pieces = pieces_of(held, low, count)
    small_parts = two_parts(small)
    gots = [
        swap(jnp.concatenate([flat(pieces[step]), small_parts], axis=0), "dp", size, step * low) for step in range(1, count)
    ]
    so_far, pieces = after(so_far, pieces)
    projected_grad, attn_held, attn_send = back(first_rows, own_rows - first_rows, so_far)

    def take(pieces, gots, small_parts, low, count):
        keep = pieces[0]
        rows = keep.size // keep.shape[-1]
        for got in gots:
            keep = keep + got[:rows].reshape(keep.shape).astype(f32)
        ordered = in_order([small_parts] + [got[rows:] for got in gots], (place // low) % count)
        return keep, sum(from_parts(part) for part in ordered)

    attn_got = swap(flat(attn_send), "head", 2, 1)
    attn_held, gots = after(attn_held, gots)
    held, small = take(pieces, gots, small_parts, low, count)
    rest = bits_of(size)[2:]
    attn_held = by_line(attn_held + attn_got.reshape(attn_held.shape).astype(f32), size)
    waiting = list(groups)
    blocks = tokens.shape[0] // FILL
    fills = [(0, blocks - blocks // 3), (blocks - blocks // 3, blocks // 3)]
    grad_tokens, grad_norm_one = None, 0.0
    while waiting or rest:
        attn_pieces, pieces, extra = [None], None, None
        if waiting:
            low, count = waiting.pop(0)
            attn_pieces = pieces_of(attn_held, low, count)
        sent = {step * low: [flat(attn_pieces[step])] for step in range(1, len(attn_pieces))}
        bit = None
        if rest:
            bit = rest.pop(0)
            pieces = pieces_of(held, bit, 2)
            small_parts = two_parts(small)
            extra = jnp.concatenate([flat(pieces[1]), small_parts], axis=0).reshape(-1, attn_held.shape[-1])
            sent.setdefault(bit, []).append(extra)
        fill = fills.pop(0) if fills else None
        if fill:
            sent, projected_grad = after(sent, projected_grad)
        gots = {step: swap(jnp.concatenate(parts, axis=0), "dp", size, step) for step, parts in sent.items()}
        if fill:
            results = tokens_back(*fill, grad_tokens, projected_grad, tokens, grad_middle, attn_use, norm_w)
            (grad_tokens, norm_one), gots = after(results, gots)
            grad_norm_one = grad_norm_one + norm_one
        if bit:
            got = gots[bit][gots[bit].shape[0] - extra.shape[0] :].reshape(-1, columns)
            held, small = take(pieces, [got], small_parts, bit, 2)
        if attn_pieces[0] is not None:
            attn_held = attn_pieces[0]
            rows = attn_held.size // attn_held.shape[-1]
            for step in range(1, len(attn_pieces)):
                attn_held = attn_held + gots[step * low][:rows].reshape(attn_held.shape).astype(f32)
    grad_attn = unfold_pairs(attn_held.reshape(attn_held.shape[:1] + attn_held.shape[2:]))
    grad_mlp = held.reshape(mlp_w.shape)
    norm_two = small[9, : 2 * width].reshape(2, width)

    weights, firsts, seconds = [attn_w, mlp_w, conv_w], [attn_m, mlp_m, conv_m], [attn_v, mlp_v, conv_v]
    scalars = pl.BlockSpec(memory_space=pltpu.SMEM)
    vectors = pl.BlockSpec(memory_space=pltpu.VMEM)
    results = pl.pallas_call(
        moments_kernel,
        in_specs=[scalars] + [vectors] * 13,
        out_specs=[vectors] * 10,
        out_shape=like(weights) * 3 + [jax.ShapeDtypeStruct((8, width), f32)],
        compiler_params=pltpu.CompilerParams(vmem_limit_bytes=16 * MIB),
    )(place.astype(jnp.int32).reshape(1), grad_norm_one, grad_attn, grad_mlp, small[:9], *weights, *firsts, *seconds)
    new_firsts, new_seconds, updates, sums = results[:3], results[3:6], results[6:9], results[9]
    new_w = pl.pallas_call(
        apply_kernel,
        in_specs=[vectors] * 11,
        out_specs=[vectors] * 6,
        out_shape=like(weights) + like([norm_w] * 3),
        compiler_params=pltpu.CompilerParams(vmem_limit_bytes=16 * MIB),
    )(sum_everywhere(sums, size), norm_two, norm_w, norm_m, norm_v, *weights, *updates)
    return (
        output, grad_tokens, new_w[0], new_firsts[0], new_seconds[0], new_w[1], new_firsts[1], new_seconds[1],
        new_w[2], new_firsts[2], new_seconds[2], *new_w[3:],
    )


def solution(mesh):
    rows, lines = P(("dp", "head"), None), P("dp", None)
    shards, columns = P(None, "dp", "head"), P(None, "head")
    in_specs = (rows, rows, lines, P("dp")) + (shards,) * 6 + (columns,) * 3 + (P(),) * 3
    out_specs = (rows, rows) + (shards,) * 6 + (columns,) * 3 + (P(),) * 3
    return jax.shard_map(
        functools.partial(body, mesh.shape["dp"]), mesh=mesh, in_specs=in_specs, out_specs=out_specs, check_vma=False
    )
```

```python
import functools
import jax
import jax.numpy as jnp
from jax import lax
from jax.experimental import pallas as pl
from jax.experimental.pallas import tpu as pltpu
from jax.sharding import PartitionSpec as P

HEAD_DIM = 64
GRID_W = 16
STEP = 10
IMAGES = 8

NORM_EPS = 1e-06
BETA_ONE = 0.9
BETA_TWO = 0.999
ADAM_EPS = 1e-06
DECAY = 0.01
RATE = 0.5
LOG2E = 1.4426950408889634
LN2 = 0.6931471805599453
BIG = 2.0**100
GELU_ONE = 0.7978845608028654
GELU_TWO = 0.044715
GELU_S = (GELU_ONE * GELU_TWO) ** (1.0 / 3.0)
GELU_A = GELU_ONE / GELU_S
ACT_SCALE = 0.5 / GELU_S
EXTRA = 32
PARTS = 4
TILE = 128
WIDE_TILE = 256
FILL = 512
LANES = 128
STRIDE = GRID_W + 8
MIB = 1024 * 1024

f32 = jnp.float32
bf16 = jnp.bfloat16
NN = (((1,), (0,)), ((), ()))
NT = (((1,), (1,)), ((), ()))
TN = (((0,), (0,)), ((), ()))


def dot(left, right, dims=NN):
    return lax.dot_general(left, right, dims, preferred_element_type=f32)


def work_of(micros):
    return pl.CostEstimate(flops=micros * 1_000_000_000, bytes_accessed=micros * 1_000_000, transcendentals=0)


def widths_for(length):
    return [w for w in (256, 384, 512, 640, 768) if w < length] + [length]


def norm_parts(values):
    average = jnp.mean(values, axis=-1, keepdims=True)
    centered = values - average
    inverse = lax.rsqrt(jnp.mean(centered * centered, axis=-1, keepdims=True) + NORM_EPS)
    return centered * inverse, inverse


def norm_back(upstream, gain_row, unit_rows, inverse):
    grad_unit = upstream * gain_row
    first_term = jnp.mean(grad_unit, axis=-1, keepdims=True)
    second_term = jnp.mean(grad_unit * unit_rows, axis=-1, keepdims=True)
    return inverse * (grad_unit - first_term - unit_rows * second_term)


def fold_rows(values):
    rows, columns = values.shape
    return jnp.sum(values.reshape(rows // 8, 8, columns), axis=0)


def pair_columns(flat):
    empty = jnp.zeros((HEAD_DIM, flat.shape[1]), flat.dtype)
    return jnp.concatenate(
        [jnp.concatenate([flat[:HEAD_DIM], empty], axis=0), jnp.concatenate([empty, flat[HEAD_DIM:]], axis=0)], axis=1
    )


def pair_rows(both):
    half = both.shape[1] // 2
    return jnp.concatenate([both[:HEAD_DIM, :half], both[HEAD_DIM:, half:]], axis=0)


def fold_max(values):
    pieces = [values[at : at + 64] for at in range(0, values.shape[0], 64)]
    while len(pieces) > 1:
        pieces = [jnp.maximum(a, b) for a, b in zip(pieces[::2], pieces[1::2])] + ([pieces[-1]] if len(pieces) % 2 else [])
    top = pieces[0]
    top = jnp.maximum(top[:32], top[32:])
    top = jnp.maximum(top[:16], top[16:])
    return jnp.max(jnp.maximum(top[:8], top[8:]), axis=0, keepdims=True)


def three_parts(value, part):
    high = value.astype(bf16).astype(f32)
    rest = value - high
    middle = rest.astype(bf16).astype(f32)
    return jnp.where(part == 0, high, jnp.where(part == 1, middle, rest - middle))


def image_tags(image_ref, start, rows):
    place = start + lax.broadcasted_iota(jnp.int32, (rows, LANES), 0)
    inside = (place >= image_ref[0, 0:1, :]) & (place < image_ref[0, 1:2, :])
    return jnp.where(inside, 1.0, 0.0).astype(bf16)


def first_norm_kernel(tokens_ref, out_grad_ref, norm_ref, normed_ref, normed_t_ref, out_grad_t_ref):
    big = 256

    def step(at, carry):
        rows = pl.ds(pl.multiple_of(at * big, big), big)
        unit, _ = norm_parts(tokens_ref[rows, :].astype(f32))
        normed_ref[rows, :] = (unit * norm_ref[0:1, :] + norm_ref[1:2, :]).astype(bf16)
        return carry

    lax.fori_loop(0, tokens_ref.shape[0] // big, step, 0)
    normed_t_ref[...] = jnp.transpose(normed_ref[...])
    out_grad_t_ref[...] = jnp.transpose(out_grad_ref[...])


def first_norm(tokens, out_grad, norm_w, row_count):
    rows_all, width = tokens.shape
    length = rows_all // row_count
    by_row = pl.BlockSpec((length, width), lambda r: (r, 0))
    turned = pl.BlockSpec((width, length), lambda r: (r, 0))
    flipped = jax.ShapeDtypeStruct((row_count * width, length), bf16)
    return pl.pallas_call(
        first_norm_kernel,
        grid=(row_count,),
        in_specs=[by_row, by_row, pl.BlockSpec(norm_w.shape, lambda r: (0, 0))],
        out_specs=[by_row, turned, turned],
        out_shape=[jax.ShapeDtypeStruct((rows_all, width), bf16), flipped, flipped],
        cost_estimate=work_of(8),
        compiler_params=pltpu.CompilerParams(vmem_limit_bytes=60 * MIB),
    )(tokens, out_grad, norm_w)


def attn_forward_kernel(
    start_ref, class_ref, count_ref, tokens_ref, normed_ref, w_ref, image_ref,
    middle_ref, qkv_ref, context_ref, ext_ref,
    tag_ref, qt_ref, vt_ref,
):
    row = pl.program_id(0)
    length, width = tokens_ref.shape
    pairs = width // LANES
    tag_ref[...] = image_tags(image_ref, 0, length)
    queries = (dot(normed_ref[...], w_ref[0]) * (HEAD_DIM**-0.5 * LOG2E)).astype(bf16)
    qkv_ref[:, :width] = queries
    qt_ref[...] = jnp.transpose(queries)
    qkv_ref[:, width : 2 * width] = dot(normed_ref[...], w_ref[1]).astype(bf16)
    values = dot(normed_ref[...], w_ref[2]).astype(bf16)
    qkv_ref[:, 2 * width :] = values
    vt_ref[...] = jnp.transpose(values)

    def tile(step, carry):
        q0 = pl.multiple_of(step * WIDE_TILE, WIDE_TILE)
        here = pl.ds(q0, WIDE_TILE)
        place = q0 + lax.broadcasted_iota(jnp.int32, (IMAGES, WIDE_TILE), 1)
        edges = [jnp.concatenate([image_ref[0, at : at + IMAGES, :]] * (WIDE_TILE // LANES), axis=1) for at in (8, 16)]
        inside = (place >= edges[0]) & (place < edges[1])
        mask = jnp.where(inside, 0.0, -BIG)
        mask_low = jnp.concatenate([mask, jnp.zeros((LANES - IMAGES, WIDE_TILE), f32)], axis=0).astype(bf16)
        ext_rows = lax.broadcasted_iota(jnp.int32, (EXTRA - IMAGES, WIDE_TILE), 0)

        def attend(window):
            there = pl.ds(pl.multiple_of(start_ref[row, step], LANES), window)
            tags = tag_ref[there, :]
            ones = jnp.ones((GRID_W, window), bf16)
            extra = jnp.zeros((EXTRA - IMAGES, WIDE_TILE), f32)
            slices = [slice(p * LANES, (p + 1) * LANES) for p in range(pairs)]
            masks = jnp.concatenate([mask_low, mask_low], axis=1)
            scores, tops, exponents, mixes = [], [], [], []
            for p, at in enumerate(slices):
                keys = qkv_ref[there, width + p * LANES : width + (p + 1) * LANES]
                right = jnp.concatenate([pair_columns(qt_ref[at, here]), masks], axis=0)
                scores.append(dot(jnp.concatenate([keys, tags], axis=1), right))
            for p in range(pairs):
                tops.append(fold_max(scores[p]))
                exponents.append(jnp.exp2(scores[p] - tops[p]).astype(bf16))
            for p, at in enumerate(slices):
                mixes.append(dot(jnp.concatenate([vt_ref[at, there], ones], axis=0), exponents[p]))
            for p, at in enumerate(slices):
                mixed = mixes[p]
                total = mixed[LANES : LANES + 1, :]
                minus_lse = -(tops[p] + jnp.log(total) * LOG2E)
                scale = 1.0 / total
                lane = lax.broadcasted_iota(jnp.int32, (1, 2 * WIDE_TILE), 1)
                head = 2 * p + jnp.where(lane < WIDE_TILE, 0, 1)
                scale = jnp.where(head < count_ref[row], scale, 0.0)
                context_ref[here, at] = jnp.transpose(pair_rows(mixed[:LANES] * scale)).astype(bf16)
                for h in range(2):
                    value = minus_lse[:, h * WIDE_TILE : (h + 1) * WIDE_TILE]
                    first = 6 * p + 3 * h
                    extra = jnp.where(
                        (ext_rows >= first) & (ext_rows < first + 3), three_parts(value, ext_rows - first), extra
                    )
            ext_ref[:, here] = jnp.concatenate([mask, extra], axis=0).astype(bf16)

        for index, window in enumerate(widths_for(length)):
            pl.when(class_ref[row, step] == index)(functools.partial(attend, window))
        return carry

    lax.fori_loop(0, length // WIDE_TILE, tile, 0)
    middle_ref[...] = tokens_ref[...].astype(f32) + dot(context_ref[...], w_ref[3], NT)


def attn_forward(starts, classes, counts, tokens, normed, attn_use, images):
    rows_all, width = tokens.shape
    row_count = counts.shape[0]
    length = rows_all // row_count
    by_row = lambda columns: pl.BlockSpec((length, columns), lambda r, *_: (r, 0))
    return pl.pallas_call(
        attn_forward_kernel,
        grid_spec=pltpu.PrefetchScalarGridSpec(
            num_scalar_prefetch=3,
            grid=(row_count,),
            in_specs=[
                by_row(width),
                by_row(width),
                pl.BlockSpec(attn_use.shape, lambda r, *_: (0, 0, 0)),
                pl.BlockSpec((1, 24, LANES), lambda r, *_: (r, 0, 0)),
            ],
            out_specs=[
                by_row(width), by_row(3 * width), by_row(width), pl.BlockSpec((EXTRA, length), lambda r, *_: (r, 0))
            ],
            scratch_shapes=[
                pltpu.VMEM((length, LANES), bf16),
                pltpu.VMEM((width, length), bf16),
                pltpu.VMEM((width, length), bf16),
            ],
        ),
        out_shape=[
            jax.ShapeDtypeStruct((rows_all, width), f32),
            jax.ShapeDtypeStruct((rows_all, 3 * width), bf16),
            jax.ShapeDtypeStruct((rows_all, width), bf16),
            jax.ShapeDtypeStruct((row_count * EXTRA, length), bf16),
        ],
        cost_estimate=work_of(30),
        compiler_params=pltpu.CompilerParams(vmem_limit_bytes=56 * MIB),
    )(starts, classes, counts, tokens, normed, attn_use, images)


def attn_backward_kernel(
    first, final, start_ref, class_ref, count_ref, rank_ref, normed_t_ref, middle_grad_ref, qkv_ref, context_ref, ext_ref, w_ref,
    image_ref, *refs,
):
    sums = None
    if first:
        sums, refs = refs[1], refs[2:]
    sent = None
    if final:
        proj_ref, keep_ref, send_ref, *scratch, w_grad_ref = refs
        sent = (keep_ref, send_ref)
    else:
        proj_ref, w_grad_ref, *scratch = refs
    attn_backward_row(
        first, sums, sent, start_ref, class_ref, count_ref, rank_ref, normed_t_ref, middle_grad_ref, qkv_ref, context_ref, ext_ref,
        w_ref, image_ref, proj_ref, w_grad_ref, *scratch,
    )


def attn_backward_row(
    first, sums, sent, start_ref, class_ref, count_ref, rank_ref, normed_t_ref, middle_grad_ref, qkv_ref, context_ref, ext_ref, w_ref,
    image_ref, proj_ref, w_grad_ref,
    tag_ref, up_ref, delta_ref, dq_ref, dk_ref, dv_ref, low_ref, qt_ref, kt_ref, upt_ref,
):
    step_at = pl.program_id(0)
    row = first + step_at
    length, width = middle_grad_ref.shape
    pairs = width // LANES
    big = 256

    @pl.when(step_at == 0)
    def _():
        w_grad_ref[...] = jnp.zeros_like(w_grad_ref) if sums is None else sums[...]

    target = lax.broadcasted_iota(jnp.int32, (EXTRA, width), 0) - IMAGES
    source = lax.broadcasted_iota(jnp.int32, (EXTRA, width), 1) // HEAD_DIM * 3
    collect = jnp.where((target >= source) & (target < source + 3), -1.0, 0.0).astype(bf16)
    active = jnp.where(
        lax.broadcasted_iota(jnp.int32, (1, width), 1) // HEAD_DIM < count_ref[row], 1.0, 0.0
    )

    def prepare(step, carry):
        rows = pl.ds(pl.multiple_of(step * big, big), big)
        tag_ref[rows, :] = image_tags(image_ref, step * big, big)
        low_ref[rows, :] = middle_grad_ref[rows, :].astype(bf16)
        dk_ref[rows, :] = jnp.zeros((big, width), f32)
        dv_ref[rows, :] = jnp.zeros((big, width), f32)
        return carry

    lax.fori_loop(0, length // big, prepare, 0)
    up = (dot(low_ref[...], w_ref[3]) * active).astype(bf16)
    up_ref[...] = up
    upt_ref[...] = jnp.transpose(up)
    qt_ref[...] = jnp.transpose(qkv_ref[:, :width])
    kt_ref[...] = jnp.transpose(qkv_ref[:, width : 2 * width])

    def gather(step, carry):
        rows = pl.ds(pl.multiple_of(step * big, big), big)
        product = up_ref[rows, :].astype(f32) * context_ref[rows, :].astype(f32)
        high = product.astype(bf16)
        rest = (product - high.astype(f32)).astype(bf16)
        delta = dot(collect, high, NT) + dot(collect, rest, NT)
        part = lax.rem(lax.broadcasted_iota(jnp.int32, (EXTRA, big), 0) + 3 * EXTRA - IMAGES, 3)
        delta_ref[:, rows] = three_parts(delta, part).astype(bf16)
        return carry

    lax.fori_loop(0, length // big, gather, 0)
    lane = lax.broadcasted_iota(jnp.int32, (1, LANES), 1)
    first_half = jnp.where(lane < HEAD_DIM, 1.0, 0.0).astype(bf16)
    second_half = jnp.where(lane >= HEAD_DIM, 1.0, 0.0).astype(bf16)

    def tile(step, carry):
        q0 = pl.multiple_of(step * TILE, TILE)
        here = pl.ds(q0, TILE)

        def attend(window):
            there = pl.ds(pl.multiple_of(start_ref[row, step], LANES), window)
            tags = tag_ref[there, :]
            ext = ext_ref[:, here]
            delta = delta_ref[:, here]
            at_row = lax.broadcasted_iota(jnp.int32, (EXTRA, LANES), 0)
            empty = jnp.zeros((LANES - EXTRA, 2 * TILE), bf16)

            def own(edge, masks):
                keep = (at_row >= edge) & (at_row < edge + 3)
                return jnp.where(keep | (at_row < IMAGES) if masks else keep, 1.0, 0.0).astype(bf16)

            slices = [slice(p * LANES, (p + 1) * LANES) for p in range(pairs)]
            scores, grad_probs, probs, grad_scores = [], [], [], []
            for p, at in enumerate(slices):
                keys = qkv_ref[there, width + p * LANES : width + (p + 1) * LANES]
                values = qkv_ref[there, 2 * width + p * LANES : 2 * width + (p + 1) * LANES]
                edge = IMAGES + 6 * p
                q_side = jnp.concatenate(
                    [
                        pair_columns(qt_ref[at, here]),
                        jnp.concatenate([ext * own(edge, True), ext * own(edge + 3, True)], axis=1),
                        empty,
                    ],
                    axis=0,
                )
                up_side = jnp.concatenate(
                    [
                        pair_columns(upt_ref[at, here]),
                        jnp.concatenate([delta * own(edge, False), delta * own(edge + 3, False)], axis=1),
                        empty,
                    ],
                    axis=0,
                )
                scores.append(dot(jnp.concatenate([keys, tags], axis=1), q_side))
                grad_probs.append(dot(jnp.concatenate([values, tags], axis=1), up_side))
            for p in range(pairs):
                weight = jnp.exp2(scores[p])
                probs.append(weight.astype(bf16))
                grad_scores.append((weight * grad_probs[p]).astype(bf16))
            for p, at in enumerate(slices):
                queries, ups = qkv_ref[here, at], up_ref[here, at]
                q_pair = jnp.concatenate([queries * first_half, queries * second_half], axis=0)
                up_pair = jnp.concatenate([ups * first_half, ups * second_half], axis=0)
                dv_ref[there, at] += dot(probs[p], up_pair)
                dk_ref[there, at] += dot(grad_scores[p], q_pair)
                dq = pair_rows(dot(kt_ref[at, there], grad_scores[p]))
                dq_ref[here, at] = jnp.transpose(dq * HEAD_DIM**-0.5).astype(bf16)

        for index, window in enumerate(widths_for(length)):
            pl.when(class_ref[row, step] == index)(functools.partial(attend, window))
        return carry

    lax.fori_loop(0, length // TILE, tile, 0)
    keys_grad = (dk_ref[...] * LN2).astype(bf16)
    values_grad = dv_ref[...].astype(bf16)
    proj_ref[...] = jnp.concatenate([dq_ref[...], keys_grad, values_grad], axis=1)
    for k in range(3):
        w_grad_ref[k] += dot(normed_t_ref[...], proj_ref[:, k * width : (k + 1) * width])
    w_grad_ref[3] += dot(jnp.transpose(low_ref[...]), context_ref[...])
    if sent:

        @pl.when(step_at == pl.num_programs(0) - 1)
        def _():
            for k in range(2):
                one, two = w_grad_ref[k], w_grad_ref[k + 2]
                halves = [jnp.concatenate([one[:, at : at + width // 2], two[:, at : at + width // 2]], axis=1) for at in (0, width // 2)]
                sent[0][k] = jnp.where(rank_ref[0] == 0, halves[0], halves[1])
                sent[1][k] = jnp.where(rank_ref[0] == 0, halves[1], halves[0]).astype(bf16)


def attn_backward(first, count, so_far, starts, classes, counts, rank, normed_t, middle_grad, qkv, context, ext, attn_use, images):
    rows_all, width = middle_grad.shape
    length = rows_all // counts.shape[0]
    by_row = lambda columns: pl.BlockSpec((length, columns), lambda r, *_: (first + r, 0))
    final = first + count == counts.shape[0]
    half = (2, width, width)
    halves = pl.BlockSpec(half, lambda r, *_: (0, 0, 0))
    whole = pl.BlockSpec(attn_use.shape, lambda r, *_: (0, 0, 0))
    return pl.pallas_call(
        functools.partial(attn_backward_kernel, first, final),
        grid_spec=pltpu.PrefetchScalarGridSpec(
            num_scalar_prefetch=4,
            grid=(count,),
            in_specs=[
                pl.BlockSpec((width, length), lambda r, *_: (first + r, 0)),
                by_row(width),
                by_row(3 * width),
                by_row(width),
                pl.BlockSpec((EXTRA, length), lambda r, *_: (first + r, 0)),
                whole,
                pl.BlockSpec((1, 24, LANES), lambda r, *_: (first + r, 0, 0)),
            ]
            + ([pl.BlockSpec(memory_space=pl.ANY), whole] if first else []),
            out_specs=[by_row(3 * width)] + ([halves, halves] if final else [whole]),
            scratch_shapes=[
                pltpu.VMEM((length, LANES), bf16),
                pltpu.VMEM((length, width), bf16),
                pltpu.VMEM((EXTRA, length), bf16),
                pltpu.VMEM((length, width), bf16),
                pltpu.VMEM((length, width), f32),
                pltpu.VMEM((length, width), f32),
                pltpu.VMEM((length, width), bf16),
                pltpu.VMEM((width, length), bf16),
                pltpu.VMEM((width, length), bf16),
                pltpu.VMEM((width, length), bf16),
            ]
            + ([pltpu.VMEM(attn_use.shape, f32)] if final else []),
        ),
        out_shape=[jax.ShapeDtypeStruct((rows_all, 3 * width), bf16)]
        + (
            [jax.ShapeDtypeStruct(half, f32), jax.ShapeDtypeStruct(half, bf16)]
            if final
            else [jax.ShapeDtypeStruct(attn_use.shape, f32)]
        ),
        input_output_aliases={11: 0} if first else {},
        cost_estimate=work_of(18 * count),
        compiler_params=pltpu.CompilerParams(vmem_limit_bytes=50 * MIB),
    )(starts, classes, counts, rank, normed_t, middle_grad, qkv, context, ext, attn_use, images, *(so_far or ()))


def tokens_back_kernel(proj_ref, tokens_ref, middle_grad_ref, w_ref, norm_ref, *refs):
    tokens_grad_ref, norm_grad_ref = refs[-2:]

    @pl.when(pl.program_id(0) == 0)
    def _():
        norm_grad_ref[...] = jnp.zeros_like(norm_grad_ref)

    w_cat = jnp.concatenate([w_ref[0], w_ref[1], w_ref[2]], axis=1)
    upstream = dot(proj_ref[...], w_cat, NT)
    unit, inverse = norm_parts(tokens_ref[...].astype(f32))
    tokens_grad_ref[...] = middle_grad_ref[...] + norm_back(upstream, norm_ref[0:1, :], unit, inverse)
    norm_grad_ref[0:8, :] += fold_rows(upstream * unit)
    norm_grad_ref[8:16, :] += fold_rows(upstream)


def tokens_back(first, count, so_far, proj, tokens, middle_grad, attn_use, norm_w):
    rows_all, width = tokens.shape
    some = lambda columns: pl.BlockSpec((FILL, columns), lambda r: (first + r, 0))
    return pl.pallas_call(
        tokens_back_kernel,
        grid=(count,),
        in_specs=[
            some(3 * width),
            some(width),
            some(width),
            pl.BlockSpec(attn_use.shape, lambda r: (0, 0, 0)),
            pl.BlockSpec(norm_w.shape, lambda r: (0, 0)),
        ]
        + ([] if so_far is None else [pl.BlockSpec(memory_space=pl.ANY)]),
        out_specs=[some(width), pl.BlockSpec((16, width), lambda r: (0, 0))],
        out_shape=[jax.ShapeDtypeStruct((rows_all, width), f32), jax.ShapeDtypeStruct((16, width), f32)],
        input_output_aliases={} if so_far is None else {5: 0},
        cost_estimate=work_of(2 * count),
        compiler_params=pltpu.CompilerParams(vmem_limit_bytes=60 * MIB),
    )(proj, tokens, middle_grad, attn_use, norm_w, *([] if so_far is None else [so_far]))


def mlp_kernel(
    place_ref, rank_ref, middle_ref, out_grad_ref, out_grad_t_ref, own_w_ref, other_w_ref, taps_ref, norm_ref,
    output_ref, middle_grad_ref, keep_ref, send_ref, taps_grad_ref, norm_grad_ref,
    w_ref, w_grad_ref, unit_ref, inverse_ref, normed_ref, normed_t_ref, out_sum_ref, up_sum_ref, tap_sum_ref,
    act_grads_ref, acts_ref, hidden_grads_ref, *buffers,
):
    row = pl.program_id(0)
    length, width = middle_ref.shape
    hidden = w_ref.shape[2]
    chunk = PARTS * LANES
    big = 256
    grid_rows = length // GRID_W
    chunks = hidden // chunk
    h_refs, g_refs = buffers[:PARTS], buffers[PARTS:]
    gain, bias = norm_ref[2:3, :], norm_ref[3:4, :]

    @pl.when(row == 0)
    def _():
        w_grad_ref[...] = jnp.zeros_like(w_grad_ref)
        norm_grad_ref[...] = jnp.zeros_like(norm_grad_ref)
        tap_sum_ref[...] = jnp.zeros_like(tap_sum_ref)
        for rank, halves in enumerate(((own_w_ref, other_w_ref), (other_w_ref, own_w_ref))):

            @pl.when(rank_ref[0] == rank)
            def _():
                w_ref[:, :, : hidden // 2] = halves[0][...]
                w_ref[:, :, hidden // 2 :] = halves[1][...]

        for ref in buffers:
            ref[...] = jnp.zeros_like(ref)

    def place(r):
        return pl.multiple_of(place_ref[row, r], 8)

    for n in range(IMAGES + 1):
        at = place(grid_rows + n)
        for ref in buffers:
            ref[pl.ds(at, GRID_W), :] = jnp.zeros((GRID_W, LANES), f32)

    def normalize(step, carry):
        rows = pl.ds(pl.multiple_of(step * big, big), big)
        middle = middle_ref[rows, :]
        unit, inverse = norm_parts(middle)
        unit_ref[rows, :] = unit
        inverse_ref[rows, :] = jnp.broadcast_to(inverse, (big, LANES))
        normed_ref[rows, :] = (unit * gain + bias).astype(bf16)
        out_sum_ref[rows, :] = jnp.zeros((big, width), f32)
        up_sum_ref[rows, :] = jnp.zeros((big, width), f32)
        return carry

    lax.fori_loop(0, length // big, normalize, 0)
    normed_t_ref[...] = jnp.transpose(normed_ref[...])

    def lanes_of(c):
        return pl.ds(pl.multiple_of(c * chunk, chunk), chunk)

    def lanes_of(c):
        return pl.ds(pl.multiple_of(c * chunk, chunk), chunk)

    def neighbours(ref, at):
        return [ref[pl.ds(at + (a * STRIDE + b), GRID_W), :] for a in (-1, 0, 1) for b in (-1, 0, 1)]

    def tall(values):
        return jnp.concatenate([values, values], axis=0)

    def total_of(terms):
        while len(terms) > 1:
            terms = [a + b for a, b in zip(terms[::2], terms[1::2])] + ([terms[-1]] if len(terms) % 2 else [])
        return terms[0]

    def taps_for(c, part, at):
        lane = pl.ds(pl.multiple_of(c * chunk + part * LANES, LANES), LANES)
        return [tall(taps_ref[at + k * 8 : at + (k + 1) * 8, lane]) for k in range(9)]

    lines = 8

    def do_chunk(c, carry):
        lanes = lanes_of(c)
        for t in range(length // big):
            rows = slice(t * big, (t + 1) * big)
            values = dot(normed_ref[rows, :], w_ref[0, :, lanes])
            for part in range(PARTS):
                for s in range(big // GRID_W):
                    at = place(t * (big // GRID_W) + s)
                    h_refs[part][pl.ds(at, GRID_W), :] = values[
                        s * GRID_W : (s + 1) * GRID_W, part * LANES : (part + 1) * LANES
                    ]
        act_grads_ref[...] = dot(out_grad_ref[...], w_ref[1, :, lanes])

        def forward(t, carry):
            tokens_base = pl.multiple_of(t * (lines * GRID_W), lines * GRID_W)
            for part in range(PARTS):
                taps = taps_for(c, part, 0)
                cols = slice(part * LANES, (part + 1) * LANES)
                for s in range(lines):
                    near = pl.ds(pl.multiple_of(tokens_base + s * GRID_W, GRID_W), GRID_W)
                    at = place(t * lines + s)
                    x = total_of([x * tap for x, tap in zip(neighbours(h_refs[part], at), taps)])
                    square = x * x
                    value = jnp.tanh(x * (GELU_A + square))
                    gate = 1.0 + value
                    twice = x * gate
                    acts_ref[near, cols] = twice.astype(bf16)
                    slope = gate + (twice * (1.0 - value)) * (GELU_A + 3.0 * square)
                    g_refs[part][pl.ds(at, GRID_W), :] = act_grads_ref[near, cols] * slope
            return carry

        lax.fori_loop(0, grid_rows // lines, forward, 0)

        def backward(t, carry):
            tokens_base = pl.multiple_of(t * (lines * GRID_W), lines * GRID_W)
            for part in range(PARTS):
                taps = taps_for(c, part, 72)
                lane = pl.ds(pl.multiple_of(c * chunk + part * LANES, LANES), LANES)
                cols = slice(part * LANES, (part + 1) * LANES)
                totals = [None] * 9
                for s in range(lines):
                    near = pl.ds(pl.multiple_of(tokens_base + s * GRID_W, GRID_W), GRID_W)
                    at = place(t * lines + s)
                    source = h_refs[part][pl.ds(at, GRID_W), :]
                    moved = neighbours(g_refs[part], at)[::-1]
                    for k in range(9):
                        product = source * moved[k]
                        folded = product[:8] + product[8:]
                        totals[k] = folded if totals[k] is None else totals[k] + folded
                    terms = [x * tap for x, tap in zip(moved, taps)]
                    hidden_grads_ref[near, cols] = total_of(terms).astype(bf16)
                for k in range(9):
                    tap_sum_ref[k * 8 : (k + 1) * 8, lane] += totals[k]
            return carry

        lax.fori_loop(0, grid_rows // lines, backward, 0)
        w_grad_ref[0, :, lanes] += dot(normed_t_ref[...], hidden_grads_ref[...])
        w_grad_ref[1, :, lanes] += dot(out_grad_t_ref[...], acts_ref[...])
        out_sum_ref[...] += dot(acts_ref[...], w_ref[1, :, lanes], NT)
        up_sum_ref[...] += dot(hidden_grads_ref[...], w_ref[0, :, lanes], NT)
        return carry

    lax.fori_loop(0, chunks, do_chunk, 0)

    def finish(step, carry):
        rows = pl.ds(pl.multiple_of(step * big, big), big)
        middle = middle_ref[rows, :]
        output_ref[rows, :] = (middle + ACT_SCALE * out_sum_ref[rows, :]).astype(bf16)
        upstream = 0.5 * up_sum_ref[rows, :]
        unit = unit_ref[rows, :]
        inverse = jnp.concatenate([inverse_ref[rows, :]] * (width // LANES), axis=1)
        middle_grad_ref[rows, :] = out_grad_ref[rows, :].astype(f32) + norm_back(upstream, gain, unit, inverse)
        norm_grad_ref[0:8, :] += fold_rows(upstream * unit)
        norm_grad_ref[8:16, :] += fold_rows(upstream)
        return carry

    lax.fori_loop(0, length // big, finish, 0)

    @pl.when(row == pl.num_programs(0) - 1)
    def _():
        for k, scale in enumerate((0.5, ACT_SCALE)):
            halves = w_grad_ref[k, :, : hidden // 2], w_grad_ref[k, :, hidden // 2 :]
            keep_ref[k] = scale * jnp.where(rank_ref[0] == 0, halves[0], halves[1])
            send_ref[k] = (scale * jnp.where(rank_ref[0] == 0, halves[1], halves[0])).astype(bf16)
        taps_grad_ref[...] = jnp.zeros_like(taps_grad_ref)
        for k in range(9):
            total = jnp.sum(tap_sum_ref[k * 8 : (k + 1) * 8, :], axis=0, keepdims=True)
            taps_grad_ref[k : k + 1, :] = 0.5 * total


def mlp_layer(places, rank, middle, out_grad, out_grad_t, own_w, other_w, taps, norm_w):
    rows_all, width = middle.shape
    row_count = places.shape[0]
    length = rows_all // row_count
    half = own_w.shape
    hidden = 2 * half[2]
    whole = half[:2] + (hidden,)
    by_row = lambda columns: pl.BlockSpec((length, columns), lambda r, *_: (r, 0))
    slots = (length // GRID_W + IMAGES + 2) * STRIDE
    return pl.pallas_call(
        mlp_kernel,
        grid_spec=pltpu.PrefetchScalarGridSpec(
            num_scalar_prefetch=2,
            grid=(row_count,),
            in_specs=[
                by_row(width),
                by_row(width),
                pl.BlockSpec((width, length), lambda r, *_: (r, 0)),
                pl.BlockSpec(half, lambda r, *_: (0, 0, 0)),
                pl.BlockSpec(half, lambda r, *_: (0, 0, 0)),
                pl.BlockSpec(taps.shape, lambda r, *_: (0, 0)),
                pl.BlockSpec(norm_w.shape, lambda r, *_: (0, 0)),
            ],
            out_specs=[
                by_row(width),
                by_row(width),
                pl.BlockSpec(half, lambda r, *_: (0, 0, 0)),
                pl.BlockSpec(half, lambda r, *_: (0, 0, 0)),
                pl.BlockSpec((16, hidden), lambda r, *_: (0, 0)),
                pl.BlockSpec((16, width), lambda r, *_: (0, 0)),
            ],
            scratch_shapes=[
                pltpu.VMEM(whole, bf16),
                pltpu.VMEM(whole, f32),
                pltpu.VMEM((length, width), f32),
                pltpu.VMEM((length, LANES), f32),
                pltpu.VMEM((length, width), bf16),
                pltpu.VMEM((width, length), bf16),
                pltpu.VMEM((length, width), f32),
                pltpu.VMEM((length, width), f32),
                pltpu.VMEM((9 * 8, hidden), f32),
                pltpu.VMEM((length, PARTS * LANES), f32),
                pltpu.VMEM((length, PARTS * LANES), bf16),
                pltpu.VMEM((length, PARTS * LANES), bf16),
            ]
            + [pltpu.VMEM((slots, LANES), f32)] * (2 * PARTS),
        ),
        out_shape=[
            jax.ShapeDtypeStruct((rows_all, width), bf16),
            jax.ShapeDtypeStruct((rows_all, width), f32),
            jax.ShapeDtypeStruct(half, f32),
            jax.ShapeDtypeStruct(half, bf16),
            jax.ShapeDtypeStruct((16, hidden), f32),
            jax.ShapeDtypeStruct((16, width), f32),
        ],
        cost_estimate=work_of(90),
        compiler_params=pltpu.CompilerParams(vmem_limit_bytes=50 * MIB),
    )(places, rank, middle, out_grad, out_grad_t, own_w, other_w, taps, norm_w)


def attention_plan(segments, tile):
    row_count, length = segments.shape
    tiles = segments.reshape(row_count, length // tile, tile)
    first, last = tiles[:, :, 0], tiles[:, :, -1]
    ids = jnp.arange(IMAGES, dtype=jnp.int32)
    begins = jnp.sum((segments[:, None, :] < ids[None, :, None]).astype(jnp.int32), axis=-1)
    ends = jnp.sum((segments[:, None, :] <= ids[None, :, None]).astype(jnp.int32), axis=-1)
    low_end = jnp.sum(jnp.where(first[:, :, None] == ids, begins[:, None, :], 0), axis=-1) // LANES * LANES
    high_end = jnp.sum(jnp.where(last[:, :, None] == ids, ends[:, None, :], 0), axis=-1)
    widths = widths_for(length)
    classes = sum(((high_end - low_end) > w).astype(jnp.int32) for w in widths[:-1])
    chosen = jnp.full_like(classes, widths[-1])
    for index, w in enumerate(widths):
        chosen = jnp.where(classes == index, w, chosen)
    starts = jnp.minimum(low_end, length - chosen)
    used = jnp.zeros((row_count, EXTRA - IMAGES), jnp.int32)
    unused = jnp.zeros((row_count, LANES - EXTRA), jnp.int32)
    first_lane = jnp.concatenate([begins, used, unused], axis=1)
    end_lane = jnp.concatenate([ends, used + length, unused], axis=1)
    by_lane = jnp.pad(jnp.stack([first_lane, end_lane], axis=1), ((0, 0), (0, 6), (0, 0)))
    by_image = jnp.broadcast_to(jnp.concatenate([begins, ends], axis=1)[:, :, None], (row_count, 2 * IMAGES, LANES))
    return starts, classes, jnp.concatenate([by_lane, by_image], axis=1)


def spread_taps(conv_use):
    taps = conv_use.astype(f32)
    own = (jnp.arange(9) == 4).astype(f32)[:, None]
    taps = jnp.repeat(taps + own, 8, axis=0)
    return jnp.concatenate([taps * GELU_S, taps], axis=0)


def line_places(segments):
    ids = segments[:, ::GRID_W]
    count = ids.shape[1]
    rows = jnp.arange(count, dtype=jnp.int32) + ids + 1
    images = jnp.arange(IMAGES, dtype=jnp.int32)
    first = jnp.sum((ids[:, None, :] < images[None, :, None]).astype(jnp.int32), axis=-1)
    gaps = jnp.concatenate([first + images, jnp.full((ids.shape[0], 1), count + IMAGES, jnp.int32)], axis=1)
    return jnp.concatenate([rows, gaps], axis=1) * STRIDE + 8


def bits_of(size):
    bits = []
    b = 1
    while b < size:
        bits.append(b)
        b *= 2
    return bits


def groups_of(size):
    bits = bits_of(size)
    return [(bits[at], 1 << len(bits[at : at + 2])) for at in range(0, len(bits), 2)]


def swap(values, axis, size, bit):
    return lax.ppermute(values, axis, [(i, i ^ bit) for i in range(size)])


def in_order(found, mine):
    ordered = []
    for target in range(len(found)):
        value = found[0]
        for step in range(1, len(found)):
            value = jnp.where((mine ^ step) == target, found[step], value)
        ordered.append(value)
    return ordered


def start_group(held, size, low, count):
    return [held] + [swap(held, "dp", size, step * low) for step in range(1, count)]


def finish_stack(found, low, count):
    held = jnp.stack(in_order(found, (lax.axis_index("dp") // low) % count), axis=1)
    return held.reshape((-1,) + held.shape[2:])


def finish_group(found, low, count):
    held = jnp.stack(in_order(found, (lax.axis_index("dp") // low) % count))
    return held.reshape((-1,) + held.shape[2:])


def fold_pairs(values):
    count = values.shape[0] // 2
    return jnp.concatenate([values[:count], values[count:]], axis=-1)


def unfold_pairs(values):
    half = values.shape[-1] // 2
    return jnp.concatenate([values[..., :half], values[..., half:]], axis=0)


def join_columns(mine, other, rank):
    first = jnp.where(rank == 0, mine, other)
    second = jnp.where(rank == 0, other, mine)
    return jnp.concatenate([first, second], axis=-1)


def join_weights(mine, other, rank, count):
    lines, _, part, columns = mine.shape
    half = columns // 2
    full = [join_columns(mine[..., at : at + half], other[..., at : at + half], rank) for at in (0, half)]
    return jnp.moveaxis(jnp.concatenate(full, axis=1), 0, 1).reshape(count, lines * part, columns)


def half_columns(values, side):
    half = values.shape[-1] // 2
    return lax.dynamic_slice_in_dim(values, side * half, half, axis=values.ndim - 1)


def by_line(values, size):
    count, rows, columns = values.shape
    return values.reshape(count, size, rows // size, columns)


def two_parts(values):
    high = values.astype(bf16)
    return jnp.concatenate([high, (values - high.astype(f32)).astype(bf16)], axis=0)


def from_parts(parts):
    count = parts.shape[0] // 2
    return parts[:count].astype(f32) + parts[count:].astype(f32)


def pieces_of(held, low, count):
    n, lines = held.shape[:2]
    split = held.reshape((n, lines // count, count) + held.shape[2:])
    mine = (lax.axis_index("dp") // low) % count
    return [lax.dynamic_index_in_dim(split, mine ^ step, 2, keepdims=False) for step in range(count)]


def flat(values):
    return values.astype(bf16).reshape(-1, values.shape[-1])


def sum_everywhere(values, size):
    values = values + swap(values, "head", 2, 1)
    for bit in bits_of(size):
        values = values + swap(values, "dp", size, bit)
    return values


def after(first, second):
    return lax.optimization_barrier((first, second))


def adam_terms(grad_sum, first_old, second):
    first_new = BETA_ONE * first_old + (1.0 - BETA_ONE) * grad_sum
    second_new = BETA_TWO * second + (1.0 - BETA_TWO) * grad_sum * grad_sum
    direction = (
        first_new
        / (1.0 - BETA_ONE**STEP)
        / (jnp.sqrt(second_new / (1.0 - BETA_TWO**STEP)) + ADAM_EPS)
    )
    return (first_new, second_new, direction)


def moments_kernel(line_ref, norm_ref, *refs):
    count = 3
    grads, weights, firsts, seconds = (refs[n * count : (n + 1) * count] for n in range(4))
    new_firsts, new_seconds, updates = (refs[(4 + n) * count : (5 + n) * count] for n in range(3))
    sums_ref = refs[7 * count]
    width = sums_ref.shape[1]
    lane = lax.broadcasted_iota(jnp.int32, (1, width), 1)
    rows = [jnp.zeros((1, width), f32), jnp.zeros((1, width), f32)]
    at = 0
    for n in range(count):
        grad, weight = grads[n][...], weights[n][...]
        new_first, new_second, direction = adam_terms(grad, firsts[n][...], seconds[n][...])
        update = direction + DECAY * weight
        new_firsts[n][...], new_seconds[n][...], updates[n][...] = new_first, new_second, update
        matrices = weight.shape[0] if weight.ndim == 3 else 1
        for k in range(matrices):
            for row, values in enumerate((weight, update)):
                values = values[k] if weight.ndim == 3 else values
                total = jnp.sum(jnp.sum(values * values, axis=0, keepdims=True), axis=1, keepdims=True)
                if weight.ndim == 2:
                    total = jnp.where(line_ref[0] == 0, total, 0.0)
                rows[row] = jnp.where(lane == at, total, rows[row])
            at += 1
    gain = jnp.sum(norm_ref[0:8, :], axis=0, keepdims=True)
    bias = jnp.sum(norm_ref[8:16, :], axis=0, keepdims=True)
    sums_ref[...] = jnp.concatenate(rows + [gain, bias, jnp.zeros((4, width), f32)], axis=0)


def apply_kernel(sums_ref, norm_two_ref, norm_w_ref, norm_m_ref, norm_v_ref, *refs):
    count = 3
    weights, updates, news = (refs[n * count : (n + 1) * count] for n in range(3))
    new_norm_w_ref, new_norm_m_ref, new_norm_v_ref = refs[3 * count :]
    ratio = jnp.sqrt(sums_ref[0:1, :]) / jnp.sqrt(sums_ref[1:2, :])
    at = 0
    for n in range(count):
        shape = weights[n].shape
        if len(shape) == 3:
            for k in range(shape[0]):
                news[n][k] = weights[n][k] - RATE * ratio[:, at : at + 1] * updates[n][k]
                at += 1
        else:
            news[n][...] = weights[n][...] - RATE * ratio[:, at : at + 1] * updates[n][...]
            at += 1
    grads = jnp.concatenate([sums_ref[2:4, :], norm_two_ref[...]], axis=0)
    new_first, new_second, direction = adam_terms(grads, norm_m_ref[...], norm_v_ref[...])
    new_norm_m_ref[...], new_norm_v_ref[...] = new_first, new_second
    new_norm_w_ref[...] = norm_w_ref[...] - RATE * direction


def like(values):
    return [jax.ShapeDtypeStruct(v.shape, f32) for v in values]


def body(
    size,
    tokens, grad_out, segments, counts,
    attn_w, attn_m, attn_v, mlp_w, mlp_m, mlp_v, conv_w, conv_m, conv_v, norm_w, norm_m, norm_v,
):
    rank = lax.axis_index("head")
    place = lax.axis_index("dp")
    own_rows = segments.shape[0] // 2
    segments = lax.dynamic_slice_in_dim(segments, rank * own_rows, own_rows, axis=0)
    counts = lax.dynamic_slice_in_dim(counts, rank * own_rows, own_rows, axis=0)
    width = norm_w.shape[1]
    groups = groups_of(size)
    attn_lines = fold_pairs(attn_w.astype(bf16))[None]
    mlp_lines = mlp_w.astype(bf16)[None]
    for near, far in zip(groups[:-1], groups[:0:-1]):
        found, more = start_group(attn_lines, size, *far), start_group(mlp_lines, size, *near)
        attn_lines, mlp_lines = finish_stack(found, *far), finish_group(more, *near)
    attn_lines, early = after(attn_lines, (tokens, grad_out))
    found = start_group(attn_lines, size, *groups[0])
    (normed, normed_t, out_grad_t), found = after(first_norm(*early, norm_w, own_rows), found)
    attn_lines = finish_stack(found, *groups[0])
    attn_use = join_weights(attn_lines, swap(attn_lines, "head", 2, 1), rank, attn_w.shape[0])
    found = start_group(mlp_lines, size, *groups[-1])
    conv_low = conv_w.astype(bf16)
    conv_use = join_columns(conv_low, swap(conv_low, "head", 2, 1), rank)
    starts, classes, images = attention_plan(segments, WIDE_TILE)
    back_starts, back_classes, _ = attention_plan(segments, TILE)
    middle, qkv, context, ext = attn_forward(starts, classes, counts, tokens, normed, attn_use, images)
    middle, found = after(middle, found)
    mlp_lines = finish_group(found, *groups[-1])
    mlp_lines = jnp.moveaxis(mlp_lines, 0, 1).reshape(mlp_w.shape[0], -1, mlp_w.shape[2])
    rank_at = rank.astype(jnp.int32).reshape(1)
    output, grad_middle, held, send, grad_conv, grad_norm_two = mlp_layer(
        line_places(segments), rank_at, middle, grad_out, out_grad_t, mlp_lines, swap(mlp_lines, "head", 2, 1),
        spread_taps(conv_use), norm_w,
    )

    def back(first, count, so_far):
        return attn_backward(
            first, count, so_far, back_starts, back_classes, counts, rank_at, normed_t, grad_middle, qkv, context, ext, attn_use, images
        )

    columns = conv_w.shape[1]
    norm_two = jnp.sum(grad_norm_two.reshape(2, 8, width), axis=1).reshape(1, 2 * width)
    norm_two = jnp.pad(norm_two, ((0, 0), (0, columns - 2 * width)))
    taps = grad_conv[:9]
    small = jnp.concatenate([half_columns(taps, rank), norm_two])
    small_send = jnp.concatenate([half_columns(taps, 1 - rank), norm_two])
    got = swap(jnp.concatenate([flat(send), two_parts(small_send)], axis=0), "head", 2, 1)
    first_rows = max(1, own_rows // 3)
    so_far, got = after(back(0, first_rows, None), got)
    rows = held.size // columns
    held = by_line(held + got[:rows].reshape(held.shape).astype(f32), size)
    small = from_parts(two_parts(small)) + from_parts(got[rows:])
    low, count = groups[0]
    pieces = pieces_of(held, low, count)
    small_parts = two_parts(small)
    gots = [
        swap(jnp.concatenate([flat(pieces[step]), small_parts], axis=0), "dp", size, step * low) for step in range(1, count)
    ]
    so_far, pieces = after(so_far, pieces)
    projected_grad, attn_held, attn_send = back(first_rows, own_rows - first_rows, so_far)

    def take(pieces, gots, small_parts, low, count):
        keep = pieces[0]
        rows = keep.size // keep.shape[-1]
        for got in gots:
            keep = keep + got[:rows].reshape(keep.shape).astype(f32)
        ordered = in_order([small_parts] + [got[rows:] for got in gots], (place // low) % count)
        return keep, sum(from_parts(part) for part in ordered)

    attn_got = swap(flat(attn_send), "head", 2, 1)
    attn_held, gots = after(attn_held, gots)
    held, small = take(pieces, gots, small_parts, low, count)
    rest = bits_of(size)[2:]
    attn_held = by_line(attn_held + attn_got.reshape(attn_held.shape).astype(f32), size)
    waiting = list(groups)
    blocks = tokens.shape[0] // FILL
    fills = [(0, blocks // 2), (blocks // 2, blocks - blocks // 2)]
    grad_tokens, grad_norm_one = None, 0.0
    while waiting or rest:
        attn_pieces, pieces, extra = [None], None, None
        if waiting:
            low, count = waiting.pop(0)
            attn_pieces = pieces_of(attn_held, low, count)
        sent = {step * low: [flat(attn_pieces[step])] for step in range(1, len(attn_pieces))}
        bit = None
        if rest:
            bit = rest.pop(0)
            pieces = pieces_of(held, bit, 2)
            small_parts = two_parts(small)
            extra = jnp.concatenate([flat(pieces[1]), small_parts], axis=0).reshape(-1, attn_held.shape[-1])
            sent.setdefault(bit, []).append(extra)
        fill = fills.pop(0) if fills else None
        if fill:
            sent, projected_grad = after(sent, projected_grad)
        gots = {step: swap(jnp.concatenate(parts, axis=0), "dp", size, step) for step, parts in sent.items()}
        if fill:
            results = tokens_back(*fill, grad_tokens, projected_grad, tokens, grad_middle, attn_use, norm_w)
            (grad_tokens, norm_one), gots = after(results, gots)
            grad_norm_one = grad_norm_one + norm_one
        if bit:
            got = gots[bit][gots[bit].shape[0] - extra.shape[0] :].reshape(-1, columns)
            held, small = take(pieces, [got], small_parts, bit, 2)
        if attn_pieces[0] is not None:
            attn_held = attn_pieces[0]
            rows = attn_held.size // attn_held.shape[-1]
            for step in range(1, len(attn_pieces)):
                attn_held = attn_held + gots[step * low][:rows].reshape(attn_held.shape).astype(f32)
    grad_attn = unfold_pairs(attn_held.reshape(attn_held.shape[:1] + attn_held.shape[2:]))
    grad_mlp = held.reshape(mlp_w.shape)
    norm_two = small[9, : 2 * width].reshape(2, width)

    weights, firsts, seconds = [attn_w, mlp_w, conv_w], [attn_m, mlp_m, conv_m], [attn_v, mlp_v, conv_v]
    scalars = pl.BlockSpec(memory_space=pltpu.SMEM)
    vectors = pl.BlockSpec(memory_space=pltpu.VMEM)
    results = pl.pallas_call(
        moments_kernel,
        in_specs=[scalars] + [vectors] * 13,
        out_specs=[vectors] * 10,
        out_shape=like(weights) * 3 + [jax.ShapeDtypeStruct((8, width), f32)],
        compiler_params=pltpu.CompilerParams(vmem_limit_bytes=16 * MIB),
    )(place.astype(jnp.int32).reshape(1), grad_norm_one, grad_attn, grad_mlp, small[:9], *weights, *firsts, *seconds)
    new_firsts, new_seconds, updates, sums = results[:3], results[3:6], results[6:9], results[9]
    new_w = pl.pallas_call(
        apply_kernel,
        in_specs=[vectors] * 11,
        out_specs=[vectors] * 6,
        out_shape=like(weights) + like([norm_w] * 3),
        compiler_params=pltpu.CompilerParams(vmem_limit_bytes=16 * MIB),
    )(sum_everywhere(sums, size), norm_two, norm_w, norm_m, norm_v, *weights, *updates)
    return (
        output, grad_tokens, new_w[0], new_firsts[0], new_seconds[0], new_w[1], new_firsts[1], new_seconds[1],
        new_w[2], new_firsts[2], new_seconds[2], *new_w[3:],
    )


def solution(mesh):
    rows, lines = P(("dp", "head"), None), P("dp", None)
    shards, columns = P(None, "dp", "head"), P(None, "head")
    in_specs = (rows, rows, lines, P("dp")) + (shards,) * 6 + (columns,) * 3 + (P(),) * 3
    out_specs = (rows, rows) + (shards,) * 6 + (columns,) * 3 + (P(),) * 3
    return jax.shard_map(
        functools.partial(body, mesh.shape["dp"]), mesh=mesh, in_specs=in_specs, out_specs=out_specs, check_vma=False
    )
```

```python
import functools
import jax
import jax.numpy as jnp
from jax import lax
from jax.experimental import pallas as pl
from jax.experimental.pallas import tpu as pltpu
from jax.sharding import PartitionSpec as P

HEAD_DIM = 64
GRID_W = 16
STEP = 10
IMAGES = 8

NORM_EPS = 1e-06
BETA_ONE = 0.9
BETA_TWO = 0.999
ADAM_EPS = 1e-06
DECAY = 0.01
RATE = 0.5
LOG2E = 1.4426950408889634
LN2 = 0.6931471805599453
BIG = 2.0**100
GELU_ONE = 0.7978845608028654
GELU_TWO = 0.044715
GELU_S = (GELU_ONE * GELU_TWO) ** (1.0 / 3.0)
GELU_A = GELU_ONE / GELU_S
ACT_SCALE = 0.5 / GELU_S
EXTRA = 32
PARTS = 4
TILE = 128
WIDE_TILE = 256
FILL = 512
LANES = 128
STRIDE = GRID_W + 8
MIB = 1024 * 1024

f32 = jnp.float32
bf16 = jnp.bfloat16
NN = (((1,), (0,)), ((), ()))
NT = (((1,), (1,)), ((), ()))
TN = (((0,), (0,)), ((), ()))


def dot(left, right, dims=NN):
    return lax.dot_general(left, right, dims, preferred_element_type=f32)


def work_of(micros):
    return pl.CostEstimate(flops=micros * 1_000_000_000, bytes_accessed=micros * 1_000_000, transcendentals=0)


def widths_for(length):
    return [w for w in (256, 384, 512, 640, 768) if w < length] + [length]


def norm_parts(values):
    average = jnp.mean(values, axis=-1, keepdims=True)
    centered = values - average
    inverse = lax.rsqrt(jnp.mean(centered * centered, axis=-1, keepdims=True) + NORM_EPS)
    return centered * inverse, inverse


def norm_back(upstream, gain_row, unit_rows, inverse):
    grad_unit = upstream * gain_row
    first_term = jnp.mean(grad_unit, axis=-1, keepdims=True)
    second_term = jnp.mean(grad_unit * unit_rows, axis=-1, keepdims=True)
    return inverse * (grad_unit - first_term - unit_rows * second_term)


def fold_rows(values):
    rows, columns = values.shape
    return jnp.sum(values.reshape(rows // 8, 8, columns), axis=0)


def pair_columns(flat):
    empty = jnp.zeros((HEAD_DIM, flat.shape[1]), flat.dtype)
    return jnp.concatenate(
        [jnp.concatenate([flat[:HEAD_DIM], empty], axis=0), jnp.concatenate([empty, flat[HEAD_DIM:]], axis=0)], axis=1
    )


def pair_rows(both):
    half = both.shape[1] // 2
    return jnp.concatenate([both[:HEAD_DIM, :half], both[HEAD_DIM:, half:]], axis=0)


def fold_max(values):
    pieces = [values[at : at + 64] for at in range(0, values.shape[0], 64)]
    while len(pieces) > 1:
        pieces = [jnp.maximum(a, b) for a, b in zip(pieces[::2], pieces[1::2])] + ([pieces[-1]] if len(pieces) % 2 else [])
    top = pieces[0]
    top = jnp.maximum(top[:32], top[32:])
    top = jnp.maximum(top[:16], top[16:])
    return jnp.max(jnp.maximum(top[:8], top[8:]), axis=0, keepdims=True)


def three_parts(value, part):
    high = value.astype(bf16).astype(f32)
    rest = value - high
    middle = rest.astype(bf16).astype(f32)
    return jnp.where(part == 0, high, jnp.where(part == 1, middle, rest - middle))


def image_tags(image_ref, start, rows):
    place = start + lax.broadcasted_iota(jnp.int32, (rows, LANES), 0)
    inside = (place >= image_ref[0, 0:1, :]) & (place < image_ref[0, 1:2, :])
    return jnp.where(inside, 1.0, 0.0).astype(bf16)


def first_norm_kernel(tokens_ref, out_grad_ref, norm_ref, normed_ref, normed_t_ref, out_grad_t_ref):
    big = 256

    def step(at, carry):
        rows = pl.ds(pl.multiple_of(at * big, big), big)
        unit, _ = norm_parts(tokens_ref[rows, :].astype(f32))
        normed_ref[rows, :] = (unit * norm_ref[0:1, :] + norm_ref[1:2, :]).astype(bf16)
        return carry

    lax.fori_loop(0, tokens_ref.shape[0] // big, step, 0)
    normed_t_ref[...] = jnp.transpose(normed_ref[...])
    out_grad_t_ref[...] = jnp.transpose(out_grad_ref[...])


def first_norm(tokens, out_grad, norm_w, row_count):
    rows_all, width = tokens.shape
    length = rows_all // row_count
    by_row = pl.BlockSpec((length, width), lambda r: (r, 0))
    turned = pl.BlockSpec((width, length), lambda r: (r, 0))
    flipped = jax.ShapeDtypeStruct((row_count * width, length), bf16)
    return pl.pallas_call(
        first_norm_kernel,
        grid=(row_count,),
        in_specs=[by_row, by_row, pl.BlockSpec(norm_w.shape, lambda r: (0, 0))],
        out_specs=[by_row, turned, turned],
        out_shape=[jax.ShapeDtypeStruct((rows_all, width), bf16), flipped, flipped],
        cost_estimate=work_of(8),
        compiler_params=pltpu.CompilerParams(vmem_limit_bytes=60 * MIB),
    )(tokens, out_grad, norm_w)


def attn_forward_kernel(
    start_ref, class_ref, count_ref, tokens_ref, normed_ref, w_ref, image_ref,
    middle_ref, qkv_ref, context_ref, ext_ref,
    tag_ref, qt_ref, vt_ref,
):
    row = pl.program_id(0)
    length, width = tokens_ref.shape
    pairs = width // LANES
    tag_ref[...] = image_tags(image_ref, 0, length)
    queries = (dot(normed_ref[...], w_ref[0]) * (HEAD_DIM**-0.5 * LOG2E)).astype(bf16)
    qkv_ref[:, :width] = queries
    qt_ref[...] = jnp.transpose(queries)
    qkv_ref[:, width : 2 * width] = dot(normed_ref[...], w_ref[1]).astype(bf16)
    values = dot(normed_ref[...], w_ref[2]).astype(bf16)
    qkv_ref[:, 2 * width :] = values
    vt_ref[...] = jnp.transpose(values)

    def tile(step, carry):
        q0 = pl.multiple_of(step * WIDE_TILE, WIDE_TILE)
        here = pl.ds(q0, WIDE_TILE)
        place = q0 + lax.broadcasted_iota(jnp.int32, (IMAGES, WIDE_TILE), 1)
        edges = [jnp.concatenate([image_ref[0, at : at + IMAGES, :]] * (WIDE_TILE // LANES), axis=1) for at in (8, 16)]
        inside = (place >= edges[0]) & (place < edges[1])
        mask = jnp.where(inside, 0.0, -BIG)
        mask_low = jnp.concatenate([mask, jnp.zeros((LANES - IMAGES, WIDE_TILE), f32)], axis=0).astype(bf16)
        ext_rows = lax.broadcasted_iota(jnp.int32, (EXTRA - IMAGES, WIDE_TILE), 0)

        def attend(window):
            there = pl.ds(pl.multiple_of(start_ref[row, step], LANES), window)
            tags = tag_ref[there, :]
            ones = jnp.ones((GRID_W, window), bf16)
            extra = jnp.zeros((EXTRA - IMAGES, WIDE_TILE), f32)
            slices = [slice(p * LANES, (p + 1) * LANES) for p in range(pairs)]
            masks = jnp.concatenate([mask_low, mask_low], axis=1)
            scores, tops, exponents, mixes = [], [], [], []
            for p, at in enumerate(slices):
                keys = qkv_ref[there, width + p * LANES : width + (p + 1) * LANES]
                right = jnp.concatenate([pair_columns(qt_ref[at, here]), masks], axis=0)
                scores.append(dot(jnp.concatenate([keys, tags], axis=1), right))
            for p in range(pairs):
                tops.append(fold_max(scores[p]))
                exponents.append(jnp.exp2(scores[p] - tops[p]).astype(bf16))
            for p, at in enumerate(slices):
                mixes.append(dot(jnp.concatenate([vt_ref[at, there], ones], axis=0), exponents[p]))
            for p, at in enumerate(slices):
                mixed = mixes[p]
                total = mixed[LANES : LANES + 1, :]
                minus_lse = -(tops[p] + jnp.log(total) * LOG2E)
                scale = 1.0 / total
                lane = lax.broadcasted_iota(jnp.int32, (1, 2 * WIDE_TILE), 1)
                head = 2 * p + jnp.where(lane < WIDE_TILE, 0, 1)
                scale = jnp.where(head < count_ref[row], scale, 0.0)
                context_ref[here, at] = jnp.transpose(pair_rows(mixed[:LANES] * scale)).astype(bf16)
                for h in range(2):
                    value = minus_lse[:, h * WIDE_TILE : (h + 1) * WIDE_TILE]
                    first = 6 * p + 3 * h
                    extra = jnp.where(
                        (ext_rows >= first) & (ext_rows < first + 3), three_parts(value, ext_rows - first), extra
                    )
            ext_ref[:, here] = jnp.concatenate([mask, extra], axis=0).astype(bf16)

        for index, window in enumerate(widths_for(length)):
            pl.when(class_ref[row, step] == index)(functools.partial(attend, window))
        return carry

    lax.fori_loop(0, length // WIDE_TILE, tile, 0)
    middle_ref[...] = tokens_ref[...].astype(f32) + dot(context_ref[...], w_ref[3], NT)


def attn_forward(starts, classes, counts, tokens, normed, attn_use, images):
    rows_all, width = tokens.shape
    row_count = counts.shape[0]
    length = rows_all // row_count
    by_row = lambda columns: pl.BlockSpec((length, columns), lambda r, *_: (r, 0))
    return pl.pallas_call(
        attn_forward_kernel,
        grid_spec=pltpu.PrefetchScalarGridSpec(
            num_scalar_prefetch=3,
            grid=(row_count,),
            in_specs=[
                by_row(width),
                by_row(width),
                pl.BlockSpec(attn_use.shape, lambda r, *_: (0, 0, 0)),
                pl.BlockSpec((1, 24, LANES), lambda r, *_: (r, 0, 0)),
            ],
            out_specs=[
                by_row(width), by_row(3 * width), by_row(width), pl.BlockSpec((EXTRA, length), lambda r, *_: (r, 0))
            ],
            scratch_shapes=[
                pltpu.VMEM((length, LANES), bf16),
                pltpu.VMEM((width, length), bf16),
                pltpu.VMEM((width, length), bf16),
            ],
        ),
        out_shape=[
            jax.ShapeDtypeStruct((rows_all, width), f32),
            jax.ShapeDtypeStruct((rows_all, 3 * width), bf16),
            jax.ShapeDtypeStruct((rows_all, width), bf16),
            jax.ShapeDtypeStruct((row_count * EXTRA, length), bf16),
        ],
        cost_estimate=work_of(30),
        compiler_params=pltpu.CompilerParams(vmem_limit_bytes=56 * MIB),
    )(starts, classes, counts, tokens, normed, attn_use, images)


def attn_backward_kernel(
    first, final, start_ref, class_ref, count_ref, rank_ref, normed_t_ref, middle_grad_ref, qkv_ref, context_ref, ext_ref, w_ref,
    image_ref, *refs,
):
    sums = None
    if first:
        sums, refs = refs[1], refs[2:]
    sent = None
    if final:
        proj_ref, keep_ref, send_ref, *scratch, w_grad_ref = refs
        sent = (keep_ref, send_ref)
    else:
        proj_ref, w_grad_ref, *scratch = refs
    attn_backward_row(
        first, sums, sent, start_ref, class_ref, count_ref, rank_ref, normed_t_ref, middle_grad_ref, qkv_ref, context_ref, ext_ref,
        w_ref, image_ref, proj_ref, w_grad_ref, *scratch,
    )


def attn_backward_row(
    first, sums, sent, start_ref, class_ref, count_ref, rank_ref, normed_t_ref, middle_grad_ref, qkv_ref, context_ref, ext_ref, w_ref,
    image_ref, proj_ref, w_grad_ref,
    tag_ref, up_ref, delta_ref, dq_ref, dk_ref, dv_ref, low_ref, qt_ref, kt_ref, upt_ref,
):
    step_at = pl.program_id(0)
    row = first + step_at
    length, width = middle_grad_ref.shape
    pairs = width // LANES
    big = 256

    @pl.when(step_at == 0)
    def _():
        w_grad_ref[...] = jnp.zeros_like(w_grad_ref) if sums is None else sums[...]

    target = lax.broadcasted_iota(jnp.int32, (EXTRA, width), 0) - IMAGES
    source = lax.broadcasted_iota(jnp.int32, (EXTRA, width), 1) // HEAD_DIM * 3
    collect = jnp.where((target >= source) & (target < source + 3), -1.0, 0.0).astype(bf16)
    active = jnp.where(
        lax.broadcasted_iota(jnp.int32, (1, width), 1) // HEAD_DIM < count_ref[row], 1.0, 0.0
    )

    def prepare(step, carry):
        rows = pl.ds(pl.multiple_of(step * big, big), big)
        tag_ref[rows, :] = image_tags(image_ref, step * big, big)
        low_ref[rows, :] = middle_grad_ref[rows, :].astype(bf16)
        dk_ref[rows, :] = jnp.zeros((big, width), f32)
        dv_ref[rows, :] = jnp.zeros((big, width), f32)
        return carry

    lax.fori_loop(0, length // big, prepare, 0)
    up = (dot(low_ref[...], w_ref[3]) * active).astype(bf16)
    up_ref[...] = up
    upt_ref[...] = jnp.transpose(up)
    qt_ref[...] = jnp.transpose(qkv_ref[:, :width])
    kt_ref[...] = jnp.transpose(qkv_ref[:, width : 2 * width])

    def gather(step, carry):
        rows = pl.ds(pl.multiple_of(step * big, big), big)
        product = up_ref[rows, :].astype(f32) * context_ref[rows, :].astype(f32)
        high = product.astype(bf16)
        rest = (product - high.astype(f32)).astype(bf16)
        delta = dot(collect, high, NT) + dot(collect, rest, NT)
        part = lax.rem(lax.broadcasted_iota(jnp.int32, (EXTRA, big), 0) + 3 * EXTRA - IMAGES, 3)
        delta_ref[:, rows] = three_parts(delta, part).astype(bf16)
        return carry

    lax.fori_loop(0, length // big, gather, 0)
    lane = lax.broadcasted_iota(jnp.int32, (1, LANES), 1)
    first_half = jnp.where(lane < HEAD_DIM, 1.0, 0.0).astype(bf16)
    second_half = jnp.where(lane >= HEAD_DIM, 1.0, 0.0).astype(bf16)

    def tile(step, carry):
        q0 = pl.multiple_of(step * TILE, TILE)
        here = pl.ds(q0, TILE)

        def attend(window):
            there = pl.ds(pl.multiple_of(start_ref[row, step], LANES), window)
            tags = tag_ref[there, :]
            ext = ext_ref[:, here]
            delta = delta_ref[:, here]
            at_row = lax.broadcasted_iota(jnp.int32, (EXTRA, LANES), 0)
            empty = jnp.zeros((LANES - EXTRA, 2 * TILE), bf16)

            def own(edge, masks):
                keep = (at_row >= edge) & (at_row < edge + 3)
                return jnp.where(keep | (at_row < IMAGES) if masks else keep, 1.0, 0.0).astype(bf16)

            slices = [slice(p * LANES, (p + 1) * LANES) for p in range(pairs)]
            scores, grad_probs, probs, grad_scores = [], [], [], []
            for p, at in enumerate(slices):
                keys = qkv_ref[there, width + p * LANES : width + (p + 1) * LANES]
                values = qkv_ref[there, 2 * width + p * LANES : 2 * width + (p + 1) * LANES]
                edge = IMAGES + 6 * p
                q_side = jnp.concatenate(
                    [
                        pair_columns(qt_ref[at, here]),
                        jnp.concatenate([ext * own(edge, True), ext * own(edge + 3, True)], axis=1),
                        empty,
                    ],
                    axis=0,
                )
                up_side = jnp.concatenate(
                    [
                        pair_columns(upt_ref[at, here]),
                        jnp.concatenate([delta * own(edge, False), delta * own(edge + 3, False)], axis=1),
                        empty,
                    ],
                    axis=0,
                )
                scores.append(dot(jnp.concatenate([keys, tags], axis=1), q_side))
                grad_probs.append(dot(jnp.concatenate([values, tags], axis=1), up_side))
            for p in range(pairs):
                weight = jnp.exp2(scores[p])
                probs.append(weight.astype(bf16))
                grad_scores.append((weight * grad_probs[p]).astype(bf16))
            for p, at in enumerate(slices):
                queries, ups = qkv_ref[here, at], up_ref[here, at]
                q_pair = jnp.concatenate([queries * first_half, queries * second_half], axis=0)
                up_pair = jnp.concatenate([ups * first_half, ups * second_half], axis=0)
                dv_ref[there, at] += dot(probs[p], up_pair)
                dk_ref[there, at] += dot(grad_scores[p], q_pair)
                dq = pair_rows(dot(kt_ref[at, there], grad_scores[p]))
                dq_ref[here, at] = jnp.transpose(dq * HEAD_DIM**-0.5).astype(bf16)

        for index, window in enumerate(widths_for(length)):
            pl.when(class_ref[row, step] == index)(functools.partial(attend, window))
        return carry

    lax.fori_loop(0, length // TILE, tile, 0)
    keys_grad = (dk_ref[...] * LN2).astype(bf16)
    values_grad = dv_ref[...].astype(bf16)
    proj_ref[...] = jnp.concatenate([dq_ref[...], keys_grad, values_grad], axis=1)
    for k in range(3):
        w_grad_ref[k] += dot(normed_t_ref[...], proj_ref[:, k * width : (k + 1) * width])
    w_grad_ref[3] += dot(jnp.transpose(low_ref[...]), context_ref[...])
    if sent:

        @pl.when(step_at == pl.num_programs(0) - 1)
        def _():
            for k in range(2):
                one, two = w_grad_ref[k], w_grad_ref[k + 2]
                halves = [jnp.concatenate([one[:, at : at + width // 2], two[:, at : at + width // 2]], axis=1) for at in (0, width // 2)]
                sent[0][k] = jnp.where(rank_ref[0] == 0, halves[0], halves[1])
                sent[1][k] = jnp.where(rank_ref[0] == 0, halves[1], halves[0]).astype(bf16)


def attn_backward(first, count, so_far, starts, classes, counts, rank, normed_t, middle_grad, qkv, context, ext, attn_use, images):
    rows_all, width = middle_grad.shape
    length = rows_all // counts.shape[0]
    by_row = lambda columns: pl.BlockSpec((length, columns), lambda r, *_: (first + r, 0))
    final = first + count == counts.shape[0]
    half = (2, width, width)
    halves = pl.BlockSpec(half, lambda r, *_: (0, 0, 0))
    whole = pl.BlockSpec(attn_use.shape, lambda r, *_: (0, 0, 0))
    return pl.pallas_call(
        functools.partial(attn_backward_kernel, first, final),
        grid_spec=pltpu.PrefetchScalarGridSpec(
            num_scalar_prefetch=4,
            grid=(count,),
            in_specs=[
                pl.BlockSpec((width, length), lambda r, *_: (first + r, 0)),
                by_row(width),
                by_row(3 * width),
                by_row(width),
                pl.BlockSpec((EXTRA, length), lambda r, *_: (first + r, 0)),
                whole,
                pl.BlockSpec((1, 24, LANES), lambda r, *_: (first + r, 0, 0)),
            ]
            + ([pl.BlockSpec(memory_space=pl.ANY), whole] if first else []),
            out_specs=[by_row(3 * width)] + ([halves, halves] if final else [whole]),
            scratch_shapes=[
                pltpu.VMEM((length, LANES), bf16),
                pltpu.VMEM((length, width), bf16),
                pltpu.VMEM((EXTRA, length), bf16),
                pltpu.VMEM((length, width), bf16),
                pltpu.VMEM((length, width), f32),
                pltpu.VMEM((length, width), f32),
                pltpu.VMEM((length, width), bf16),
                pltpu.VMEM((width, length), bf16),
                pltpu.VMEM((width, length), bf16),
                pltpu.VMEM((width, length), bf16),
            ]
            + ([pltpu.VMEM(attn_use.shape, f32)] if final else []),
        ),
        out_shape=[jax.ShapeDtypeStruct((rows_all, 3 * width), bf16)]
        + (
            [jax.ShapeDtypeStruct(half, f32), jax.ShapeDtypeStruct(half, bf16)]
            if final
            else [jax.ShapeDtypeStruct(attn_use.shape, f32)]
        ),
        input_output_aliases={11: 0} if first else {},
        cost_estimate=work_of(18 * count),
        compiler_params=pltpu.CompilerParams(vmem_limit_bytes=50 * MIB),
    )(starts, classes, counts, rank, normed_t, middle_grad, qkv, context, ext, attn_use, images, *(so_far or ()))


def tokens_back_kernel(proj_ref, tokens_ref, middle_grad_ref, w_ref, norm_ref, *refs):
    tokens_grad_ref, norm_grad_ref = refs[-2:]

    @pl.when(pl.program_id(0) == 0)
    def _():
        norm_grad_ref[...] = jnp.zeros_like(norm_grad_ref)

    w_cat = jnp.concatenate([w_ref[0], w_ref[1], w_ref[2]], axis=1)
    upstream = dot(proj_ref[...], w_cat, NT)
    unit, inverse = norm_parts(tokens_ref[...].astype(f32))
    tokens_grad_ref[...] = middle_grad_ref[...] + norm_back(upstream, norm_ref[0:1, :], unit, inverse)
    norm_grad_ref[0:8, :] += fold_rows(upstream * unit)
    norm_grad_ref[8:16, :] += fold_rows(upstream)


def tokens_back(first, count, so_far, proj, tokens, middle_grad, attn_use, norm_w):
    rows_all, width = tokens.shape
    some = lambda columns: pl.BlockSpec((FILL, columns), lambda r: (first + r, 0))
    return pl.pallas_call(
        tokens_back_kernel,
        grid=(count,),
        in_specs=[
            some(3 * width),
            some(width),
            some(width),
            pl.BlockSpec(attn_use.shape, lambda r: (0, 0, 0)),
            pl.BlockSpec(norm_w.shape, lambda r: (0, 0)),
        ]
        + ([] if so_far is None else [pl.BlockSpec(memory_space=pl.ANY)]),
        out_specs=[some(width), pl.BlockSpec((16, width), lambda r: (0, 0))],
        out_shape=[jax.ShapeDtypeStruct((rows_all, width), f32), jax.ShapeDtypeStruct((16, width), f32)],
        input_output_aliases={} if so_far is None else {5: 0},
        cost_estimate=work_of(2 * count),
        compiler_params=pltpu.CompilerParams(vmem_limit_bytes=60 * MIB),
    )(proj, tokens, middle_grad, attn_use, norm_w, *([] if so_far is None else [so_far]))


def mlp_kernel(
    place_ref, rank_ref, middle_ref, out_grad_ref, out_grad_t_ref, own_w_ref, other_w_ref, taps_ref, norm_ref,
    output_ref, middle_grad_ref, keep_ref, send_ref, taps_grad_ref, norm_grad_ref,
    w_ref, w_grad_ref, unit_ref, inverse_ref, normed_ref, normed_t_ref, out_sum_ref, up_sum_ref, tap_sum_ref,
    act_grads_ref, acts_ref, hidden_grads_ref, *buffers,
):
    row = pl.program_id(0)
    length, width = middle_ref.shape
    hidden = w_ref.shape[2]
    chunk = PARTS * LANES
    big = 256
    grid_rows = length // GRID_W
    chunks = hidden // chunk
    h_refs, g_refs = buffers[:PARTS], buffers[PARTS:]
    gain, bias = norm_ref[2:3, :], norm_ref[3:4, :]

    @pl.when(row == 0)
    def _():
        w_grad_ref[...] = jnp.zeros_like(w_grad_ref)
        norm_grad_ref[...] = jnp.zeros_like(norm_grad_ref)
        tap_sum_ref[...] = jnp.zeros_like(tap_sum_ref)
        for rank, halves in enumerate(((own_w_ref, other_w_ref), (other_w_ref, own_w_ref))):

            @pl.when(rank_ref[0] == rank)
            def _():
                w_ref[:, :, : hidden // 2] = halves[0][...]
                w_ref[:, :, hidden // 2 :] = halves[1][...]

        for ref in buffers:
            ref[...] = jnp.zeros_like(ref)

    def place(r):
        return pl.multiple_of(place_ref[row, r], 8)

    for n in range(IMAGES + 1):
        at = place(grid_rows + n)
        for ref in buffers:
            ref[pl.ds(at, GRID_W), :] = jnp.zeros((GRID_W, LANES), f32)

    def normalize(step, carry):
        rows = pl.ds(pl.multiple_of(step * big, big), big)
        middle = middle_ref[rows, :]
        unit, inverse = norm_parts(middle)
        unit_ref[rows, :] = unit
        inverse_ref[rows, :] = jnp.broadcast_to(inverse, (big, LANES))
        normed_ref[rows, :] = (unit * gain + bias).astype(bf16)
        out_sum_ref[rows, :] = jnp.zeros((big, width), f32)
        up_sum_ref[rows, :] = jnp.zeros((big, width), f32)
        return carry

    lax.fori_loop(0, length // big, normalize, 0)
    normed_t_ref[...] = jnp.transpose(normed_ref[...])

    def lanes_of(c):
        return pl.ds(pl.multiple_of(c * chunk, chunk), chunk)

    def lanes_of(c):
        return pl.ds(pl.multiple_of(c * chunk, chunk), chunk)

    def neighbours(ref, at):
        return [ref[pl.ds(at + (a * STRIDE + b), GRID_W), :] for a in (-1, 0, 1) for b in (-1, 0, 1)]

    def tall(values):
        return jnp.concatenate([values, values], axis=0)

    def total_of(terms):
        while len(terms) > 1:
            terms = [a + b for a, b in zip(terms[::2], terms[1::2])] + ([terms[-1]] if len(terms) % 2 else [])
        return terms[0]

    def taps_for(c, part, at):
        lane = pl.ds(pl.multiple_of(c * chunk + part * LANES, LANES), LANES)
        return [tall(taps_ref[at + k * 8 : at + (k + 1) * 8, lane]) for k in range(9)]

    lines = 8

    def do_chunk(c, carry):
        lanes = lanes_of(c)
        for t in range(length // big):
            rows = slice(t * big, (t + 1) * big)
            values = dot(normed_ref[rows, :], w_ref[0, :, lanes])
            for part in range(PARTS):
                for s in range(big // GRID_W):
                    at = place(t * (big // GRID_W) + s)
                    h_refs[part][pl.ds(at, GRID_W), :] = values[
                        s * GRID_W : (s + 1) * GRID_W, part * LANES : (part + 1) * LANES
                    ]
        act_grads_ref[...] = dot(out_grad_ref[...], w_ref[1, :, lanes])

        def forward(t, carry):
            tokens_base = pl.multiple_of(t * (lines * GRID_W), lines * GRID_W)
            for part in range(PARTS):
                taps = taps_for(c, part, 0)
                cols = slice(part * LANES, (part + 1) * LANES)
                for s in range(lines):
                    near = pl.ds(pl.multiple_of(tokens_base + s * GRID_W, GRID_W), GRID_W)
                    at = place(t * lines + s)
                    x = total_of([x * tap for x, tap in zip(neighbours(h_refs[part], at), taps)])
                    square = x * x
                    value = jnp.tanh(x * (GELU_A + square))
                    gate = 1.0 + value
                    twice = x * gate
                    acts_ref[near, cols] = twice.astype(bf16)
                    slope = gate + (twice * (1.0 - value)) * (GELU_A + 3.0 * square)
                    g_refs[part][pl.ds(at, GRID_W), :] = act_grads_ref[near, cols] * slope
            return carry

        lax.fori_loop(0, grid_rows // lines, forward, 0)

        def backward(t, carry):
            tokens_base = pl.multiple_of(t * (lines * GRID_W), lines * GRID_W)
            for part in range(PARTS):
                taps = taps_for(c, part, 72)
                lane = pl.ds(pl.multiple_of(c * chunk + part * LANES, LANES), LANES)
                cols = slice(part * LANES, (part + 1) * LANES)
                totals = [None] * 9
                for s in range(lines):
                    near = pl.ds(pl.multiple_of(tokens_base + s * GRID_W, GRID_W), GRID_W)
                    at = place(t * lines + s)
                    source = h_refs[part][pl.ds(at, GRID_W), :]
                    moved = neighbours(g_refs[part], at)[::-1]
                    for k in range(9):
                        product = source * moved[k]
                        folded = product[:8] + product[8:]
                        totals[k] = folded if totals[k] is None else totals[k] + folded
                    terms = [x * tap for x, tap in zip(moved, taps)]
                    hidden_grads_ref[near, cols] = total_of(terms).astype(bf16)
                for k in range(9):
                    tap_sum_ref[k * 8 : (k + 1) * 8, lane] += totals[k]
            return carry

        lax.fori_loop(0, grid_rows // lines, backward, 0)
        w_grad_ref[0, :, lanes] += dot(normed_t_ref[...], hidden_grads_ref[...])
        w_grad_ref[1, :, lanes] += dot(out_grad_t_ref[...], acts_ref[...])
        out_sum_ref[...] += dot(acts_ref[...], w_ref[1, :, lanes], NT)
        up_sum_ref[...] += dot(hidden_grads_ref[...], w_ref[0, :, lanes], NT)
        return carry

    lax.fori_loop(0, chunks, do_chunk, 0)

    def finish(step, carry):
        rows = pl.ds(pl.multiple_of(step * big, big), big)
        middle = middle_ref[rows, :]
        output_ref[rows, :] = (middle + ACT_SCALE * out_sum_ref[rows, :]).astype(bf16)
        upstream = 0.5 * up_sum_ref[rows, :]
        unit = unit_ref[rows, :]
        inverse = jnp.concatenate([inverse_ref[rows, :]] * (width // LANES), axis=1)
        middle_grad_ref[rows, :] = out_grad_ref[rows, :].astype(f32) + norm_back(upstream, gain, unit, inverse)
        norm_grad_ref[0:8, :] += fold_rows(upstream * unit)
        norm_grad_ref[8:16, :] += fold_rows(upstream)
        return carry

    lax.fori_loop(0, length // big, finish, 0)

    @pl.when(row == pl.num_programs(0) - 1)
    def _():
        for k, scale in enumerate((0.5, ACT_SCALE)):
            halves = w_grad_ref[k, :, : hidden // 2], w_grad_ref[k, :, hidden // 2 :]
            keep_ref[k] = scale * jnp.where(rank_ref[0] == 0, halves[0], halves[1])
            send_ref[k] = (scale * jnp.where(rank_ref[0] == 0, halves[1], halves[0])).astype(bf16)
        taps_grad_ref[...] = jnp.zeros_like(taps_grad_ref)
        for k in range(9):
            total = jnp.sum(tap_sum_ref[k * 8 : (k + 1) * 8, :], axis=0, keepdims=True)
            taps_grad_ref[k : k + 1, :] = 0.5 * total


def mlp_layer(places, rank, middle, out_grad, out_grad_t, own_w, other_w, taps, norm_w):
    rows_all, width = middle.shape
    row_count = places.shape[0]
    length = rows_all // row_count
    half = own_w.shape
    hidden = 2 * half[2]
    whole = half[:2] + (hidden,)
    by_row = lambda columns: pl.BlockSpec((length, columns), lambda r, *_: (r, 0))
    slots = (length // GRID_W + IMAGES + 2) * STRIDE
    return pl.pallas_call(
        mlp_kernel,
        grid_spec=pltpu.PrefetchScalarGridSpec(
            num_scalar_prefetch=2,
            grid=(row_count,),
            in_specs=[
                by_row(width),
                by_row(width),
                pl.BlockSpec((width, length), lambda r, *_: (r, 0)),
                pl.BlockSpec(half, lambda r, *_: (0, 0, 0)),
                pl.BlockSpec(half, lambda r, *_: (0, 0, 0)),
                pl.BlockSpec(taps.shape, lambda r, *_: (0, 0)),
                pl.BlockSpec(norm_w.shape, lambda r, *_: (0, 0)),
            ],
            out_specs=[
                by_row(width),
                by_row(width),
                pl.BlockSpec(half, lambda r, *_: (0, 0, 0)),
                pl.BlockSpec(half, lambda r, *_: (0, 0, 0)),
                pl.BlockSpec((16, hidden), lambda r, *_: (0, 0)),
                pl.BlockSpec((16, width), lambda r, *_: (0, 0)),
            ],
            scratch_shapes=[
                pltpu.VMEM(whole, bf16),
                pltpu.VMEM(whole, f32),
                pltpu.VMEM((length, width), f32),
                pltpu.VMEM((length, LANES), f32),
                pltpu.VMEM((length, width), bf16),
                pltpu.VMEM((width, length), bf16),
                pltpu.VMEM((length, width), f32),
                pltpu.VMEM((length, width), f32),
                pltpu.VMEM((9 * 8, hidden), f32),
                pltpu.VMEM((length, PARTS * LANES), f32),
                pltpu.VMEM((length, PARTS * LANES), bf16),
                pltpu.VMEM((length, PARTS * LANES), bf16),
            ]
            + [pltpu.VMEM((slots, LANES), f32)] * (2 * PARTS),
        ),
        out_shape=[
            jax.ShapeDtypeStruct((rows_all, width), bf16),
            jax.ShapeDtypeStruct((rows_all, width), f32),
            jax.ShapeDtypeStruct(half, f32),
            jax.ShapeDtypeStruct(half, bf16),
            jax.ShapeDtypeStruct((16, hidden), f32),
            jax.ShapeDtypeStruct((16, width), f32),
        ],
        cost_estimate=work_of(90),
        compiler_params=pltpu.CompilerParams(vmem_limit_bytes=50 * MIB),
    )(places, rank, middle, out_grad, out_grad_t, own_w, other_w, taps, norm_w)


def attention_plan(segments, tile):
    row_count, length = segments.shape
    tiles = segments.reshape(row_count, length // tile, tile)
    first, last = tiles[:, :, 0], tiles[:, :, -1]
    ids = jnp.arange(IMAGES, dtype=jnp.int32)
    begins = jnp.sum((segments[:, None, :] < ids[None, :, None]).astype(jnp.int32), axis=-1)
    ends = jnp.sum((segments[:, None, :] <= ids[None, :, None]).astype(jnp.int32), axis=-1)
    low_end = jnp.sum(jnp.where(first[:, :, None] == ids, begins[:, None, :], 0), axis=-1) // LANES * LANES
    high_end = jnp.sum(jnp.where(last[:, :, None] == ids, ends[:, None, :], 0), axis=-1)
    widths = widths_for(length)
    classes = sum(((high_end - low_end) > w).astype(jnp.int32) for w in widths[:-1])
    chosen = jnp.full_like(classes, widths[-1])
    for index, w in enumerate(widths):
        chosen = jnp.where(classes == index, w, chosen)
    starts = jnp.minimum(low_end, length - chosen)
    used = jnp.zeros((row_count, EXTRA - IMAGES), jnp.int32)
    unused = jnp.zeros((row_count, LANES - EXTRA), jnp.int32)
    first_lane = jnp.concatenate([begins, used, unused], axis=1)
    end_lane = jnp.concatenate([ends, used + length, unused], axis=1)
    by_lane = jnp.pad(jnp.stack([first_lane, end_lane], axis=1), ((0, 0), (0, 6), (0, 0)))
    by_image = jnp.broadcast_to(jnp.concatenate([begins, ends], axis=1)[:, :, None], (row_count, 2 * IMAGES, LANES))
    return starts, classes, jnp.concatenate([by_lane, by_image], axis=1)


def spread_taps(conv_use):
    taps = conv_use.astype(f32)
    own = (jnp.arange(9) == 4).astype(f32)[:, None]
    taps = jnp.repeat(taps + own, 8, axis=0)
    return jnp.concatenate([taps * GELU_S, taps], axis=0)


def line_places(segments):
    ids = segments[:, ::GRID_W]
    count = ids.shape[1]
    rows = jnp.arange(count, dtype=jnp.int32) + ids + 1
    images = jnp.arange(IMAGES, dtype=jnp.int32)
    first = jnp.sum((ids[:, None, :] < images[None, :, None]).astype(jnp.int32), axis=-1)
    gaps = jnp.concatenate([first + images, jnp.full((ids.shape[0], 1), count + IMAGES, jnp.int32)], axis=1)
    return jnp.concatenate([rows, gaps], axis=1) * STRIDE + 8


def bits_of(size):
    bits = []
    b = 1
    while b < size:
        bits.append(b)
        b *= 2
    return bits


def groups_of(size):
    bits = bits_of(size)
    return [(bits[at], 1 << len(bits[at : at + 2])) for at in range(0, len(bits), 2)]


def swap(values, axis, size, bit):
    return lax.ppermute(values, axis, [(i, i ^ bit) for i in range(size)])


def in_order(found, mine):
    ordered = []
    for target in range(len(found)):
        value = found[0]
        for step in range(1, len(found)):
            value = jnp.where((mine ^ step) == target, found[step], value)
        ordered.append(value)
    return ordered


def start_group(held, size, low, count):
    return [held] + [swap(held, "dp", size, step * low) for step in range(1, count)]


def finish_stack(found, low, count):
    held = jnp.stack(in_order(found, (lax.axis_index("dp") // low) % count), axis=1)
    return held.reshape((-1,) + held.shape[2:])


def finish_group(found, low, count):
    held = jnp.stack(in_order(found, (lax.axis_index("dp") // low) % count))
    return held.reshape((-1,) + held.shape[2:])


def fold_pairs(values):
    count = values.shape[0] // 2
    return jnp.concatenate([values[:count], values[count:]], axis=-1)


def unfold_pairs(values):
    half = values.shape[-1] // 2
    return jnp.concatenate([values[..., :half], values[..., half:]], axis=0)


def join_columns(mine, other, rank):
    first = jnp.where(rank == 0, mine, other)
    second = jnp.where(rank == 0, other, mine)
    return jnp.concatenate([first, second], axis=-1)


def join_weights(mine, other, rank, count):
    lines, _, part, columns = mine.shape
    half = columns // 2
    full = [join_columns(mine[..., at : at + half], other[..., at : at + half], rank) for at in (0, half)]
    return jnp.moveaxis(jnp.concatenate(full, axis=1), 0, 1).reshape(count, lines * part, columns)


def half_columns(values, side):
    half = values.shape[-1] // 2
    return lax.dynamic_slice_in_dim(values, side * half, half, axis=values.ndim - 1)


def by_line(values, size):
    count, rows, columns = values.shape
    return values.reshape(count, size, rows // size, columns)


def two_parts(values):
    high = values.astype(bf16)
    return jnp.concatenate([high, (values - high.astype(f32)).astype(bf16)], axis=0)


def from_parts(parts):
    count = parts.shape[0] // 2
    return parts[:count].astype(f32) + parts[count:].astype(f32)


def pieces_of(held, low, count):
    n, lines = held.shape[:2]
    split = held.reshape((n, lines // count, count) + held.shape[2:])
    mine = (lax.axis_index("dp") // low) % count
    return [lax.dynamic_index_in_dim(split, mine ^ step, 2, keepdims=False) for step in range(count)]


def flat(values):
    return values.astype(bf16).reshape(-1, values.shape[-1])


def sum_everywhere(values, size):
    values = values + swap(values, "head", 2, 1)
    for bit in bits_of(size):
        values = values + swap(values, "dp", size, bit)
    return values


def after(first, second):
    return lax.optimization_barrier((first, second))


def adam_terms(grad_sum, first_old, second):
    first_new = BETA_ONE * first_old + (1.0 - BETA_ONE) * grad_sum
    second_new = BETA_TWO * second + (1.0 - BETA_TWO) * grad_sum * grad_sum
    direction = (
        first_new
        / (1.0 - BETA_ONE**STEP)
        / (jnp.sqrt(second_new / (1.0 - BETA_TWO**STEP)) + ADAM_EPS)
    )
    return (first_new, second_new, direction)


def moments_kernel(line_ref, norm_ref, *refs):
    count = 3
    grads, weights, firsts, seconds = (refs[n * count : (n + 1) * count] for n in range(4))
    new_firsts, new_seconds, updates = (refs[(4 + n) * count : (5 + n) * count] for n in range(3))
    sums_ref = refs[7 * count]
    width = sums_ref.shape[1]
    lane = lax.broadcasted_iota(jnp.int32, (1, width), 1)
    rows = [jnp.zeros((1, width), f32), jnp.zeros((1, width), f32)]
    at = 0
    for n in range(count):
        grad, weight = grads[n][...], weights[n][...]
        new_first, new_second, direction = adam_terms(grad, firsts[n][...], seconds[n][...])
        update = direction + DECAY * weight
        new_firsts[n][...], new_seconds[n][...], updates[n][...] = new_first, new_second, update
        matrices = weight.shape[0] if weight.ndim == 3 else 1
        for k in range(matrices):
            for row, values in enumerate((weight, update)):
                values = values[k] if weight.ndim == 3 else values
                total = jnp.sum(jnp.sum(values * values, axis=0, keepdims=True), axis=1, keepdims=True)
                if weight.ndim == 2:
                    total = jnp.where(line_ref[0] == 0, total, 0.0)
                rows[row] = jnp.where(lane == at, total, rows[row])
            at += 1
    gain = jnp.sum(norm_ref[0:8, :], axis=0, keepdims=True)
    bias = jnp.sum(norm_ref[8:16, :], axis=0, keepdims=True)
    sums_ref[...] = jnp.concatenate(rows + [gain, bias, jnp.zeros((4, width), f32)], axis=0)


def apply_kernel(sums_ref, norm_two_ref, norm_w_ref, norm_m_ref, norm_v_ref, *refs):
    count = 3
    weights, updates, news = (refs[n * count : (n + 1) * count] for n in range(3))
    new_norm_w_ref, new_norm_m_ref, new_norm_v_ref = refs[3 * count :]
    ratio = jnp.sqrt(sums_ref[0:1, :]) / jnp.sqrt(sums_ref[1:2, :])
    at = 0
    for n in range(count):
        shape = weights[n].shape
        if len(shape) == 3:
            for k in range(shape[0]):
                news[n][k] = weights[n][k] - RATE * ratio[:, at : at + 1] * updates[n][k]
                at += 1
        else:
            news[n][...] = weights[n][...] - RATE * ratio[:, at : at + 1] * updates[n][...]
            at += 1
    grads = jnp.concatenate([sums_ref[2:4, :], norm_two_ref[...]], axis=0)
    new_first, new_second, direction = adam_terms(grads, norm_m_ref[...], norm_v_ref[...])
    new_norm_m_ref[...], new_norm_v_ref[...] = new_first, new_second
    new_norm_w_ref[...] = norm_w_ref[...] - RATE * direction


def like(values):
    return [jax.ShapeDtypeStruct(v.shape, f32) for v in values]


def body(
    size,
    tokens, grad_out, segments, counts,
    attn_w, attn_m, attn_v, mlp_w, mlp_m, mlp_v, conv_w, conv_m, conv_v, norm_w, norm_m, norm_v,
):
    rank = lax.axis_index("head")
    place = lax.axis_index("dp")
    own_rows = segments.shape[0] // 2
    segments = lax.dynamic_slice_in_dim(segments, rank * own_rows, own_rows, axis=0)
    counts = lax.dynamic_slice_in_dim(counts, rank * own_rows, own_rows, axis=0)
    width = norm_w.shape[1]
    groups = groups_of(size)
    attn_lines = fold_pairs(attn_w.astype(bf16))[None]
    mlp_lines = mlp_w.astype(bf16)[None]
    for near, far in zip(groups[:-1], groups[:0:-1]):
        found, more = start_group(attn_lines, size, *far), start_group(mlp_lines, size, *near)
        attn_lines, mlp_lines = finish_stack(found, *far), finish_group(more, *near)
    _, early = after((attn_lines, mlp_lines), (tokens, grad_out))
    found = start_group(attn_lines, size, *groups[0])
    (normed, normed_t, out_grad_t), found = after(first_norm(*early, norm_w, own_rows), found)
    attn_lines = finish_stack(found, *groups[0])
    attn_use = join_weights(attn_lines, swap(attn_lines, "head", 2, 1), rank, attn_w.shape[0])
    found = start_group(mlp_lines, size, *groups[-1])
    conv_low = conv_w.astype(bf16)
    conv_use = join_columns(conv_low, swap(conv_low, "head", 2, 1), rank)
    starts, classes, images = attention_plan(segments, WIDE_TILE)
    back_starts, back_classes, _ = attention_plan(segments, TILE)
    middle, qkv, context, ext = attn_forward(starts, classes, counts, tokens, normed, attn_use, images)
    middle, found = after(middle, found)
    mlp_lines = finish_group(found, *groups[-1])
    mlp_lines = jnp.moveaxis(mlp_lines, 0, 1).reshape(mlp_w.shape[0], -1, mlp_w.shape[2])
    rank_at = rank.astype(jnp.int32).reshape(1)
    output, grad_middle, held, send, grad_conv, grad_norm_two = mlp_layer(
        line_places(segments), rank_at, middle, grad_out, out_grad_t, mlp_lines, swap(mlp_lines, "head", 2, 1),
        spread_taps(conv_use), norm_w,
    )

    def back(first, count, so_far):
        return attn_backward(
            first, count, so_far, back_starts, back_classes, counts, rank_at, normed_t, grad_middle, qkv, context, ext, attn_use, images
        )

    columns = conv_w.shape[1]
    norm_two = jnp.sum(grad_norm_two.reshape(2, 8, width), axis=1).reshape(1, 2 * width)
    norm_two = jnp.pad(norm_two, ((0, 0), (0, columns - 2 * width)))
    taps = grad_conv[:9]
    small = jnp.concatenate([half_columns(taps, rank), norm_two])
    small_send = jnp.concatenate([half_columns(taps, 1 - rank), norm_two])
    got = swap(jnp.concatenate([flat(send), two_parts(small_send)], axis=0), "head", 2, 1)
    first_rows = max(1, own_rows // 3)
    so_far, got = after(back(0, first_rows, None), got)
    rows = held.size // columns
    held = by_line(held + got[:rows].reshape(held.shape).astype(f32), size)
    small = from_parts(two_parts(small)) + from_parts(got[rows:])
    low, count = groups[0]
    pieces = pieces_of(held, low, count)
    small_parts = two_parts(small)
    gots = [
        swap(jnp.concatenate([flat(pieces[step]), small_parts], axis=0), "dp", size, step * low) for step in range(1, count)
    ]
    so_far, pieces = after(so_far, pieces)
    projected_grad, attn_held, attn_send = back(first_rows, own_rows - first_rows, so_far)

    def take(pieces, gots, small_parts, low, count):
        keep = pieces[0]
        rows = keep.size // keep.shape[-1]
        for got in gots:
            keep = keep + got[:rows].reshape(keep.shape).astype(f32)
        ordered = in_order([small_parts] + [got[rows:] for got in gots], (place // low) % count)
        return keep, sum(from_parts(part) for part in ordered)

    attn_got = swap(flat(attn_send), "head", 2, 1)
    attn_held, gots = after(attn_held, gots)
    held, small = take(pieces, gots, small_parts, low, count)
    rest = bits_of(size)[2:]
    attn_held = by_line(attn_held + attn_got.reshape(attn_held.shape).astype(f32), size)
    waiting = list(groups)
    blocks = tokens.shape[0] // FILL
    fills = [(0, blocks // 2), (blocks // 2, blocks - blocks // 2)]
    grad_tokens, grad_norm_one = None, 0.0
    while waiting or rest:
        attn_pieces, pieces, extra = [None], None, None
        if waiting:
            low, count = waiting.pop(0)
            attn_pieces = pieces_of(attn_held, low, count)
        sent = {step * low: [flat(attn_pieces[step])] for step in range(1, len(attn_pieces))}
        bit = None
        if rest:
            bit = rest.pop(0)
            pieces = pieces_of(held, bit, 2)
            small_parts = two_parts(small)
            extra = jnp.concatenate([flat(pieces[1]), small_parts], axis=0).reshape(-1, attn_held.shape[-1])
            sent.setdefault(bit, []).append(extra)
        fill = fills.pop(0) if fills else None
        if fill:
            sent, projected_grad = after(sent, projected_grad)
        gots = {step: swap(jnp.concatenate(parts, axis=0), "dp", size, step) for step, parts in sent.items()}
        if fill:
            results = tokens_back(*fill, grad_tokens, projected_grad, tokens, grad_middle, attn_use, norm_w)
            (grad_tokens, norm_one), gots = after(results, gots)
            grad_norm_one = grad_norm_one + norm_one
        if bit:
            got = gots[bit][gots[bit].shape[0] - extra.shape[0] :].reshape(-1, columns)
            held, small = take(pieces, [got], small_parts, bit, 2)
        if attn_pieces[0] is not None:
            attn_held = attn_pieces[0]
            rows = attn_held.size // attn_held.shape[-1]
            for step in range(1, len(attn_pieces)):
                attn_held = attn_held + gots[step * low][:rows].reshape(attn_held.shape).astype(f32)
    grad_attn = unfold_pairs(attn_held.reshape(attn_held.shape[:1] + attn_held.shape[2:]))
    grad_mlp = held.reshape(mlp_w.shape)
    norm_two = small[9, : 2 * width].reshape(2, width)

    weights, firsts, seconds = [attn_w, mlp_w, conv_w], [attn_m, mlp_m, conv_m], [attn_v, mlp_v, conv_v]
    scalars = pl.BlockSpec(memory_space=pltpu.SMEM)
    vectors = pl.BlockSpec(memory_space=pltpu.VMEM)
    results = pl.pallas_call(
        moments_kernel,
        in_specs=[scalars] + [vectors] * 13,
        out_specs=[vectors] * 10,
        out_shape=like(weights) * 3 + [jax.ShapeDtypeStruct((8, width), f32)],
        compiler_params=pltpu.CompilerParams(vmem_limit_bytes=16 * MIB),
    )(place.astype(jnp.int32).reshape(1), grad_norm_one, grad_attn, grad_mlp, small[:9], *weights, *firsts, *seconds)
    new_firsts, new_seconds, updates, sums = results[:3], results[3:6], results[6:9], results[9]
    new_w = pl.pallas_call(
        apply_kernel,
        in_specs=[vectors] * 11,
        out_specs=[vectors] * 6,
        out_shape=like(weights) + like([norm_w] * 3),
        compiler_params=pltpu.CompilerParams(vmem_limit_bytes=16 * MIB),
    )(sum_everywhere(sums, size), norm_two, norm_w, norm_m, norm_v, *weights, *updates)
    return (
        output, grad_tokens, new_w[0], new_firsts[0], new_seconds[0], new_w[1], new_firsts[1], new_seconds[1],
        new_w[2], new_firsts[2], new_seconds[2], *new_w[3:],
    )


def solution(mesh):
    rows, lines = P(("dp", "head"), None), P("dp", None)
    shards, columns = P(None, "dp", "head"), P(None, "head")
    in_specs = (rows, rows, lines, P("dp")) + (shards,) * 6 + (columns,) * 3 + (P(),) * 3
    out_specs = (rows, rows) + (shards,) * 6 + (columns,) * 3 + (P(),) * 3
    return jax.shard_map(
        functools.partial(body, mesh.shape["dp"]), mesh=mesh, in_specs=in_specs, out_specs=out_specs, check_vma=False
    )
```

```python
import functools
import jax
import jax.numpy as jnp
from jax import lax
from jax.experimental import pallas as pl
from jax.experimental.pallas import tpu as pltpu
from jax.sharding import PartitionSpec as P

HEAD_DIM = 64
GRID_W = 16
STEP = 10
IMAGES = 8

NORM_EPS = 1e-06
BETA_ONE = 0.9
BETA_TWO = 0.999
ADAM_EPS = 1e-06
DECAY = 0.01
RATE = 0.5
LOG2E = 1.4426950408889634
LN2 = 0.6931471805599453
BIG = 2.0**100
GELU_ONE = 0.7978845608028654
GELU_TWO = 0.044715
GELU_S = (GELU_ONE * GELU_TWO) ** (1.0 / 3.0)
GELU_A = GELU_ONE / GELU_S
ACT_SCALE = 0.5 / GELU_S
EXTRA = 32
PARTS = 4
TILE = 128
WIDE_TILE = 256
FILL = 512
LANES = 128
STRIDE = GRID_W + 8
MIB = 1024 * 1024

f32 = jnp.float32
bf16 = jnp.bfloat16
NN = (((1,), (0,)), ((), ()))
NT = (((1,), (1,)), ((), ()))
TN = (((0,), (0,)), ((), ()))


def dot(left, right, dims=NN):
    return lax.dot_general(left, right, dims, preferred_element_type=f32)


def work_of(micros):
    return pl.CostEstimate(flops=micros * 1_000_000_000, bytes_accessed=micros * 1_000_000, transcendentals=0)


def widths_for(length):
    return [w for w in (256, 384, 512, 640, 768) if w < length] + [length]


def norm_parts(values):
    average = jnp.mean(values, axis=-1, keepdims=True)
    centered = values - average
    inverse = lax.rsqrt(jnp.mean(centered * centered, axis=-1, keepdims=True) + NORM_EPS)
    return centered * inverse, inverse


def norm_back(upstream, gain_row, unit_rows, inverse):
    grad_unit = upstream * gain_row
    first_term = jnp.mean(grad_unit, axis=-1, keepdims=True)
    second_term = jnp.mean(grad_unit * unit_rows, axis=-1, keepdims=True)
    return inverse * (grad_unit - first_term - unit_rows * second_term)


def fold_rows(values):
    rows, columns = values.shape
    return jnp.sum(values.reshape(rows // 8, 8, columns), axis=0)


def pair_columns(flat):
    empty = jnp.zeros((HEAD_DIM, flat.shape[1]), flat.dtype)
    return jnp.concatenate(
        [jnp.concatenate([flat[:HEAD_DIM], empty], axis=0), jnp.concatenate([empty, flat[HEAD_DIM:]], axis=0)], axis=1
    )


def pair_rows(both):
    half = both.shape[1] // 2
    return jnp.concatenate([both[:HEAD_DIM, :half], both[HEAD_DIM:, half:]], axis=0)


def fold_max(values):
    pieces = [values[at : at + 64] for at in range(0, values.shape[0], 64)]
    while len(pieces) > 1:
        pieces = [jnp.maximum(a, b) for a, b in zip(pieces[::2], pieces[1::2])] + ([pieces[-1]] if len(pieces) % 2 else [])
    top = pieces[0]
    top = jnp.maximum(top[:32], top[32:])
    top = jnp.maximum(top[:16], top[16:])
    return jnp.max(jnp.maximum(top[:8], top[8:]), axis=0, keepdims=True)


def three_parts(value, part):
    high = value.astype(bf16).astype(f32)
    rest = value - high
    middle = rest.astype(bf16).astype(f32)
    return jnp.where(part == 0, high, jnp.where(part == 1, middle, rest - middle))


def image_tags(image_ref, start, rows):
    place = start + lax.broadcasted_iota(jnp.int32, (rows, LANES), 0)
    inside = (place >= image_ref[0, 0:1, :]) & (place < image_ref[0, 1:2, :])
    return jnp.where(inside, 1.0, 0.0).astype(bf16)


def first_norm_kernel(tokens_ref, out_grad_ref, norm_ref, normed_ref, normed_t_ref, out_grad_t_ref):
    big = 256

    def step(at, carry):
        rows = pl.ds(pl.multiple_of(at * big, big), big)
        unit, _ = norm_parts(tokens_ref[rows, :].astype(f32))
        normed_ref[rows, :] = (unit * norm_ref[0:1, :] + norm_ref[1:2, :]).astype(bf16)
        return carry

    lax.fori_loop(0, tokens_ref.shape[0] // big, step, 0)
    normed_t_ref[...] = jnp.transpose(normed_ref[...])
    out_grad_t_ref[...] = jnp.transpose(out_grad_ref[...])


def first_norm(tokens, out_grad, norm_w, row_count):
    rows_all, width = tokens.shape
    length = rows_all // row_count
    by_row = pl.BlockSpec((length, width), lambda r: (r, 0))
    turned = pl.BlockSpec((width, length), lambda r: (r, 0))
    flipped = jax.ShapeDtypeStruct((row_count * width, length), bf16)
    return pl.pallas_call(
        first_norm_kernel,
        grid=(row_count,),
        in_specs=[by_row, by_row, pl.BlockSpec(norm_w.shape, lambda r: (0, 0))],
        out_specs=[by_row, turned, turned],
        out_shape=[jax.ShapeDtypeStruct((rows_all, width), bf16), flipped, flipped],
        cost_estimate=work_of(8),
        compiler_params=pltpu.CompilerParams(vmem_limit_bytes=60 * MIB),
    )(tokens, out_grad, norm_w)


def attn_forward_kernel(
    start_ref, class_ref, count_ref, tokens_ref, normed_ref, w_ref, image_ref,
    middle_ref, qkv_ref, context_ref, ext_ref,
    tag_ref, qt_ref, vt_ref,
):
    row = pl.program_id(0)
    length, width = tokens_ref.shape
    pairs = width // LANES
    tag_ref[...] = image_tags(image_ref, 0, length)
    queries = (dot(normed_ref[...], w_ref[0]) * (HEAD_DIM**-0.5 * LOG2E)).astype(bf16)
    qkv_ref[:, :width] = queries
    qt_ref[...] = jnp.transpose(queries)
    qkv_ref[:, width : 2 * width] = dot(normed_ref[...], w_ref[1]).astype(bf16)
    values = dot(normed_ref[...], w_ref[2]).astype(bf16)
    qkv_ref[:, 2 * width :] = values
    vt_ref[...] = jnp.transpose(values)

    def tile(step, carry):
        q0 = pl.multiple_of(step * WIDE_TILE, WIDE_TILE)
        here = pl.ds(q0, WIDE_TILE)
        place = q0 + lax.broadcasted_iota(jnp.int32, (IMAGES, WIDE_TILE), 1)
        edges = [jnp.concatenate([image_ref[0, at : at + IMAGES, :]] * (WIDE_TILE // LANES), axis=1) for at in (8, 16)]
        inside = (place >= edges[0]) & (place < edges[1])
        mask = jnp.where(inside, 0.0, -BIG)
        mask_low = jnp.concatenate([mask, jnp.zeros((LANES - IMAGES, WIDE_TILE), f32)], axis=0).astype(bf16)
        ext_rows = lax.broadcasted_iota(jnp.int32, (EXTRA - IMAGES, WIDE_TILE), 0)

        def attend(window):
            there = pl.ds(pl.multiple_of(start_ref[row, step], LANES), window)
            tags = tag_ref[there, :]
            ones = jnp.ones((GRID_W, window), bf16)
            extra = jnp.zeros((EXTRA - IMAGES, WIDE_TILE), f32)
            slices = [slice(p * LANES, (p + 1) * LANES) for p in range(pairs)]
            masks = jnp.concatenate([mask_low, mask_low], axis=1)
            scores, tops, exponents, mixes = [], [], [], []
            for p, at in enumerate(slices):
                keys = qkv_ref[there, width + p * LANES : width + (p + 1) * LANES]
                right = jnp.concatenate([pair_columns(qt_ref[at, here]), masks], axis=0)
                scores.append(dot(jnp.concatenate([keys, tags], axis=1), right))
            for p in range(pairs):
                tops.append(fold_max(scores[p]))
                exponents.append(jnp.exp2(scores[p] - tops[p]).astype(bf16))
            for p, at in enumerate(slices):
                mixes.append(dot(jnp.concatenate([vt_ref[at, there], ones], axis=0), exponents[p]))
            for p, at in enumerate(slices):
                mixed = mixes[p]
                total = mixed[LANES : LANES + 1, :]
                minus_lse = -(tops[p] + jnp.log(total) * LOG2E)
                scale = 1.0 / total
                lane = lax.broadcasted_iota(jnp.int32, (1, 2 * WIDE_TILE), 1)
                head = 2 * p + jnp.where(lane < WIDE_TILE, 0, 1)
                scale = jnp.where(head < count_ref[row], scale, 0.0)
                context_ref[here, at] = jnp.transpose(pair_rows(mixed[:LANES] * scale)).astype(bf16)
                for h in range(2):
                    value = minus_lse[:, h * WIDE_TILE : (h + 1) * WIDE_TILE]
                    first = 6 * p + 3 * h
                    extra = jnp.where(
                        (ext_rows >= first) & (ext_rows < first + 3), three_parts(value, ext_rows - first), extra
                    )
            ext_ref[:, here] = jnp.concatenate([mask, extra], axis=0).astype(bf16)

        for index, window in enumerate(widths_for(length)):
            pl.when(class_ref[row, step] == index)(functools.partial(attend, window))
        return carry

    lax.fori_loop(0, length // WIDE_TILE, tile, 0)
    middle_ref[...] = tokens_ref[...].astype(f32) + dot(context_ref[...], w_ref[3], NT)


def attn_forward(starts, classes, counts, tokens, normed, attn_use, images):
    rows_all, width = tokens.shape
    row_count = counts.shape[0]
    length = rows_all // row_count
    by_row = lambda columns: pl.BlockSpec((length, columns), lambda r, *_: (r, 0))
    return pl.pallas_call(
        attn_forward_kernel,
        grid_spec=pltpu.PrefetchScalarGridSpec(
            num_scalar_prefetch=3,
            grid=(row_count,),
            in_specs=[
                by_row(width),
                by_row(width),
                pl.BlockSpec(attn_use.shape, lambda r, *_: (0, 0, 0)),
                pl.BlockSpec((1, 24, LANES), lambda r, *_: (r, 0, 0)),
            ],
            out_specs=[
                by_row(width), by_row(3 * width), by_row(width), pl.BlockSpec((EXTRA, length), lambda r, *_: (r, 0))
            ],
            scratch_shapes=[
                pltpu.VMEM((length, LANES), bf16),
                pltpu.VMEM((width, length), bf16),
                pltpu.VMEM((width, length), bf16),
            ],
        ),
        out_shape=[
            jax.ShapeDtypeStruct((rows_all, width), f32),
            jax.ShapeDtypeStruct((rows_all, 3 * width), bf16),
            jax.ShapeDtypeStruct((rows_all, width), bf16),
            jax.ShapeDtypeStruct((row_count * EXTRA, length), bf16),
        ],
        cost_estimate=work_of(30),
        compiler_params=pltpu.CompilerParams(vmem_limit_bytes=56 * MIB),
    )(starts, classes, counts, tokens, normed, attn_use, images)


def attn_backward_kernel(
    first, final, start_ref, class_ref, count_ref, rank_ref, normed_t_ref, middle_grad_ref, qkv_ref, context_ref, ext_ref, w_ref,
    image_ref, *refs,
):
    sums = None
    if first:
        sums, refs = refs[1], refs[2:]
    sent = None
    if final:
        proj_ref, keep_ref, send_ref, *scratch, w_grad_ref = refs
        sent = (keep_ref, send_ref)
    else:
        proj_ref, w_grad_ref, *scratch = refs
    attn_backward_row(
        first, sums, sent, start_ref, class_ref, count_ref, rank_ref, normed_t_ref, middle_grad_ref, qkv_ref, context_ref, ext_ref,
        w_ref, image_ref, proj_ref, w_grad_ref, *scratch,
    )


def attn_backward_row(
    first, sums, sent, start_ref, class_ref, count_ref, rank_ref, normed_t_ref, middle_grad_ref, qkv_ref, context_ref, ext_ref, w_ref,
    image_ref, proj_ref, w_grad_ref,
    tag_ref, up_ref, delta_ref, dq_ref, dk_ref, dv_ref, low_ref, qt_ref, kt_ref, upt_ref,
):
    step_at = pl.program_id(0)
    row = first + step_at
    length, width = middle_grad_ref.shape
    pairs = width // LANES
    big = 256

    @pl.when(step_at == 0)
    def _():
        w_grad_ref[...] = jnp.zeros_like(w_grad_ref) if sums is None else sums[...]

    target = lax.broadcasted_iota(jnp.int32, (EXTRA, width), 0) - IMAGES
    source = lax.broadcasted_iota(jnp.int32, (EXTRA, width), 1) // HEAD_DIM * 3
    collect = jnp.where((target >= source) & (target < source + 3), -1.0, 0.0).astype(bf16)
    active = jnp.where(
        lax.broadcasted_iota(jnp.int32, (1, width), 1) // HEAD_DIM < count_ref[row], 1.0, 0.0
    )

    def prepare(step, carry):
        rows = pl.ds(pl.multiple_of(step * big, big), big)
        tag_ref[rows, :] = image_tags(image_ref, step * big, big)
        low_ref[rows, :] = middle_grad_ref[rows, :].astype(bf16)
        dk_ref[rows, :] = jnp.zeros((big, width), f32)
        dv_ref[rows, :] = jnp.zeros((big, width), f32)
        return carry

    lax.fori_loop(0, length // big, prepare, 0)
    up = (dot(low_ref[...], w_ref[3]) * active).astype(bf16)
    up_ref[...] = up
    upt_ref[...] = jnp.transpose(up)
    qt_ref[...] = jnp.transpose(qkv_ref[:, :width])
    kt_ref[...] = jnp.transpose(qkv_ref[:, width : 2 * width])

    def gather(step, carry):
        rows = pl.ds(pl.multiple_of(step * big, big), big)
        product = up_ref[rows, :].astype(f32) * context_ref[rows, :].astype(f32)
        high = product.astype(bf16)
        rest = (product - high.astype(f32)).astype(bf16)
        delta = dot(collect, high, NT) + dot(collect, rest, NT)
        part = lax.rem(lax.broadcasted_iota(jnp.int32, (EXTRA, big), 0) + 3 * EXTRA - IMAGES, 3)
        delta_ref[:, rows] = three_parts(delta, part).astype(bf16)
        return carry

    lax.fori_loop(0, length // big, gather, 0)
    lane = lax.broadcasted_iota(jnp.int32, (1, LANES), 1)
    first_half = jnp.where(lane < HEAD_DIM, 1.0, 0.0).astype(bf16)
    second_half = jnp.where(lane >= HEAD_DIM, 1.0, 0.0).astype(bf16)

    def tile(step, carry):
        q0 = pl.multiple_of(step * TILE, TILE)
        here = pl.ds(q0, TILE)

        def attend(window):
            there = pl.ds(pl.multiple_of(start_ref[row, step], LANES), window)
            tags = tag_ref[there, :]
            ext = ext_ref[:, here]
            delta = delta_ref[:, here]
            at_row = lax.broadcasted_iota(jnp.int32, (EXTRA, LANES), 0)
            empty = jnp.zeros((LANES - EXTRA, 2 * TILE), bf16)

            def own(edge, masks):
                keep = (at_row >= edge) & (at_row < edge + 3)
                return jnp.where(keep | (at_row < IMAGES) if masks else keep, 1.0, 0.0).astype(bf16)

            slices = [slice(p * LANES, (p + 1) * LANES) for p in range(pairs)]
            scores, grad_probs, probs, grad_scores = [], [], [], []
            for p, at in enumerate(slices):
                keys = qkv_ref[there, width + p * LANES : width + (p + 1) * LANES]
                values = qkv_ref[there, 2 * width + p * LANES : 2 * width + (p + 1) * LANES]
                edge = IMAGES + 6 * p
                q_side = jnp.concatenate(
                    [
                        pair_columns(qt_ref[at, here]),
                        jnp.concatenate([ext * own(edge, True), ext * own(edge + 3, True)], axis=1),
                        empty,
                    ],
                    axis=0,
                )
                up_side = jnp.concatenate(
                    [
                        pair_columns(upt_ref[at, here]),
                        jnp.concatenate([delta * own(edge, False), delta * own(edge + 3, False)], axis=1),
                        empty,
                    ],
                    axis=0,
                )
                scores.append(dot(jnp.concatenate([keys, tags], axis=1), q_side))
                grad_probs.append(dot(jnp.concatenate([values, tags], axis=1), up_side))
            for p in range(pairs):
                weight = jnp.exp2(scores[p])
                probs.append(weight.astype(bf16))
                grad_scores.append((weight * grad_probs[p]).astype(bf16))
            for p, at in enumerate(slices):
                queries, ups = qkv_ref[here, at], up_ref[here, at]
                q_pair = jnp.concatenate([queries * first_half, queries * second_half], axis=0)
                up_pair = jnp.concatenate([ups * first_half, ups * second_half], axis=0)
                dv_ref[there, at] += dot(probs[p], up_pair)
                dk_ref[there, at] += dot(grad_scores[p], q_pair)
                dq = pair_rows(dot(kt_ref[at, there], grad_scores[p]))
                dq_ref[here, at] = jnp.transpose(dq * HEAD_DIM**-0.5).astype(bf16)

        for index, window in enumerate(widths_for(length)):
            pl.when(class_ref[row, step] == index)(functools.partial(attend, window))
        return carry

    lax.fori_loop(0, length // TILE, tile, 0)
    keys_grad = (dk_ref[...] * LN2).astype(bf16)
    values_grad = dv_ref[...].astype(bf16)
    proj_ref[...] = jnp.concatenate([dq_ref[...], keys_grad, values_grad], axis=1)
    for k in range(3):
        w_grad_ref[k] += dot(normed_t_ref[...], proj_ref[:, k * width : (k + 1) * width])
    w_grad_ref[3] += dot(jnp.transpose(low_ref[...]), context_ref[...])
    if sent:

        @pl.when(step_at == pl.num_programs(0) - 1)
        def _():
            for k in range(2):
                one, two = w_grad_ref[k], w_grad_ref[k + 2]
                halves = [jnp.concatenate([one[:, at : at + width // 2], two[:, at : at + width // 2]], axis=1) for at in (0, width // 2)]
                sent[0][k] = jnp.where(rank_ref[0] == 0, halves[0], halves[1])
                sent[1][k] = jnp.where(rank_ref[0] == 0, halves[1], halves[0]).astype(bf16)


def attn_backward(first, count, so_far, starts, classes, counts, rank, normed_t, middle_grad, qkv, context, ext, attn_use, images):
    rows_all, width = middle_grad.shape
    length = rows_all // counts.shape[0]
    by_row = lambda columns: pl.BlockSpec((length, columns), lambda r, *_: (first + r, 0))
    final = first + count == counts.shape[0]
    half = (2, width, width)
    halves = pl.BlockSpec(half, lambda r, *_: (0, 0, 0))
    whole = pl.BlockSpec(attn_use.shape, lambda r, *_: (0, 0, 0))
    return pl.pallas_call(
        functools.partial(attn_backward_kernel, first, final),
        grid_spec=pltpu.PrefetchScalarGridSpec(
            num_scalar_prefetch=4,
            grid=(count,),
            in_specs=[
                pl.BlockSpec((width, length), lambda r, *_: (first + r, 0)),
                by_row(width),
                by_row(3 * width),
                by_row(width),
                pl.BlockSpec((EXTRA, length), lambda r, *_: (first + r, 0)),
                whole,
                pl.BlockSpec((1, 24, LANES), lambda r, *_: (first + r, 0, 0)),
            ]
            + ([pl.BlockSpec(memory_space=pl.ANY), whole] if first else []),
            out_specs=[by_row(3 * width)] + ([halves, halves] if final else [whole]),
            scratch_shapes=[
                pltpu.VMEM((length, LANES), bf16),
                pltpu.VMEM((length, width), bf16),
                pltpu.VMEM((EXTRA, length), bf16),
                pltpu.VMEM((length, width), bf16),
                pltpu.VMEM((length, width), f32),
                pltpu.VMEM((length, width), f32),
                pltpu.VMEM((length, width), bf16),
                pltpu.VMEM((width, length), bf16),
                pltpu.VMEM((width, length), bf16),
                pltpu.VMEM((width, length), bf16),
            ]
            + ([pltpu.VMEM(attn_use.shape, f32)] if final else []),
        ),
        out_shape=[jax.ShapeDtypeStruct((rows_all, 3 * width), bf16)]
        + (
            [jax.ShapeDtypeStruct(half, f32), jax.ShapeDtypeStruct(half, bf16)]
            if final
            else [jax.ShapeDtypeStruct(attn_use.shape, f32)]
        ),
        input_output_aliases={11: 0} if first else {},
        cost_estimate=work_of(18 * count),
        compiler_params=pltpu.CompilerParams(vmem_limit_bytes=60 * MIB),
    )(starts, classes, counts, rank, normed_t, middle_grad, qkv, context, ext, attn_use, images, *(so_far or ()))


def tokens_back_kernel(proj_ref, tokens_ref, middle_grad_ref, w_ref, norm_ref, *refs):
    tokens_grad_ref, norm_grad_ref = refs[-2:]

    @pl.when(pl.program_id(0) == 0)
    def _():
        norm_grad_ref[...] = jnp.zeros_like(norm_grad_ref)

    w_cat = jnp.concatenate([w_ref[0], w_ref[1], w_ref[2]], axis=1)
    upstream = dot(proj_ref[...], w_cat, NT)
    unit, inverse = norm_parts(tokens_ref[...].astype(f32))
    tokens_grad_ref[...] = middle_grad_ref[...] + norm_back(upstream, norm_ref[0:1, :], unit, inverse)
    norm_grad_ref[0:8, :] += fold_rows(upstream * unit)
    norm_grad_ref[8:16, :] += fold_rows(upstream)


def tokens_back(first, count, so_far, proj, tokens, middle_grad, attn_use, norm_w):
    rows_all, width = tokens.shape
    some = lambda columns: pl.BlockSpec((FILL, columns), lambda r: (first + r, 0))
    return pl.pallas_call(
        tokens_back_kernel,
        grid=(count,),
        in_specs=[
            some(3 * width),
            some(width),
            some(width),
            pl.BlockSpec(attn_use.shape, lambda r: (0, 0, 0)),
            pl.BlockSpec(norm_w.shape, lambda r: (0, 0)),
        ]
        + ([] if so_far is None else [pl.BlockSpec(memory_space=pl.ANY)]),
        out_specs=[some(width), pl.BlockSpec((16, width), lambda r: (0, 0))],
        out_shape=[jax.ShapeDtypeStruct((rows_all, width), f32), jax.ShapeDtypeStruct((16, width), f32)],
        input_output_aliases={} if so_far is None else {5: 0},
        cost_estimate=work_of(2 * count),
        compiler_params=pltpu.CompilerParams(vmem_limit_bytes=60 * MIB),
    )(proj, tokens, middle_grad, attn_use, norm_w, *([] if so_far is None else [so_far]))


def mlp_kernel(
    place_ref, rank_ref, middle_ref, out_grad_ref, out_grad_t_ref, own_w_ref, other_w_ref, taps_ref, norm_ref,
    output_ref, middle_grad_ref, keep_ref, send_ref, taps_grad_ref, norm_grad_ref,
    w_ref, w_grad_ref, unit_ref, inverse_ref, normed_ref, normed_t_ref, out_sum_ref, up_sum_ref, tap_sum_ref,
    act_grads_ref, acts_ref, hidden_grads_ref, *buffers,
):
    row = pl.program_id(0)
    length, width = middle_ref.shape
    hidden = w_ref.shape[2]
    chunk = PARTS * LANES
    big = 256
    grid_rows = length // GRID_W
    chunks = hidden // chunk
    h_refs, g_refs = buffers[:PARTS], buffers[PARTS:]
    gain, bias = norm_ref[2:3, :], norm_ref[3:4, :]

    @pl.when(row == 0)
    def _():
        w_grad_ref[...] = jnp.zeros_like(w_grad_ref)
        norm_grad_ref[...] = jnp.zeros_like(norm_grad_ref)
        tap_sum_ref[...] = jnp.zeros_like(tap_sum_ref)
        for rank, halves in enumerate(((own_w_ref, other_w_ref), (other_w_ref, own_w_ref))):

            @pl.when(rank_ref[0] == rank)
            def _():
                w_ref[:, :, : hidden // 2] = halves[0][...]
                w_ref[:, :, hidden // 2 :] = halves[1][...]

        for ref in buffers:
            ref[...] = jnp.zeros_like(ref)

    def place(r):
        return pl.multiple_of(place_ref[row, r], 8)

    for n in range(IMAGES + 1):
        at = place(grid_rows + n)
        for ref in buffers:
            ref[pl.ds(at, GRID_W), :] = jnp.zeros((GRID_W, LANES), f32)

    def normalize(step, carry):
        rows = pl.ds(pl.multiple_of(step * big, big), big)
        middle = middle_ref[rows, :]
        unit, inverse = norm_parts(middle)
        unit_ref[rows, :] = unit
        inverse_ref[rows, :] = jnp.broadcast_to(inverse, (big, LANES))
        normed_ref[rows, :] = (unit * gain + bias).astype(bf16)
        out_sum_ref[rows, :] = jnp.zeros((big, width), f32)
        up_sum_ref[rows, :] = jnp.zeros((big, width), f32)
        return carry

    lax.fori_loop(0, length // big, normalize, 0)
    normed_t_ref[...] = jnp.transpose(normed_ref[...])

    def lanes_of(c):
        return pl.ds(pl.multiple_of(c * chunk, chunk), chunk)

    def lanes_of(c):
        return pl.ds(pl.multiple_of(c * chunk, chunk), chunk)

    def neighbours(ref, at):
        return [ref[pl.ds(at + (a * STRIDE + b), GRID_W), :] for a in (-1, 0, 1) for b in (-1, 0, 1)]

    def tall(values):
        return jnp.concatenate([values, values], axis=0)

    def total_of(terms):
        while len(terms) > 1:
            terms = [a + b for a, b in zip(terms[::2], terms[1::2])] + ([terms[-1]] if len(terms) % 2 else [])
        return terms[0]

    def taps_for(c, part, at):
        lane = pl.ds(pl.multiple_of(c * chunk + part * LANES, LANES), LANES)
        return [tall(taps_ref[at + k * 8 : at + (k + 1) * 8, lane]) for k in range(9)]

    lines = 8

    def do_chunk(c, carry):
        lanes = lanes_of(c)
        for t in range(length // big):
            rows = slice(t * big, (t + 1) * big)
            values = dot(normed_ref[rows, :], w_ref[0, :, lanes])
            for part in range(PARTS):
                for s in range(big // GRID_W):
                    at = place(t * (big // GRID_W) + s)
                    h_refs[part][pl.ds(at, GRID_W), :] = values[
                        s * GRID_W : (s + 1) * GRID_W, part * LANES : (part + 1) * LANES
                    ]
        act_grads_ref[...] = dot(out_grad_ref[...], w_ref[1, :, lanes])

        def forward(t, carry):
            tokens_base = pl.multiple_of(t * (lines * GRID_W), lines * GRID_W)
            for part in range(PARTS):
                taps = taps_for(c, part, 0)
                cols = slice(part * LANES, (part + 1) * LANES)
                for s in range(lines):
                    near = pl.ds(pl.multiple_of(tokens_base + s * GRID_W, GRID_W), GRID_W)
                    at = place(t * lines + s)
                    x = total_of([x * tap for x, tap in zip(neighbours(h_refs[part], at), taps)])
                    square = x * x
                    value = jnp.tanh(x * (GELU_A + square))
                    gate = 1.0 + value
                    twice = x * gate
                    acts_ref[near, cols] = twice.astype(bf16)
                    slope = gate + (twice * (1.0 - value)) * (GELU_A + 3.0 * square)
                    g_refs[part][pl.ds(at, GRID_W), :] = act_grads_ref[near, cols] * slope
            return carry

        lax.fori_loop(0, grid_rows // lines, forward, 0)

        def backward(t, carry):
            tokens_base = pl.multiple_of(t * (lines * GRID_W), lines * GRID_W)
            for part in range(PARTS):
                taps = taps_for(c, part, 72)
                lane = pl.ds(pl.multiple_of(c * chunk + part * LANES, LANES), LANES)
                cols = slice(part * LANES, (part + 1) * LANES)
                totals = [None] * 9
                for s in range(lines):
                    near = pl.ds(pl.multiple_of(tokens_base + s * GRID_W, GRID_W), GRID_W)
                    at = place(t * lines + s)
                    source = h_refs[part][pl.ds(at, GRID_W), :]
                    moved = neighbours(g_refs[part], at)[::-1]
                    for k in range(9):
                        product = source * moved[k]
                        folded = product[:8] + product[8:]
                        totals[k] = folded if totals[k] is None else totals[k] + folded
                    terms = [x * tap for x, tap in zip(moved, taps)]
                    hidden_grads_ref[near, cols] = total_of(terms).astype(bf16)
                for k in range(9):
                    tap_sum_ref[k * 8 : (k + 1) * 8, lane] += totals[k]
            return carry

        lax.fori_loop(0, grid_rows // lines, backward, 0)
        w_grad_ref[0, :, lanes] += dot(normed_t_ref[...], hidden_grads_ref[...])
        w_grad_ref[1, :, lanes] += dot(out_grad_t_ref[...], acts_ref[...])
        out_sum_ref[...] += dot(acts_ref[...], w_ref[1, :, lanes], NT)
        up_sum_ref[...] += dot(hidden_grads_ref[...], w_ref[0, :, lanes], NT)
        return carry

    lax.fori_loop(0, chunks, do_chunk, 0)

    def finish(step, carry):
        rows = pl.ds(pl.multiple_of(step * big, big), big)
        middle = middle_ref[rows, :]
        output_ref[rows, :] = (middle + ACT_SCALE * out_sum_ref[rows, :]).astype(bf16)
        upstream = 0.5 * up_sum_ref[rows, :]
        unit = unit_ref[rows, :]
        inverse = jnp.concatenate([inverse_ref[rows, :]] * (width // LANES), axis=1)
        middle_grad_ref[rows, :] = out_grad_ref[rows, :].astype(f32) + norm_back(upstream, gain, unit, inverse)
        norm_grad_ref[0:8, :] += fold_rows(upstream * unit)
        norm_grad_ref[8:16, :] += fold_rows(upstream)
        return carry

    lax.fori_loop(0, length // big, finish, 0)

    @pl.when(row == pl.num_programs(0) - 1)
    def _():
        for k, scale in enumerate((0.5, ACT_SCALE)):
            halves = w_grad_ref[k, :, : hidden // 2], w_grad_ref[k, :, hidden // 2 :]
            keep_ref[k] = scale * jnp.where(rank_ref[0] == 0, halves[0], halves[1])
            send_ref[k] = (scale * jnp.where(rank_ref[0] == 0, halves[1], halves[0])).astype(bf16)
        taps_grad_ref[...] = jnp.zeros_like(taps_grad_ref)
        for k in range(9):
            total = jnp.sum(tap_sum_ref[k * 8 : (k + 1) * 8, :], axis=0, keepdims=True)
            taps_grad_ref[k : k + 1, :] = 0.5 * total


def mlp_layer(places, rank, middle, out_grad, out_grad_t, own_w, other_w, taps, norm_w):
    rows_all, width = middle.shape
    row_count = places.shape[0]
    length = rows_all // row_count
    half = own_w.shape
    hidden = 2 * half[2]
    whole = half[:2] + (hidden,)
    by_row = lambda columns: pl.BlockSpec((length, columns), lambda r, *_: (r, 0))
    slots = (length // GRID_W + IMAGES + 2) * STRIDE
    return pl.pallas_call(
        mlp_kernel,
        grid_spec=pltpu.PrefetchScalarGridSpec(
            num_scalar_prefetch=2,
            grid=(row_count,),
            in_specs=[
                by_row(width),
                by_row(width),
                pl.BlockSpec((width, length), lambda r, *_: (r, 0)),
                pl.BlockSpec(half, lambda r, *_: (0, 0, 0)),
                pl.BlockSpec(half, lambda r, *_: (0, 0, 0)),
                pl.BlockSpec(taps.shape, lambda r, *_: (0, 0)),
                pl.BlockSpec(norm_w.shape, lambda r, *_: (0, 0)),
            ],
            out_specs=[
                by_row(width),
                by_row(width),
                pl.BlockSpec(half, lambda r, *_: (0, 0, 0)),
                pl.BlockSpec(half, lambda r, *_: (0, 0, 0)),
                pl.BlockSpec((16, hidden), lambda r, *_: (0, 0)),
                pl.BlockSpec((16, width), lambda r, *_: (0, 0)),
            ],
            scratch_shapes=[
                pltpu.VMEM(whole, bf16),
                pltpu.VMEM(whole, f32),
                pltpu.VMEM((length, width), f32),
                pltpu.VMEM((length, LANES), f32),
                pltpu.VMEM((length, width), bf16),
                pltpu.VMEM((width, length), bf16),
                pltpu.VMEM((length, width), f32),
                pltpu.VMEM((length, width), f32),
                pltpu.VMEM((9 * 8, hidden), f32),
                pltpu.VMEM((length, PARTS * LANES), f32),
                pltpu.VMEM((length, PARTS * LANES), bf16),
                pltpu.VMEM((length, PARTS * LANES), bf16),
            ]
            + [pltpu.VMEM((slots, LANES), f32)] * (2 * PARTS),
        ),
        out_shape=[
            jax.ShapeDtypeStruct((rows_all, width), bf16),
            jax.ShapeDtypeStruct((rows_all, width), f32),
            jax.ShapeDtypeStruct(half, f32),
            jax.ShapeDtypeStruct(half, bf16),
            jax.ShapeDtypeStruct((16, hidden), f32),
            jax.ShapeDtypeStruct((16, width), f32),
        ],
        cost_estimate=work_of(90),
        compiler_params=pltpu.CompilerParams(vmem_limit_bytes=50 * MIB),
    )(places, rank, middle, out_grad, out_grad_t, own_w, other_w, taps, norm_w)


def attention_plan(segments, tile):
    row_count, length = segments.shape
    tiles = segments.reshape(row_count, length // tile, tile)
    first, last = tiles[:, :, 0], tiles[:, :, -1]
    ids = jnp.arange(IMAGES, dtype=jnp.int32)
    begins = jnp.sum((segments[:, None, :] < ids[None, :, None]).astype(jnp.int32), axis=-1)
    ends = jnp.sum((segments[:, None, :] <= ids[None, :, None]).astype(jnp.int32), axis=-1)
    low_end = jnp.sum(jnp.where(first[:, :, None] == ids, begins[:, None, :], 0), axis=-1) // LANES * LANES
    high_end = jnp.sum(jnp.where(last[:, :, None] == ids, ends[:, None, :], 0), axis=-1)
    widths = widths_for(length)
    classes = sum(((high_end - low_end) > w).astype(jnp.int32) for w in widths[:-1])
    chosen = jnp.full_like(classes, widths[-1])
    for index, w in enumerate(widths):
        chosen = jnp.where(classes == index, w, chosen)
    starts = jnp.minimum(low_end, length - chosen)
    used = jnp.zeros((row_count, EXTRA - IMAGES), jnp.int32)
    unused = jnp.zeros((row_count, LANES - EXTRA), jnp.int32)
    first_lane = jnp.concatenate([begins, used, unused], axis=1)
    end_lane = jnp.concatenate([ends, used + length, unused], axis=1)
    by_lane = jnp.pad(jnp.stack([first_lane, end_lane], axis=1), ((0, 0), (0, 6), (0, 0)))
    by_image = jnp.broadcast_to(jnp.concatenate([begins, ends], axis=1)[:, :, None], (row_count, 2 * IMAGES, LANES))
    return starts, classes, jnp.concatenate([by_lane, by_image], axis=1)


def spread_taps(conv_use):
    taps = conv_use.astype(f32)
    own = (jnp.arange(9) == 4).astype(f32)[:, None]
    taps = jnp.repeat(taps + own, 8, axis=0)
    return jnp.concatenate([taps * GELU_S, taps], axis=0)


def line_places(segments):
    ids = segments[:, ::GRID_W]
    count = ids.shape[1]
    rows = jnp.arange(count, dtype=jnp.int32) + ids + 1
    images = jnp.arange(IMAGES, dtype=jnp.int32)
    first = jnp.sum((ids[:, None, :] < images[None, :, None]).astype(jnp.int32), axis=-1)
    gaps = jnp.concatenate([first + images, jnp.full((ids.shape[0], 1), count + IMAGES, jnp.int32)], axis=1)
    return jnp.concatenate([rows, gaps], axis=1) * STRIDE + 8


def bits_of(size):
    bits = []
    b = 1
    while b < size:
        bits.append(b)
        b *= 2
    return bits


def groups_of(size):
    bits = bits_of(size)
    return [(bits[at], 1 << len(bits[at : at + 2])) for at in range(0, len(bits), 2)]


def swap(values, axis, size, bit):
    return lax.ppermute(values, axis, [(i, i ^ bit) for i in range(size)])


def in_order(found, mine):
    ordered = []
    for target in range(len(found)):
        value = found[0]
        for step in range(1, len(found)):
            value = jnp.where((mine ^ step) == target, found[step], value)
        ordered.append(value)
    return ordered


def start_group(held, size, low, count):
    return [held] + [swap(held, "dp", size, step * low) for step in range(1, count)]


def finish_stack(found, low, count):
    held = jnp.stack(in_order(found, (lax.axis_index("dp") // low) % count), axis=1)
    return held.reshape((-1,) + held.shape[2:])


def finish_group(found, low, count):
    held = jnp.stack(in_order(found, (lax.axis_index("dp") // low) % count))
    return held.reshape((-1,) + held.shape[2:])


def fold_pairs(values):
    count = values.shape[0] // 2
    return jnp.concatenate([values[:count], values[count:]], axis=-1)


def unfold_pairs(values):
    half = values.shape[-1] // 2
    return jnp.concatenate([values[..., :half], values[..., half:]], axis=0)


def join_columns(mine, other, rank):
    first = jnp.where(rank == 0, mine, other)
    second = jnp.where(rank == 0, other, mine)
    return jnp.concatenate([first, second], axis=-1)


def join_weights(mine, other, rank, count):
    lines, _, part, columns = mine.shape
    half = columns // 2
    full = [join_columns(mine[..., at : at + half], other[..., at : at + half], rank) for at in (0, half)]
    return jnp.moveaxis(jnp.concatenate(full, axis=1), 0, 1).reshape(count, lines * part, columns)


def half_columns(values, side):
    half = values.shape[-1] // 2
    return lax.dynamic_slice_in_dim(values, side * half, half, axis=values.ndim - 1)


def by_line(values, size):
    count, rows, columns = values.shape
    return values.reshape(count, size, rows // size, columns)


def two_parts(values):
    high = values.astype(bf16)
    return jnp.concatenate([high, (values - high.astype(f32)).astype(bf16)], axis=0)


def from_parts(parts):
    count = parts.shape[0] // 2
    return parts[:count].astype(f32) + parts[count:].astype(f32)


def pieces_of(held, low, count):
    n, lines = held.shape[:2]
    split = held.reshape((n, lines // count, count) + held.shape[2:])
    mine = (lax.axis_index("dp") // low) % count
    return [lax.dynamic_index_in_dim(split, mine ^ step, 2, keepdims=False) for step in range(count)]


def flat(values):
    return values.astype(bf16).reshape(-1, values.shape[-1])


def sum_everywhere(values, size):
    values = values + swap(values, "head", 2, 1)
    for bit in bits_of(size):
        values = values + swap(values, "dp", size, bit)
    return values


def after(first, second):
    return lax.optimization_barrier((first, second))


def adam_terms(grad_sum, first_old, second):
    first_new = BETA_ONE * first_old + (1.0 - BETA_ONE) * grad_sum
    second_new = BETA_TWO * second + (1.0 - BETA_TWO) * grad_sum * grad_sum
    direction = (
        first_new
        / (1.0 - BETA_ONE**STEP)
        / (jnp.sqrt(second_new / (1.0 - BETA_TWO**STEP)) + ADAM_EPS)
    )
    return (first_new, second_new, direction)


def moments_kernel(line_ref, norm_ref, *refs):
    count = 3
    grads, weights, firsts, seconds = (refs[n * count : (n + 1) * count] for n in range(4))
    new_firsts, new_seconds, updates = (refs[(4 + n) * count : (5 + n) * count] for n in range(3))
    sums_ref = refs[7 * count]
    width = sums_ref.shape[1]
    lane = lax.broadcasted_iota(jnp.int32, (1, width), 1)
    rows = [jnp.zeros((1, width), f32), jnp.zeros((1, width), f32)]
    at = 0
    for n in range(count):
        grad, weight = grads[n][...], weights[n][...]
        new_first, new_second, direction = adam_terms(grad, firsts[n][...], seconds[n][...])
        update = direction + DECAY * weight
        new_firsts[n][...], new_seconds[n][...], updates[n][...] = new_first, new_second, update
        matrices = weight.shape[0] if weight.ndim == 3 else 1
        for k in range(matrices):
            for row, values in enumerate((weight, update)):
                values = values[k] if weight.ndim == 3 else values
                total = jnp.sum(jnp.sum(values * values, axis=0, keepdims=True), axis=1, keepdims=True)
                if weight.ndim == 2:
                    total = jnp.where(line_ref[0] == 0, total, 0.0)
                rows[row] = jnp.where(lane == at, total, rows[row])
            at += 1
    gain = jnp.sum(norm_ref[0:8, :], axis=0, keepdims=True)
    bias = jnp.sum(norm_ref[8:16, :], axis=0, keepdims=True)
    sums_ref[...] = jnp.concatenate(rows + [gain, bias, jnp.zeros((4, width), f32)], axis=0)


def apply_kernel(sums_ref, norm_two_ref, norm_w_ref, norm_m_ref, norm_v_ref, *refs):
    count = 3
    weights, updates, news = (refs[n * count : (n + 1) * count] for n in range(3))
    new_norm_w_ref, new_norm_m_ref, new_norm_v_ref = refs[3 * count :]
    ratio = jnp.sqrt(sums_ref[0:1, :]) / jnp.sqrt(sums_ref[1:2, :])
    at = 0
    for n in range(count):
        shape = weights[n].shape
        if len(shape) == 3:
            for k in range(shape[0]):
                news[n][k] = weights[n][k] - RATE * ratio[:, at : at + 1] * updates[n][k]
                at += 1
        else:
            news[n][...] = weights[n][...] - RATE * ratio[:, at : at + 1] * updates[n][...]
            at += 1
    grads = jnp.concatenate([sums_ref[2:4, :], norm_two_ref[...]], axis=0)
    new_first, new_second, direction = adam_terms(grads, norm_m_ref[...], norm_v_ref[...])
    new_norm_m_ref[...], new_norm_v_ref[...] = new_first, new_second
    new_norm_w_ref[...] = norm_w_ref[...] - RATE * direction


def like(values):
    return [jax.ShapeDtypeStruct(v.shape, f32) for v in values]


def body(
    size,
    tokens, grad_out, segments, counts,
    attn_w, attn_m, attn_v, mlp_w, mlp_m, mlp_v, conv_w, conv_m, conv_v, norm_w, norm_m, norm_v,
):
    rank = lax.axis_index("head")
    place = lax.axis_index("dp")
    own_rows = segments.shape[0] // 2
    segments = lax.dynamic_slice_in_dim(segments, rank * own_rows, own_rows, axis=0)
    counts = lax.dynamic_slice_in_dim(counts, rank * own_rows, own_rows, axis=0)
    width = norm_w.shape[1]
    groups = groups_of(size)
    attn_lines = fold_pairs(attn_w.astype(bf16))[None]
    mlp_lines = mlp_w.astype(bf16)[None]
    for near, far in zip(groups[:-1], groups[:0:-1]):
        found, more = start_group(attn_lines, size, *far), start_group(mlp_lines, size, *near)
        attn_lines, mlp_lines = finish_stack(found, *far), finish_group(more, *near)
    _, early = after((attn_lines, mlp_lines), (tokens, grad_out))
    found = start_group(attn_lines, size, *groups[0])
    (normed, normed_t, out_grad_t), found = after(first_norm(*early, norm_w, own_rows), found)
    attn_lines = finish_stack(found, *groups[0])
    attn_use = join_weights(attn_lines, swap(attn_lines, "head", 2, 1), rank, attn_w.shape[0])
    found = start_group(mlp_lines, size, *groups[-1])
    conv_low = conv_w.astype(bf16)
    conv_use = join_columns(conv_low, swap(conv_low, "head", 2, 1), rank)
    starts, classes, images = attention_plan(segments, WIDE_TILE)
    back_starts, back_classes, _ = attention_plan(segments, TILE)
    middle, qkv, context, ext = attn_forward(starts, classes, counts, tokens, normed, attn_use, images)
    middle, found = after(middle, found)
    mlp_lines = finish_group(found, *groups[-1])
    mlp_lines = jnp.moveaxis(mlp_lines, 0, 1).reshape(mlp_w.shape[0], -1, mlp_w.shape[2])
    rank_at = rank.astype(jnp.int32).reshape(1)
    output, grad_middle, held, send, grad_conv, grad_norm_two = mlp_layer(
        line_places(segments), rank_at, middle, grad_out, out_grad_t, mlp_lines, swap(mlp_lines, "head", 2, 1),
        spread_taps(conv_use), norm_w,
    )

    def back(first, count, so_far):
        return attn_backward(
            first, count, so_far, back_starts, back_classes, counts, rank_at, normed_t, grad_middle, qkv, context, ext, attn_use, images
        )

    columns = conv_w.shape[1]
    norm_two = jnp.sum(grad_norm_two.reshape(2, 8, width), axis=1).reshape(1, 2 * width)
    norm_two = jnp.pad(norm_two, ((0, 0), (0, columns - 2 * width)))
    taps = grad_conv[:9]
    small = jnp.concatenate([half_columns(taps, rank), norm_two])
    small_send = jnp.concatenate([half_columns(taps, 1 - rank), norm_two])
    got = swap(jnp.concatenate([flat(send), two_parts(small_send)], axis=0), "head", 2, 1)
    first_rows = max(1, own_rows // 3)
    so_far, got = after(back(0, first_rows, None), got)
    rows = held.size // columns
    held = by_line(held + got[:rows].reshape(held.shape).astype(f32), size)
    small = from_parts(two_parts(small)) + from_parts(got[rows:])
    low, count = groups[0]
    pieces = pieces_of(held, low, count)
    small_parts = two_parts(small)
    gots = [
        swap(jnp.concatenate([flat(pieces[step]), small_parts], axis=0), "dp", size, step * low) for step in range(1, count)
    ]
    so_far, pieces = after(so_far, pieces)
    projected_grad, attn_held, attn_send = back(first_rows, own_rows - first_rows, so_far)

    def take(pieces, gots, small_parts, low, count):
        keep = pieces[0]
        rows = keep.size // keep.shape[-1]
        for got in gots:
            keep = keep + got[:rows].reshape(keep.shape).astype(f32)
        ordered = in_order([small_parts] + [got[rows:] for got in gots], (place // low) % count)
        return keep, sum(from_parts(part) for part in ordered)

    attn_got = swap(flat(attn_send), "head", 2, 1)
    attn_held, gots = after(attn_held, gots)
    held, small = take(pieces, gots, small_parts, low, count)
    rest = bits_of(size)[2:]
    attn_held = by_line(attn_held + attn_got.reshape(attn_held.shape).astype(f32), size)
    waiting = list(groups)
    blocks = tokens.shape[0] // FILL
    fills = [(0, blocks // 2), (blocks // 2, blocks - blocks // 2)]
    grad_tokens, grad_norm_one = None, 0.0
    while waiting or rest:
        attn_pieces, pieces, extra = [None], None, None
        if waiting:
            low, count = waiting.pop(0)
            attn_pieces = pieces_of(attn_held, low, count)
        sent = {step * low: [flat(attn_pieces[step])] for step in range(1, len(attn_pieces))}
        bit = None
        if rest:
            bit = rest.pop(0)
            pieces = pieces_of(held, bit, 2)
            small_parts = two_parts(small)
            extra = jnp.concatenate([flat(pieces[1]), small_parts], axis=0).reshape(-1, attn_held.shape[-1])
            sent.setdefault(bit, []).append(extra)
        fill = fills.pop(0) if fills else None
        if fill:
            sent, projected_grad = after(sent, projected_grad)
        gots = {step: swap(jnp.concatenate(parts, axis=0), "dp", size, step) for step, parts in sent.items()}
        if fill:
            results = tokens_back(*fill, grad_tokens, projected_grad, tokens, grad_middle, attn_use, norm_w)
            (grad_tokens, norm_one), gots = after(results, gots)
            grad_norm_one = grad_norm_one + norm_one
        if bit:
            got = gots[bit][gots[bit].shape[0] - extra.shape[0] :].reshape(-1, columns)
            held, small = take(pieces, [got], small_parts, bit, 2)
        if attn_pieces[0] is not None:
            attn_held = attn_pieces[0]
            rows = attn_held.size // attn_held.shape[-1]
            for step in range(1, len(attn_pieces)):
                attn_held = attn_held + gots[step * low][:rows].reshape(attn_held.shape).astype(f32)
    grad_attn = unfold_pairs(attn_held.reshape(attn_held.shape[:1] + attn_held.shape[2:]))
    grad_mlp = held.reshape(mlp_w.shape)
    norm_two = small[9, : 2 * width].reshape(2, width)

    weights, firsts, seconds = [attn_w, mlp_w, conv_w], [attn_m, mlp_m, conv_m], [attn_v, mlp_v, conv_v]
    scalars = pl.BlockSpec(memory_space=pltpu.SMEM)
    vectors = pl.BlockSpec(memory_space=pltpu.VMEM)
    results = pl.pallas_call(
        moments_kernel,
        in_specs=[scalars] + [vectors] * 13,
        out_specs=[vectors] * 10,
        out_shape=like(weights) * 3 + [jax.ShapeDtypeStruct((8, width), f32)],
        compiler_params=pltpu.CompilerParams(vmem_limit_bytes=16 * MIB),
    )(place.astype(jnp.int32).reshape(1), grad_norm_one, grad_attn, grad_mlp, small[:9], *weights, *firsts, *seconds)
    new_firsts, new_seconds, updates, sums = results[:3], results[3:6], results[6:9], results[9]
    new_w = pl.pallas_call(
        apply_kernel,
        in_specs=[vectors] * 11,
        out_specs=[vectors] * 6,
        out_shape=like(weights) + like([norm_w] * 3),
        compiler_params=pltpu.CompilerParams(vmem_limit_bytes=16 * MIB),
    )(sum_everywhere(sums, size), norm_two, norm_w, norm_m, norm_v, *weights, *updates)
    return (
        output, grad_tokens, new_w[0], new_firsts[0], new_seconds[0], new_w[1], new_firsts[1], new_seconds[1],
        new_w[2], new_firsts[2], new_seconds[2], *new_w[3:],
    )


def solution(mesh):
    rows, lines = P(("dp", "head"), None), P("dp", None)
    shards, columns = P(None, "dp", "head"), P(None, "head")
    in_specs = (rows, rows, lines, P("dp")) + (shards,) * 6 + (columns,) * 3 + (P(),) * 3
    out_specs = (rows, rows) + (shards,) * 6 + (columns,) * 3 + (P(),) * 3
    return jax.shard_map(
        functools.partial(body, mesh.shape["dp"]), mesh=mesh, in_specs=in_specs, out_specs=out_specs, check_vma=False
    )
```
